32 devices in a mesh: dp: 8 (over z, x), section: 4 (over y, core).
Axes of the slice: x: 2, y: 2, z: 4, core: 2. Of those that a mesh axis runs over, the one named last changes fastest.
Arguments:
- latents: float32 [16, 32, 32, 4], P('dp'), may hold values from -6 to 6
- noise: float32 [16, 32, 32, 4], P('dp'), may hold values from -6 to 6
- timesteps: int32 [16], P('dp'), may hold values from 0 to 999
- labels: int32 [16], P('dp'), may hold values from 0 to 999
- null_mask: int32 [16], P('dp'), may hold values 0 or 1
- valid: int32 [16], P('dp'), may hold values from 0 to 1, as said below
- mod_w: float32 [4, 1152, 3456], P('section', 'dp'), may hold values from -0.1875 to 0.1875
- mod_m: float32 [4, 1152, 3456], P('section', 'dp'), may hold values from -1 to 1
- mod_e: float32 [4, 1152, 3456], P('section', 'dp'), may hold values from -0.1875 to 0.1875
- block_w: float32 [4, 1152, 4608], P('section', 'dp'), may hold values from -2 to 2
- block_m: float32 [4, 1152, 4608], P('section', 'dp'), may hold values from -1 to 1
- block_e: float32 [4, 1152, 4608], P('section', 'dp'), may hold values from -0.1875 to 0.1875
- down_w: float32 [2, 4608, 1152], P(None, None, 'dp'), may hold values from -0.09375 to 0.09375
- down_m: float32 [2, 4608, 1152], P(None, None, 'dp'), may hold values from -1 to 1
- down_e: float32 [2, 4608, 1152], P(None, None, 'dp'), may hold values from -0.09375 to 0.09375
- stem_w: float32 [2425, 1152], P(None, 'dp'), may hold values from -1 to 1
- stem_m: float32 [2425, 1152], P(None, 'dp'), may hold values from -1 to 1
- stem_e: float32 [2425, 1152], P(None, 'dp'), may hold values from -0.1875 to 0.1875
- tail_w: float32 [1152, 2336], P('dp'), may hold values from -0.1875 to 0.1875
- tail_m: float32 [1152, 2336], P('dp'), may hold values from -1 to 1
- tail_e: float32 [1152, 2336], P('dp'), may hold values from -0.1875 to 0.1875
- biases: float32 [40352], replicated, may hold values from -3 to 5
- bias_m: float32 [40352], replicated, may hold values from -1 to 1
- bias_e: float32 [40352], replicated, may hold values from -3 to 3
Outputs:
- loss_sum: float32 [], replicated
- count: float32 [], replicated
- grad_norm: float32 [], replicated
- mod_new: float32 [4, 1152, 3456], P('section', 'dp')
- mod_mom: float32 [4, 1152, 3456], P('section', 'dp')
- mod_avg: float32 [4, 1152, 3456], P('section', 'dp')
- mod_half: bfloat16 [4, 1152, 3456], P('section', 'dp')
- block_new: float32 [4, 1152, 4608], P('section', 'dp')
- block_mom: float32 [4, 1152, 4608], P('section', 'dp')
- block_avg: float32 [4, 1152, 4608], P('section', 'dp')
- block_half: bfloat16 [4, 1152, 4608], P('section', 'dp')
- down_new: float32 [2, 4608, 1152], P(None, None, 'dp')
- down_mom: float32 [2, 4608, 1152], P(None, None, 'dp')
- down_avg: float32 [2, 4608, 1152], P(None, None, 'dp')
- down_half: bfloat16 [2, 4608, 1152], P(None, None, 'dp')
- stem_new: float32 [2425, 1152], P(None, 'dp')
- stem_mom: float32 [2425, 1152], P(None, 'dp')
- stem_avg: float32 [2425, 1152], P(None, 'dp')
- stem_half: bfloat16 [2425, 1152], P(None, 'dp')
- tail_new: float32 [1152, 2336], P('dp')
- tail_mom: float32 [1152, 2336], P('dp')
- tail_avg: float32 [1152, 2336], P('dp')
- tail_half: bfloat16 [1152, 2336], P('dp')
- bias_new: float32 [40352], replicated
- bias_mom: float32 [40352], replicated
- bias_avg: float32 [40352], replicated
- bias_half: bfloat16 [40352], replicated
The draws below stay inside these ranges and needn't reach their ends.
Inputs may be any that keep to these rules, and one draw needn't show every extreme that they name: `valid`: an image of the i-th of n indices of dp counts with chance (1 + 2 i / (n - 1)) / 3; every image of the last index counts.
All inputs are finite; a program needn't handle non-finite values. No bound on the sum of `null_mask` on one device may be relied on, other than what follows from the above.
Results may differ from the reference program's by a relative error of at most 0.0095.
Values may be sent and summed in bfloat16 or wider, within the bound.
A program may use at most 1.125 GiB of HBM per device.

```python
import math
import jax
import jax.numpy as jnp
from jax import lax

HEADS = 16
HEAD_DIM = 72
D = 1152
FF = 4608
NCLS = 1001
FREQ = 256
GRID = 32
PATCHES = 256
PATCH_IN = 16
HEAD_OUT = 32
LAYERS = 2
IMG_DEV = 2
IMAGES = 16
STEM_ROWS = 2425
NBIAS = 40352
N_DP = 8
N_SECTION = 4


clip_limit = 0.02


def bounded_normal(key, shape):
    return jnp.clip(jax.random.normal(key, shape, jnp.float32), -4.0, 4.0)


def moment_scale():
    total = N_SECTION * 7 * D * D + LAYERS * FF * D + STEM_ROWS * D + D * (2 * D + HEAD_OUT) + NBIAS
    return 1.1 * clip_limit / math.sqrt(total)


def draw_valid(key, part):
    key = jax.random.fold_in(key, 1)
    devices = IMAGES // IMG_DEV
    span = max(devices - 1, 1)
    place = jnp.arange(IMAGES, dtype=jnp.int32) // IMG_DEV
    roll = jax.random.randint(key, (IMAGES,), 0, 3 * span)
    return (roll < span + 2 * place).astype(jnp.int32)


def draw_block_w(key, part):
    key = jax.random.fold_in(key, 2)
    slots = (jnp.arange(N_SECTION) % 2 == 0)[:, None, None]
    columns = (jnp.arange(4 * D) < 3 * D)[None, None, :]
    scale = jnp.where(slots, jnp.where(columns, 0.6, 3.0), 1.0) * D ** (-0.5)
    return bounded_normal(key, (N_SECTION, D, 4 * D)) * scale


def draw_stem_w(key, part):
    key = jax.random.fold_in(key, 3)
    rows = jnp.arange(STEM_ROWS)
    scale = jnp.where(rows < NCLS, 0.2, jnp.where(rows < NCLS + PATCH_IN, PATCH_IN ** (-0.5), jnp.where(rows < NCLS + PATCH_IN + FREQ, FREQ ** (-0.5), D ** (-0.5))))
    return bounded_normal(key, (STEM_ROWS, D)) * scale[:, None]


def draw_biases(key, part):
    key = jax.random.fold_in(key, 4)
    noise_all = bounded_normal(key, (NBIAS,))
    ramp = jnp.arange(D, dtype=jnp.float32) / (D - 1)
    empty = jnp.zeros((D,), jnp.float32)
    level_mod = jnp.concatenate([empty, 2.0 * ramp, 0.3 + 1.2 * ramp])
    level = jnp.concatenate([jnp.tile(level_mod, N_SECTION), jnp.zeros((21 * D,), jnp.float32), empty, 2.0 * ramp, jnp.zeros((HEAD_OUT,), jnp.float32)])
    spread_mod = jnp.concatenate([jnp.full((D,), 0.4), jnp.full((2 * D,), 0.2)])
    spread = jnp.concatenate([jnp.tile(spread_mod, N_SECTION), jnp.full((21 * D,), 0.1), jnp.full((D,), 0.4), jnp.full((D,), 0.2), jnp.full((HEAD_OUT,), 0.3)])
    return level + spread * noise_all


def draw_mod_m(key, part):
    key = jax.random.fold_in(key, 11)
    return bounded_normal(key, (N_SECTION, D, 3 * D)) * moment_scale()


def draw_block_m(key, part):
    key = jax.random.fold_in(key, 12)
    return bounded_normal(key, (N_SECTION, D, 4 * D)) * moment_scale()


def draw_down_m(key, part):
    key = jax.random.fold_in(key, 13)
    return bounded_normal(key, (LAYERS, FF, D)) * moment_scale()


def draw_stem_m(key, part):
    key = jax.random.fold_in(key, 14)
    return bounded_normal(key, (STEM_ROWS, D)) * moment_scale()


def draw_tail_m(key, part):
    key = jax.random.fold_in(key, 15)
    return bounded_normal(key, (D, 2 * D + HEAD_OUT)) * moment_scale()


def draw_bias_m(key, part):
    key = jax.random.fold_in(key, 16)
    return bounded_normal(key, (NBIAS,)) * (3.0 * moment_scale())


def set_ends(drawn, own_key, least, largest):
    longest = drawn.shape.index(max(drawn.shape))
    spots = []
    for shift in (0, 1):
        where = [jax.random.randint(jax.random.fold_in(own_key, axis), (), 0, length) for axis, length in enumerate(drawn.shape)]
        where[longest] = (where[longest] + shift) % drawn.shape[longest]
        spots.append(tuple(where))
    return drawn.at[spots[0]].set(least).at[spots[1]].set(largest)


def block_levels(rng, extent, pieces, least, high):
    loudness, own = 1.0, jax.random.fold_in(rng, 6)
    for position, blocks in pieces:
        heights = jnp.exp(jax.random.uniform(jax.random.fold_in(own, position), (blocks,), jnp.float32, least / len(pieces), high / len(pieces)))
        loudness = loudness * jnp.repeat(heights, extent[position] // blocks).reshape([-1 if axis == position else 1 for axis in range(len(extent))])
    return loudness


def bell_draw(rng, dims, deviation, limit, cuts=(), kind=jnp.bfloat16):
    values = deviation * jax.random.normal(rng, dims, jnp.float32)
    if cuts:
        values = values * block_levels(rng, dims, cuts, -0.22, 0.18)
    return jnp.clip(values, -limit, limit).astype(kind)


def setup_inputs(seed: int = 0) -> dict:
    arg_keys = jax.random.split(jax.random.key(seed), 25)
    latents = bell_draw(arg_keys[0], (IMAGES, GRID, GRID, 4), 1.0, 6.0, ((0, 8),), jnp.float32)
    noise = bell_draw(arg_keys[1], (IMAGES, GRID, GRID, 4), 1.0, 6.0, ((0, 8),), jnp.float32)
    timesteps = set_ends(jax.random.randint(arg_keys[2], (IMAGES,), 0, 1000), jax.random.fold_in(arg_keys[2], 1), 0, 999).astype(jnp.int32)
    labels = set_ends(jax.random.randint(arg_keys[3], (IMAGES,), 0, NCLS - 1), jax.random.fold_in(arg_keys[3], 1), 0, (NCLS - 1) - 1).astype(jnp.int32)
    null_mask = set_ends((jax.random.randint(arg_keys[4], (IMAGES,), 0, 10) < 1).astype(jnp.int32), jax.random.fold_in(arg_keys[4], 1), 0, 1)
    valid = draw_valid(jax.random.fold_in(arg_keys[24], 71), 0)
    mod_w = bell_draw(arg_keys[6], (N_SECTION, D, 3 * D), D ** -0.5, 0.1875, ((0, 4), (1, 8)), jnp.float32)
    mod_m = draw_mod_m(jax.random.fold_in(arg_keys[24], 71), 0)
    mod_e = bell_draw(arg_keys[8], (N_SECTION, D, 3 * D), D ** -0.5, 0.1875, ((0, 4), (1, 8)), jnp.float32)
    block_w = draw_block_w(jax.random.fold_in(arg_keys[24], 71), 0)
    block_m = draw_block_m(jax.random.fold_in(arg_keys[24], 71), 0)
    block_e = bell_draw(arg_keys[11], (N_SECTION, D, 4 * D), D ** -0.5, 0.1875, ((0, 4), (1, 8)), jnp.float32)
    down_w = bell_draw(arg_keys[12], (LAYERS, FF, D), FF ** -0.5, 0.09375, ((2, 8),), jnp.float32)
    down_m = draw_down_m(jax.random.fold_in(arg_keys[24], 71), 0)
    down_e = bell_draw(arg_keys[14], (LAYERS, FF, D), FF ** -0.5, 0.09375, ((2, 8),), jnp.float32)
    stem_w = draw_stem_w(jax.random.fold_in(arg_keys[24], 71), 0)
    stem_m = draw_stem_m(jax.random.fold_in(arg_keys[24], 71), 0)
    stem_e = bell_draw(arg_keys[17], (STEM_ROWS, D), D ** -0.5, 0.1875, ((1, 8),), jnp.float32)
    tail_w = bell_draw(arg_keys[18], (D, 2 * D + HEAD_OUT), D ** -0.5, 0.1875, ((0, 8),), jnp.float32)
    tail_m = draw_tail_m(jax.random.fold_in(arg_keys[24], 71), 0)
    tail_e = bell_draw(arg_keys[20], (D, 2 * D + HEAD_OUT), D ** -0.5, 0.1875, ((0, 8),), jnp.float32)
    biases = draw_biases(jax.random.fold_in(arg_keys[24], 71), 0)
    bias_m = draw_bias_m(jax.random.fold_in(arg_keys[24], 71), 0)
    bias_e = bell_draw(arg_keys[23], (NBIAS,), 0.5, 3.0, (), jnp.float32)
    return {"latents": latents, "noise": noise, "timesteps": timesteps, "labels": labels, "null_mask": null_mask, "valid": valid, "mod_w": mod_w, "mod_m": mod_m, "mod_e": mod_e, "block_w": block_w, "block_m": block_m, "block_e": block_e, "down_w": down_w, "down_m": down_m, "down_e": down_e, "stem_w": stem_w, "stem_m": stem_m, "stem_e": stem_e, "tail_w": tail_w, "tail_m": tail_m, "tail_e": tail_e, "biases": biases, "bias_m": bias_m, "bias_e": bias_e}


highest = lax.Precision.HIGHEST
epsilon_norm = 1e-06
momentum_rate = 0.9
ema_decay = 0.9
learn_rate = 4000.0
clip_limit = 0.02

@jax.custom_vjp
def low(v):
    return lax.optimization_barrier(v.astype(jnp.bfloat16)).astype(jnp.float32)

@jax.custom_vjp
def low_back(v):
    return v

def low_keep(v):
    return (low(v), None)

def low_pass(kept, grad):
    return (grad,)

def back_keep(v):
    return (v, None)

def back_low(kept, grad):
    return (low(grad),)
low.defvjp(low_keep, low_pass)
low_back.defvjp(back_keep, back_low)

def matmul_high(left, right):
    return jnp.matmul(left, right, precision=highest)

def round_trip(value):
    return low_back(low(value))

def layer_modulate(tokens, shift, scale):
    centered = tokens - lax.optimization_barrier(jnp.mean(tokens, axis=-1, keepdims=True))
    normed = centered * lax.rsqrt(lax.optimization_barrier(jnp.mean(centered * centered, axis=-1, keepdims=True)) + epsilon_norm)
    return normed * (1.0 + scale[:, None]) + shift[:, None]

def patchify(field):
    images, side = (field.shape[0], field.shape[1] // 2)
    return field.reshape(images, side, 2, side, 2, 4).transpose(0, 1, 3, 2, 4, 5).reshape(images, side * side, 16)

def sincos_rows(places, width):
    omega = 1.0 / 10000.0 ** (jnp.arange(width // 2, dtype=jnp.float32) / (width // 2))
    angle = places[:, None] * omega[None, :]
    return jnp.concatenate([jnp.sin(angle), jnp.cos(angle)], axis=1)

def position_table(side, width):
    index = jnp.arange(side * side, dtype=jnp.int32)
    column = (index % side).astype(jnp.float32)
    row = (index // side).astype(jnp.float32)
    return jnp.concatenate([sincos_rows(column, width // 2), sincos_rows(row, width // 2)], axis=1)

def time_features(steps):
    half = FREQ // 2
    freqs = jnp.exp(-math.log(10000.0) * jnp.arange(half, dtype=jnp.float32) / half)
    angle = steps[:, None] * freqs[None, :]
    return jnp.concatenate([jnp.cos(angle), jnp.sin(angle)], axis=1)

def noise_levels(steps):
    level = jnp.cos((steps / 1000.0 + 0.008) / 1.008 * (math.pi / 2)) ** 2
    return (jnp.sqrt(level), jnp.sqrt(1.0 - level))

def modulation(cond, weight, bias):
    return low_back(matmul_high(low(jax.nn.silu(cond)), low(weight)) + bias)

def attention_layer(x, cond, wmod, bmod, wblk, bblk):
    mod = modulation(cond, wmod, bmod)
    shift, scale, gate = (mod[:, :D], mod[:, D:2 * D], mod[:, 2 * D:])
    xm = low(layer_modulate(x, shift, scale))
    images, length = (x.shape[0], x.shape[1])
    qkv = round_trip(matmul_high(xm, low(wblk[:, :3 * D])) + bblk[:3 * D])
    parts = qkv.reshape(images, length, 3, HEADS, HEAD_DIM)
    scores = low_back(jnp.einsum('bqhd,bkhd->bhqk', parts[:, :, 0], parts[:, :, 1], precision=highest) * HEAD_DIM ** (-0.5))
    probs = low(jax.nn.softmax(scores, axis=-1))
    attended = round_trip(jnp.einsum('bhqk,bkhd->bqhd', probs, parts[:, :, 2], precision=highest).reshape(images, length, D))
    branch = low_back(matmul_high(attended, low(wblk[:, 3 * D:])) + bblk[3 * D:])
    return x + gate[:, None] * branch

def mlp_layer(x, cond, wmod, bmod, wup, bup, wdown, bdown):
    mod = modulation(cond, wmod, bmod)
    shift, scale, gate = (mod[:, :D], mod[:, D:2 * D], mod[:, 2 * D:])
    xm = low(layer_modulate(x, shift, scale))
    pre = low_back(matmul_high(xm, low(wup)) + bup)
    act = low(jax.nn.gelu(pre, approximate=True))
    branch = low_back(matmul_high(act, low(wdown)) + bdown)
    return x + gate[:, None] * branch

def group_loss(params, data, loss_scale):
    mod_w, block_w, down_w, stem_w, tail_w, biases = params
    lat, noi, steps, labs, nulls, vals = data
    steps_f = steps.astype(jnp.float32)
    signal, spread = noise_levels(steps_f)
    signal = signal[:, None, None, None]
    spread = spread[:, None, None, None]
    tokens = patchify(signal * lat + spread * noi)
    target = jnp.concatenate([patchify(signal * noi - spread * lat), patchify(noi)], axis=2)
    table = stem_w[:NCLS]
    wpatch = stem_w[NCLS:NCLS + PATCH_IN]
    wone = stem_w[NCLS + PATCH_IN:NCLS + PATCH_IN + FREQ]
    wtwo = stem_w[NCLS + PATCH_IN + FREQ:]
    x = low_back(matmul_high(low(tokens), low(wpatch)) + biases[30 * D:31 * D]) + position_table(GRID // 2, D)[None]
    pre = low_back(matmul_high(low(time_features(steps_f)), low(wone)) + biases[31 * D:32 * D])
    temb = matmul_high(low(jax.nn.silu(pre)), low(wtwo)) + biases[32 * D:33 * D]
    classes = jnp.where(nulls > 0, NCLS - 1, labs)
    cond = low_back(temb + jnp.take(low(table), classes, axis=0))
    cond_one = round_trip(cond)
    cond_two = round_trip(cond_one)
    cond_three = round_trip(cond_two)
    conds = (cond, cond_one, cond_two, cond_three)
    for slot in range(N_SECTION):
        if slot > 0:
            x = round_trip(x)
        bmod = biases[3 * D * slot:3 * D * (slot + 1)]
        bblk = biases[12 * D + 4 * D * slot:12 * D + 4 * D * (slot + 1)]
        if slot % 2 == 0:
            x = attention_layer(x, conds[slot], mod_w[slot], bmod, block_w[slot], bblk)
        else:
            layer = slot // 2
            bdown = biases[28 * D + D * layer:28 * D + D * (layer + 1)]
            x = mlp_layer(x, conds[slot], mod_w[slot], bmod, block_w[slot], bblk, down_w[layer], bdown)
    fmod = low_back(matmul_high(low(jax.nn.silu(cond_three)), low(tail_w[:, :2 * D])) + biases[33 * D:35 * D])
    xf = low(layer_modulate(x, fmod[:, :D], fmod[:, D:]))
    pred = low_back(matmul_high(xf, low(tail_w[:, 2 * D:])) + biases[35 * D:])
    error = pred - target
    loss = jnp.sum(vals.astype(jnp.float32)[:, None, None] * error * error)
    return (loss * loss_scale, loss)

def nesterov(weight, moment, average, grad, factor):
    clipped = grad * factor
    moment_new = momentum_rate * moment + clipped
    weight_new = weight - learn_rate * (clipped + momentum_rate * moment_new)
    average_new = ema_decay * average + (1.0 - ema_decay) * weight_new
    return (weight_new, moment_new, average_new, weight_new.astype(jnp.bfloat16))

def reference(latents, noise, timesteps, labels, null_mask, valid, mod_w, mod_m, mod_e, block_w, block_m, block_e, down_w, down_m, down_e, stem_w, stem_m, stem_e, tail_w, tail_m, tail_e, biases, bias_m, bias_e):
    count = jnp.sum(valid.astype(jnp.float32))
    loss_scale = 1.0 / (count * PATCHES * HEAD_OUT)
    groups = tuple((value.reshape((N_DP, IMG_DEV) + value.shape[1:]) for value in (latents, noise, timesteps, labels, null_mask, valid)))

    def total(params):

        def one(data):
            return group_loss(params, data, loss_scale)
        scaled, raw = lax.map(jax.checkpoint(one), groups)
        return (jnp.sum(scaled), jnp.sum(raw))
    params = (mod_w, block_w, down_w, stem_w, tail_w, biases)
    unused, pull, loss_sum = jax.vjp(total, params, has_aux=True)
    grads = pull(jnp.ones((), jnp.float32))[0]
    squares = jnp.zeros((), jnp.float32)
    for grad in grads:
        squares = squares + jnp.sum(grad * grad)
    grad_norm = jnp.sqrt(squares)
    factor = jnp.minimum(1.0, clip_limit / (grad_norm + 1e-06))
    mod_new, mod_mom, mod_avg, mod_half = nesterov(mod_w, mod_m, mod_e, grads[0], factor)
    block_new, block_mom, block_avg, block_half = nesterov(block_w, block_m, block_e, grads[1], factor)
    down_new, down_mom, down_avg, down_half = nesterov(down_w, down_m, down_e, grads[2], factor)
    stem_new, stem_mom, stem_avg, stem_half = nesterov(stem_w, stem_m, stem_e, grads[3], factor)
    tail_new, tail_mom, tail_avg, tail_half = nesterov(tail_w, tail_m, tail_e, grads[4], factor)
    bias_new, bias_mom, bias_avg, bias_half = nesterov(biases, bias_m, bias_e, grads[5], factor)
    return (loss_sum, count, grad_norm, mod_new, mod_mom, mod_avg, mod_half, block_new, block_mom, block_avg, block_half, down_new, down_mom, down_avg, down_half, stem_new, stem_mom, stem_avg, stem_half, tail_new, tail_mom, tail_avg, tail_half, bias_new, bias_mom, bias_avg, bias_half)
```

```python
from functools import partial
import math

import jax
import jax.numpy as jnp
from jax import lax
from jax.experimental import pallas as pl
from jax.experimental.pallas import tpu as pltpu
from jax.sharding import PartitionSpec as P

HEADS = 16
HEAD_DIM = 72
D = 1152
FF = 4608
HALF = FF // 2
NCLS = 1001
FREQ = 256
GRID = 32
PATCHES = 256
PATCH_IN = 16
HEAD_OUT = 32
LAYERS = 2
NBIAS = 40352


epsilon_norm = 1e-06
momentum_rate = 0.9
ema_decay = 0.9
learn_rate = 4000.0
clip_limit = 0.02
MESH = pl.DeviceIdType.MESH
BF = jnp.bfloat16


def matmul(left, right):
    return jnp.dot(left, right, preferred_element_type=jnp.float32)


def matmul_nt(left, right):
    return lax.dot_general(
        left, right, (((1,), (1,)), ((), ())), preferred_element_type=jnp.float32
    )


def matmul_tn(left, right):
    return lax.dot_general(
        left, right, (((0,), (0,)), ((), ())), preferred_element_type=jnp.float32
    )


def to_half(value):
    return value.astype(BF)


def column_sums(value):
    return jnp.sum(value.astype(jnp.float32), axis=0)


def silu_back(value, grad):
    return jax.vjp(jax.nn.silu, value)[1](grad)[0]


def layer_modulate(tokens, shift, scale):
    centered = tokens - jnp.mean(tokens, axis=-1, keepdims=True)
    normed = centered * lax.rsqrt(
        jnp.mean(centered * centered, axis=-1, keepdims=True) + epsilon_norm
    )
    return normed * (1.0 + scale) + shift


def patchify(field):
    images, side = (field.shape[0], field.shape[1] // 2)
    return (
        field.reshape(images, side, 2, side, 2, 4)
        .transpose(0, 1, 3, 2, 4, 5)
        .reshape(images, side * side, 16)
    )


def sincos_rows(places, width):
    omega = 1.0 / 10000.0 ** (jnp.arange(width // 2, dtype=jnp.float32) / (width // 2))
    angle = places[:, None] * omega[None, :]
    return jnp.concatenate([jnp.sin(angle), jnp.cos(angle)], axis=1)


def position_table(side, width):
    line = sincos_rows(jnp.arange(side, dtype=jnp.float32), width // 2)
    column = jnp.broadcast_to(line[None], (side, side, width // 2))
    row = jnp.broadcast_to(line[:, None], (side, side, width // 2))
    return jnp.concatenate([column, row], axis=2).reshape(side * side, width)


def time_features(steps):
    half = FREQ // 2
    freqs = jnp.exp(-math.log(10000.0) * jnp.arange(half, dtype=jnp.float32) / half)
    angle = steps[:, None] * freqs[None, :]
    return jnp.concatenate([jnp.cos(angle), jnp.sin(angle)], axis=1)


def noise_levels(steps):
    level = jnp.cos((steps / 1000.0 + 0.008) / 1.008 * (math.pi / 2)) ** 2
    return (jnp.sqrt(level), jnp.sqrt(1.0 - level))


Z, X = 4, 2
PART = 48
GATHER_CHUNKS = ((0, 0, False), (0, 48, False), (0, 96, False), (1, 0, False), (1, 48, False), (1, 96, True))


def ring_fits(n, rows):
    return n == Z * X and rows == 144


def gather_kernel(blk_ref, dn_ref, out_blk, out_dn, up_sem, down_sem, x_sem, sib_sem, recv_sem, sib_recv, own_sem):
    me = lax.axis_index("dp")
    section = lax.axis_index("section")
    z, x = me // X, lax.rem(me, X)
    core = lax.rem(section, 2)
    sibling = section + 1 - 2 * core
    across = me + 1 - 2 * x
    chunks = len(GATHER_CHUNKS)
    has_up, has_down = z < Z - 1, z > 0

    barrier = pltpu.get_barrier_semaphore()
    pl.semaphore_signal(barrier, 1, device_id={"section": sibling}, device_id_type=MESH)
    pl.semaphore_signal(barrier, 1, device_id={"dp": across}, device_id_type=MESH)

    @pl.when(has_up)
    def _():
        pl.semaphore_signal(barrier, 1, device_id={"dp": me + X}, device_id_type=MESH)

    @pl.when(has_down)
    def _():
        pl.semaphore_signal(barrier, 1, device_id={"dp": me - X}, device_id_type=MESH)

    pl.semaphore_wait(barrier, 2 + has_up.astype(jnp.int32) + has_down.astype(jnp.int32))

    def place(owner, k, side):
        which, first, unused = GATHER_CHUNKS[k]
        rows = pl.ds(pl.multiple_of(owner * 144 + first, 16), PART)
        return (out_dn if which else out_blk).at[side, rows]

    def source(owner, k, mine):
        if not mine:
            return place(owner, k, core)
        which, first, unused = GATHER_CHUNKS[k]
        return (dn_ref if which else blk_ref).at[pl.ds(first, PART)]

    def copy(owner, k, mine, sem, target):
        unit = owner * chunks + k
        return pltpu.make_async_remote_copy(
            src_ref=source(owner, k, mine),
            dst_ref=place(owner, k, core),
            send_sem=sem.at[unit],
            recv_sem=recv_sem.at[unit],
            device_id={"dp": target},
            device_id_type=MESH,
        )

    def to_sibling(owner, k, mine):
        unit = owner * chunks + k
        return pltpu.make_async_remote_copy(
            src_ref=source(owner, k, mine),
            dst_ref=place(owner, k, core),
            send_sem=sib_sem.at[unit],
            recv_sem=sib_recv.at[unit],
            device_id={"section": sibling},
            device_id_type=MESH,
        )

    def own_copy(k):
        return pltpu.make_async_copy(source(me, k, True), place(me, k, core), own_sem.at[k])

    def arrived(owner, k):
        copy(owner, k, False, x_sem, across).wait_recv()

    for k in range(chunks):
        @pl.when(has_up)
        def _():
            copy(me, k, True, up_sem, me + X).start()

        @pl.when(has_down)
        def _():
            copy(me, k, True, down_sem, me - X).start()

        copy(me, k, True, x_sem, across).start()
        own_copy(k).start()
        to_sibling(me, k, True).start()

    def along(step, k, first_across):
        shift = 1 - 2 * x if first_across else 0
        crosses = (not first_across) and (not GATHER_CHUNKS[k][2])

        @pl.when(z >= step)
        def _():
            owner = me - X * step + shift
            arrived(owner, k)

            @pl.when(has_up)
            def _():
                copy(owner, k, False, up_sem, me + X).start()

            if crosses:
                copy(owner, k, False, x_sem, across).start()
            to_sibling(owner, k, False).start()

        @pl.when(z + step < Z)
        def _():
            owner = me + X * step + shift
            arrived(owner, k)

            @pl.when(has_down)
            def _():
                copy(owner, k, False, down_sem, me - X).start()

            if crosses:
                copy(owner, k, False, x_sem, across).start()
            to_sibling(owner, k, False).start()

    def crossed(step, k):
        direct = GATHER_CHUNKS[k][2]
        if step == 0:
            owner = across
            arrived(owner, k)
            if direct:
                @pl.when(has_up)
                def _():
                    copy(owner, k, False, up_sem, me + X).start()

                @pl.when(has_down)
                def _():
                    copy(owner, k, False, down_sem, me - X).start()
            to_sibling(owner, k, False).start()
        elif not direct:
            for sign in (-1, 1):
                @pl.when((z >= step) if sign < 0 else (z + step < Z))
                def _():
                    owner = across + sign * X * step
                    arrived(owner, k)
                    to_sibling(owner, k, False).start()

    for step in range(1, Z + 1):
        for k in range(chunks):
            if step < Z:
                along(step, k, False)
            crossed(step - 1, k)
            if step < Z and GATHER_CHUNKS[k][2]:
                along(step, k, True)

    for k in range(chunks):
        direct = GATHER_CHUNKS[k][2]
        own_copy(k).wait()
        for column in range(2):
            base = me if column == 0 else across
            for step in range(0, Z):
                for sign in (-1, 1) if step else (1,):
                    @pl.when((z >= step) if sign < 0 else (z + step < Z))
                    def _():
                        owner = base + sign * X * step
                        mine = column == 0 and step == 0
                        to_sibling(owner, k, mine).wait_send()
                        pltpu.make_async_remote_copy(
                            src_ref=place(owner, k, 1 - core),
                            dst_ref=place(owner, k, 1 - core),
                            send_sem=sib_sem.at[owner * chunks + k],
                            recv_sem=sib_recv.at[owner * chunks + k],
                            device_id={"section": sibling},
                            device_id_type=MESH,
                        ).wait_recv()
                        runs = column == 0 or direct
                        if runs and (step == 0 or sign < 0):
                            @pl.when(has_up)
                            def _():
                                copy(owner, k, mine, up_sem, me + X).wait_send()
                        if runs and (step == 0 or sign > 0):
                            @pl.when(has_down)
                            def _():
                                copy(owner, k, mine, down_sem, me - X).wait_send()
                        if column == 0 and (step == 0 or not direct):
                            copy(owner, k, mine, x_sem, across).wait_send()


def gather_weights(blk, dn):
    n = lax.axis_size("dp")
    if not ring_fits(n, blk.shape[0]):
        blk_all = lax.all_gather(blk, "dp", axis=0, tiled=True)
        dn_all = lax.all_gather(dn, "dp", axis=0, tiled=True)
        pairs = [(k, k ^ 1) for k in range(lax.axis_size("section"))]
        blk_sib, dn_sib = lax.ppermute((blk_all, dn_all), "section", pairs)
        even = lax.rem(lax.axis_index("section"), 2) == 0
        both = lambda a, b: jnp.where(even, jnp.stack([a, b]), jnp.stack([b, a]))
        return (both(blk_all, blk_sib), both(dn_all, dn_sib))
    units = n * len(GATHER_CHUNKS)
    return pl.pallas_call(
        gather_kernel,
        out_shape=(
            jax.ShapeDtypeStruct((2, D, FF), BF),
            jax.ShapeDtypeStruct((2, D, HALF), BF),
        ),
        in_specs=[pl.BlockSpec(memory_space=pl.ANY)] * 2,
        out_specs=(pl.BlockSpec(memory_space=pl.ANY),) * 2,
        scratch_shapes=[pltpu.SemaphoreType.DMA((units,))] * 6
        + [pltpu.SemaphoreType.DMA((len(GATHER_CHUNKS),))],
        compiler_params=pltpu.CompilerParams(collective_id=0, has_side_effects=True),
        name="gather_weights",
    )(blk, dn)


SUM_CHUNKS = ((1, 0, False), (1, 48, False), (1, 96, True), (0, 0, False), (0, 48, False), (0, 96, False))
VMEM_BYTES = 60 * 1024 * 1024


def sum_kernel(
    g_ref, gd_ref, blk_out, dn_out,
    own_b, own_d, other_d, xb, xd, xq, up_b, up_d, up_o, down_b, down_d, down_o, acc,
    load_sem, x_send, x_recv, up_send, up_recv, down_send, down_recv, sib_send, sib_recv, y_send, y_recv,
):
    me = lax.axis_index("dp")
    section = lax.axis_index("section")
    z, x = me // X, lax.rem(me, X)
    core = lax.rem(section, 2)
    sibling = section + 1 - 2 * core
    facing = lax.rem(section + 2, 4)
    across = me + 1 - 2 * x
    chunks = len(SUM_CHUNKS)
    has_up, has_down = z < Z - 1, z > 0

    barrier = pltpu.get_barrier_semaphore()
    for target in ({"section": sibling}, {"section": facing}, {"dp": across}):
        pl.semaphore_signal(barrier, 1, device_id=target, device_id_type=MESH)

    @pl.when(has_up)
    def _():
        pl.semaphore_signal(barrier, 1, device_id={"dp": me + X}, device_id_type=MESH)

    @pl.when(has_down)
    def _():
        pl.semaphore_signal(barrier, 1, device_id={"dp": me - X}, device_id_type=MESH)

    def each(distance, run):
        if distance == 0:
            run(z, None)
            return

        @pl.when(z + distance < Z)
        def _():
            run(z + distance, True)

        @pl.when(z >= distance)
        def _():
            run(z - distance, False)

    def hbm(k, zz, column):
        which, first, unused = SUM_CHUNKS[k]
        rows = pl.ds(pl.multiple_of((zz * X + column) * 144 + first, 16), PART)
        return (gd_ref if which else g_ref).at[rows]

    def own(k, zz):
        which, first, unused = SUM_CHUNKS[k]
        return (own_d if which else own_b).at[zz, pl.ds(first, PART)]

    def from_x(k, zz):
        which, first, direct = SUM_CHUNKS[k]
        if direct:
            return xq
        return (xd if which else xb).at[zz, pl.ds(first, PART)]

    def from_z(k, zz, up, other):
        which, first, unused = SUM_CHUNKS[k]
        if other:
            return (up_o if up else down_o).at[zz]
        if which:
            return (up_d if up else down_d).at[zz, pl.ds(first, PART)]
        return (up_b if up else down_b).at[zz, pl.ds(first, PART)]

    def load(k, zz, other=False):
        index = ((chunks if other else 0) + k) * Z + zz
        return pltpu.make_async_copy(
            hbm(k, zz, (1 - x) if other else x),
            other_d.at[zz] if other else own(k, zz),
            load_sem.at[index],
        )

    def x_copy(k, zz, src):
        unit = k * Z + zz
        return pltpu.make_async_remote_copy(
            src_ref=src, dst_ref=from_x(k, zz), send_sem=x_send.at[unit], recv_sem=x_recv.at[unit],
            device_id={"dp": across}, device_id_type=MESH,
        )

    def z_copy(k, zz, up, other):
        unit = ((chunks if other else 0) + k) * Z + zz
        return pltpu.make_async_remote_copy(
            src_ref=other_d.at[zz] if other else own(k, zz),
            dst_ref=from_z(k, zz, up, other),
            send_sem=(up_send if up else down_send).at[unit],
            recv_sem=(up_recv if up else down_recv).at[unit],
            device_id={"dp": me + X if up else me - X},
            device_id_type=MESH,
        )

    def dn_copy(k, slot, to_sib):
        rows = pl.ds(SUM_CHUNKS[k][1], PART)
        unit = slot * chunks + k
        return pltpu.make_async_remote_copy(
            src_ref=dn_out.at[slot, rows], dst_ref=dn_out.at[slot, rows],
            send_sem=(sib_send if to_sib else y_send).at[unit],
            recv_sem=(sib_recv if to_sib else y_recv).at[unit],
            device_id={"section": sibling if to_sib else facing},
            device_id_type=MESH,
        )

    def total(dst, srcs):
        @pl.loop(0, PART // 16)
        def _(step):
            rows = pl.ds(pl.multiple_of(step * 16, 16), 16)
            value = srcs[0][rows].astype(jnp.float32)
            for src in srcs[1:]:
                value = value + src[rows].astype(jnp.float32)
            dst[rows] = value.astype(dst.dtype)

    for k in range(chunks):
        for distance in (3, 2, 1, 0):
            def run(zz, up):
                load(k, zz).start()
                if SUM_CHUNKS[k][2]:
                    load(k, zz, True).start()
            each(distance, run)

    pl.semaphore_wait(barrier, 3 + has_up.astype(jnp.int32) + has_down.astype(jnp.int32))

    for which in (1, 0):
        for distance in (3, 2, 1, 0):
            for k in range(chunks):
                if SUM_CHUNKS[k][0] == which and not SUM_CHUNKS[k][2]:
                    each(distance, lambda zz, up: x_copy(k, zz, hbm(k, zz, 1 - x)).start())

    def pass_on(k, distance):
        def run(zz, up):
            behind = has_down if up else has_up
            if SUM_CHUNKS[k][2]:
                for other in (False, True):
                    mine = other_d.at[zz] if other else own(k, zz)
                    load(k, zz, other).wait()

                    @pl.when(behind)
                    def _():
                        z_copy(k, zz, up, other).wait_recv()
                        total(mine, [mine, from_z(k, zz, up, other)])

                    z_copy(k, zz, up, other).start()
                return
            load(k, zz).wait()
            x_copy(k, zz, hbm(k, zz, 1 - x)).wait_recv()

            @pl.when(behind)
            def _():
                z_copy(k, zz, up, False).wait_recv()
                total(own(k, zz), [own(k, zz), from_x(k, zz), from_z(k, zz, up, False)])

            @pl.when(jnp.logical_not(behind))
            def _():
                total(own(k, zz), [own(k, zz), from_x(k, zz)])

            z_copy(k, zz, up, False).start()
        each(distance, run)

    def add_z(dst, k, other):
        @pl.when(has_down)
        def _():
            z_copy(k, z, True, other).wait_recv()
            total(dst, [dst, from_z(k, z, True, other)])

        @pl.when(has_up)
        def _():
            z_copy(k, z, False, other).wait_recv()
            total(dst, [dst, from_z(k, z, False, other)])

    def send_direct(k):
        load(k, z, True).wait()
        acc[...] = other_d[z].astype(jnp.float32)
        add_z(acc, k, True)
        other_d[z] = acc[...].astype(BF)
        x_copy(k, z, other_d.at[z]).start()

    def finish(k):
        which, first, direct = SUM_CHUNKS[k]
        rows = pl.ds(first, PART)
        dst = acc if which else blk_out.at[rows]
        load(k, z).wait()
        if direct:
            total(dst, [own(k, z)])
            add_z(dst, k, False)
            x_copy(k, z, other_d.at[z]).wait_recv()
            total(dst, [dst, from_x(k, z)])
        else:
            x_copy(k, z, hbm(k, z, 1 - x)).wait_recv()
            total(dst, [own(k, z), from_x(k, z)])
            add_z(dst, k, False)
        if which:
            total(dn_out.at[section, rows], [acc])
            dn_copy(k, section, True).start()
            dn_copy(k, section, False).start()

    dn_chunks = [k for k in range(chunks) if SUM_CHUNKS[k][0]]
    blk_chunks = [k for k in range(chunks) if not SUM_CHUNKS[k][0]]
    for distance in (3, 2, 1):
        for k in dn_chunks:
            pass_on(k, distance)
    for k in blk_chunks:
        pass_on(k, 3)
    for k in dn_chunks:
        if SUM_CHUNKS[k][2]:
            send_direct(k)
    for k in dn_chunks:
        finish(k)
    for k in blk_chunks:
        pass_on(k, 2)
    for k in dn_chunks:
        dn_copy(k, facing, False).wait_recv()
        dn_copy(k, facing, True).start()
    for k in blk_chunks:
        pass_on(k, 1)
    for k in blk_chunks:
        finish(k)

    for k in range(chunks):
        direct = SUM_CHUNKS[k][2]
        for distance in (3, 2, 1, 0):
            def run(zz, up):
                if not direct:
                    x_copy(k, zz, hbm(k, zz, 1 - x)).wait_send()
                elif distance == 0:
                    x_copy(k, zz, other_d.at[zz]).wait_send()
                if distance:
                    z_copy(k, zz, up, False).wait_send()
                    if direct:
                        z_copy(k, zz, up, True).wait_send()
            each(distance, run)
        if SUM_CHUNKS[k][0]:
            dn_copy(k, section, True).wait_send()
            dn_copy(k, section, False).wait_send()
            dn_copy(k, facing, True).wait_send()
            dn_copy(k, sibling, True).wait_recv()
            dn_copy(k, lax.rem(sibling + 2, 4), True).wait_recv()


def sum_gradients(g_blk, g_dn):
    n = lax.axis_size("dp")
    if not ring_fits(n, D // n):
        blk = lax.psum_scatter(g_blk, "dp", scatter_dimension=0, tiled=True)
        dn = lax.psum_scatter(g_dn, "dp", scatter_dimension=0, tiled=True)
        return (blk.astype(jnp.float32), lax.all_gather(dn, "section"))
    chunks = len(SUM_CHUNKS)
    dma = lambda count: pltpu.SemaphoreType.DMA((count,))
    ring_b = pltpu.VMEM((Z, 144, FF), BF)
    ring_d = pltpu.VMEM((Z, 144, HALF), BF)
    ring_o = pltpu.VMEM((Z, PART, HALF), BF)
    vmem = pl.BlockSpec(memory_space=pltpu.VMEM)
    return pl.pallas_call(
        sum_kernel,
        out_shape=(
            jax.ShapeDtypeStruct((144, FF), jnp.float32),
            jax.ShapeDtypeStruct((4, 144, HALF), BF),
        ),
        in_specs=[pl.BlockSpec(memory_space=pl.ANY)] * 2,
        out_specs=(vmem, vmem),
        scratch_shapes=[
            ring_b, ring_d, ring_o, ring_b, pltpu.VMEM((Z, 96, HALF), BF), pltpu.VMEM((PART, HALF), BF),
            ring_b, ring_d, ring_o, ring_b, ring_d, ring_o, pltpu.VMEM((PART, HALF), jnp.float32),
            dma(2 * chunks * Z), dma(chunks * Z), dma(chunks * Z),
            dma(2 * chunks * Z), dma(2 * chunks * Z), dma(2 * chunks * Z), dma(2 * chunks * Z),
            dma(4 * chunks), dma(4 * chunks), dma(4 * chunks), dma(4 * chunks),
        ],
        compiler_params=pltpu.CompilerParams(
            collective_id=1, has_side_effects=True, vmem_limit_bytes=VMEM_BYTES
        ),
        name="sum_gradients",
    )(g_blk, g_dn)


def heads_of(value):
    return value.reshape(PATCHES, HEADS, HEAD_DIM)


def attention_forward(xm_half, wblk, bblk):
    qkv = to_half(matmul(xm_half, wblk[:, : 3 * D]) + bblk[: 3 * D])
    parts = qkv.reshape(PATCHES, 3, HEADS, HEAD_DIM)
    scores = jnp.einsum(
        "qhd,khd->hqk", parts[:, 0], parts[:, 1], preferred_element_type=jnp.float32
    ) * HEAD_DIM ** (-0.5)
    probs = jax.nn.softmax(scores, axis=-1)
    attended = to_half(
        jnp.einsum("hqk,khd->qhd", to_half(probs), parts[:, 2], preferred_element_type=jnp.float32)
    ).reshape(PATCHES, D)
    branch = matmul(attended, wblk[:, 3 * D :]) + bblk[3 * D :]
    return (branch, (parts, probs, attended))


def attention_backward(grad_half, saved, wblk):
    parts, probs, attended = saved
    d_att = heads_of(to_half(matmul_nt(grad_half, wblk[:, 3 * D :])))
    d_value = jnp.einsum(
        "hqk,qhd->khd", to_half(probs), d_att, preferred_element_type=jnp.float32
    )
    d_probs = jnp.einsum("qhd,khd->hqk", d_att, parts[:, 2], preferred_element_type=jnp.float32)
    d_scores = to_half(probs * (d_probs - jnp.sum(probs * d_probs, axis=-1, keepdims=True)))
    d_query = jnp.einsum(
        "hqk,khd->qhd", d_scores, parts[:, 1], preferred_element_type=jnp.float32
    ) * HEAD_DIM ** (-0.5)
    d_key = jnp.einsum(
        "hqk,qhd->khd", d_scores, parts[:, 0], preferred_element_type=jnp.float32
    ) * HEAD_DIM ** (-0.5)
    d_qkv = to_half(jnp.stack([d_query, d_key, d_value], axis=1).reshape(PATCHES, 3 * D))
    return (matmul_nt(d_qkv, wblk[:, : 3 * D]), d_qkv)


def modulated(x, mod):
    return layer_modulate(x, mod[None, :D], mod[None, D : 2 * D])


def modulated_back(x, mod, d_xm):
    pull = jax.vjp(layer_modulate, x, mod[None, :D], mod[None, D : 2 * D])[1]
    d_x, d_shift, d_scale = pull(d_xm)
    return (d_x, d_shift[0], d_scale[0])


def stage_forward(x_in, weights):
    mod_a, mod_m, w_blk, w_dn, b_attn, b_up, b_down = weights
    xm_a = to_half(modulated(x_in, mod_a))
    branch_a, saved = attention_forward(xm_a, w_blk[0], b_attn)
    x_mid = to_half(x_in + mod_a[None, 2 * D :] * branch_a).astype(jnp.float32)
    xm_m = to_half(modulated(x_mid, mod_m))
    pre = matmul(xm_m, w_blk[1]) + b_up
    act = to_half(jax.nn.gelu(pre, approximate=True))
    branch_m = matmul_nt(act[:, :HALF], w_dn[0]) + matmul_nt(act[:, HALF:], w_dn[1]) + b_down
    x_out = x_mid + mod_m[None, 2 * D :] * branch_m
    return (x_out, (xm_a, branch_a, saved, x_mid, xm_m, pre, act, branch_m))


def mlp_backward(d_out, weights, kept):
    mod_a, mod_m, w_blk, w_dn, b_attn, b_up, b_down = weights
    xm_a, branch_a, saved, x_mid, xm_m, pre, act, branch_m = kept
    d_gate = jnp.sum(d_out * branch_m, axis=0)
    grad_half = to_half(d_out * mod_m[None, 2 * D :])
    d_act = jnp.concatenate([matmul(grad_half, w_dn[0]), matmul(grad_half, w_dn[1])], axis=1)
    d_pre = to_half(jax.vjp(partial(jax.nn.gelu, approximate=True), pre)[1](d_act)[0])
    d_x, d_shift, d_scale = modulated_back(x_mid, mod_m, matmul_nt(d_pre, w_blk[1]))
    d_mod = to_half(jnp.concatenate([d_shift, d_scale, d_gate]))
    return (to_half(d_out + d_x).astype(jnp.float32), d_mod, grad_half, d_pre)


def attn_backward(d_out, x_in, weights, kept):
    mod_a, mod_m, w_blk, w_dn, b_attn, b_up, b_down = weights
    xm_a, branch_a, saved, x_mid, xm_m, pre, act, branch_m = kept
    d_gate = jnp.sum(d_out * branch_a, axis=0)
    grad_half = to_half(d_out * mod_a[None, 2 * D :])
    d_xm, d_qkv = attention_backward(grad_half, saved, w_blk[0])
    d_x, d_shift, d_scale = modulated_back(x_in, mod_a, d_xm)
    d_mod = to_half(jnp.concatenate([d_shift, d_scale, d_gate]))
    return (to_half(d_out + d_x), d_mod, grad_half, d_qkv)


def final_step(x_out, fmod, w_head, b_head, target, counts, loss_scale):
    xf_half = to_half(modulated(x_out, fmod))
    error = matmul(xf_half, w_head) + b_head - target
    loss = counts * jnp.sum(error * error)
    d_pred = to_half(2.0 * loss_scale * counts * error)
    g_head = matmul_tn(xf_half, d_pred)
    d_x, d_shift, d_scale = modulated_back(x_out, fmod, matmul_nt(d_pred, w_head))
    return (loss, d_x, to_half(jnp.concatenate([d_shift, d_scale])), g_head, column_sums(d_pred))


def nesterov(weight, moment, average, grad, factor):
    clipped = grad * factor
    moment_new = momentum_rate * moment + clipped
    weight_new = weight - learn_rate * (clipped + momentum_rate * moment_new)
    average_new = ema_decay * average + (1.0 - ema_decay) * weight_new
    return (weight_new, moment_new, average_new, weight_new.astype(jnp.bfloat16))


def swap(array, by):
    peers = lax.axis_size("section")
    return lax.ppermute(array, "section", [(k, k ^ by) for k in range(peers)])


def pick(parts, index):
    return lax.dynamic_index_in_dim(parts, index, 0, keepdims=False)


def body(
    latents, noise, timesteps, labels, null_mask, valid,
    mod_w, mod_m, mod_e, block_w, block_m, block_e, down_w, down_m, down_e,
    stem_w, stem_m, stem_e, tail_w, tail_m, tail_e, biases, bias_m, bias_e,
):
    place = lax.axis_index("dp")
    section = lax.axis_index("section")
    stage = section // 2
    core = lax.rem(section, 2)
    even = core == 0
    n = lax.axis_size("dp")
    width = D // n

    downs = jnp.swapaxes(down_w, 1, 2)
    blk_half = to_half(block_w[0])
    dn_half = to_half(lax.dynamic_slice(downs, (stage, 0, core * HALF), (1, width, HALF))[0])
    w_blk, w_dn = gather_weights(blk_half, dn_half)

    stems = stem_w.T
    classes_own = jnp.where(null_mask > 0, NCLS - 1, labels)
    meta = lax.all_gather(jnp.stack([timesteps, classes_own, valid], axis=1), "dp", axis=0, tiled=True)
    images = meta.shape[0]
    steps_all = meta[:, 0].astype(jnp.float32)
    picks = (meta[:, 1][:, None] == jnp.arange(NCLS, dtype=jnp.int32)[None, :]).astype(BF)
    count = jnp.sum(meta[:, 2].astype(jnp.float32))
    loss_scale = 1.0 / (count * PATCHES * HEAD_OUT)
    freq = to_half(time_features(steps_all))

    stem_half = to_half(stems)
    table = stem_half[:, :NCLS]
    w_patch = stem_half[:, NCLS : NCLS + PATCH_IN]
    w_one = stem_half[:, NCLS + PATCH_IN : NCLS + PATCH_IN + FREQ]
    w_two = stem_half[:, NCLS + PATCH_IN + FREQ :]
    b_one = lax.dynamic_slice_in_dim(biases, 31 * D + place * width, width)
    b_two = lax.dynamic_slice_in_dim(biases, 32 * D + place * width, width)
    hidden_pre = matmul_nt(w_one, freq) + b_one[:, None]
    hidden = to_half(jax.nn.silu(hidden_pre))
    tail_half = to_half(tail_w)
    small = jnp.concatenate([hidden, w_patch, tail_half[:, 2 * D :]], axis=1)
    small = lax.all_gather(small, "dp", axis=0, tiled=True)
    hidden_all = small[:, :images]
    w_patch_all = small[:, images : images + PATCH_IN]
    w_head_all = small[:, images + PATCH_IN :]
    cond = matmul(w_two, hidden_all) + b_two[:, None] + matmul_nt(table, picks)
    cond_low = to_half(cond).astype(jnp.float32)
    cond_own = jnp.where(section == 0, cond, cond_low)
    silu_own = to_half(jax.nn.silu(cond_own))
    silu_low = to_half(jax.nn.silu(cond_low))
    mod_half_w = to_half(mod_w[0])
    part_mod = matmul_tn(silu_own, mod_half_w)
    part_fm = matmul_tn(silu_low, tail_half[:, : 2 * D])
    parts = jnp.concatenate([part_mod, part_fm], axis=1).reshape(n, images // n, 5 * D)
    mods = jnp.sum(lax.all_to_all(parts, "dp", 0, 0), axis=0)
    own_mod = mods[:, : 3 * D]
    sib_mod = swap(own_mod, 1)
    mod_a = pick(jnp.where(even, own_mod, sib_mod), core)
    mod_b = pick(jnp.where(even, sib_mod, own_mod), core)
    bias_of = lambda first, length: lax.dynamic_slice_in_dim(biases, first, length)
    mod_a = mod_a + bias_of(6 * D * stage, 3 * D)
    mod_b = mod_b + bias_of(6 * D * stage + 3 * D, 3 * D)
    fmod = pick(mods[:, 3 * D :], core) + biases[33 * D : 35 * D]
    weights = (
        mod_a, mod_b, w_blk, w_dn,
        bias_of(12 * D + 8 * D * stage, 4 * D),
        bias_of(16 * D + 8 * D * stage, 4 * D),
        bias_of(28 * D + D * stage, D),
    )

    step = pick(timesteps, core).astype(jnp.float32)
    signal, spread = noise_levels(step)
    lat, noi = pick(latents, core)[None], pick(noise, core)[None]
    counts = pick(valid, core).astype(jnp.float32)
    tok_half = to_half(patchify(signal * lat + spread * noi))[0]
    target = jnp.concatenate([patchify(signal * noi - spread * lat), patchify(noi)], axis=2)[0]
    x_first = matmul_nt(tok_half, w_patch_all) + biases[30 * D : 31 * D] + position_table(GRID // 2, D)

    x_hop = swap(to_half(stage_forward(x_first, weights)[0]), 2)
    x_in = jnp.where(stage == 0, x_first, x_hop.astype(jnp.float32))
    x_out, kept = stage_forward(x_in, weights)
    loss, d_final, d_fmod, g_head, b_head = final_step(
        x_out, fmod, w_head_all, biases[35 * D :], target, counts, loss_scale
    )
    d_mid = mlp_backward(d_final, weights, kept)[0]
    d_hop = swap(attn_backward(d_mid, x_in, weights, kept)[0], 2)
    d_out = jnp.where(stage == 1, d_final, d_hop.astype(jnp.float32))
    d_mid, d_mod_b, d_branch_b, d_pre = mlp_backward(d_out, weights, kept)
    d_first, d_mod_a, d_branch_a, d_qkv = attn_backward(d_mid, x_in, weights, kept)
    xm_a, branch_a, saved, x_mid, xm_b, pre, act, branch_b = kept
    attended = saved[2]

    act_own = jnp.where(even, act[:, :HALF], act[:, HALF:])
    act_sib, branch_sib = swap((jnp.where(even, act[:, HALF:], act[:, :HALF]), d_branch_b), 1)
    g_dn = to_half(matmul_tn(d_branch_b, act_own) + matmul_tn(branch_sib, act_sib))
    d_attn = jnp.concatenate([d_qkv, d_branch_a], axis=1)
    left_sib, last_sib, right_sib = swap(
        (
            jnp.where(even, xm_b, xm_a),
            jnp.where(even, xm_b, attended),
            jnp.where(even, d_pre, d_attn),
        ),
        1,
    )
    left = jnp.concatenate([jnp.where(even, xm_a, xm_b), left_sib], axis=0)
    last = jnp.concatenate([jnp.where(even, attended, xm_b), last_sib], axis=0)
    right = jnp.concatenate([jnp.where(even, d_attn, d_pre), right_sib], axis=0)
    g_blk = jnp.concatenate(
        [
            to_half(matmul_tn(left, right[:, : 3 * D])),
            to_half(matmul_tn(last, right[:, 3 * D :])),
        ],
        axis=1,
    )
    g_blk, g_dn = sum_gradients(g_blk, g_dn)

    last_stage = (stage == 1).astype(jnp.float32)
    first_stage = (stage == 0).astype(jnp.float32)
    d_mod_sib = swap(jnp.where(even, d_mod_b, d_mod_a), 1)
    d_mod_own = jnp.where(even, d_mod_a, d_mod_b)
    d_fmod = jnp.where(stage == 1, d_fmod, jnp.zeros_like(d_fmod))
    d_fmod_sib = swap(d_fmod, 1)
    pair = lambda own, sib: jnp.where(even, jnp.stack([own, sib]), jnp.stack([sib, own]))
    d_fmods = pair(d_fmod, d_fmod_sib)
    d_fmods = d_fmods + swap(d_fmods, 2)
    d_mods = jnp.concatenate([pair(d_mod_own, d_mod_sib), d_fmods], axis=1)
    d_mods = lax.all_gather(d_mods, "dp", axis=0, tiled=True)
    d_mod_all, d_fm_all = d_mods[:, : 3 * D], d_mods[:, 3 * D :]
    g_mod = matmul(silu_own, d_mod_all)
    g_fm = matmul(silu_low, d_fm_all)
    c_own = silu_back(cond_own, matmul_nt(mod_half_w, d_mod_all))
    c_fm = silu_back(cond_low, matmul_nt(tail_half[:, : 2 * D], d_fm_all))
    c_all = lax.all_gather(c_own, "section")
    d_cond = to_half(c_all[3] + c_fm)
    for slot in (2, 1, 0):
        d_cond = to_half(d_cond.astype(jnp.float32) + c_all[slot])
    part_hidden = matmul_tn(w_two, d_cond).reshape(n, width, images)
    d_hidden = jnp.sum(lax.all_to_all(part_hidden, "dp", 0, 0), axis=0)
    d_pre_one = to_half(silu_back(hidden_pre, d_hidden))
    g_table = matmul(d_cond, picks)
    g_one = matmul(d_pre_one, freq)
    g_two = matmul_nt(d_cond, hidden_all)

    row_sums = lambda value: jnp.sum(value.astype(jnp.float32), axis=1)
    anchor = (place == 0).astype(jnp.float32)
    corner = anchor * (section == 0).astype(jnp.float32)
    once = (section == 0).astype(jnp.float32)
    vector = jnp.zeros((NBIAS,), jnp.float32)
    put = lambda vector, piece, start: lax.dynamic_update_slice_in_dim(vector, piece, start, 0)
    vector = put(vector, anchor * column_sums(d_mod_all), 3 * D * section)
    vector = put(
        vector,
        jnp.concatenate([column_sums(d_qkv), column_sums(d_branch_a), column_sums(d_pre)]),
        12 * D + 8 * D * stage,
    )
    vector = put(vector, column_sums(d_branch_b), 28 * D + D * stage)
    vector = put(vector, first_stage * column_sums(d_first), 30 * D)
    vector = put(vector, once * row_sums(d_pre_one), 31 * D + place * width)
    vector = put(vector, once * row_sums(d_cond), 32 * D + place * width)
    vector = put(vector, corner * column_sums(d_fm_all), 33 * D)
    vector = put(vector, last_stage * b_head, 35 * D)
    g_patch = first_stage * matmul_tn(d_first, tok_half)
    ends = jnp.concatenate([g_patch, last_stage * g_head], axis=1)
    ends = lax.psum_scatter(ends, "dp", scatter_dimension=0, tiled=True)
    vector = jnp.concatenate([vector, (last_stage * loss)[None]])
    vector = lax.psum(vector, ("dp", "section"))
    ends = lax.psum(ends, "section")
    bias_grad, loss_sum = vector[:NBIAS], vector[NBIAS]
    g_stem = jnp.concatenate([g_table, ends[:, :PATCH_IN], g_one, g_two], axis=1)
    g_tail = jnp.concatenate([g_fm, ends[:, PATCH_IN:]], axis=1)
    g_dn = g_dn.astype(jnp.float32)
    down_both = jnp.stack(
        [jnp.concatenate([g_dn[0], g_dn[1]], axis=1), jnp.concatenate([g_dn[2], g_dn[3]], axis=1)]
    )

    square = lambda value: jnp.sum(value * value)
    squares = square(g_mod) + square(g_blk)
    squares = squares + once * (square(down_both) + square(g_stem) + square(g_tail))
    squares = squares + corner * square(bias_grad)
    grad_norm = jnp.sqrt(lax.psum(squares, ("dp", "section")))
    factor = jnp.minimum(1.0, clip_limit / (grad_norm + 1e-06))
    mod_out = nesterov(mod_w, mod_m, mod_e, g_mod[None], factor)
    block_out = nesterov(block_w, block_m, block_e, g_blk[None], factor)
    flip = lambda value: jnp.swapaxes(value, 1, 2)
    down_out = tuple(map(flip, nesterov(downs, flip(down_m), flip(down_e), down_both, factor)))
    stem_out = tuple(value.T for value in nesterov(stems, stem_m.T, stem_e.T, g_stem, factor))
    tail_out = nesterov(tail_w, tail_m, tail_e, g_tail, factor)
    bias_out = nesterov(biases, bias_m, bias_e, bias_grad, factor)
    return (
        (loss_sum, count, grad_norm)
        + mod_out + block_out + down_out + stem_out + tail_out + bias_out
    )


def solution(mesh):
    images = (P("dp", None, None, None),) * 2 + (P("dp"),) * 4
    owned = P("section", "dp", None)
    states = (owned,) * 6 + (P(None, None, "dp"),) * 3 + (P(None, "dp"),) * 3 + (P("dp", None),) * 3 + (P(),) * 3
    updates = (owned,) * 8 + (P(None, None, "dp"),) * 4 + (P(None, "dp"),) * 4 + (P("dp", None),) * 4 + (P(),) * 4
    return jax.shard_map(
        body,
        mesh=mesh,
        in_specs=images + states,
        out_specs=(P(), P(), P()) + updates,
        check_vma=False,
    )
```

```python
from functools import partial
import math

import jax
import jax.numpy as jnp
from jax import lax
from jax.experimental import pallas as pl
from jax.experimental.pallas import tpu as pltpu
from jax.sharding import PartitionSpec as P

HEADS = 16
HEAD_DIM = 72
D = 1152
FF = 4608
HALF = FF // 2
NCLS = 1001
FREQ = 256
GRID = 32
PATCHES = 256
PATCH_IN = 16
HEAD_OUT = 32
LAYERS = 2
NBIAS = 40352


epsilon_norm = 1e-06
momentum_rate = 0.9
ema_decay = 0.9
learn_rate = 4000.0
clip_limit = 0.02
MESH = pl.DeviceIdType.MESH
BF = jnp.bfloat16


def matmul(left, right):
    return jnp.dot(left, right, preferred_element_type=jnp.float32)


def matmul_nt(left, right):
    return lax.dot_general(
        left, right, (((1,), (1,)), ((), ())), preferred_element_type=jnp.float32
    )


def matmul_tn(left, right):
    return lax.dot_general(
        left, right, (((0,), (0,)), ((), ())), preferred_element_type=jnp.float32
    )


def to_half(value):
    return value.astype(BF)


def column_sums(value):
    return jnp.sum(value.astype(jnp.float32), axis=0)


def silu_back(value, grad):
    return jax.vjp(jax.nn.silu, value)[1](grad)[0]


def layer_modulate(tokens, shift, scale):
    centered = tokens - jnp.mean(tokens, axis=-1, keepdims=True)
    normed = centered * lax.rsqrt(
        jnp.mean(centered * centered, axis=-1, keepdims=True) + epsilon_norm
    )
    return normed * (1.0 + scale) + shift


def patchify(field):
    images, side = (field.shape[0], field.shape[1] // 2)
    return (
        field.reshape(images, side, 2, side, 2, 4)
        .transpose(0, 1, 3, 2, 4, 5)
        .reshape(images, side * side, 16)
    )


def sincos_rows(places, width):
    omega = 1.0 / 10000.0 ** (jnp.arange(width // 2, dtype=jnp.float32) / (width // 2))
    angle = places[:, None] * omega[None, :]
    return jnp.concatenate([jnp.sin(angle), jnp.cos(angle)], axis=1)


def position_table(side, width):
    line = sincos_rows(jnp.arange(side, dtype=jnp.float32), width // 2)
    column = jnp.broadcast_to(line[None], (side, side, width // 2))
    row = jnp.broadcast_to(line[:, None], (side, side, width // 2))
    return jnp.concatenate([column, row], axis=2).reshape(side * side, width)


def time_features(steps):
    half = FREQ // 2
    freqs = jnp.exp(-math.log(10000.0) * jnp.arange(half, dtype=jnp.float32) / half)
    angle = steps[:, None] * freqs[None, :]
    return jnp.concatenate([jnp.cos(angle), jnp.sin(angle)], axis=1)


def noise_levels(steps):
    level = jnp.cos((steps / 1000.0 + 0.008) / 1.008 * (math.pi / 2)) ** 2
    return (jnp.sqrt(level), jnp.sqrt(1.0 - level))


Z, X = 4, 2
PART = 48
GATHER_CHUNKS = ((0, 0, False), (0, 48, False), (0, 96, False), (1, 0, False), (1, 48, False), (1, 96, True))


def ring_fits(n, rows):
    return n == Z * X and rows == 144


def gather_kernel(blk_ref, dn_ref, out_blk, out_dn, up_sem, down_sem, x_sem, sib_sem, recv_sem, sib_recv, own_sem):
    me = lax.axis_index("dp")
    section = lax.axis_index("section")
    z, x = me // X, lax.rem(me, X)
    core = lax.rem(section, 2)
    sibling = section + 1 - 2 * core
    across = me + 1 - 2 * x
    chunks = len(GATHER_CHUNKS)
    has_up, has_down = z < Z - 1, z > 0

    barrier = pltpu.get_barrier_semaphore()
    pl.semaphore_signal(barrier, 1, device_id={"section": sibling}, device_id_type=MESH)
    pl.semaphore_signal(barrier, 1, device_id={"dp": across}, device_id_type=MESH)

    @pl.when(has_up)
    def _():
        pl.semaphore_signal(barrier, 1, device_id={"dp": me + X}, device_id_type=MESH)

    @pl.when(has_down)
    def _():
        pl.semaphore_signal(barrier, 1, device_id={"dp": me - X}, device_id_type=MESH)

    pl.semaphore_wait(barrier, 2 + has_up.astype(jnp.int32) + has_down.astype(jnp.int32))

    def place(owner, k, side):
        which, first, unused = GATHER_CHUNKS[k]
        rows = pl.ds(pl.multiple_of(owner * 144 + first, 16), PART)
        return (out_dn if which else out_blk).at[side, rows]

    def source(owner, k, mine):
        if not mine:
            return place(owner, k, core)
        which, first, unused = GATHER_CHUNKS[k]
        return (dn_ref if which else blk_ref).at[pl.ds(first, PART)]

    def copy(owner, k, mine, sem, target):
        unit = owner * chunks + k
        return pltpu.make_async_remote_copy(
            src_ref=source(owner, k, mine),
            dst_ref=place(owner, k, core),
            send_sem=sem.at[unit],
            recv_sem=recv_sem.at[unit],
            device_id={"dp": target},
            device_id_type=MESH,
        )

    def to_sibling(owner, k, mine):
        unit = owner * chunks + k
        return pltpu.make_async_remote_copy(
            src_ref=source(owner, k, mine),
            dst_ref=place(owner, k, core),
            send_sem=sib_sem.at[unit],
            recv_sem=sib_recv.at[unit],
            device_id={"section": sibling},
            device_id_type=MESH,
        )

    def own_copy(k):
        return pltpu.make_async_copy(source(me, k, True), place(me, k, core), own_sem.at[k])

    def arrived(owner, k):
        copy(owner, k, False, x_sem, across).wait_recv()

    for k in range(chunks):
        @pl.when(has_up)
        def _():
            copy(me, k, True, up_sem, me + X).start()

        @pl.when(has_down)
        def _():
            copy(me, k, True, down_sem, me - X).start()

        copy(me, k, True, x_sem, across).start()
        own_copy(k).start()
        to_sibling(me, k, True).start()

    def along(step, k, first_across):
        shift = 1 - 2 * x if first_across else 0
        crosses = (not first_across) and (not GATHER_CHUNKS[k][2])

        @pl.when(z >= step)
        def _():
            owner = me - X * step + shift
            arrived(owner, k)

            @pl.when(has_up)
            def _():
                copy(owner, k, False, up_sem, me + X).start()

            if crosses:
                copy(owner, k, False, x_sem, across).start()
            to_sibling(owner, k, False).start()

        @pl.when(z + step < Z)
        def _():
            owner = me + X * step + shift
            arrived(owner, k)

            @pl.when(has_down)
            def _():
                copy(owner, k, False, down_sem, me - X).start()

            if crosses:
                copy(owner, k, False, x_sem, across).start()
            to_sibling(owner, k, False).start()

    def crossed(step, k):
        direct = GATHER_CHUNKS[k][2]
        if step == 0:
            owner = across
            arrived(owner, k)
            if direct:
                @pl.when(has_up)
                def _():
                    copy(owner, k, False, up_sem, me + X).start()

                @pl.when(has_down)
                def _():
                    copy(owner, k, False, down_sem, me - X).start()
            to_sibling(owner, k, False).start()
        elif not direct:
            for sign in (-1, 1):
                @pl.when((z >= step) if sign < 0 else (z + step < Z))
                def _():
                    owner = across + sign * X * step
                    arrived(owner, k)
                    to_sibling(owner, k, False).start()

    for step in range(1, Z + 1):
        for k in range(chunks):
            if step < Z:
                along(step, k, False)
            crossed(step - 1, k)
            if step < Z and GATHER_CHUNKS[k][2]:
                along(step, k, True)

    for k in range(chunks):
        direct = GATHER_CHUNKS[k][2]
        own_copy(k).wait()
        for column in range(2):
            base = me if column == 0 else across
            for step in range(0, Z):
                for sign in (-1, 1) if step else (1,):
                    @pl.when((z >= step) if sign < 0 else (z + step < Z))
                    def _():
                        owner = base + sign * X * step
                        mine = column == 0 and step == 0
                        to_sibling(owner, k, mine).wait_send()
                        pltpu.make_async_remote_copy(
                            src_ref=place(owner, k, 1 - core),
                            dst_ref=place(owner, k, 1 - core),
                            send_sem=sib_sem.at[owner * chunks + k],
                            recv_sem=sib_recv.at[owner * chunks + k],
                            device_id={"section": sibling},
                            device_id_type=MESH,
                        ).wait_recv()
                        runs = column == 0 or direct
                        if runs and (step == 0 or sign < 0):
                            @pl.when(has_up)
                            def _():
                                copy(owner, k, mine, up_sem, me + X).wait_send()
                        if runs and (step == 0 or sign > 0):
                            @pl.when(has_down)
                            def _():
                                copy(owner, k, mine, down_sem, me - X).wait_send()
                        if column == 0 and (step == 0 or not direct):
                            copy(owner, k, mine, x_sem, across).wait_send()


def gather_weights(blk, dn):
    n = lax.axis_size("dp")
    if not ring_fits(n, blk.shape[0]):
        blk_all = lax.all_gather(blk, "dp", axis=0, tiled=True)
        dn_all = lax.all_gather(dn, "dp", axis=0, tiled=True)
        pairs = [(k, k ^ 1) for k in range(lax.axis_size("section"))]
        blk_sib, dn_sib = lax.ppermute((blk_all, dn_all), "section", pairs)
        even = lax.rem(lax.axis_index("section"), 2) == 0
        both = lambda a, b: jnp.where(even, jnp.stack([a, b]), jnp.stack([b, a]))
        return (both(blk_all, blk_sib), both(dn_all, dn_sib))
    units = n * len(GATHER_CHUNKS)
    return pl.pallas_call(
        gather_kernel,
        out_shape=(
            jax.ShapeDtypeStruct((2, D, FF), BF),
            jax.ShapeDtypeStruct((2, D, HALF), BF),
        ),
        in_specs=[pl.BlockSpec(memory_space=pl.ANY)] * 2,
        out_specs=(pl.BlockSpec(memory_space=pl.ANY),) * 2,
        scratch_shapes=[pltpu.SemaphoreType.DMA((units,))] * 6
        + [pltpu.SemaphoreType.DMA((len(GATHER_CHUNKS),))],
        compiler_params=pltpu.CompilerParams(collective_id=0, has_side_effects=True),
        name="gather_weights",
    )(blk, dn)


SUM_CHUNKS = ((1, 0, False), (1, 48, False), (1, 96, True), (0, 0, False), (0, 48, False), (0, 96, False))
VMEM_BYTES = 60 * 1024 * 1024


def sum_kernel(
    g_ref, gd_ref, blk_out, dn_out,
    own_b, own_d, other_d, xb, xd, xq, up_b, up_d, up_o, down_b, down_d, down_o, acc,
    load_sem, x_send, x_recv, up_send, up_recv, down_send, down_recv, sib_send, sib_recv, y_send, y_recv,
):
    me = lax.axis_index("dp")
    section = lax.axis_index("section")
    z, x = me // X, lax.rem(me, X)
    core = lax.rem(section, 2)
    sibling = section + 1 - 2 * core
    facing = lax.rem(section + 2, 4)
    across = me + 1 - 2 * x
    chunks = len(SUM_CHUNKS)
    has_up, has_down = z < Z - 1, z > 0

    barrier = pltpu.get_barrier_semaphore()
    for target in ({"section": sibling}, {"section": facing}, {"dp": across}):
        pl.semaphore_signal(barrier, 1, device_id=target, device_id_type=MESH)

    @pl.when(has_up)
    def _():
        pl.semaphore_signal(barrier, 1, device_id={"dp": me + X}, device_id_type=MESH)

    @pl.when(has_down)
    def _():
        pl.semaphore_signal(barrier, 1, device_id={"dp": me - X}, device_id_type=MESH)

    def each(distance, run):
        if distance == 0:
            run(z, None)
            return

        @pl.when(z + distance < Z)
        def _():
            run(z + distance, True)

        @pl.when(z >= distance)
        def _():
            run(z - distance, False)

    def hbm(k, zz, column):
        which, first, unused = SUM_CHUNKS[k]
        rows = pl.ds(pl.multiple_of((zz * X + column) * 144 + first, 16), PART)
        return (gd_ref if which else g_ref).at[rows]

    def own(k, zz):
        which, first, unused = SUM_CHUNKS[k]
        return (own_d if which else own_b).at[zz, pl.ds(first, PART)]

    def from_x(k, zz):
        which, first, direct = SUM_CHUNKS[k]
        if direct:
            return xq
        return (xd if which else xb).at[zz, pl.ds(first, PART)]

    def from_z(k, zz, up, other):
        which, first, unused = SUM_CHUNKS[k]
        if other:
            return (up_o if up else down_o).at[zz]
        if which:
            return (up_d if up else down_d).at[zz, pl.ds(first, PART)]
        return (up_b if up else down_b).at[zz, pl.ds(first, PART)]

    def load(k, zz, other=False):
        index = ((chunks if other else 0) + k) * Z + zz
        return pltpu.make_async_copy(
            hbm(k, zz, (1 - x) if other else x),
            other_d.at[zz] if other else own(k, zz),
            load_sem.at[index],
        )

    def x_copy(k, zz, src):
        unit = k * Z + zz
        return pltpu.make_async_remote_copy(
            src_ref=src, dst_ref=from_x(k, zz), send_sem=x_send.at[unit], recv_sem=x_recv.at[unit],
            device_id={"dp": across}, device_id_type=MESH,
        )

    def z_copy(k, zz, up, other):
        unit = ((chunks if other else 0) + k) * Z + zz
        return pltpu.make_async_remote_copy(
            src_ref=other_d.at[zz] if other else own(k, zz),
            dst_ref=from_z(k, zz, up, other),
            send_sem=(up_send if up else down_send).at[unit],
            recv_sem=(up_recv if up else down_recv).at[unit],
            device_id={"dp": me + X if up else me - X},
            device_id_type=MESH,
        )

    def dn_copy(k, slot, to_sib):
        rows = pl.ds(SUM_CHUNKS[k][1], PART)
        unit = slot * chunks + k
        return pltpu.make_async_remote_copy(
            src_ref=dn_out.at[slot, rows], dst_ref=dn_out.at[slot, rows],
            send_sem=(sib_send if to_sib else y_send).at[unit],
            recv_sem=(sib_recv if to_sib else y_recv).at[unit],
            device_id={"section": sibling if to_sib else facing},
            device_id_type=MESH,
        )

    def total(dst, srcs):
        @pl.loop(0, PART // 16)
        def _(step):
            rows = pl.ds(pl.multiple_of(step * 16, 16), 16)
            value = srcs[0][rows].astype(jnp.float32)
            for src in srcs[1:]:
                value = value + src[rows].astype(jnp.float32)
            dst[rows] = value.astype(dst.dtype)

    for k in range(chunks):
        for distance in (3, 2, 1, 0):
            def run(zz, up):
                load(k, zz).start()
                if SUM_CHUNKS[k][2]:
                    load(k, zz, True).start()
            each(distance, run)

    pl.semaphore_wait(barrier, 3 + has_up.astype(jnp.int32) + has_down.astype(jnp.int32))

    for which in (1, 0):
        for distance in (3, 2, 1, 0):
            for k in range(chunks):
                if SUM_CHUNKS[k][0] == which and not SUM_CHUNKS[k][2]:
                    each(distance, lambda zz, up: x_copy(k, zz, hbm(k, zz, 1 - x)).start())

    def pass_on(k, distance):
        def run(zz, up):
            behind = has_down if up else has_up
            if SUM_CHUNKS[k][2]:
                for other in (False, True):
                    mine = other_d.at[zz] if other else own(k, zz)
                    load(k, zz, other).wait()

                    @pl.when(behind)
                    def _():
                        z_copy(k, zz, up, other).wait_recv()
                        total(mine, [mine, from_z(k, zz, up, other)])

                    z_copy(k, zz, up, other).start()
                return
            load(k, zz).wait()
            x_copy(k, zz, hbm(k, zz, 1 - x)).wait_recv()

            @pl.when(behind)
            def _():
                z_copy(k, zz, up, False).wait_recv()
                total(own(k, zz), [own(k, zz), from_x(k, zz), from_z(k, zz, up, False)])

            @pl.when(jnp.logical_not(behind))
            def _():
                total(own(k, zz), [own(k, zz), from_x(k, zz)])

            z_copy(k, zz, up, False).start()
        each(distance, run)

    def add_z(dst, k, other):
        @pl.when(has_down)
        def _():
            z_copy(k, z, True, other).wait_recv()
            total(dst, [dst, from_z(k, z, True, other)])

        @pl.when(has_up)
        def _():
            z_copy(k, z, False, other).wait_recv()
            total(dst, [dst, from_z(k, z, False, other)])

    def send_direct(k):
        load(k, z, True).wait()
        acc[...] = other_d[z].astype(jnp.float32)
        add_z(acc, k, True)
        other_d[z] = acc[...].astype(BF)
        x_copy(k, z, other_d.at[z]).start()

    def finish(k):
        which, first, direct = SUM_CHUNKS[k]
        rows = pl.ds(first, PART)
        dst = acc if which else blk_out.at[rows]
        load(k, z).wait()
        if direct:
            total(dst, [own(k, z)])
            add_z(dst, k, False)
            x_copy(k, z, other_d.at[z]).wait_recv()
            total(dst, [dst, from_x(k, z)])
        else:
            x_copy(k, z, hbm(k, z, 1 - x)).wait_recv()
            total(dst, [own(k, z), from_x(k, z)])
            add_z(dst, k, False)
        if which:
            total(dn_out.at[section, rows], [acc])
            dn_copy(k, section, True).start()
            dn_copy(k, section, False).start()

    dn_chunks = [k for k in range(chunks) if SUM_CHUNKS[k][0]]
    blk_chunks = [k for k in range(chunks) if not SUM_CHUNKS[k][0]]
    for distance in (3, 2, 1):
        for k in dn_chunks:
            pass_on(k, distance)
    for k in blk_chunks:
        pass_on(k, 3)
    for k in dn_chunks:
        if SUM_CHUNKS[k][2]:
            send_direct(k)
    for k in dn_chunks:
        finish(k)
    for k in blk_chunks:
        pass_on(k, 2)
    for k in dn_chunks:
        dn_copy(k, facing, False).wait_recv()
        dn_copy(k, facing, True).start()
    for k in blk_chunks:
        pass_on(k, 1)
    for k in blk_chunks:
        finish(k)

    for k in range(chunks):
        direct = SUM_CHUNKS[k][2]
        for distance in (3, 2, 1, 0):
            def run(zz, up):
                if not direct:
                    x_copy(k, zz, hbm(k, zz, 1 - x)).wait_send()
                elif distance == 0:
                    x_copy(k, zz, other_d.at[zz]).wait_send()
                if distance:
                    z_copy(k, zz, up, False).wait_send()
                    if direct:
                        z_copy(k, zz, up, True).wait_send()
            each(distance, run)
        if SUM_CHUNKS[k][0]:
            dn_copy(k, section, True).wait_send()
            dn_copy(k, section, False).wait_send()
            dn_copy(k, facing, True).wait_send()
            dn_copy(k, sibling, True).wait_recv()
            dn_copy(k, lax.rem(sibling + 2, 4), True).wait_recv()


def sum_gradients(g_blk, g_dn):
    n = lax.axis_size("dp")
    if not ring_fits(n, D // n):
        blk = lax.psum_scatter(g_blk, "dp", scatter_dimension=0, tiled=True)
        dn = lax.psum_scatter(g_dn, "dp", scatter_dimension=0, tiled=True)
        return (blk.astype(jnp.float32), lax.all_gather(dn, "section"))
    chunks = len(SUM_CHUNKS)
    dma = lambda count: pltpu.SemaphoreType.DMA((count,))
    ring_b = pltpu.VMEM((Z, 144, FF), BF)
    ring_d = pltpu.VMEM((Z, 144, HALF), BF)
    ring_o = pltpu.VMEM((Z, PART, HALF), BF)
    vmem = pl.BlockSpec(memory_space=pltpu.VMEM)
    return pl.pallas_call(
        sum_kernel,
        out_shape=(
            jax.ShapeDtypeStruct((144, FF), jnp.float32),
            jax.ShapeDtypeStruct((4, 144, HALF), BF),
        ),
        in_specs=[pl.BlockSpec(memory_space=pl.ANY)] * 2,
        out_specs=(vmem, vmem),
        scratch_shapes=[
            ring_b, ring_d, ring_o, ring_b, pltpu.VMEM((Z, 96, HALF), BF), pltpu.VMEM((PART, HALF), BF),
            ring_b, ring_d, ring_o, ring_b, ring_d, ring_o, pltpu.VMEM((PART, HALF), jnp.float32),
            dma(2 * chunks * Z), dma(chunks * Z), dma(chunks * Z),
            dma(2 * chunks * Z), dma(2 * chunks * Z), dma(2 * chunks * Z), dma(2 * chunks * Z),
            dma(4 * chunks), dma(4 * chunks), dma(4 * chunks), dma(4 * chunks),
        ],
        compiler_params=pltpu.CompilerParams(
            collective_id=1, has_side_effects=True, vmem_limit_bytes=VMEM_BYTES
        ),
        name="sum_gradients",
    )(g_blk, g_dn)


def exchange_kernel(axes, modes, *refs):
    count = len(modes)
    ins, outs = refs[:count], refs[count : 2 * count]
    send_sem, recv_sem, own_sem = refs[2 * count :]
    dp, section = lax.axis_index("dp"), lax.axis_index("section")
    n, sections = lax.axis_size("dp"), lax.axis_size("section")
    if axes == "dp":
        size, me, where = n, dp, lambda p: {"dp": p}
    elif axes == "section":
        size, me, where = sections, section, lambda p: {"section": p}
    elif axes == "stage":
        low = section - lax.rem(section, 2)
        size, me = 2 * n, dp * 2 + lax.rem(section, 2)
        where = lambda p: {"dp": p // 2, "section": low + lax.rem(p, 2)}
    else:
        size, me = n * sections, dp * sections + section
        where = lambda p: {"dp": p // sections, "section": lax.rem(p, sections)}

    def part(k, p):
        if modes[k] == "all":
            return ins[k]
        index = {"each": p, "dp": p // 2, "core": lax.rem(p, 2)}[modes[k]]
        return ins[k].at[index]

    def copy(k, step, src, slot, p):
        return pltpu.make_async_remote_copy(
            src_ref=src, dst_ref=outs[k].at[slot],
            send_sem=send_sem.at[k, step], recv_sem=recv_sem.at[k, step],
            device_id=where(p), device_id_type=MESH,
        )

    barrier = pltpu.get_barrier_semaphore()

    @pl.loop(1, size)
    def _(step):
        pl.semaphore_signal(barrier, 1, device_id=where(lax.rem(me + step, size)), device_id_type=MESH)

    for k in range(count):
        pltpu.make_async_copy(part(k, me), outs[k].at[me], own_sem.at[k]).start()
    pl.semaphore_wait(barrier, size - 1)

    @pl.loop(1, size)
    def _(step):
        p = lax.rem(me + step, size)
        for k in range(count):
            copy(k, step, part(k, p), me, p).start()

    for k in range(count):
        pltpu.make_async_copy(part(k, me), outs[k].at[me], own_sem.at[k]).wait()

    @pl.loop(1, size)
    def _(step):
        p = lax.rem(me + size - step, size)
        for k in range(count):
            copy(k, step, part(k, p), p, p).wait_recv()
            copy(k, step, part(k, p), p, p).wait_send()


def exchange(ident, axes, modes, *arrays):
    n, sections = lax.axis_size("dp"), lax.axis_size("section")
    size = {"dp": n, "section": sections, "stage": 2 * n, "every": n * sections}[axes]
    blocks = [a.shape if mode == "all" else a.shape[1:] for a, mode in zip(arrays, modes)]
    count = len(arrays)
    vmem = pl.BlockSpec(memory_space=pltpu.VMEM)
    return pl.pallas_call(
        partial(exchange_kernel, axes, modes),
        out_shape=tuple(jax.ShapeDtypeStruct((size,) + b, a.dtype) for a, b in zip(arrays, blocks)),
        in_specs=[vmem] * count,
        out_specs=(vmem,) * count,
        scratch_shapes=[
            pltpu.SemaphoreType.DMA((count, size)),
            pltpu.SemaphoreType.DMA((count, size)),
            pltpu.SemaphoreType.DMA((count,)),
        ],
        compiler_params=pltpu.CompilerParams(
            collective_id=ident, has_side_effects=True, vmem_limit_bytes=VMEM_BYTES
        ),
        name="exchange_" + axes,
    )(*arrays)


def rows_of(value, size):
    value = value.reshape(-1)
    return jnp.pad(value, (0, size * 128 - value.shape[0])).reshape(size, 128)


def row_count(length, unit=8):
    return -(-length // (128 * unit)) * unit


def heads_of(value):
    return value.reshape(PATCHES, HEADS, HEAD_DIM)


def attention_forward(xm_half, wblk, bblk):
    qkv = to_half(matmul(xm_half, wblk[:, : 3 * D]) + bblk[: 3 * D])
    parts = qkv.reshape(PATCHES, 3, HEADS, HEAD_DIM)
    scores = jnp.einsum(
        "qhd,khd->hqk", parts[:, 0], parts[:, 1], preferred_element_type=jnp.float32
    ) * HEAD_DIM ** (-0.5)
    probs = jax.nn.softmax(scores, axis=-1)
    attended = to_half(
        jnp.einsum("hqk,khd->qhd", to_half(probs), parts[:, 2], preferred_element_type=jnp.float32)
    ).reshape(PATCHES, D)
    branch = matmul(attended, wblk[:, 3 * D :]) + bblk[3 * D :]
    return (branch, (parts, probs, attended))


def attention_backward(grad_half, saved, wblk):
    parts, probs, attended = saved
    d_att = heads_of(to_half(matmul_nt(grad_half, wblk[:, 3 * D :])))
    d_value = jnp.einsum(
        "hqk,qhd->khd", to_half(probs), d_att, preferred_element_type=jnp.float32
    )
    d_probs = jnp.einsum("qhd,khd->hqk", d_att, parts[:, 2], preferred_element_type=jnp.float32)
    d_scores = to_half(probs * (d_probs - jnp.sum(probs * d_probs, axis=-1, keepdims=True)))
    d_query = jnp.einsum(
        "hqk,khd->qhd", d_scores, parts[:, 1], preferred_element_type=jnp.float32
    ) * HEAD_DIM ** (-0.5)
    d_key = jnp.einsum(
        "hqk,qhd->khd", d_scores, parts[:, 0], preferred_element_type=jnp.float32
    ) * HEAD_DIM ** (-0.5)
    d_qkv = to_half(jnp.stack([d_query, d_key, d_value], axis=1).reshape(PATCHES, 3 * D))
    return (matmul_nt(d_qkv, wblk[:, : 3 * D]), d_qkv)


def modulated(x, mod):
    return layer_modulate(x, mod[None, :D], mod[None, D : 2 * D])


def modulated_back(x, mod, d_xm):
    pull = jax.vjp(layer_modulate, x, mod[None, :D], mod[None, D : 2 * D])[1]
    d_x, d_shift, d_scale = pull(d_xm)
    return (d_x, d_shift[0], d_scale[0])


def stage_forward(x_in, weights):
    mod_a, mod_m, w_blk, w_dn, b_attn, b_up, b_down = weights
    xm_a = to_half(modulated(x_in, mod_a))
    branch_a, saved = attention_forward(xm_a, w_blk[0], b_attn)
    x_mid = to_half(x_in + mod_a[None, 2 * D :] * branch_a).astype(jnp.float32)
    xm_m = to_half(modulated(x_mid, mod_m))
    pre = matmul(xm_m, w_blk[1]) + b_up
    act = to_half(jax.nn.gelu(pre, approximate=True))
    branch_m = matmul_nt(act[:, :HALF], w_dn[0]) + matmul_nt(act[:, HALF:], w_dn[1]) + b_down
    x_out = x_mid + mod_m[None, 2 * D :] * branch_m
    return (x_out, (xm_a, branch_a, saved, x_mid, xm_m, pre, act, branch_m))


def mlp_backward(d_out, weights, kept):
    mod_a, mod_m, w_blk, w_dn, b_attn, b_up, b_down = weights
    xm_a, branch_a, saved, x_mid, xm_m, pre, act, branch_m = kept
    d_gate = jnp.sum(d_out * branch_m, axis=0)
    grad_half = to_half(d_out * mod_m[None, 2 * D :])
    d_act = jnp.concatenate([matmul(grad_half, w_dn[0]), matmul(grad_half, w_dn[1])], axis=1)
    d_pre = to_half(jax.vjp(partial(jax.nn.gelu, approximate=True), pre)[1](d_act)[0])
    d_x, d_shift, d_scale = modulated_back(x_mid, mod_m, matmul_nt(d_pre, w_blk[1]))
    d_mod = to_half(jnp.concatenate([d_shift, d_scale, d_gate]))
    return (to_half(d_out + d_x).astype(jnp.float32), d_mod, grad_half, d_pre)


def attn_backward(d_out, x_in, weights, kept):
    mod_a, mod_m, w_blk, w_dn, b_attn, b_up, b_down = weights
    xm_a, branch_a, saved, x_mid, xm_m, pre, act, branch_m = kept
    d_gate = jnp.sum(d_out * branch_a, axis=0)
    grad_half = to_half(d_out * mod_a[None, 2 * D :])
    d_xm, d_qkv = attention_backward(grad_half, saved, w_blk[0])
    d_x, d_shift, d_scale = modulated_back(x_in, mod_a, d_xm)
    d_mod = to_half(jnp.concatenate([d_shift, d_scale, d_gate]))
    return (to_half(d_out + d_x), d_mod, grad_half, d_qkv)


def final_step(x_out, fmod, w_head, b_head, target, counts, loss_scale):
    xf_half = to_half(modulated(x_out, fmod))
    error = matmul(xf_half, w_head) + b_head - target
    loss = counts * jnp.sum(error * error)
    d_pred = to_half(2.0 * loss_scale * counts * error)
    g_head = matmul_tn(xf_half, d_pred)
    d_x, d_shift, d_scale = modulated_back(x_out, fmod, matmul_nt(d_pred, w_head))
    return (loss, d_x, to_half(jnp.concatenate([d_shift, d_scale])), g_head, column_sums(d_pred))


def nesterov(weight, moment, average, grad, factor):
    clipped = grad * factor
    moment_new = momentum_rate * moment + clipped
    weight_new = weight - learn_rate * (clipped + momentum_rate * moment_new)
    average_new = ema_decay * average + (1.0 - ema_decay) * weight_new
    return (weight_new, moment_new, average_new, weight_new.astype(jnp.bfloat16))


def swap(array, by):
    peers = lax.axis_size("section")
    return lax.ppermute(array, "section", [(k, k ^ by) for k in range(peers)])


def pick(parts, index):
    return lax.dynamic_index_in_dim(parts, index, 0, keepdims=False)


def body(
    latents, noise, timesteps, labels, null_mask, valid,
    mod_w, mod_m, mod_e, block_w, block_m, block_e, down_w, down_m, down_e,
    stem_w, stem_m, stem_e, tail_w, tail_m, tail_e, biases, bias_m, bias_e,
):
    place = lax.axis_index("dp")
    section = lax.axis_index("section")
    stage = section // 2
    core = lax.rem(section, 2)
    even = core == 0
    n = lax.axis_size("dp")
    width = D // n

    downs = jnp.swapaxes(down_w, 1, 2)
    blk_half = to_half(block_w[0])
    dn_half = to_half(lax.dynamic_slice(downs, (stage, 0, core * HALF), (1, width, HALF))[0])
    w_blk, w_dn = gather_weights(blk_half, dn_half)

    stems = stem_w.T
    classes_own = jnp.where(null_mask > 0, NCLS - 1, labels)
    meta = jnp.stack([timesteps, classes_own, valid], axis=1)
    images_own = meta.shape[0]
    meta = jnp.pad(meta, ((0, 8 - images_own), (0, 125)))
    stem_half = to_half(stems)
    tail_half = to_half(tail_w)
    table = stem_half[:, :NCLS]
    w_two = stem_half[:, NCLS + PATCH_IN + FREQ :]
    ends = NCLS, NCLS + PATCH_IN + FREQ
    small = jnp.concatenate([stem_half[:, ends[0] : ends[1]], tail_half[:, 2 * D :]], axis=1)
    small = jnp.pad(small, ((0, -width % 16), (0, -small.shape[1] % 128)))
    meta, small = exchange(2, "dp", ("all", "all"), meta, small)
    meta = meta[:, :images_own].reshape(n * images_own, 128)
    small = small[:, :width].reshape(D, -1)
    w_patch_all = small[:, :PATCH_IN]
    w_one_all = small[:, PATCH_IN : PATCH_IN + FREQ]
    w_head_all = small[:, PATCH_IN + FREQ : PATCH_IN + FREQ + HEAD_OUT]
    images = meta.shape[0]
    steps_all = meta[:, 0].astype(jnp.float32)
    picks = (meta[:, 1][:, None] == jnp.arange(NCLS, dtype=jnp.int32)[None, :]).astype(BF)
    count = jnp.sum(meta[:, 2].astype(jnp.float32))
    loss_scale = 1.0 / (count * PATCHES * HEAD_OUT)
    freq = to_half(time_features(steps_all))

    b_two = lax.dynamic_slice_in_dim(biases, 32 * D + place * width, width)
    hidden_pre = matmul_nt(w_one_all, freq) + biases[31 * D : 32 * D, None]
    hidden_all = to_half(jax.nn.silu(hidden_pre))
    cond = matmul(w_two, hidden_all) + b_two[:, None] + matmul_nt(table, picks)
    cond_low = to_half(cond).astype(jnp.float32)
    cond_own = jnp.where(section == 0, cond, cond_low)
    silu_own = to_half(jax.nn.silu(cond_own))
    silu_low = to_half(jax.nn.silu(cond_low))
    mod_half_w = to_half(mod_w[0])
    part_mod = matmul_tn(silu_own, mod_half_w)
    part_fm = matmul_tn(silu_low, tail_half[:, : 2 * D])
    parts = jnp.concatenate([part_mod, part_fm, jnp.zeros((images, 384), jnp.float32)], axis=1)
    (mods,) = exchange(3, "stage", ("each",), parts.reshape(images, 48, 128))
    mods = jnp.sum(mods.reshape(n, 2, 48 * 128), axis=0)
    bias_of = lambda first, length: lax.dynamic_slice_in_dim(biases, first, length)
    mod_a = mods[0, : 3 * D] + bias_of(6 * D * stage, 3 * D)
    mod_b = mods[1, : 3 * D] + bias_of(6 * D * stage + 3 * D, 3 * D)
    fmod = mods[0, 3 * D : 5 * D] + biases[33 * D : 35 * D]
    weights = (
        mod_a, mod_b, w_blk, w_dn,
        bias_of(12 * D + 8 * D * stage, 4 * D),
        bias_of(16 * D + 8 * D * stage, 4 * D),
        bias_of(28 * D + D * stage, D),
    )

    step = pick(timesteps, core).astype(jnp.float32)
    signal, spread = noise_levels(step)
    lat, noi = pick(latents, core)[None], pick(noise, core)[None]
    counts = pick(valid, core).astype(jnp.float32)
    tok_half = to_half(patchify(signal * lat + spread * noi))[0]
    target = jnp.concatenate([patchify(signal * noi - spread * lat), patchify(noi)], axis=2)[0]
    x_first = matmul_nt(tok_half, w_patch_all) + biases[30 * D : 31 * D] + position_table(GRID // 2, D)

    x_hop = swap(to_half(stage_forward(x_first, weights)[0]), 2)
    x_in = jnp.where(stage == 0, x_first, x_hop.astype(jnp.float32))
    x_out, kept = stage_forward(x_in, weights)
    loss, d_final, d_fmod, g_head, b_head = final_step(
        x_out, fmod, w_head_all, biases[35 * D :], target, counts, loss_scale
    )
    d_mid = mlp_backward(d_final, weights, kept)[0]
    d_hop = swap(attn_backward(d_mid, x_in, weights, kept)[0], 2)
    d_out = jnp.where(stage == 1, d_final, d_hop.astype(jnp.float32))
    d_mid, d_mod_b, d_branch_b, d_pre = mlp_backward(d_out, weights, kept)
    d_first, d_mod_a, d_branch_a, d_qkv = attn_backward(d_mid, x_in, weights, kept)
    xm_a, branch_a, saved, x_mid, xm_b, pre, act, branch_b = kept
    attended = saved[2]

    act_own = jnp.where(even, act[:, :HALF], act[:, HALF:])
    act_sib, branch_sib = swap((jnp.where(even, act[:, HALF:], act[:, :HALF]), d_branch_b), 1)
    g_dn = to_half(matmul_tn(d_branch_b, act_own) + matmul_tn(branch_sib, act_sib))
    d_attn = jnp.concatenate([d_qkv, d_branch_a], axis=1)
    left_sib, last_sib, right_sib = swap(
        (
            jnp.where(even, xm_b, xm_a),
            jnp.where(even, xm_b, attended),
            jnp.where(even, d_pre, d_attn),
        ),
        1,
    )
    left = jnp.concatenate([jnp.where(even, xm_a, xm_b), left_sib], axis=0)
    last = jnp.concatenate([jnp.where(even, attended, xm_b), last_sib], axis=0)
    right = jnp.concatenate([jnp.where(even, d_attn, d_pre), right_sib], axis=0)
    g_blk = jnp.concatenate(
        [
            to_half(matmul_tn(left, right[:, : 3 * D])),
            to_half(matmul_tn(last, right[:, 3 * D :])),
        ],
        axis=1,
    )
    g_blk, g_dn = sum_gradients(g_blk, g_dn)

    last_stage = (stage == 1).astype(jnp.float32)
    zeros_fm = jnp.zeros((2 * D + 384,), BF)
    d_fmod = jnp.concatenate([jnp.where(stage == 1, d_fmod, zeros_fm[: 2 * D]), zeros_fm[2 * D :]])
    d_mods = jnp.stack([jnp.concatenate([d_mod_a, d_fmod]), jnp.concatenate([d_mod_b, d_fmod])])
    last_own = jnp.where(stage == 0, column_sums(d_first), jnp.pad(b_head, (0, D - HEAD_OUT)))
    own_biases = jnp.concatenate(
        [
            column_sums(d_qkv), column_sums(d_branch_a), column_sums(d_pre), column_sums(d_branch_b),
            last_own, loss[None],
        ]
    )
    piece = row_count(-(-own_biases.shape[0] // (2 * n)))
    own_biases = rows_of(own_biases, 2 * n * piece).reshape(2 * n, piece, 128)
    g_patch = jnp.pad(matmul_tn(d_first, tok_half), ((0, 0), (0, HEAD_OUT - PATCH_IN)))
    end_rows = row_count(width * HEAD_OUT)
    own_ends = jnp.where(stage == 0, g_patch, g_head).reshape(n, width * HEAD_OUT)
    own_ends = jnp.pad(own_ends, ((0, 0), (0, end_rows * 128 - width * HEAD_OUT))).reshape(n, end_rows, 128)
    d_mods, own_biases, own_ends = exchange(
        4, "stage", ("core", "each", "dp"), d_mods.reshape(2, 48, 128), own_biases, own_ends
    )
    d_mods = d_mods.reshape(images, 48 * 128)
    bias_piece = jnp.sum(own_biases, axis=0)
    own_ends = jnp.sum(own_ends, axis=0)
    d_mod_all, d_fm_all = d_mods[:, : 3 * D], d_mods[:, 3 * D : 5 * D]
    g_mod = matmul(silu_own, d_mod_all)
    c_own = matmul_nt(mod_half_w, d_mod_all)
    c_own = c_own + matmul_nt(tail_half[:, : 2 * D], jnp.where(section == 3, d_fm_all, jnp.zeros_like(d_fm_all)))
    c_own = silu_back(cond_own, c_own)
    cond_rows = row_count(width * images)
    c_all, end_pair, d_fm_all = exchange(
        5, "section", ("all", "all", "all"), rows_of(c_own, cond_rows), own_ends, d_fm_all
    )
    d_fm_all = d_fm_all[3]
    ends = [end_pair[k].reshape(-1)[: width * HEAD_OUT].reshape(width, HEAD_OUT) for k in (0, 3)]
    g_fm = matmul(silu_low, d_fm_all)
    c_all = [c_all[k].reshape(-1)[: width * images].reshape(width, images) for k in range(4)]
    d_cond = to_half(c_all[3])
    for slot in (2, 1, 0):
        d_cond = to_half(d_cond.astype(jnp.float32) + c_all[slot])
    part_hidden = matmul_tn(w_two, d_cond).reshape(n, width * images)
    part_hidden = jnp.pad(part_hidden, ((0, 0), (0, cond_rows * 128 - width * images)))
    (d_hidden,) = exchange(6, "dp", ("each",), part_hidden.reshape(n, cond_rows, 128))
    d_hidden = jnp.sum(d_hidden, axis=0).reshape(-1)[: width * images].reshape(width, images)
    pre_own = lax.dynamic_slice_in_dim(hidden_pre, place * width, width)
    d_pre_one = to_half(silu_back(pre_own, d_hidden))
    g_table = matmul(d_cond, picks)
    g_one = matmul(d_pre_one, freq)
    g_two = matmul_nt(d_cond, hidden_all)
    g_stem = jnp.concatenate([g_table, ends[0][:, :PATCH_IN], g_one, g_two], axis=1)
    g_tail = jnp.concatenate([g_fm, ends[1]], axis=1)
    g_dn = g_dn.astype(jnp.float32)
    down_both = jnp.stack(
        [jnp.concatenate([g_dn[0], g_dn[1]], axis=1), jnp.concatenate([g_dn[2], g_dn[3]], axis=1)]
    )

    square = lambda value: jnp.sum(value * value)
    once = (section == 0).astype(jnp.float32)
    squares = square(g_mod) + square(g_blk)
    squares = squares + once * (square(down_both) + square(g_stem) + square(g_tail))
    row_sums = lambda value: jnp.sum(value.astype(jnp.float32), axis=1)
    mod_piece = 3 * D // n
    mod_rows, slice_rows = row_count(mod_piece, 1), row_count(2 * width, 1)
    bias_mod = lax.dynamic_slice_in_dim(column_sums(d_mod_all), place * mod_piece, mod_piece)
    slices = jnp.concatenate([row_sums(d_pre_one), row_sums(d_cond)])
    news = jnp.concatenate(
        [bias_piece, rows_of(bias_mod, mod_rows), rows_of(slices, slice_rows), rows_of(squares[None], 1)]
    )
    news = jnp.pad(news, ((0, -news.shape[0] % 8), (0, 0)))
    (news,) = exchange(7, "every", ("all",), news)
    news = news.reshape(n, 4, -1, 128)
    first, second = piece + mod_rows, piece + mod_rows + slice_rows
    stages = [news[:, 2 * k : 2 * k + 2, :piece].reshape(-1) for k in range(2)]
    bias_mods = news[:, :, piece:first].reshape(n, 4, mod_rows * 128)[:, :, :mod_piece]
    bias_mods = bias_mods.transpose(1, 0, 2).reshape(-1)
    slices = news[:, 0, first:second].reshape(n, slice_rows * 128)[:, : 2 * width]
    bias_grad = jnp.concatenate(
        [bias_mods]
        + [part[: 8 * D] for part in stages]
        + [part[8 * D : 9 * D] for part in stages]
        + [stages[0][9 * D : 10 * D]]
        + [slices[:, :width].reshape(-1), slices[:, width:].reshape(-1)]
        + [column_sums(d_fm_all), stages[1][9 * D : 9 * D + HEAD_OUT]]
    )
    loss_sum = stages[1][10 * D]
    grad_norm = jnp.sqrt(jnp.sum(news[:, :, second, 0]) + square(bias_grad))
    factor = jnp.minimum(1.0, clip_limit / (grad_norm + 1e-06))
    mod_out = nesterov(mod_w, mod_m, mod_e, g_mod[None], factor)
    block_out = nesterov(block_w, block_m, block_e, g_blk[None], factor)
    flip = lambda value: jnp.swapaxes(value, 1, 2)
    down_out = tuple(map(flip, nesterov(downs, flip(down_m), flip(down_e), down_both, factor)))
    stem_out = tuple(value.T for value in nesterov(stems, stem_m.T, stem_e.T, g_stem, factor))
    tail_out = nesterov(tail_w, tail_m, tail_e, g_tail, factor)
    bias_out = nesterov(biases, bias_m, bias_e, bias_grad, factor)
    return (
        (loss_sum, count, grad_norm)
        + mod_out + block_out + down_out + stem_out + tail_out + bias_out
    )


def solution(mesh):
    images = (P("dp", None, None, None),) * 2 + (P("dp"),) * 4
    owned = P("section", "dp", None)
    states = (owned,) * 6 + (P(None, None, "dp"),) * 3 + (P(None, "dp"),) * 3 + (P("dp", None),) * 3 + (P(),) * 3
    updates = (owned,) * 8 + (P(None, None, "dp"),) * 4 + (P(None, "dp"),) * 4 + (P("dp", None),) * 4 + (P(),) * 4
    return jax.shard_map(
        body,
        mesh=mesh,
        in_specs=images + states,
        out_specs=(P(), P(), P()) + updates,
        check_vma=False,
    )
```

```python
from functools import partial
import math

import jax
import jax.numpy as jnp
from jax import lax
from jax.experimental import pallas as pl
from jax.experimental.pallas import tpu as pltpu
from jax.sharding import PartitionSpec as P

HEADS = 16
HEAD_DIM = 72
D = 1152
FF = 4608
HALF = FF // 2
NCLS = 1001
FREQ = 256
GRID = 32
PATCHES = 256
PATCH_IN = 16
HEAD_OUT = 32
LAYERS = 2
NBIAS = 40352


epsilon_norm = 1e-06
momentum_rate = 0.9
ema_decay = 0.9
learn_rate = 4000.0
clip_limit = 0.02
MESH = pl.DeviceIdType.MESH
BF = jnp.bfloat16


def matmul(left, right):
    return jnp.dot(left, right, preferred_element_type=jnp.float32)


def matmul_nt(left, right):
    return lax.dot_general(
        left, right, (((1,), (1,)), ((), ())), preferred_element_type=jnp.float32
    )


def matmul_tn(left, right):
    return lax.dot_general(
        left, right, (((0,), (0,)), ((), ())), preferred_element_type=jnp.float32
    )


def to_half(value):
    return value.astype(BF)


def column_sums(value):
    return jnp.sum(value.astype(jnp.float32), axis=0)


def silu_back(value, grad):
    return jax.vjp(jax.nn.silu, value)[1](grad)[0]


def layer_modulate(tokens, shift, scale):
    centered = tokens - jnp.mean(tokens, axis=-1, keepdims=True)
    normed = centered * lax.rsqrt(
        jnp.mean(centered * centered, axis=-1, keepdims=True) + epsilon_norm
    )
    return normed * (1.0 + scale) + shift


def patchify(field):
    images, side = (field.shape[0], field.shape[1] // 2)
    return (
        field.reshape(images, side, 2, side, 2, 4)
        .transpose(0, 1, 3, 2, 4, 5)
        .reshape(images, side * side, 16)
    )


def sincos_rows(places, width):
    omega = 1.0 / 10000.0 ** (jnp.arange(width // 2, dtype=jnp.float32) / (width // 2))
    angle = places[:, None] * omega[None, :]
    return jnp.concatenate([jnp.sin(angle), jnp.cos(angle)], axis=1)


def position_table(side, width):
    line = sincos_rows(jnp.arange(side, dtype=jnp.float32), width // 2)
    column = jnp.broadcast_to(line[None], (side, side, width // 2))
    row = jnp.broadcast_to(line[:, None], (side, side, width // 2))
    return jnp.concatenate([column, row], axis=2).reshape(side * side, width)


def time_features(steps):
    half = FREQ // 2
    freqs = jnp.exp(-math.log(10000.0) * jnp.arange(half, dtype=jnp.float32) / half)
    angle = steps[:, None] * freqs[None, :]
    return jnp.concatenate([jnp.cos(angle), jnp.sin(angle)], axis=1)


def noise_levels(steps):
    level = jnp.cos((steps / 1000.0 + 0.008) / 1.008 * (math.pi / 2)) ** 2
    return (jnp.sqrt(level), jnp.sqrt(1.0 - level))


Z, X = 4, 2
CHUNKS = ((0, 16, True), (16, 32, False), (48, 32, False), (80, 32, False), (112, 32, False))


def ring_fits(n, rows):
    return n == Z * X and rows == 144


def gather_kernel(blk_ref, out_blk, up_sem, down_sem, x_sem, sib_sem, recv_sem, sib_recv, own_sem):
    me = lax.axis_index("dp")
    section = lax.axis_index("section")
    z, x = me // X, lax.rem(me, X)
    core = lax.rem(section, 2)
    sibling = section + 1 - 2 * core
    across = me + 1 - 2 * x
    chunks = len(CHUNKS)
    has_up, has_down = z < Z - 1, z > 0

    barrier = pltpu.get_barrier_semaphore()
    pl.semaphore_signal(barrier, 1, device_id={"section": sibling}, device_id_type=MESH)
    pl.semaphore_signal(barrier, 1, device_id={"dp": across}, device_id_type=MESH)

    @pl.when(has_up)
    def _():
        pl.semaphore_signal(barrier, 1, device_id={"dp": me + X}, device_id_type=MESH)

    @pl.when(has_down)
    def _():
        pl.semaphore_signal(barrier, 1, device_id={"dp": me - X}, device_id_type=MESH)

    pl.semaphore_wait(barrier, 2 + has_up.astype(jnp.int32) + has_down.astype(jnp.int32))

    def place(owner, k, side):
        first, rows, unused = CHUNKS[k]
        return out_blk.at[side, pl.ds(pl.multiple_of(owner * 144 + first, 16), rows)]

    def source(owner, k, mine):
        if not mine:
            return place(owner, k, core)
        first, rows, unused = CHUNKS[k]
        return blk_ref.at[pl.ds(first, rows)]

    def copy(owner, k, mine, sem, target):
        unit = owner * chunks + k
        return pltpu.make_async_remote_copy(
            src_ref=source(owner, k, mine),
            dst_ref=place(owner, k, core),
            send_sem=sem.at[unit],
            recv_sem=recv_sem.at[unit],
            device_id={"dp": target},
            device_id_type=MESH,
        )

    def to_sibling(owner, k, mine):
        unit = owner * chunks + k
        return pltpu.make_async_remote_copy(
            src_ref=source(owner, k, mine),
            dst_ref=place(owner, k, core),
            send_sem=sib_sem.at[unit],
            recv_sem=sib_recv.at[unit],
            device_id={"section": sibling},
            device_id_type=MESH,
        )

    def own_copy(k):
        return pltpu.make_async_copy(source(me, k, True), place(me, k, core), own_sem.at[k])

    def arrived(owner, k):
        copy(owner, k, False, x_sem, across).wait_recv()

    for k in range(chunks):
        @pl.when(has_up)
        def _():
            copy(me, k, True, up_sem, me + X).start()

        @pl.when(has_down)
        def _():
            copy(me, k, True, down_sem, me - X).start()

        copy(me, k, True, x_sem, across).start()
        own_copy(k).start()
        to_sibling(me, k, True).start()

    def along(step, k, first_across):
        shift = 1 - 2 * x if first_across else 0
        crosses = (not first_across) and (not CHUNKS[k][2])

        @pl.when(z >= step)
        def _():
            owner = me - X * step + shift
            arrived(owner, k)

            @pl.when(has_up)
            def _():
                copy(owner, k, False, up_sem, me + X).start()

            if crosses:
                copy(owner, k, False, x_sem, across).start()
            to_sibling(owner, k, False).start()

        @pl.when(z + step < Z)
        def _():
            owner = me + X * step + shift
            arrived(owner, k)

            @pl.when(has_down)
            def _():
                copy(owner, k, False, down_sem, me - X).start()

            if crosses:
                copy(owner, k, False, x_sem, across).start()
            to_sibling(owner, k, False).start()

    def crossed(step, k):
        direct = CHUNKS[k][2]
        if step == 0:
            owner = across
            arrived(owner, k)
            if direct:
                @pl.when(has_up)
                def _():
                    copy(owner, k, False, up_sem, me + X).start()

                @pl.when(has_down)
                def _():
                    copy(owner, k, False, down_sem, me - X).start()
            to_sibling(owner, k, False).start()
        elif not direct:
            for sign in (-1, 1):
                @pl.when((z >= step) if sign < 0 else (z + step < Z))
                def _():
                    owner = across + sign * X * step
                    arrived(owner, k)
                    to_sibling(owner, k, False).start()

    for step in range(1, Z + 1):
        for k in range(chunks):
            if step < Z:
                along(step, k, False)
            crossed(step - 1, k)
            if step < Z and CHUNKS[k][2]:
                along(step, k, True)

    for k in range(chunks):
        direct = CHUNKS[k][2]
        own_copy(k).wait()
        for column in range(2):
            base = me if column == 0 else across
            for step in range(0, Z):
                for sign in (-1, 1) if step else (1,):
                    @pl.when((z >= step) if sign < 0 else (z + step < Z))
                    def _():
                        owner = base + sign * X * step
                        mine = column == 0 and step == 0
                        to_sibling(owner, k, mine).wait_send()
                        pltpu.make_async_remote_copy(
                            src_ref=place(owner, k, 1 - core),
                            dst_ref=place(owner, k, 1 - core),
                            send_sem=sib_sem.at[owner * chunks + k],
                            recv_sem=sib_recv.at[owner * chunks + k],
                            device_id={"section": sibling},
                            device_id_type=MESH,
                        ).wait_recv()
                        runs = column == 0 or direct
                        if runs and (step == 0 or sign < 0):
                            @pl.when(has_up)
                            def _():
                                copy(owner, k, mine, up_sem, me + X).wait_send()
                        if runs and (step == 0 or sign > 0):
                            @pl.when(has_down)
                            def _():
                                copy(owner, k, mine, down_sem, me - X).wait_send()
                        if column == 0 and (step == 0 or not direct):
                            copy(owner, k, mine, x_sem, across).wait_send()


def gather_weights(half):
    n = lax.axis_size("dp")
    if not ring_fits(n, half.shape[0]):
        own = lax.all_gather(half, "dp", axis=0, tiled=True)
        sib = swap(own, 1)
        even = lax.rem(lax.axis_index("section"), 2) == 0
        return jnp.where(even, jnp.stack([own, sib]), jnp.stack([sib, own]))
    units = n * len(CHUNKS)
    return pl.pallas_call(
        gather_kernel,
        out_shape=jax.ShapeDtypeStruct((2, D, HALF), BF),
        in_specs=[pl.BlockSpec(memory_space=pl.ANY)],
        out_specs=pl.BlockSpec(memory_space=pl.ANY),
        scratch_shapes=[pltpu.SemaphoreType.DMA((units,))] * 6
        + [pltpu.SemaphoreType.DMA((len(CHUNKS),))],
        compiler_params=pltpu.CompilerParams(collective_id=0, has_side_effects=True),
        cost_estimate=pl.CostEstimate(flops=0, bytes_accessed=200_000_000, transcendentals=0),
        name="gather_weights",
    )(half)


VMEM_BYTES = 60 * 1024 * 1024


def sum_kernel(
    g_ref, out, own_b, other_d, xb, xq, up_b, up_o, down_b, down_o, acc,
    load_sem, x_send, x_recv, up_send, up_recv, down_send, down_recv,
):
    me = lax.axis_index("dp")
    z, x = me // X, lax.rem(me, X)
    across = me + 1 - 2 * x
    chunks = len(CHUNKS)
    has_up, has_down = z < Z - 1, z > 0

    barrier = pltpu.get_barrier_semaphore()
    pl.semaphore_signal(barrier, 1, device_id={"dp": across}, device_id_type=MESH)

    @pl.when(has_up)
    def _():
        pl.semaphore_signal(barrier, 1, device_id={"dp": me + X}, device_id_type=MESH)

    @pl.when(has_down)
    def _():
        pl.semaphore_signal(barrier, 1, device_id={"dp": me - X}, device_id_type=MESH)

    def each(distance, run):
        if distance == 0:
            run(z, None)
            return

        @pl.when(z + distance < Z)
        def _():
            run(z + distance, True)

        @pl.when(z >= distance)
        def _():
            run(z - distance, False)

    def part(k):
        return pl.ds(CHUNKS[k][0], CHUNKS[k][1])

    def hbm(k, zz, column):
        start = pl.multiple_of((zz * X + column) * 144 + CHUNKS[k][0], 16)
        return g_ref.at[pl.ds(start, CHUNKS[k][1])]

    def own(k, zz):
        return own_b.at[zz, part(k)]

    def from_x(k, zz):
        return xq if CHUNKS[k][2] else xb.at[zz, part(k)]

    def from_z(k, zz, up, other):
        if other:
            return (up_o if up else down_o).at[zz]
        return (up_b if up else down_b).at[zz, part(k)]

    def load(k, zz, other=False):
        index = ((chunks if other else 0) + k) * Z + zz
        return pltpu.make_async_copy(
            hbm(k, zz, (1 - x) if other else x),
            other_d.at[zz] if other else own(k, zz),
            load_sem.at[index],
        )

    def x_copy(k, zz, src):
        unit = k * Z + zz
        return pltpu.make_async_remote_copy(
            src_ref=src, dst_ref=from_x(k, zz), send_sem=x_send.at[unit], recv_sem=x_recv.at[unit],
            device_id={"dp": across}, device_id_type=MESH,
        )

    def z_copy(k, zz, up, other):
        unit = ((chunks if other else 0) + k) * Z + zz
        return pltpu.make_async_remote_copy(
            src_ref=other_d.at[zz] if other else own(k, zz),
            dst_ref=from_z(k, zz, up, other),
            send_sem=(up_send if up else down_send).at[unit],
            recv_sem=(up_recv if up else down_recv).at[unit],
            device_id={"dp": me + X if up else me - X},
            device_id_type=MESH,
        )

    def total(k, dst, srcs):
        @pl.loop(0, CHUNKS[k][1] // 16)
        def _(step):
            rows = pl.ds(pl.multiple_of(step * 16, 16), 16)
            value = srcs[0][rows].astype(jnp.float32)
            for src in srcs[1:]:
                value = value + src[rows].astype(jnp.float32)
            dst[rows] = value.astype(dst.dtype)

    for distance in (3, 2, 1, 0):
        for k in range(chunks):
            def run(zz, up):
                load(k, zz).start()
                if CHUNKS[k][2]:
                    load(k, zz, True).start()
            each(distance, run)

    pl.semaphore_wait(barrier, 1 + has_up.astype(jnp.int32) + has_down.astype(jnp.int32))

    for distance in (3, 2, 1, 0):
        for k in range(chunks):
            if not CHUNKS[k][2]:
                each(distance, lambda zz, up: x_copy(k, zz, hbm(k, zz, 1 - x)).start())

    def pass_on(k, distance):
        def run(zz, up):
            behind = has_down if up else has_up
            if CHUNKS[k][2]:
                for other in (False, True):
                    mine = other_d.at[zz] if other else own(k, zz)
                    load(k, zz, other).wait()

                    @pl.when(behind)
                    def _():
                        z_copy(k, zz, up, other).wait_recv()
                        total(k, mine, [mine, from_z(k, zz, up, other)])

                    z_copy(k, zz, up, other).start()
                return
            load(k, zz).wait()
            x_copy(k, zz, hbm(k, zz, 1 - x)).wait_recv()

            @pl.when(behind)
            def _():
                z_copy(k, zz, up, False).wait_recv()
                total(k, own(k, zz), [own(k, zz), from_x(k, zz), from_z(k, zz, up, False)])

            @pl.when(jnp.logical_not(behind))
            def _():
                total(k, own(k, zz), [own(k, zz), from_x(k, zz)])

            z_copy(k, zz, up, False).start()
        each(distance, run)

    def add_z(dst, k, other):
        @pl.when(has_down)
        def _():
            z_copy(k, z, True, other).wait_recv()
            total(k, dst, [dst, from_z(k, z, True, other)])

        @pl.when(has_up)
        def _():
            z_copy(k, z, False, other).wait_recv()
            total(k, dst, [dst, from_z(k, z, False, other)])

    def send_direct(k):
        load(k, z, True).wait()
        total(k, acc, [other_d.at[z]])
        add_z(acc, k, True)
        total(k, other_d.at[z], [acc])
        x_copy(k, z, other_d.at[z]).start()

    def finish(k):
        dst = out.at[part(k)]
        load(k, z).wait()
        if CHUNKS[k][2]:
            total(k, dst, [own(k, z)])
            add_z(dst, k, False)
            x_copy(k, z, other_d.at[z]).wait_recv()
            total(k, dst, [dst, from_x(k, z)])
        else:
            x_copy(k, z, hbm(k, z, 1 - x)).wait_recv()
            total(k, dst, [own(k, z), from_x(k, z)])
            add_z(dst, k, False)

    straight = [k for k in range(chunks) if not CHUNKS[k][2]]
    direct = [k for k in range(chunks) if CHUNKS[k][2]]
    for distance in (3, 2, 1):
        for k in range(chunks):
            pass_on(k, distance)
    for k in direct:
        send_direct(k)
    for k in straight + direct:
        finish(k)

    for k in range(chunks):
        for distance in (3, 2, 1, 0):
            def run(zz, up):
                if not CHUNKS[k][2]:
                    x_copy(k, zz, hbm(k, zz, 1 - x)).wait_send()
                elif distance == 0:
                    x_copy(k, zz, other_d.at[zz]).wait_send()
                if distance:
                    z_copy(k, zz, up, False).wait_send()
                    if CHUNKS[k][2]:
                        z_copy(k, zz, up, True).wait_send()
            each(distance, run)


def sum_gradients(grad):
    n = lax.axis_size("dp")
    if not ring_fits(n, D // n):
        return lax.psum_scatter(grad, "dp", scatter_dimension=0, tiled=True).astype(jnp.float32)
    chunks = len(CHUNKS)
    dma = lambda count: pltpu.SemaphoreType.DMA((count,))
    ring = pltpu.VMEM((Z, 144, HALF), BF)
    short = [rows for first, rows, direct in CHUNKS if direct][0]
    ring_o = pltpu.VMEM((Z, short, HALF), BF)
    return pl.pallas_call(
        sum_kernel,
        out_shape=jax.ShapeDtypeStruct((144, HALF), jnp.float32),
        in_specs=[pl.BlockSpec(memory_space=pl.ANY)],
        out_specs=pl.BlockSpec(memory_space=pltpu.VMEM),
        scratch_shapes=[
            ring, ring_o, ring, pltpu.VMEM((short, HALF), BF),
            ring, ring_o, ring, ring_o, pltpu.VMEM((short, HALF), jnp.float32),
            dma(2 * chunks * Z), dma(chunks * Z), dma(chunks * Z),
            dma(2 * chunks * Z), dma(2 * chunks * Z), dma(2 * chunks * Z), dma(2 * chunks * Z),
        ],
        compiler_params=pltpu.CompilerParams(
            collective_id=1, has_side_effects=True, vmem_limit_bytes=VMEM_BYTES
        ),
        cost_estimate=pl.CostEstimate(flops=0, bytes_accessed=200_000_000, transcendentals=0),
        name="sum_gradients",
    )(grad)


def exchange_kernel(axes, modes, *refs):
    count = len(modes)
    ins, outs = refs[:count], refs[count : 2 * count]
    send_sem, recv_sem, own_sem = refs[2 * count :]
    dp, section = lax.axis_index("dp"), lax.axis_index("section")
    n, sections = lax.axis_size("dp"), lax.axis_size("section")
    if axes == "dp":
        size, me, where = n, dp, lambda p: {"dp": p}
    elif axes == "section":
        size, me, where = sections, section, lambda p: {"section": p}
    elif axes == "stage":
        low = section - lax.rem(section, 2)
        size, me = 2 * n, dp * 2 + lax.rem(section, 2)
        where = lambda p: {"dp": p // 2, "section": low + lax.rem(p, 2)}
    else:
        size, me = n * sections, dp * sections + section
        where = lambda p: {"dp": p // sections, "section": lax.rem(p, sections)}

    def part(k, p):
        if modes[k] == "all":
            return ins[k]
        index = {"each": p, "dp": p // 2, "core": lax.rem(p, 2)}[modes[k]]
        return ins[k].at[index]

    def copy(k, step, src, slot, p):
        return pltpu.make_async_remote_copy(
            src_ref=src, dst_ref=outs[k].at[slot],
            send_sem=send_sem.at[k, step], recv_sem=recv_sem.at[k, step],
            device_id=where(p), device_id_type=MESH,
        )

    barrier = pltpu.get_barrier_semaphore()

    @pl.loop(1, size)
    def _(step):
        pl.semaphore_signal(barrier, 1, device_id=where(lax.rem(me + step, size)), device_id_type=MESH)

    for k in range(count):
        pltpu.make_async_copy(part(k, me), outs[k].at[me], own_sem.at[k]).start()
    pl.semaphore_wait(barrier, size - 1)

    @pl.loop(1, size)
    def _(step):
        p = lax.rem(me + step, size)
        for k in range(count):
            copy(k, step, part(k, p), me, p).start()

    for k in range(count):
        pltpu.make_async_copy(part(k, me), outs[k].at[me], own_sem.at[k]).wait()

    @pl.loop(1, size)
    def _(step):
        p = lax.rem(me + size - step, size)
        for k in range(count):
            copy(k, step, part(k, p), p, p).wait_recv()
            copy(k, step, part(k, p), p, p).wait_send()


def exchange(ident, axes, modes, *arrays):
    n, sections = lax.axis_size("dp"), lax.axis_size("section")
    size = {"dp": n, "section": sections, "stage": 2 * n, "every": n * sections}[axes]
    blocks = [a.shape if mode == "all" else a.shape[1:] for a, mode in zip(arrays, modes)]
    count = len(arrays)
    vmem = pl.BlockSpec(memory_space=pltpu.VMEM)
    return pl.pallas_call(
        partial(exchange_kernel, axes, modes),
        out_shape=tuple(jax.ShapeDtypeStruct((size,) + b, a.dtype) for a, b in zip(arrays, blocks)),
        in_specs=[vmem] * count,
        out_specs=(vmem,) * count,
        scratch_shapes=[
            pltpu.SemaphoreType.DMA((count, size)),
            pltpu.SemaphoreType.DMA((count, size)),
            pltpu.SemaphoreType.DMA((count,)),
        ],
        compiler_params=pltpu.CompilerParams(
            collective_id=ident, has_side_effects=True, vmem_limit_bytes=VMEM_BYTES
        ),
        cost_estimate=pl.CostEstimate(flops=0, bytes_accessed=30_000_000, transcendentals=0),
        name="exchange_" + axes,
    )(*arrays)


def rows_of(value, size):
    value = value.reshape(-1)
    return jnp.pad(value, (0, size * 128 - value.shape[0])).reshape(size, 128)


def row_count(length, unit=8):
    return -(-length // (128 * unit)) * unit


def heads_of(value):
    return value.reshape(PATCHES, HEADS, HEAD_DIM)


def attention_forward(xm_half, w_attn, bblk):
    pair = to_half(matmul(xm_half, w_attn[0]) + bblk[:HALF])
    value = heads_of(to_half(matmul(xm_half, w_attn[1][:, :D]) + bblk[HALF : 3 * D]))
    query, key = heads_of(pair[:, :D]), heads_of(pair[:, D:])
    scores = jnp.einsum(
        "qhd,khd->hqk", query, key, preferred_element_type=jnp.float32
    ) * HEAD_DIM ** (-0.5)
    probs = jax.nn.softmax(scores, axis=-1)
    attended = to_half(
        jnp.einsum("hqk,khd->qhd", to_half(probs), value, preferred_element_type=jnp.float32)
    ).reshape(PATCHES, D)
    branch = matmul(attended, w_attn[1][:, D:]) + bblk[3 * D :]
    return (branch, (query, key, value, probs, attended))


def attention_backward(grad_half, saved, w_attn):
    query, key, value, probs, attended = saved
    d_att = heads_of(to_half(matmul_nt(grad_half, w_attn[1][:, D:])))
    flat = lambda grad: to_half(grad).reshape(PATCHES, D)
    d_value = flat(
        jnp.einsum("hqk,qhd->khd", to_half(probs), d_att, preferred_element_type=jnp.float32)
    )
    d_probs = jnp.einsum("qhd,khd->hqk", d_att, value, preferred_element_type=jnp.float32)
    d_scores = to_half(probs * (d_probs - jnp.sum(probs * d_probs, axis=-1, keepdims=True)))
    d_query = flat(
        jnp.einsum("hqk,khd->qhd", d_scores, key, preferred_element_type=jnp.float32)
        * HEAD_DIM ** (-0.5)
    )
    d_key = flat(
        jnp.einsum("hqk,qhd->khd", d_scores, query, preferred_element_type=jnp.float32)
        * HEAD_DIM ** (-0.5)
    )
    d_pair = jnp.concatenate([d_query, d_key], axis=1)
    d_xm = matmul_nt(d_pair, w_attn[0]) + matmul_nt(d_value, w_attn[1][:, :D])
    return (d_xm, d_query, d_key, d_value)


def modulated(x, mod):
    return layer_modulate(x, mod[None, :D], mod[None, D : 2 * D])


def modulated_back(x, mod, d_xm):
    pull = jax.vjp(layer_modulate, x, mod[None, :D], mod[None, D : 2 * D])[1]
    d_x, d_shift, d_scale = pull(d_xm)
    return (d_x, d_shift[0], d_scale[0])


def stage_forward(x_in, weights):
    mod_a, mod_m, w_attn, w_up, w_dn, b_attn, b_up, b_down = weights
    xm_a = to_half(modulated(x_in, mod_a))
    branch_a, saved = attention_forward(xm_a, w_attn, b_attn)
    x_mid = to_half(x_in + mod_a[None, 2 * D :] * branch_a).astype(jnp.float32)
    xm_m = to_half(modulated(x_mid, mod_m))
    pre = [matmul(xm_m, w_up[k]) + b_up[k] for k in range(2)]
    act = [to_half(jax.nn.gelu(half, approximate=True)) for half in pre]
    branch_m = matmul_nt(act[0], w_dn[0]) + matmul_nt(act[1], w_dn[1]) + b_down
    x_out = x_mid + mod_m[None, 2 * D :] * branch_m
    return (x_out, (xm_a, branch_a, saved, x_mid, xm_m, pre, act, branch_m))


def mlp_backward(d_out, weights, kept):
    mod_a, mod_m, w_attn, w_up, w_dn, b_attn, b_up, b_down = weights
    xm_a, branch_a, saved, x_mid, xm_m, pre, act, branch_m = kept
    d_gate = jnp.sum(d_out * branch_m, axis=0)
    grad_half = to_half(d_out * mod_m[None, 2 * D :])
    gelu_back = lambda half, grad: jax.vjp(partial(jax.nn.gelu, approximate=True), half)[1](grad)[0]
    d_pre = [to_half(gelu_back(pre[k], matmul(grad_half, w_dn[k]))) for k in range(2)]
    d_xm = matmul_nt(d_pre[0], w_up[0]) + matmul_nt(d_pre[1], w_up[1])
    d_x, d_shift, d_scale = modulated_back(x_mid, mod_m, d_xm)
    d_mod = to_half(jnp.concatenate([d_shift, d_scale, d_gate]))
    return (to_half(d_out + d_x).astype(jnp.float32), d_mod, grad_half, d_pre)


def attn_backward(d_out, x_in, weights, kept):
    mod_a, mod_m, w_attn, w_up, w_dn, b_attn, b_up, b_down = weights
    xm_a, branch_a, saved, x_mid, xm_m, pre, act, branch_m = kept
    d_gate = jnp.sum(d_out * branch_a, axis=0)
    grad_half = to_half(d_out * mod_a[None, 2 * D :])
    d_xm, d_query, d_key, d_value = attention_backward(grad_half, saved, w_attn)
    d_x, d_shift, d_scale = modulated_back(x_in, mod_a, d_xm)
    d_mod = to_half(jnp.concatenate([d_shift, d_scale, d_gate]))
    return (to_half(d_out + d_x), d_mod, grad_half, (d_query, d_key, d_value))


def final_step(x_out, fmod, w_head, b_head, target, counts, loss_scale):
    xf_half = to_half(modulated(x_out, fmod))
    error = matmul(xf_half, w_head) + b_head - target
    loss = counts * jnp.sum(error * error)
    d_pred = to_half(2.0 * loss_scale * counts * error)
    g_head = matmul_tn(xf_half, d_pred)
    d_x, d_shift, d_scale = modulated_back(x_out, fmod, matmul_nt(d_pred, w_head))
    return (loss, d_x, to_half(jnp.concatenate([d_shift, d_scale])), g_head, column_sums(d_pred))


def nesterov(weight, moment, average, grad, factor):
    clipped = grad * factor
    moment_new = momentum_rate * moment + clipped
    weight_new = weight - learn_rate * (clipped + momentum_rate * moment_new)
    average_new = ema_decay * average + (1.0 - ema_decay) * weight_new
    return (weight_new, moment_new, average_new, weight_new.astype(jnp.bfloat16))


def swap(array, by):
    peers = lax.axis_size("section")
    return lax.ppermute(array, "section", [(k, k ^ by) for k in range(peers)])


def pick(parts, index):
    return lax.dynamic_index_in_dim(parts, index, 0, keepdims=False)


def body(
    latents, noise, timesteps, labels, null_mask, valid,
    mod_w, mod_m, mod_e, block_w, block_m, block_e, down_w, down_m, down_e,
    stem_w, stem_m, stem_e, tail_w, tail_m, tail_e, biases, bias_m, bias_e,
):
    place = lax.axis_index("dp")
    section = lax.axis_index("section")
    stage = section // 2
    core = lax.rem(section, 2)
    even = core == 0
    n = lax.axis_size("dp")
    width = D // n

    downs = jnp.swapaxes(down_w, 1, 2)
    blk_half = to_half(block_w[0])
    crossing = swap(jnp.where(even, blk_half[:, HALF:], blk_half[:, :HALF]), 1)
    attn_half = jnp.where(even, blk_half[:, :HALF], crossing)
    up_half = jnp.where(even, crossing, blk_half[:, HALF:])
    dn_half = to_half(lax.dynamic_slice(downs, (stage, 0, core * HALF), (1, width, HALF))[0])
    up_own = lax.all_gather(up_half, "dp", axis=0, tiled=True)
    dn_own = lax.all_gather(dn_half, "dp", axis=0, tiled=True)
    w_up = (up_own, swap(up_own, 1))
    w_dn = (dn_own, swap(dn_own, 1))
    w_attn = gather_weights(attn_half)

    stems = stem_w.T
    classes_own = jnp.where(null_mask > 0, NCLS - 1, labels)
    meta = jnp.stack([timesteps, classes_own, valid], axis=1)
    images_own = meta.shape[0]
    meta = jnp.pad(meta, ((0, 8 - images_own), (0, 125)))
    stem_half = to_half(stems)
    tail_half = to_half(tail_w)
    table = stem_half[:, :NCLS]
    w_two = stem_half[:, NCLS + PATCH_IN + FREQ :]
    ends = NCLS, NCLS + PATCH_IN + FREQ
    small = jnp.concatenate([stem_half[:, ends[0] : ends[1]], tail_half[:, 2 * D :]], axis=1)
    small = jnp.pad(small, ((0, -width % 16), (0, -small.shape[1] % 128)))
    meta, small = exchange(2, "dp", ("all", "all"), meta, small)
    meta = meta[:, :images_own].reshape(n * images_own, 128)
    small = small[:, :width].reshape(D, -1)
    w_patch_all = small[:, :PATCH_IN]
    w_one_all = small[:, PATCH_IN : PATCH_IN + FREQ]
    w_head_all = small[:, PATCH_IN + FREQ : PATCH_IN + FREQ + HEAD_OUT]
    images = meta.shape[0]
    steps_all = meta[:, 0].astype(jnp.float32)
    picks = (meta[:, 1][:, None] == jnp.arange(NCLS, dtype=jnp.int32)[None, :]).astype(BF)
    count = jnp.sum(meta[:, 2].astype(jnp.float32))
    loss_scale = 1.0 / (count * PATCHES * HEAD_OUT)
    freq = to_half(time_features(steps_all))

    b_two = lax.dynamic_slice_in_dim(biases, 32 * D + place * width, width)
    hidden_pre = matmul_nt(w_one_all, freq) + biases[31 * D : 32 * D, None]
    hidden_all = to_half(jax.nn.silu(hidden_pre))
    cond = matmul(w_two, hidden_all) + b_two[:, None] + matmul_nt(table, picks)
    cond_low = to_half(cond).astype(jnp.float32)
    cond_own = jnp.where(section == 0, cond, cond_low)
    silu_own = to_half(jax.nn.silu(cond_own))
    silu_low = to_half(jax.nn.silu(cond_low))
    mod_half_w = to_half(mod_w[0])
    part_mod = matmul_tn(silu_own, mod_half_w)
    part_fm = matmul_tn(silu_low, tail_half[:, : 2 * D])
    parts = jnp.concatenate([part_mod, part_fm, jnp.zeros((images, 384), jnp.float32)], axis=1)
    (mods,) = exchange(3, "stage", ("each",), parts.reshape(images, 48, 128))
    mods = jnp.sum(mods.reshape(n, 2, 48 * 128), axis=0)
    bias_of = lambda first, length: lax.dynamic_slice_in_dim(biases, first, length)
    mod_a = mods[0, : 3 * D] + bias_of(6 * D * stage, 3 * D)
    mod_b = mods[1, : 3 * D] + bias_of(6 * D * stage + 3 * D, 3 * D)
    fmod = mods[0, 3 * D : 5 * D] + biases[33 * D : 35 * D]
    weights = (
        mod_a, mod_b, w_attn, w_up, w_dn,
        bias_of(12 * D + 8 * D * stage, 4 * D),
        [bias_of(16 * D + 8 * D * stage + HALF * half, HALF) for half in (core, 1 - core)],
        bias_of(28 * D + D * stage, D),
    )

    step = pick(timesteps, core).astype(jnp.float32)
    signal, spread = noise_levels(step)
    lat, noi = pick(latents, core)[None], pick(noise, core)[None]
    counts = pick(valid, core).astype(jnp.float32)
    tok_half = to_half(patchify(signal * lat + spread * noi))[0]
    target = jnp.concatenate([patchify(signal * noi - spread * lat), patchify(noi)], axis=2)[0]
    x_first = matmul_nt(tok_half, w_patch_all) + biases[30 * D : 31 * D] + position_table(GRID // 2, D)

    x_hop = swap(to_half(stage_forward(x_first, weights)[0]), 2)
    x_in = jnp.where(stage == 0, x_first, x_hop.astype(jnp.float32))
    x_out, kept = stage_forward(x_in, weights)
    loss, d_final, d_fmod, g_head, b_head = final_step(
        x_out, fmod, w_head_all, biases[35 * D :], target, counts, loss_scale
    )
    d_mid = mlp_backward(d_final, weights, kept)[0]
    d_hop = swap(attn_backward(d_mid, x_in, weights, kept)[0], 2)
    d_out = jnp.where(stage == 1, d_final, d_hop.astype(jnp.float32))
    xm_a, branch_a, saved, x_mid, xm_b, pre, act, branch_b = kept
    attended = saved[-1]

    d_mid, d_mod_b, d_branch_b, d_pre = mlp_backward(d_out, weights, kept)
    act_sib, branch_sib, xm_sib, pre_sib = swap((act[1], d_branch_b, xm_b, d_pre[1]), 1)
    g_dn = to_half(matmul_tn(d_branch_b, act[0]) + matmul_tn(branch_sib, act_sib))
    g_up = to_half(matmul_tn(xm_b, d_pre[0]) + matmul_tn(xm_sib, pre_sib))
    g_dn = lax.psum_scatter(g_dn, "dp", scatter_dimension=0, tiled=True)
    g_up = lax.psum_scatter(g_up, "dp", scatter_dimension=0, tiled=True)

    d_first, d_mod_a, d_branch_a, d_qkv = attn_backward(d_mid, x_in, weights, kept)
    d_query, d_key, d_value = d_qkv
    xa_sib, last_sib, one_sib, two_sib = swap(
        (
            xm_a,
            jnp.where(even, attended, xm_a),
            jnp.where(even, d_value, d_query),
            jnp.where(even, d_branch_a, d_key),
        ),
        1,
    )
    last = jnp.where(even, xm_a, attended)
    one = jnp.where(even, d_query, d_value)
    two = jnp.where(even, d_key, d_branch_a)
    g_attn = jnp.concatenate(
        [
            to_half(matmul_tn(xm_a, one) + matmul_tn(xa_sib, one_sib)),
            to_half(matmul_tn(last, two) + matmul_tn(last_sib, two_sib)),
        ],
        axis=1,
    )
    g_attn = sum_gradients(g_attn)
    crossing = swap(jnp.where(even, g_up, to_half(g_attn)), 1).astype(jnp.float32)
    g_up = g_up.astype(jnp.float32)
    g_blk = jnp.concatenate(
        [jnp.where(even, g_attn, crossing), jnp.where(even, crossing, g_up)], axis=1
    )
    g_facing = swap(g_dn, 2)
    g_sib, g_corner = swap((g_dn, g_facing), 1)
    in_core = lambda own, sib: jnp.concatenate(
        [jnp.where(even, own, sib), jnp.where(even, sib, own)], axis=1
    ).astype(jnp.float32)
    here, there = in_core(g_dn, g_sib), in_core(g_facing, g_corner)
    down_both = jnp.where(stage == 0, jnp.stack([here, there]), jnp.stack([there, here]))

    last_stage = (stage == 1).astype(jnp.float32)
    zeros_fm = jnp.zeros((2 * D + 384,), BF)
    d_fmod = jnp.concatenate([jnp.where(stage == 1, d_fmod, zeros_fm[: 2 * D]), zeros_fm[2 * D :]])
    d_mods = jnp.stack([jnp.concatenate([d_mod_a, d_fmod]), jnp.concatenate([d_mod_b, d_fmod])])
    last_own = jnp.where(stage == 0, column_sums(d_first), jnp.pad(b_head, (0, D - HEAD_OUT)))
    in_order = lambda own, sib: jnp.where(
        even, jnp.concatenate([own, sib]), jnp.concatenate([sib, own])
    )
    own_biases = jnp.concatenate(
        [
            *map(column_sums, d_qkv), column_sums(d_branch_a), in_order(*map(column_sums, d_pre)),
            column_sums(d_branch_b),
            last_own, loss[None],
        ]
    )
    piece = row_count(-(-own_biases.shape[0] // (2 * n)))
    own_biases = rows_of(own_biases, 2 * n * piece).reshape(2 * n, piece, 128)
    g_patch = jnp.pad(matmul_tn(d_first, tok_half), ((0, 0), (0, HEAD_OUT - PATCH_IN)))
    end_rows = row_count(width * HEAD_OUT)
    own_ends = jnp.where(stage == 0, g_patch, g_head).reshape(n, width * HEAD_OUT)
    own_ends = jnp.pad(own_ends, ((0, 0), (0, end_rows * 128 - width * HEAD_OUT))).reshape(n, end_rows, 128)
    d_mods, own_biases, own_ends = exchange(
        4, "stage", ("core", "each", "dp"), d_mods.reshape(2, 48, 128), own_biases, own_ends
    )
    d_mods = d_mods.reshape(images, 48 * 128)
    bias_piece = jnp.sum(own_biases, axis=0)
    own_ends = jnp.sum(own_ends, axis=0)
    d_mod_all, d_fm_all = d_mods[:, : 3 * D], d_mods[:, 3 * D : 5 * D]
    g_mod = matmul(silu_own, d_mod_all)
    c_own = matmul_nt(mod_half_w, d_mod_all)
    c_own = c_own + matmul_nt(tail_half[:, : 2 * D], jnp.where(section == 3, d_fm_all, jnp.zeros_like(d_fm_all)))
    c_own = silu_back(cond_own, c_own)
    cond_rows = row_count(width * images)
    c_all, end_pair, d_fm_all = exchange(
        5, "section", ("all", "all", "all"), rows_of(c_own, cond_rows), own_ends, d_fm_all
    )
    d_fm_all = d_fm_all[3]
    ends = [end_pair[k].reshape(-1)[: width * HEAD_OUT].reshape(width, HEAD_OUT) for k in (0, 3)]
    g_fm = matmul(silu_low, d_fm_all)
    c_all = [c_all[k].reshape(-1)[: width * images].reshape(width, images) for k in range(4)]
    d_cond = to_half(c_all[3])
    for slot in (2, 1, 0):
        d_cond = to_half(d_cond.astype(jnp.float32) + c_all[slot])
    part_hidden = matmul_tn(w_two, d_cond).reshape(n, width * images)
    part_hidden = jnp.pad(part_hidden, ((0, 0), (0, cond_rows * 128 - width * images)))
    (d_hidden,) = exchange(6, "dp", ("each",), part_hidden.reshape(n, cond_rows, 128))
    d_hidden = jnp.sum(d_hidden, axis=0).reshape(-1)[: width * images].reshape(width, images)
    pre_own = lax.dynamic_slice_in_dim(hidden_pre, place * width, width)
    d_pre_one = to_half(silu_back(pre_own, d_hidden))
    g_table = matmul(d_cond, picks)
    g_one = matmul(d_pre_one, freq)
    g_two = matmul_nt(d_cond, hidden_all)
    g_stem = jnp.concatenate([g_table, ends[0][:, :PATCH_IN], g_one, g_two], axis=1)
    g_tail = jnp.concatenate([g_fm, ends[1]], axis=1)

    square = lambda value: jnp.sum(value * value)
    once = (section == 0).astype(jnp.float32)
    squares = square(g_mod) + square(g_blk)
    squares = squares + once * (square(down_both) + square(g_stem) + square(g_tail))
    row_sums = lambda value: jnp.sum(value.astype(jnp.float32), axis=1)
    mod_piece = 3 * D // n
    mod_rows, slice_rows = row_count(mod_piece, 1), row_count(2 * width, 1)
    bias_mod = lax.dynamic_slice_in_dim(column_sums(d_mod_all), place * mod_piece, mod_piece)
    slices = jnp.concatenate([row_sums(d_pre_one), row_sums(d_cond)])
    news = jnp.concatenate(
        [bias_piece, rows_of(bias_mod, mod_rows), rows_of(slices, slice_rows), rows_of(squares[None], 1)]
    )
    news = jnp.pad(news, ((0, -news.shape[0] % 8), (0, 0)))
    (news,) = exchange(7, "every", ("all",), news)
    news = news.reshape(n, 4, -1, 128)
    first, second = piece + mod_rows, piece + mod_rows + slice_rows
    stages = [news[:, 2 * k : 2 * k + 2, :piece].reshape(-1) for k in range(2)]
    bias_mods = news[:, :, piece:first].reshape(n, 4, mod_rows * 128)[:, :, :mod_piece]
    bias_mods = bias_mods.transpose(1, 0, 2).reshape(-1)
    slices = news[:, 0, first:second].reshape(n, slice_rows * 128)[:, : 2 * width]
    bias_grad = jnp.concatenate(
        [bias_mods]
        + [part[: 8 * D] for part in stages]
        + [part[8 * D : 9 * D] for part in stages]
        + [stages[0][9 * D : 10 * D]]
        + [slices[:, :width].reshape(-1), slices[:, width:].reshape(-1)]
        + [column_sums(d_fm_all), stages[1][9 * D : 9 * D + HEAD_OUT]]
    )
    loss_sum = stages[1][10 * D]
    grad_norm = jnp.sqrt(jnp.sum(news[:, :, second, 0]) + square(bias_grad))
    factor = jnp.minimum(1.0, clip_limit / (grad_norm + 1e-06))
    mod_out = nesterov(mod_w, mod_m, mod_e, g_mod[None], factor)
    block_out = nesterov(block_w, block_m, block_e, g_blk[None], factor)
    flip = lambda value: jnp.swapaxes(value, 1, 2)
    down_out = tuple(map(flip, nesterov(downs, flip(down_m), flip(down_e), down_both, factor)))
    stem_out = tuple(value.T for value in nesterov(stems, stem_m.T, stem_e.T, g_stem, factor))
    tail_out = nesterov(tail_w, tail_m, tail_e, g_tail, factor)
    bias_out = nesterov(biases, bias_m, bias_e, bias_grad, factor)
    return (
        (loss_sum, count, grad_norm)
        + mod_out + block_out + down_out + stem_out + tail_out + bias_out
    )


def solution(mesh):
    images = (P("dp", None, None, None),) * 2 + (P("dp"),) * 4
    owned = P("section", "dp", None)
    states = (owned,) * 6 + (P(None, None, "dp"),) * 3 + (P(None, "dp"),) * 3 + (P("dp", None),) * 3 + (P(),) * 3
    updates = (owned,) * 8 + (P(None, None, "dp"),) * 4 + (P(None, "dp"),) * 4 + (P("dp", None),) * 4 + (P(),) * 4
    return jax.shard_map(
        body,
        mesh=mesh,
        in_specs=images + states,
        out_specs=(P(), P(), P()) + updates,
        check_vma=False,
    )
```

```python
from functools import partial
import math

import jax
import jax.numpy as jnp
from jax import lax
from jax.experimental import pallas as pl
from jax.experimental.pallas import tpu as pltpu
from jax.sharding import PartitionSpec as P

HEADS = 16
HEAD_DIM = 72
D = 1152
FF = 4608
HALF = FF // 2
NCLS = 1001
FREQ = 256
GRID = 32
PATCHES = 256
PATCH_IN = 16
HEAD_OUT = 32
LAYERS = 2
NBIAS = 40352


epsilon_norm = 1e-06
momentum_rate = 0.9
ema_decay = 0.9
learn_rate = 4000.0
clip_limit = 0.02
MESH = pl.DeviceIdType.MESH
BF = jnp.bfloat16


def matmul(left, right):
    return jnp.dot(left, right, preferred_element_type=jnp.float32)


def matmul_nt(left, right):
    return lax.dot_general(
        left, right, (((1,), (1,)), ((), ())), preferred_element_type=jnp.float32
    )


def matmul_tn(left, right):
    return lax.dot_general(
        left, right, (((0,), (0,)), ((), ())), preferred_element_type=jnp.float32
    )


def to_half(value):
    return value.astype(BF)


def column_sums(value):
    return jnp.sum(value.astype(jnp.float32), axis=0)


def silu_back(value, grad):
    return jax.vjp(jax.nn.silu, value)[1](grad)[0]


def patchify(field):
    images, side = (field.shape[0], field.shape[1] // 2)
    return (
        field.reshape(images, side, 2, side, 2, 4)
        .transpose(0, 1, 3, 2, 4, 5)
        .reshape(images, side * side, 16)
    )


def sincos_rows(places, width):
    omega = 1.0 / 10000.0 ** (jnp.arange(width // 2, dtype=jnp.float32) / (width // 2))
    angle = places[:, None] * omega[None, :]
    return jnp.concatenate([jnp.sin(angle), jnp.cos(angle)], axis=1)


def position_table(side, width):
    line = sincos_rows(jnp.arange(side, dtype=jnp.float32), width // 2)
    column = jnp.broadcast_to(line[None], (side, side, width // 2))
    row = jnp.broadcast_to(line[:, None], (side, side, width // 2))
    return jnp.concatenate([column, row], axis=2).reshape(side * side, width)


def time_features(steps):
    half = FREQ // 2
    freqs = jnp.exp(-math.log(10000.0) * jnp.arange(half, dtype=jnp.float32) / half)
    angle = steps[:, None] * freqs[None, :]
    return jnp.concatenate([jnp.cos(angle), jnp.sin(angle)], axis=1)


def noise_levels(steps):
    level = jnp.cos((steps / 1000.0 + 0.008) / 1.008 * (math.pi / 2)) ** 2
    return (jnp.sqrt(level), jnp.sqrt(1.0 - level))


Z, X = 4, 2
CHUNKS = ((0, 16, True), (16, 32, False), (48, 32, False), (80, 32, False), (112, 32, False))


def ring_fits(n, rows):
    return n == Z * X and rows == 144


def gather_kernel(blk_ref, out_blk, up_sem, down_sem, x_sem, sib_sem, recv_sem, sib_recv, own_sem):
    me = lax.axis_index("dp")
    section = lax.axis_index("section")
    z, x = me // X, lax.rem(me, X)
    core = lax.rem(section, 2)
    sibling = section + 1 - 2 * core
    across = me + 1 - 2 * x
    chunks = len(CHUNKS)
    has_up, has_down = z < Z - 1, z > 0

    barrier = pltpu.get_barrier_semaphore()
    pl.semaphore_signal(barrier, 1, device_id={"section": sibling}, device_id_type=MESH)
    pl.semaphore_signal(barrier, 1, device_id={"dp": across}, device_id_type=MESH)

    @pl.when(has_up)
    def _():
        pl.semaphore_signal(barrier, 1, device_id={"dp": me + X}, device_id_type=MESH)

    @pl.when(has_down)
    def _():
        pl.semaphore_signal(barrier, 1, device_id={"dp": me - X}, device_id_type=MESH)

    pl.semaphore_wait(barrier, 2 + has_up.astype(jnp.int32) + has_down.astype(jnp.int32))

    def place(owner, k, side):
        first, rows, unused = CHUNKS[k]
        return out_blk.at[side, pl.ds(pl.multiple_of(owner * 144 + first, 16), rows)]

    def source(owner, k, mine):
        if not mine:
            return place(owner, k, core)
        first, rows, unused = CHUNKS[k]
        return blk_ref.at[pl.ds(first, rows)]

    def copy(owner, k, mine, sem, target):
        unit = owner * chunks + k
        return pltpu.make_async_remote_copy(
            src_ref=source(owner, k, mine),
            dst_ref=place(owner, k, core),
            send_sem=sem.at[unit],
            recv_sem=recv_sem.at[unit],
            device_id={"dp": target},
            device_id_type=MESH,
        )

    def to_sibling(owner, k, mine):
        unit = owner * chunks + k
        return pltpu.make_async_remote_copy(
            src_ref=source(owner, k, mine),
            dst_ref=place(owner, k, core),
            send_sem=sib_sem.at[unit],
            recv_sem=sib_recv.at[unit],
            device_id={"section": sibling},
            device_id_type=MESH,
        )

    def own_copy(k):
        return pltpu.make_async_copy(source(me, k, True), place(me, k, core), own_sem.at[k])

    def arrived(owner, k):
        copy(owner, k, False, x_sem, across).wait_recv()

    for k in range(chunks):
        @pl.when(has_up)
        def _():
            copy(me, k, True, up_sem, me + X).start()

        @pl.when(has_down)
        def _():
            copy(me, k, True, down_sem, me - X).start()

        copy(me, k, True, x_sem, across).start()
        own_copy(k).start()
        to_sibling(me, k, True).start()

    def along(step, k, first_across):
        shift = 1 - 2 * x if first_across else 0
        crosses = (not first_across) and (not CHUNKS[k][2])

        @pl.when(z >= step)
        def _():
            owner = me - X * step + shift
            arrived(owner, k)

            @pl.when(has_up)
            def _():
                copy(owner, k, False, up_sem, me + X).start()

            if crosses:
                copy(owner, k, False, x_sem, across).start()
            to_sibling(owner, k, False).start()

        @pl.when(z + step < Z)
        def _():
            owner = me + X * step + shift
            arrived(owner, k)

            @pl.when(has_down)
            def _():
                copy(owner, k, False, down_sem, me - X).start()

            if crosses:
                copy(owner, k, False, x_sem, across).start()
            to_sibling(owner, k, False).start()

    def crossed(step, k):
        direct = CHUNKS[k][2]
        if step == 0:
            owner = across
            arrived(owner, k)
            if direct:
                @pl.when(has_up)
                def _():
                    copy(owner, k, False, up_sem, me + X).start()

                @pl.when(has_down)
                def _():
                    copy(owner, k, False, down_sem, me - X).start()
            to_sibling(owner, k, False).start()
        elif not direct:
            for sign in (-1, 1):
                @pl.when((z >= step) if sign < 0 else (z + step < Z))
                def _():
                    owner = across + sign * X * step
                    arrived(owner, k)
                    to_sibling(owner, k, False).start()

    for step in range(1, Z + 1):
        for k in range(chunks):
            if step < Z:
                along(step, k, False)
            crossed(step - 1, k)
            if step < Z and CHUNKS[k][2]:
                along(step, k, True)

    for k in range(chunks):
        direct = CHUNKS[k][2]
        own_copy(k).wait()
        for column in range(2):
            base = me if column == 0 else across
            for step in range(0, Z):
                for sign in (-1, 1) if step else (1,):
                    @pl.when((z >= step) if sign < 0 else (z + step < Z))
                    def _():
                        owner = base + sign * X * step
                        mine = column == 0 and step == 0
                        to_sibling(owner, k, mine).wait_send()
                        pltpu.make_async_remote_copy(
                            src_ref=place(owner, k, 1 - core),
                            dst_ref=place(owner, k, 1 - core),
                            send_sem=sib_sem.at[owner * chunks + k],
                            recv_sem=sib_recv.at[owner * chunks + k],
                            device_id={"section": sibling},
                            device_id_type=MESH,
                        ).wait_recv()
                        runs = column == 0 or direct
                        if runs and (step == 0 or sign < 0):
                            @pl.when(has_up)
                            def _():
                                copy(owner, k, mine, up_sem, me + X).wait_send()
                        if runs and (step == 0 or sign > 0):
                            @pl.when(has_down)
                            def _():
                                copy(owner, k, mine, down_sem, me - X).wait_send()
                        if column == 0 and (step == 0 or not direct):
                            copy(owner, k, mine, x_sem, across).wait_send()


def gather_weights(half):
    n = lax.axis_size("dp")
    if not ring_fits(n, half.shape[0]):
        own = lax.all_gather(half, "dp", axis=0, tiled=True)
        sib = swap(own, 1)
        even = lax.rem(lax.axis_index("section"), 2) == 0
        return jnp.where(even, jnp.stack([own, sib]), jnp.stack([sib, own]))
    units = n * len(CHUNKS)
    return pl.pallas_call(
        gather_kernel,
        out_shape=jax.ShapeDtypeStruct((2, D, HALF), BF),
        in_specs=[pl.BlockSpec(memory_space=pl.ANY)],
        out_specs=pl.BlockSpec(memory_space=pl.ANY),
        scratch_shapes=[pltpu.SemaphoreType.DMA((units,))] * 6
        + [pltpu.SemaphoreType.DMA((len(CHUNKS),))],
        compiler_params=pltpu.CompilerParams(collective_id=0, has_side_effects=True),
        cost_estimate=pl.CostEstimate(flops=0, bytes_accessed=200_000_000, transcendentals=0),
        name="gather_weights",
    )(half)


VMEM_BYTES = 60 * 1024 * 1024
SUM_CHUNKS = tuple((which,) + chunk for which in range(2) for chunk in CHUNKS)


def sum_kernel(
    g_first, g_second, out, own_b, other_d, xb, xq, up_b, up_o, down_b, down_o, acc,
    load_sem, x_send, x_recv, up_send, up_recv, down_send, down_recv,
):
    me = lax.axis_index("dp")
    z, x = me // X, lax.rem(me, X)
    across = me + 1 - 2 * x
    sources = (g_first, g_second)
    chunks = len(SUM_CHUNKS)
    has_up, has_down = z < Z - 1, z > 0

    barrier = pltpu.get_barrier_semaphore()
    pl.semaphore_signal(barrier, 1, device_id={"dp": across}, device_id_type=MESH)

    @pl.when(has_up)
    def _():
        pl.semaphore_signal(barrier, 1, device_id={"dp": me + X}, device_id_type=MESH)

    @pl.when(has_down)
    def _():
        pl.semaphore_signal(barrier, 1, device_id={"dp": me - X}, device_id_type=MESH)

    def each(distance, run):
        if distance == 0:
            run(z, None)
            return

        @pl.when(z + distance < Z)
        def _():
            run(z + distance, True)

        @pl.when(z >= distance)
        def _():
            run(z - distance, False)

    def part(k):
        return pl.ds(SUM_CHUNKS[k][1], SUM_CHUNKS[k][2])

    def hbm(k, zz, column):
        start = pl.multiple_of((zz * X + column) * 144 + SUM_CHUNKS[k][1], 16)
        return sources[SUM_CHUNKS[k][0]].at[pl.ds(start, SUM_CHUNKS[k][2])]

    def own(k, zz):
        return own_b.at[SUM_CHUNKS[k][0], zz, part(k)]

    def from_x(k, zz):
        return xq.at[SUM_CHUNKS[k][0]] if SUM_CHUNKS[k][3] else xb.at[SUM_CHUNKS[k][0], zz, part(k)]

    def from_z(k, zz, up, other):
        if other:
            return (up_o if up else down_o).at[SUM_CHUNKS[k][0], zz]
        return (up_b if up else down_b).at[SUM_CHUNKS[k][0], zz, part(k)]

    def other_of(k, zz):
        return other_d.at[SUM_CHUNKS[k][0], zz]

    def load(k, zz, other=False):
        index = ((chunks if other else 0) + k) * Z + zz
        return pltpu.make_async_copy(
            hbm(k, zz, (1 - x) if other else x),
            other_of(k, zz) if other else own(k, zz),
            load_sem.at[index],
        )

    def x_copy(k, zz, src):
        unit = k * Z + zz
        return pltpu.make_async_remote_copy(
            src_ref=src, dst_ref=from_x(k, zz), send_sem=x_send.at[unit], recv_sem=x_recv.at[unit],
            device_id={"dp": across}, device_id_type=MESH,
        )

    def z_copy(k, zz, up, other):
        unit = ((chunks if other else 0) + k) * Z + zz
        return pltpu.make_async_remote_copy(
            src_ref=other_of(k, zz) if other else own(k, zz),
            dst_ref=from_z(k, zz, up, other),
            send_sem=(up_send if up else down_send).at[unit],
            recv_sem=(up_recv if up else down_recv).at[unit],
            device_id={"dp": me + X if up else me - X},
            device_id_type=MESH,
        )

    def total(k, dst, srcs):
        @pl.loop(0, SUM_CHUNKS[k][2] // 16)
        def _(step):
            rows = pl.ds(pl.multiple_of(step * 16, 16), 16)
            value = srcs[0][rows].astype(jnp.float32)
            for src in srcs[1:]:
                value = value + src[rows].astype(jnp.float32)
            dst[rows] = value.astype(dst.dtype)

    for distance in (3, 2, 1, 0):
        for k in range(chunks):
            def run(zz, up):
                load(k, zz).start()
                if SUM_CHUNKS[k][3]:
                    load(k, zz, True).start()
            each(distance, run)

    pl.semaphore_wait(barrier, 1 + has_up.astype(jnp.int32) + has_down.astype(jnp.int32))

    for which in range(2):
        for distance in (3, 2, 1, 0):
            for k in range(chunks):
                if SUM_CHUNKS[k][0] == which and not SUM_CHUNKS[k][3]:
                    each(distance, lambda zz, up: x_copy(k, zz, hbm(k, zz, 1 - x)).start())

    def pass_on(k, distance):
        def run(zz, up):
            behind = has_down if up else has_up
            if SUM_CHUNKS[k][3]:
                for other in (False, True):
                    mine = other_of(k, zz) if other else own(k, zz)
                    load(k, zz, other).wait()

                    @pl.when(behind)
                    def _():
                        z_copy(k, zz, up, other).wait_recv()
                        total(k, mine, [mine, from_z(k, zz, up, other)])

                    z_copy(k, zz, up, other).start()
                return
            load(k, zz).wait()
            x_copy(k, zz, hbm(k, zz, 1 - x)).wait_recv()

            @pl.when(behind)
            def _():
                z_copy(k, zz, up, False).wait_recv()
                total(k, own(k, zz), [own(k, zz), from_x(k, zz), from_z(k, zz, up, False)])

            @pl.when(jnp.logical_not(behind))
            def _():
                total(k, own(k, zz), [own(k, zz), from_x(k, zz)])

            z_copy(k, zz, up, False).start()
        each(distance, run)

    def add_z(dst, k, other):
        @pl.when(has_down)
        def _():
            z_copy(k, z, True, other).wait_recv()
            total(k, dst, [dst, from_z(k, z, True, other)])

        @pl.when(has_up)
        def _():
            z_copy(k, z, False, other).wait_recv()
            total(k, dst, [dst, from_z(k, z, False, other)])

    def send_direct(k):
        load(k, z, True).wait()
        total(k, acc, [other_of(k, z)])
        add_z(acc, k, True)
        total(k, other_of(k, z), [acc])
        x_copy(k, z, other_of(k, z)).start()

    def finish(k):
        dst = out.at[SUM_CHUNKS[k][0], part(k)]
        load(k, z).wait()
        if SUM_CHUNKS[k][3]:
            total(k, dst, [own(k, z)])
            add_z(dst, k, False)
            x_copy(k, z, other_of(k, z)).wait_recv()
            total(k, dst, [dst, from_x(k, z)])
        else:
            x_copy(k, z, hbm(k, z, 1 - x)).wait_recv()
            total(k, dst, [own(k, z), from_x(k, z)])
            add_z(dst, k, False)

    straight = [k for k in range(chunks) if not SUM_CHUNKS[k][3]]
    direct = [k for k in range(chunks) if SUM_CHUNKS[k][3]]
    for which in range(2):
        of = lambda group: [k for k in group if SUM_CHUNKS[k][0] == which]
        for distance in (3, 2, 1):
            for k in of(range(chunks)):
                pass_on(k, distance)
        for k in of(direct):
            send_direct(k)
    for k in straight + direct:
        finish(k)

    for k in range(chunks):
        for distance in (3, 2, 1, 0):
            def run(zz, up):
                if not SUM_CHUNKS[k][3]:
                    x_copy(k, zz, hbm(k, zz, 1 - x)).wait_send()
                elif distance == 0:
                    x_copy(k, zz, other_of(k, zz)).wait_send()
                if distance:
                    z_copy(k, zz, up, False).wait_send()
                    if SUM_CHUNKS[k][3]:
                        z_copy(k, zz, up, True).wait_send()
            each(distance, run)


def sum_gradients(first, second):
    n = lax.axis_size("dp")
    if not ring_fits(n, D // n):
        total = lambda grad: lax.psum_scatter(grad, "dp", scatter_dimension=0, tiled=True)
        return jnp.stack([total(first), total(second)]).astype(jnp.float32)
    chunks = len(SUM_CHUNKS)
    dma = lambda count: pltpu.SemaphoreType.DMA((count,))
    ring = pltpu.VMEM((2, Z, 144, HALF), BF)
    short = [rows for start, rows, direct in CHUNKS if direct][0]
    ring_o = pltpu.VMEM((2, Z, short, HALF), BF)
    return pl.pallas_call(
        sum_kernel,
        out_shape=jax.ShapeDtypeStruct((2, 144, HALF), jnp.float32),
        in_specs=[pl.BlockSpec(memory_space=pl.ANY)] * 2,
        out_specs=pl.BlockSpec(memory_space=pltpu.VMEM),
        scratch_shapes=[
            ring, ring_o, ring, pltpu.VMEM((2, short, HALF), BF),
            ring, ring_o, ring, ring_o, pltpu.VMEM((short, HALF), jnp.float32),
            dma(2 * chunks * Z), dma(chunks * Z), dma(chunks * Z),
            dma(2 * chunks * Z), dma(2 * chunks * Z), dma(2 * chunks * Z), dma(2 * chunks * Z),
        ],
        compiler_params=pltpu.CompilerParams(
            collective_id=1, has_side_effects=True, vmem_limit_bytes=VMEM_BYTES
        ),
        cost_estimate=pl.CostEstimate(flops=0, bytes_accessed=300_000_000, transcendentals=0),
        name="sum_gradients",
    )(first, second)


def exchange_kernel(axes, modes, *refs):
    count = len(modes)
    ins, outs = refs[:count], refs[count : 2 * count]
    send_sem, recv_sem, own_sem = refs[2 * count :]
    dp, section = lax.axis_index("dp"), lax.axis_index("section")
    n, sections = lax.axis_size("dp"), lax.axis_size("section")
    if axes == "dp":
        size, me, where = n, dp, lambda p: {"dp": p}
    elif axes == "section":
        size, me, where = sections, section, lambda p: {"section": p}
    elif axes == "stage":
        low = section - lax.rem(section, 2)
        size, me = 2 * n, dp * 2 + lax.rem(section, 2)
        where = lambda p: {"dp": p // 2, "section": low + lax.rem(p, 2)}
    else:
        size, me = n * sections, dp * sections + section
        where = lambda p: {"dp": p // sections, "section": lax.rem(p, sections)}

    def part(k, p):
        if modes[k] == "all":
            return ins[k]
        index = {"each": p, "dp": p // 2, "core": lax.rem(p, 2)}[modes[k]]
        return ins[k].at[index]

    def copy(k, step, src, slot, p):
        return pltpu.make_async_remote_copy(
            src_ref=src, dst_ref=outs[k].at[slot],
            send_sem=send_sem.at[k, step], recv_sem=recv_sem.at[k, step],
            device_id=where(p), device_id_type=MESH,
        )

    barrier = pltpu.get_barrier_semaphore()

    @pl.loop(1, size)
    def _(step):
        pl.semaphore_signal(barrier, 1, device_id=where(lax.rem(me + step, size)), device_id_type=MESH)

    for k in range(count):
        pltpu.make_async_copy(part(k, me), outs[k].at[me], own_sem.at[k]).start()
    pl.semaphore_wait(barrier, size - 1)

    @pl.loop(1, size)
    def _(step):
        p = lax.rem(me + step, size)
        for k in range(count):
            copy(k, step, part(k, p), me, p).start()

    for k in range(count):
        pltpu.make_async_copy(part(k, me), outs[k].at[me], own_sem.at[k]).wait()

    @pl.loop(1, size)
    def _(step):
        p = lax.rem(me + size - step, size)
        for k in range(count):
            copy(k, step, part(k, p), p, p).wait_recv()
            copy(k, step, part(k, p), p, p).wait_send()


def exchange(ident, axes, modes, *arrays):
    n, sections = lax.axis_size("dp"), lax.axis_size("section")
    size = {"dp": n, "section": sections, "stage": 2 * n, "every": n * sections}[axes]
    blocks = [a.shape if mode == "all" else a.shape[1:] for a, mode in zip(arrays, modes)]
    count = len(arrays)
    vmem = pl.BlockSpec(memory_space=pltpu.VMEM)
    return pl.pallas_call(
        partial(exchange_kernel, axes, modes),
        out_shape=tuple(jax.ShapeDtypeStruct((size,) + b, a.dtype) for a, b in zip(arrays, blocks)),
        in_specs=[vmem] * count,
        out_specs=(vmem,) * count,
        scratch_shapes=[
            pltpu.SemaphoreType.DMA((count, size)),
            pltpu.SemaphoreType.DMA((count, size)),
            pltpu.SemaphoreType.DMA((count,)),
        ],
        compiler_params=pltpu.CompilerParams(
            collective_id=ident, has_side_effects=True, vmem_limit_bytes=VMEM_BYTES
        ),
        cost_estimate=pl.CostEstimate(flops=0, bytes_accessed=30_000_000, transcendentals=0),
        name="exchange_" + axes,
    )(*arrays)


def rows_of(value, size):
    value = value.reshape(-1)
    return jnp.pad(value, (0, size * 128 - value.shape[0])).reshape(size, 128)


def row_count(length, unit=8):
    return -(-length // (128 * unit)) * unit


TILE = 768
STEPS = HALF // TILE
GELU_SCALE = math.sqrt(2.0 / math.pi)


def mean_rows(value):
    return jnp.mean(value, axis=-1, keepdims=True)


def normalized(x):
    centered = x - mean_rows(x)
    inverse = lax.rsqrt(mean_rows(centered * centered) + epsilon_norm)
    return (centered * inverse, inverse)


def modulated_back(normed, inverse, scale, d_xm):
    d_normed = d_xm * (1.0 + scale)
    d_x = inverse * (d_normed - mean_rows(d_normed) - normed * mean_rows(d_normed * normed))
    return (d_x, jnp.sum(d_xm, axis=0), jnp.sum(d_xm * normed, axis=0))


def mlp_forward_kernel(
    x_ref, mod_ref, b_up_ref, b_down_ref, up_a, up_b, dn_a, dn_b,
    out_ref, xm_ref, branch_ref, pre_ref, act_ref, acc,
):
    step = pl.program_id(0)

    @pl.when(step == 0)
    def _():
        normed, unused = normalized(x_ref[...])
        xm_ref[...] = to_half(normed * (1.0 + mod_ref[1:2]) + mod_ref[0:1])
        acc[...] = jnp.zeros_like(acc)

    def tile(up, dn):
        pre = matmul(xm_ref[...], up[...]) + b_up_ref[...]
        cube = pre + 0.044715 * (pre * pre * pre)
        act = to_half(pre * (0.5 * (1.0 + jnp.tanh(GELU_SCALE * cube))))
        pre_ref[...] = pre
        act_ref[...] = act
        acc[...] += matmul_nt(act, dn[...])

    @pl.when(step < STEPS)
    def _():
        tile(up_a, dn_a)

    @pl.when(step >= STEPS)
    def _():
        tile(up_b, dn_b)

    @pl.when(step == 2 * STEPS - 1)
    def _():
        branch = acc[...] + b_down_ref[...]
        branch_ref[...] = branch
        out_ref[...] = x_ref[...] + mod_ref[2:3] * branch


def mlp_backward_kernel(
    d_ref, x_ref, mod_ref, branch_ref, pre_ref, up_a, up_b, dn_a, dn_b,
    d_in_ref, d_mod_ref, grad_ref, d_pre_ref, acc,
):
    step = pl.program_id(0)

    @pl.when(step == 0)
    def _():
        grad_ref[...] = to_half(d_ref[...] * mod_ref[2:3])
        acc[...] = jnp.zeros_like(acc)

    def tile(up, dn):
        d_act = matmul(grad_ref[...], dn[...])
        pre = pre_ref[...]
        square = pre * pre
        tanh = jnp.tanh(GELU_SCALE * (pre + 0.044715 * (square * pre)))
        slope = 0.5 * (1.0 + tanh) + (0.5 * pre) * (1.0 - tanh * tanh) * (
            GELU_SCALE * (1.0 + (3.0 * 0.044715) * square)
        )
        d_pre = to_half(d_act * slope)
        d_pre_ref[...] = d_pre
        acc[...] += matmul_nt(d_pre, up[...])

    @pl.when(step < STEPS)
    def _():
        tile(up_a, dn_a)

    @pl.when(step >= STEPS)
    def _():
        tile(up_b, dn_b)

    @pl.when(step == 2 * STEPS - 1)
    def _():
        normed, inverse = normalized(x_ref[...])
        d_x, d_shift, d_scale = modulated_back(normed, inverse, mod_ref[1:2], acc[...])
        d_in_ref[...] = to_half(d_ref[...] + d_x)
        d_mod_ref[0:1] = d_shift[None]
        d_mod_ref[1:2] = d_scale[None]
        d_mod_ref[2:3] = jnp.sum(d_ref[...] * branch_ref[...], axis=0)[None]


def whole_spec(shape):
    return pl.BlockSpec(shape, lambda step: (0,) * len(shape))


def tile_specs():
    first = lambda step: (0, jnp.minimum(step, STEPS - 1))
    second = lambda step: (0, jnp.maximum(step - STEPS, 0))
    return [pl.BlockSpec((D, TILE), first), pl.BlockSpec((D, TILE), second)] * 2


def mlp_forward(x, mod, b_up, b_down, w_up, w_dn):
    token = whole_spec((PATCHES, D))
    hidden = pl.BlockSpec((PATCHES, TILE), lambda step: (0, step))
    f32 = jax.ShapeDtypeStruct((PATCHES, D), jnp.float32)
    return pl.pallas_call(
        mlp_forward_kernel,
        grid=(2 * STEPS,),
        out_shape=(
            f32, jax.ShapeDtypeStruct((PATCHES, D), BF), f32,
            jax.ShapeDtypeStruct((PATCHES, FF), jnp.float32), jax.ShapeDtypeStruct((PATCHES, FF), BF),
        ),
        in_specs=[
            token, whole_spec((3, D)), pl.BlockSpec((1, TILE), lambda step: (0, step)), whole_spec((1, D)),
        ] + tile_specs(),
        out_specs=(token, token, token, hidden, hidden),
        scratch_shapes=[pltpu.VMEM((PATCHES, D), jnp.float32)],
        compiler_params=pltpu.CompilerParams(vmem_limit_bytes=VMEM_BYTES),
        cost_estimate=pl.CostEstimate(
            flops=4 * PATCHES * D * FF, bytes_accessed=4 * D * FF, transcendentals=PATCHES * FF
        ),
        name="mlp_forward",
    )(x, mod, b_up, b_down, *w_up, *w_dn)


def mlp_backward(d_out, x, mod, branch, pre, w_up, w_dn):
    token = whole_spec((PATCHES, D))
    hidden = pl.BlockSpec((PATCHES, TILE), lambda step: (0, step))
    half = jax.ShapeDtypeStruct((PATCHES, D), BF)
    return pl.pallas_call(
        mlp_backward_kernel,
        grid=(2 * STEPS,),
        out_shape=(
            half, jax.ShapeDtypeStruct((3, D), jnp.float32), half,
            jax.ShapeDtypeStruct((PATCHES, FF), BF),
        ),
        in_specs=[token, token, whole_spec((3, D)), token, hidden] + tile_specs(),
        out_specs=(token, whole_spec((3, D)), token, hidden),
        scratch_shapes=[pltpu.VMEM((PATCHES, D), jnp.float32)],
        compiler_params=pltpu.CompilerParams(vmem_limit_bytes=VMEM_BYTES),
        cost_estimate=pl.CostEstimate(
            flops=4 * PATCHES * D * FF, bytes_accessed=4 * D * FF, transcendentals=PATCHES * FF
        ),
        name="mlp_backward",
    )(d_out, x, mod, branch, pre, *w_up, *w_dn)


SUM_ROWS = 16


def collect_kernel(peers, flags_ref, *refs):
    tokens, d_pre_ref, mods, fm_ref, extra_ref = refs[:6], refs[6], refs[7:9], refs[9], refs[10]
    sums_ref, mods_ref = refs[11:]
    core, stage = flags_ref[0], flags_ref[1]
    ones = jnp.ones((8, PATCHES), BF)
    total = lambda value: matmul(ones, value)[0:1]
    sums_ref[...] = jnp.zeros_like(sums_ref)
    rows = [total(ref[...]) for ref in tokens]
    halves = [[total(d_pre_ref[:, D * k : D * (k + 1)]) for k in range(4)]]
    own = halves[0]
    order = [jnp.where(core == 0, own[k], own[(k + 2) % 4]) for k in range(4)]
    last = jnp.where(stage == 0, rows[5], extra_ref[0:1])
    for place, row in enumerate(rows[:4] + order + [rows[4], last, extra_ref[1:2]]):
        sums_ref[place : place + 1, :D] = row
    for k in range(2):
        block = jnp.concatenate([mods[k][...], fm_ref[...]], axis=0)
        mods_ref[k] = to_half(jnp.concatenate([block, jnp.zeros((16 - 5, D), jnp.float32)], axis=0))


def collect(flags, tokens, d_pre, mods, fm, extra):
    peers = 2 * lax.axis_size("dp")
    vmem = pl.BlockSpec(memory_space=pltpu.VMEM)
    return pl.pallas_call(
        partial(collect_kernel, peers),
        out_shape=(
            jax.ShapeDtypeStruct((SUM_ROWS, 128 * max(peers, 9)), jnp.float32),
            jax.ShapeDtypeStruct((2, 16, D), BF),
        ),
        in_specs=[pl.BlockSpec(memory_space=pltpu.SMEM)] + [vmem] * 11,
        out_specs=(vmem, vmem),
        compiler_params=pltpu.CompilerParams(vmem_limit_bytes=VMEM_BYTES),
        name="collect",
    )(flags, *tokens, d_pre, *mods, fm, extra)


def heads_of(value):
    return value.reshape(PATCHES, HEADS, HEAD_DIM)


def attention_forward(xm_half, w_attn, bblk):
    pair = to_half(matmul(xm_half, w_attn[0]) + bblk[:HALF])
    value = heads_of(to_half(matmul(xm_half, w_attn[1][:, :D]) + bblk[HALF : 3 * D]))
    query, key = heads_of(pair[:, :D]), heads_of(pair[:, D:])
    scores = jnp.einsum(
        "qhd,khd->hqk", query, key, preferred_element_type=jnp.float32
    ) * HEAD_DIM ** (-0.5)
    probs = jax.nn.softmax(scores, axis=-1)
    attended = to_half(
        jnp.einsum("hqk,khd->qhd", to_half(probs), value, preferred_element_type=jnp.float32)
    ).reshape(PATCHES, D)
    branch = matmul(attended, w_attn[1][:, D:]) + bblk[3 * D :]
    return (branch, (query, key, value, probs, attended))


def attention_backward(grad_half, saved, w_attn):
    query, key, value, probs, attended = saved
    d_att = heads_of(to_half(matmul_nt(grad_half, w_attn[1][:, D:])))
    flat = lambda grad: to_half(grad).reshape(PATCHES, D)
    d_value = flat(
        jnp.einsum("hqk,qhd->khd", to_half(probs), d_att, preferred_element_type=jnp.float32)
    )
    d_probs = jnp.einsum("qhd,khd->hqk", d_att, value, preferred_element_type=jnp.float32)
    d_scores = to_half(probs * (d_probs - jnp.sum(probs * d_probs, axis=-1, keepdims=True)))
    d_query = flat(
        jnp.einsum("hqk,khd->qhd", d_scores, key, preferred_element_type=jnp.float32)
        * HEAD_DIM ** (-0.5)
    )
    d_key = flat(
        jnp.einsum("hqk,qhd->khd", d_scores, query, preferred_element_type=jnp.float32)
        * HEAD_DIM ** (-0.5)
    )
    d_pair = jnp.concatenate([d_query, d_key], axis=1)
    d_xm = matmul_nt(d_pair, w_attn[0]) + matmul_nt(d_value, w_attn[1][:, :D])
    return (d_xm, d_query, d_key, d_value)


def stage_forward(x_in, weights):
    mod_a, mod_m, w_attn, w_up, w_dn, b_attn, b_up, b_down = weights
    normed, inverse = normalized(x_in)
    xm_a = to_half(normed * (1.0 + mod_a[1:2]) + mod_a[0:1])
    branch_a, saved = attention_forward(xm_a, w_attn, b_attn)
    x_mid = to_half(x_in + mod_a[2:3] * branch_a).astype(jnp.float32)
    x_out, xm_m, branch_m, pre, act = mlp_forward(x_mid, mod_m, b_up, b_down, w_up, w_dn)
    return (x_out, (xm_a, branch_a, saved, x_mid, xm_m, branch_m, pre, act))


def attn_backward(d_out, x_in, weights, kept):
    mod_a, mod_m, w_attn, w_up, w_dn, b_attn, b_up, b_down = weights
    branch_a, saved = kept[1:3]
    d_gate = jnp.sum(d_out * branch_a, axis=0)
    grad_half = to_half(d_out * mod_a[2:3])
    d_xm, d_query, d_key, d_value = attention_backward(grad_half, saved, w_attn)
    normed, inverse = normalized(x_in)
    d_x, d_shift, d_scale = modulated_back(normed, inverse, mod_a[1:2], d_xm)
    d_mod = jnp.stack([d_shift, d_scale, d_gate])
    return (to_half(d_out + d_x), d_mod, grad_half, (d_query, d_key, d_value))


def final_step(x_out, fmod, w_head, b_head, target, counts, loss_scale):
    normed, inverse = normalized(x_out)
    xf_half = to_half(normed * (1.0 + fmod[1:2]) + fmod[0:1])
    error = matmul(xf_half, w_head) + b_head - target
    loss = counts * jnp.sum(error * error)
    d_pred = to_half(2.0 * loss_scale * counts * error)
    g_head = matmul_tn(xf_half, d_pred)
    d_x, d_shift, d_scale = modulated_back(normed, inverse, fmod[1:2], matmul_nt(d_pred, w_head))
    return (loss, d_x, jnp.stack([d_shift, d_scale]), g_head, column_sums(d_pred))


def nesterov(weight, moment, average, grad, factor):
    clipped = grad * factor
    moment_new = momentum_rate * moment + clipped
    weight_new = weight - learn_rate * (clipped + momentum_rate * moment_new)
    average_new = ema_decay * average + (1.0 - ema_decay) * weight_new
    return (weight_new, moment_new, average_new, weight_new.astype(jnp.bfloat16))


def swap(array, by):
    peers = lax.axis_size("section")
    return lax.ppermute(array, "section", [(k, k ^ by) for k in range(peers)])


def pick(parts, index):
    return lax.dynamic_index_in_dim(parts, index, 0, keepdims=False)


def body(
    latents, noise, timesteps, labels, null_mask, valid,
    mod_w, mod_m, mod_e, block_w, block_m, block_e, down_w, down_m, down_e,
    stem_w, stem_m, stem_e, tail_w, tail_m, tail_e, biases, bias_m, bias_e,
):
    place = lax.axis_index("dp")
    section = lax.axis_index("section")
    stage = section // 2
    core = lax.rem(section, 2)
    even = core == 0
    n = lax.axis_size("dp")
    width = D // n

    downs = jnp.swapaxes(down_w, 1, 2)
    blk_half = to_half(block_w[0])
    crossing = swap(jnp.where(even, blk_half[:, HALF:], blk_half[:, :HALF]), 1)
    attn_half = jnp.where(even, blk_half[:, :HALF], crossing)
    up_half = jnp.where(even, crossing, blk_half[:, HALF:])
    dn_half = to_half(lax.dynamic_slice(downs, (stage, 0, core * HALF), (1, width, HALF))[0])
    up_own = lax.all_gather(up_half, "dp", axis=0, tiled=True)
    dn_own = lax.all_gather(dn_half, "dp", axis=0, tiled=True)
    w_up = (up_own, swap(up_own, 1))
    w_dn = (dn_own, swap(dn_own, 1))
    w_attn = gather_weights(attn_half)

    stems = stem_w.T
    classes_own = jnp.where(null_mask > 0, NCLS - 1, labels)
    meta = jnp.stack([timesteps, classes_own, valid], axis=1)
    images_own = meta.shape[0]
    meta = jnp.pad(meta, ((0, 8 - images_own), (0, 125)))
    stem_half = to_half(stems)
    tail_half = to_half(tail_w)
    table = stem_half[:, :NCLS]
    w_two = stem_half[:, NCLS + PATCH_IN + FREQ :]
    ends = NCLS, NCLS + PATCH_IN + FREQ
    small = jnp.concatenate([stem_half[:, ends[0] : ends[1]], tail_half[:, 2 * D :]], axis=1)
    small = jnp.pad(small, ((0, -width % 16), (0, -small.shape[1] % 128)))
    meta, small = exchange(2, "dp", ("all", "all"), meta, small)
    meta = meta[:, :images_own].reshape(n * images_own, 128)
    small = small[:, :width].reshape(D, -1)
    w_patch_all = small[:, :PATCH_IN]
    w_one_all = small[:, PATCH_IN : PATCH_IN + FREQ]
    w_head_all = small[:, PATCH_IN + FREQ : PATCH_IN + FREQ + HEAD_OUT]
    images = meta.shape[0]
    steps_all = meta[:, 0].astype(jnp.float32)
    picks = (meta[:, 1][:, None] == jnp.arange(NCLS, dtype=jnp.int32)[None, :]).astype(BF)
    count = jnp.sum(meta[:, 2].astype(jnp.float32))
    loss_scale = 1.0 / (count * PATCHES * HEAD_OUT)
    freq = to_half(time_features(steps_all))

    b_two = lax.dynamic_slice_in_dim(biases, 32 * D + place * width, width)
    hidden_pre = matmul_nt(w_one_all, freq) + biases[31 * D : 32 * D, None]
    hidden_all = to_half(jax.nn.silu(hidden_pre))
    cond = matmul(w_two, hidden_all) + b_two[:, None] + matmul_nt(table, picks)
    cond_low = to_half(cond).astype(jnp.float32)
    cond_own = jnp.where(section == 0, cond, cond_low)
    silu_own = to_half(jax.nn.silu(cond_own))
    silu_low = to_half(jax.nn.silu(cond_low))
    mod_half_w = to_half(mod_w[0])
    part_mod = matmul_tn(silu_own, mod_half_w)
    part_fm = matmul_tn(silu_low, tail_half[:, : 2 * D])
    parts = jnp.concatenate([part_mod, part_fm, jnp.zeros((images, 384), jnp.float32)], axis=1)
    (mods,) = exchange(3, "stage", ("each",), parts.reshape(images, 48, 128))
    mods = jnp.sum(mods.reshape(n, 2, 48 * 128), axis=0)
    bias_of = lambda first, length: lax.dynamic_slice_in_dim(biases, first, length)
    mod_a = (mods[0, : 3 * D] + bias_of(6 * D * stage, 3 * D)).reshape(3, D)
    mod_b = (mods[1, : 3 * D] + bias_of(6 * D * stage + 3 * D, 3 * D)).reshape(3, D)
    fmod = (mods[0, 3 * D : 5 * D] + biases[33 * D : 35 * D]).reshape(2, D)
    weights = (
        mod_a, mod_b, w_attn, w_up, w_dn,
        bias_of(12 * D + 8 * D * stage, 4 * D),
        jnp.concatenate(
            [bias_of(16 * D + 8 * D * stage + HALF * half, HALF)[None] for half in (core, 1 - core)], axis=1
        ),
        bias_of(28 * D + D * stage, D)[None],
    )

    step = pick(timesteps, core).astype(jnp.float32)
    signal, spread = noise_levels(step)
    lat, noi = pick(latents, core)[None], pick(noise, core)[None]
    counts = pick(valid, core).astype(jnp.float32)
    tok_half = to_half(patchify(signal * lat + spread * noi))[0]
    target = jnp.concatenate([patchify(signal * noi - spread * lat), patchify(noi)], axis=2)[0]
    x_first = matmul_nt(tok_half, w_patch_all) + biases[30 * D : 31 * D] + position_table(GRID // 2, D)

    x_hop = swap(to_half(stage_forward(x_first, weights)[0]), 2)
    x_in = jnp.where(stage == 0, x_first, x_hop.astype(jnp.float32))
    x_out, kept = stage_forward(x_in, weights)
    loss, d_final, d_fmod, g_head, b_head = final_step(
        x_out, fmod, w_head_all, biases[35 * D :], target, counts, loss_scale
    )
    xm_a, branch_a, saved, x_mid, xm_b, branch_b, pre, act = kept
    attended = saved[-1]
    back = lambda d_out: mlp_backward(d_out, x_mid, mod_b, branch_b, pre, w_up, w_dn)
    d_mid = back(d_final)[0].astype(jnp.float32)
    d_hop = swap(attn_backward(d_mid, x_in, weights, kept)[0], 2)
    d_out = jnp.where(stage == 1, d_final, d_hop.astype(jnp.float32))

    d_mid, d_mod_b, d_branch_b, d_pre = back(d_out)
    d_mid = d_mid.astype(jnp.float32)
    act_sib, branch_sib, xm_sib, pre_sib = swap((act[:, HALF:], d_branch_b, xm_b, d_pre[:, HALF:]), 1)
    g_dn = to_half(matmul_tn(d_branch_b, act[:, :HALF]) + matmul_tn(branch_sib, act_sib))
    g_up = to_half(matmul_tn(xm_b, d_pre[:, :HALF]) + matmul_tn(xm_sib, pre_sib))
    g_dn = lax.psum_scatter(g_dn, "dp", scatter_dimension=0, tiled=True)

    d_first, d_mod_a, d_branch_a, d_qkv = attn_backward(d_mid, x_in, weights, kept)
    d_query, d_key, d_value = d_qkv
    xa_sib, last_sib, one_sib, two_sib = swap(
        (
            xm_a,
            jnp.where(even, attended, xm_a),
            jnp.where(even, d_value, d_query),
            jnp.where(even, d_branch_a, d_key),
        ),
        1,
    )
    last = jnp.where(even, xm_a, attended)
    one = jnp.where(even, d_query, d_value)
    two = jnp.where(even, d_key, d_branch_a)
    g_attn = jnp.concatenate(
        [
            to_half(matmul_tn(xm_a, one) + matmul_tn(xa_sib, one_sib)),
            to_half(matmul_tn(last, two) + matmul_tn(last_sib, two_sib)),
        ],
        axis=1,
    )
    g_up, g_attn = sum_gradients(g_up, g_attn)
    crossing = swap(to_half(jnp.where(even, g_up, g_attn)), 1).astype(jnp.float32)
    g_blk = jnp.concatenate(
        [jnp.where(even, g_attn, crossing), jnp.where(even, crossing, g_up)], axis=1
    )
    g_facing = swap(g_dn, 2)
    g_sib, g_corner = swap((g_dn, g_facing), 1)
    in_core = lambda own, sib: jnp.concatenate(
        [jnp.where(even, own, sib), jnp.where(even, sib, own)], axis=1
    ).astype(jnp.float32)
    here, there = in_core(g_dn, g_sib), in_core(g_facing, g_corner)
    down_both = jnp.where(stage == 0, jnp.stack([here, there]), jnp.stack([there, here]))

    flags = jnp.stack([core, stage]).astype(jnp.int32)
    extra = jnp.stack([jnp.pad(b_head, (0, D - HEAD_OUT)), jnp.pad(loss[None], (0, D - 1))])
    d_fmod = jnp.where(stage == 1, d_fmod, jnp.zeros_like(d_fmod))
    own_biases, d_mods = collect(
        flags, d_qkv + (d_branch_a, d_branch_b, d_first), d_pre, (d_mod_a, d_mod_b), d_fmod, extra
    )
    g_patch = jnp.pad(matmul_tn(d_first, tok_half), ((0, 0), (0, HEAD_OUT - PATCH_IN)))
    end_rows = row_count(width * HEAD_OUT)
    own_ends = jnp.where(stage == 0, g_patch, g_head).reshape(n, width * HEAD_OUT)
    own_ends = jnp.pad(own_ends, ((0, 0), (0, end_rows * 128 - width * HEAD_OUT))).reshape(n, end_rows, 128)
    own_biases = own_biases.reshape(SUM_ROWS, -1, 128).transpose(1, 0, 2)[: 2 * n]
    d_mods, own_biases, own_ends = exchange(
        4, "stage", ("core", "each", "dp"), d_mods, own_biases, own_ends
    )
    bias_piece = jnp.sum(own_biases, axis=0)
    own_ends = jnp.sum(own_ends, axis=0)
    d_mod_all = d_mods[:, :3].reshape(images, 3 * D)
    d_fm_all = d_mods[:, 3:5].reshape(images, 2 * D)
    g_mod = matmul(silu_own, d_mod_all)
    c_own = matmul_nt(mod_half_w, d_mod_all)
    c_own = c_own + matmul_nt(tail_half[:, : 2 * D], jnp.where(section == 3, d_fm_all, jnp.zeros_like(d_fm_all)))
    c_own = silu_back(cond_own, c_own)
    cond_rows = row_count(width * images)
    c_all, end_pair, d_fm_all = exchange(
        5, "section", ("all", "all", "all"), rows_of(c_own, cond_rows), own_ends, d_fm_all
    )
    d_fm_all = d_fm_all[3]
    ends = [end_pair[k].reshape(-1)[: width * HEAD_OUT].reshape(width, HEAD_OUT) for k in (0, 3)]
    g_fm = matmul(silu_low, d_fm_all)
    c_all = [c_all[k].reshape(-1)[: width * images].reshape(width, images) for k in range(4)]
    d_cond = to_half(c_all[3])
    for slot in (2, 1, 0):
        d_cond = to_half(d_cond.astype(jnp.float32) + c_all[slot])
    part_hidden = matmul_tn(w_two, d_cond).reshape(n, width * images)
    part_hidden = jnp.pad(part_hidden, ((0, 0), (0, cond_rows * 128 - width * images)))
    (d_hidden,) = exchange(6, "dp", ("each",), part_hidden.reshape(n, cond_rows, 128))
    d_hidden = jnp.sum(d_hidden, axis=0).reshape(-1)[: width * images].reshape(width, images)
    pre_own = lax.dynamic_slice_in_dim(hidden_pre, place * width, width)
    d_pre_one = to_half(silu_back(pre_own, d_hidden))
    g_table = matmul(d_cond, picks)
    g_one = matmul(d_pre_one, freq)
    g_two = matmul_nt(d_cond, hidden_all)
    g_stem = jnp.concatenate([g_table, ends[0][:, :PATCH_IN], g_one, g_two], axis=1)
    g_tail = jnp.concatenate([g_fm, ends[1]], axis=1)

    square = lambda value: jnp.sum(value * value)
    once = (section == 0).astype(jnp.float32)
    squares = square(g_mod) + square(g_blk)
    squares = squares + once * (square(down_both) + square(g_stem) + square(g_tail))
    row_sums = lambda value: jnp.sum(value.astype(jnp.float32), axis=1)
    mod_piece = 3 * D // n
    mod_rows, slice_rows = row_count(mod_piece, 1), row_count(2 * width, 1)
    bias_mod = lax.dynamic_slice_in_dim(column_sums(d_mod_all), place * mod_piece, mod_piece)
    slices = jnp.concatenate([row_sums(d_pre_one), row_sums(d_cond)])
    news = jnp.concatenate(
        [bias_piece, rows_of(bias_mod, mod_rows), rows_of(slices, slice_rows), rows_of(squares[None], 1)]
    )
    news = jnp.pad(news, ((0, -news.shape[0] % 8), (0, 0)))
    (news,) = exchange(7, "every", ("all",), news)
    news = news.reshape(n, 4, -1, 128)
    piece = SUM_ROWS
    first, second = piece + mod_rows, piece + mod_rows + slice_rows
    stages = []
    for k in range(2):
        pieces = news[:, 2 * k : 2 * k + 2, :piece].reshape(2 * n, SUM_ROWS, 128)[: D // 128]
        stages.append(pieces.transpose(1, 0, 2).reshape(-1))
    bias_mods = news[:, :, piece:first].reshape(n, 4, mod_rows * 128)[:, :, :mod_piece]
    bias_mods = bias_mods.transpose(1, 0, 2).reshape(-1)
    slices = news[:, 0, first:second].reshape(n, slice_rows * 128)[:, : 2 * width]
    bias_grad = jnp.concatenate(
        [bias_mods]
        + [part[: 8 * D] for part in stages]
        + [part[8 * D : 9 * D] for part in stages]
        + [stages[0][9 * D : 10 * D]]
        + [slices[:, :width].reshape(-1), slices[:, width:].reshape(-1)]
        + [column_sums(d_fm_all), stages[1][9 * D : 9 * D + HEAD_OUT]]
    )
    loss_sum = stages[1][10 * D]
    grad_norm = jnp.sqrt(jnp.sum(news[:, :, second, 0]) + square(bias_grad))
    factor = jnp.minimum(1.0, clip_limit / (grad_norm + 1e-06))
    mod_out = nesterov(mod_w, mod_m, mod_e, g_mod[None], factor)
    block_out = nesterov(block_w, block_m, block_e, g_blk[None], factor)
    flip = lambda value: jnp.swapaxes(value, 1, 2)
    down_out = tuple(map(flip, nesterov(downs, flip(down_m), flip(down_e), down_both, factor)))
    stem_out = tuple(value.T for value in nesterov(stems, stem_m.T, stem_e.T, g_stem, factor))
    tail_out = nesterov(tail_w, tail_m, tail_e, g_tail, factor)
    bias_out = nesterov(biases, bias_m, bias_e, bias_grad, factor)
    return (
        (loss_sum, count, grad_norm)
        + mod_out + block_out + down_out + stem_out + tail_out + bias_out
    )


def solution(mesh):
    images = (P("dp", None, None, None),) * 2 + (P("dp"),) * 4
    owned = P("section", "dp", None)
    states = (owned,) * 6 + (P(None, None, "dp"),) * 3 + (P(None, "dp"),) * 3 + (P("dp", None),) * 3 + (P(),) * 3
    updates = (owned,) * 8 + (P(None, None, "dp"),) * 4 + (P(None, "dp"),) * 4 + (P("dp", None),) * 4 + (P(),) * 4
    return jax.shard_map(
        body,
        mesh=mesh,
        in_specs=images + states,
        out_specs=(P(), P(), P()) + updates,
        check_vma=False,
    )
```

```python
from functools import partial
import math

import jax
import jax.numpy as jnp
from jax import lax
from jax.experimental import pallas as pl
from jax.experimental.pallas import tpu as pltpu
from jax.sharding import PartitionSpec as P

HEADS = 16
HEAD_DIM = 72
D = 1152
FF = 4608
HALF = FF // 2
NCLS = 1001
FREQ = 256
GRID = 32
PATCHES = 256
PATCH_IN = 16
HEAD_OUT = 32
LAYERS = 2
NBIAS = 40352


epsilon_norm = 1e-06
momentum_rate = 0.9
ema_decay = 0.9
learn_rate = 4000.0
clip_limit = 0.02
MESH = pl.DeviceIdType.MESH
BF = jnp.bfloat16


def matmul(left, right):
    return jnp.dot(left, right, preferred_element_type=jnp.float32)


def matmul_nt(left, right):
    return lax.dot_general(
        left, right, (((1,), (1,)), ((), ())), preferred_element_type=jnp.float32
    )


def matmul_tn(left, right):
    return lax.dot_general(
        left, right, (((0,), (0,)), ((), ())), preferred_element_type=jnp.float32
    )


def to_half(value):
    return value.astype(BF)


def column_sums(value):
    return jnp.sum(value.astype(jnp.float32), axis=0)


def silu_back(value, grad):
    return jax.vjp(jax.nn.silu, value)[1](grad)[0]


def patchify(field):
    images, side = (field.shape[0], field.shape[1] // 2)
    return (
        field.reshape(images, side, 2, side, 2, 4)
        .transpose(0, 1, 3, 2, 4, 5)
        .reshape(images, side * side, 16)
    )


def sincos_rows(places, width):
    omega = 1.0 / 10000.0 ** (jnp.arange(width // 2, dtype=jnp.float32) / (width // 2))
    angle = places[:, None] * omega[None, :]
    return jnp.concatenate([jnp.sin(angle), jnp.cos(angle)], axis=1)


def position_table(side, width):
    line = sincos_rows(jnp.arange(side, dtype=jnp.float32), width // 2)
    column = jnp.broadcast_to(line[None], (side, side, width // 2))
    row = jnp.broadcast_to(line[:, None], (side, side, width // 2))
    return jnp.concatenate([column, row], axis=2).reshape(side * side, width)


def time_features(steps):
    half = FREQ // 2
    freqs = jnp.exp(-math.log(10000.0) * jnp.arange(half, dtype=jnp.float32) / half)
    angle = steps[:, None] * freqs[None, :]
    return jnp.concatenate([jnp.cos(angle), jnp.sin(angle)], axis=1)


def noise_levels(steps):
    level = jnp.cos((steps / 1000.0 + 0.008) / 1.008 * (math.pi / 2)) ** 2
    return (jnp.sqrt(level), jnp.sqrt(1.0 - level))


Z, X = 4, 2
GATHER_CHUNKS = (
    (0, 0, 16, True), (0, 16, 32, False), (0, 48, 32, False), (0, 80, 32, False), (0, 112, 32, False),
    (1, 0, 48, True), (1, 48, 48, False), (1, 96, 48, False),
)
CHUNKS = ((0, 16, True), (16, 32, False), (48, 32, False), (80, 32, False), (112, 32, False))
META = 1280
PIECE = 768


def ring_fits(n, rows):
    return n == Z * X and rows == 144


def gather_kernel(
    blk_ref, dn_ref, meta_ref, small_ref, two_ref, table_ref, mod_ref, fm_ref, b_one, b_two,
    out_blk, out_dn, meta_out, small_out, pre_out, cond_out, mods_out,
    part, parts, arrived_parts, meta_send, meta_recv, small_send, small_recv, part_send, part_recv, local_sem,
    up_sem, down_sem, x_sem, sib_sem, recv_sem, sib_recv, own_sem,
):
    me = lax.axis_index("dp")
    section = lax.axis_index("section")
    z, x = me // X, lax.rem(me, X)
    core = lax.rem(section, 2)
    sibling = section + 1 - 2 * core
    across = me + 1 - 2 * x
    chunks = len(GATHER_CHUNKS)
    low = section - core
    group, place_in = Z * X * 2, me * 2 + core
    where = lambda p: {"dp": p // 2, "section": low + lax.rem(p, 2)}
    has_up, has_down = z < Z - 1, z > 0

    barrier = pltpu.get_barrier_semaphore()

    @pl.loop(1, group)
    def _(step):
        pl.semaphore_signal(
            barrier, 1, device_id=where(lax.rem(place_in + step, group)), device_id_type=MESH
        )

    pl.semaphore_wait(barrier, group - 1)

    def news(step, p, slot):
        copies = []
        for src, dst, send, recv in (
            (meta_ref, meta_out, meta_send, meta_recv), (small_ref, small_out, small_send, small_recv)
        ):
            copies.append(
                pltpu.make_async_remote_copy(
                    src_ref=src, dst_ref=dst.at[slot], send_sem=send.at[step], recv_sem=recv.at[step],
                    device_id={"dp": p}, device_id_type=MESH,
                )
            )
        return copies

    def own_news():
        return [
            pltpu.make_async_copy(meta_ref, meta_out.at[me], local_sem.at[0]),
            pltpu.make_async_copy(small_ref, small_out.at[me], local_sem.at[1]),
        ]

    def part_copy(step, p, slot):
        return pltpu.make_async_remote_copy(
            src_ref=parts.at[p], dst_ref=arrived_parts.at[slot],
            send_sem=part_send.at[step], recv_sem=part_recv.at[step],
            device_id=where(p), device_id_type=MESH,
        )

    own_part = pltpu.make_async_copy(parts.at[place_in], arrived_parts.at[place_in], local_sem.at[2])

    for copy_in in own_news():
        copy_in.start()

    @pl.loop(1, Z * X)
    def _(step):
        p = lax.rem(me + step, Z * X)
        for copy_out in news(step, p, me):
            copy_out.start()

    def place(owner, k, side):
        which, first, rows, unused = GATHER_CHUNKS[k]
        return (out_dn if which else out_blk).at[side, pl.ds(pl.multiple_of(owner * 144 + first, 16), rows)]

    def source(owner, k, mine):
        if not mine:
            return place(owner, k, core)
        which, first, rows, unused = GATHER_CHUNKS[k]
        return (dn_ref if which else blk_ref).at[pl.ds(first, rows)]

    def copy(owner, k, mine, sem, target):
        unit = owner * chunks + k
        return pltpu.make_async_remote_copy(
            src_ref=source(owner, k, mine),
            dst_ref=place(owner, k, core),
            send_sem=sem.at[unit],
            recv_sem=recv_sem.at[unit],
            device_id={"dp": target},
            device_id_type=MESH,
        )

    def to_sibling(owner, k, mine):
        unit = owner * chunks + k
        return pltpu.make_async_remote_copy(
            src_ref=source(owner, k, mine),
            dst_ref=place(owner, k, core),
            send_sem=sib_sem.at[unit],
            recv_sem=sib_recv.at[unit],
            device_id={"section": sibling},
            device_id_type=MESH,
        )

    def own_copy(k):
        return pltpu.make_async_copy(source(me, k, True), place(me, k, core), own_sem.at[k])

    def arrived(owner, k):
        copy(owner, k, False, x_sem, across).wait_recv()

    for k in range(chunks):
        @pl.when(has_up)
        def _():
            copy(me, k, True, up_sem, me + X).start()

        @pl.when(has_down)
        def _():
            copy(me, k, True, down_sem, me - X).start()

        copy(me, k, True, x_sem, across).start()
        own_copy(k).start()
        to_sibling(me, k, True).start()

    for copy_in in own_news():
        copy_in.wait()

    @pl.loop(1, Z * X)
    def _(step):
        p = lax.rem(me + Z * X - step, Z * X)
        for copy_in in news(step, p, p):
            copy_in.wait_recv()
            copy_in.wait_send()

    rows_all = Z * X * 8
    meta = to_half(meta_out[...].reshape(rows_all, META))
    one = small_out[:, :, :FREQ].reshape(D, FREQ)
    pre = matmul_nt(meta[:, :FREQ], one) + b_one[...]
    pre_out[...] = pre
    hidden = to_half(jax.nn.silu(pre))
    cond = matmul_nt(hidden, two_ref[...]) + b_two[...] + matmul_nt(meta[:, FREQ:], table_ref[...])
    cond_out[...] = cond
    cond_low = to_half(cond).astype(jnp.float32)
    own_cond = jnp.where(section == 0, cond, cond_low)
    part[:, : 3 * D] = matmul(to_half(jax.nn.silu(own_cond)), mod_ref[...])
    part[:, 3 * D : 5 * D] = matmul(to_half(jax.nn.silu(cond_low)), fm_ref[...])
    part[:, 5 * D :] = jnp.zeros((rows_all, 8 * PIECE - 5 * D), jnp.float32)
    for index in range(Z * X):
        for image in range(2):
            row = 8 * index + image
            for k in range(8):
                parts[2 * index + image, k : k + 1] = part[row : row + 1, PIECE * k : PIECE * (k + 1)]
    own_part.start()

    @pl.loop(1, group)
    def _(step):
        p = lax.rem(place_in + step, group)
        part_copy(step, p, place_in).start()

    def along(step, k, first_across):
        shift = 1 - 2 * x if first_across else 0
        crosses = (not first_across) and (not GATHER_CHUNKS[k][3])

        @pl.when(z >= step)
        def _():
            owner = me - X * step + shift
            arrived(owner, k)

            @pl.when(has_up)
            def _():
                copy(owner, k, False, up_sem, me + X).start()

            if crosses:
                copy(owner, k, False, x_sem, across).start()
            to_sibling(owner, k, False).start()

        @pl.when(z + step < Z)
        def _():
            owner = me + X * step + shift
            arrived(owner, k)

            @pl.when(has_down)
            def _():
                copy(owner, k, False, down_sem, me - X).start()

            if crosses:
                copy(owner, k, False, x_sem, across).start()
            to_sibling(owner, k, False).start()

    def crossed(step, k):
        direct = GATHER_CHUNKS[k][3]
        if step == 0:
            owner = across
            arrived(owner, k)
            if direct:
                @pl.when(has_up)
                def _():
                    copy(owner, k, False, up_sem, me + X).start()

                @pl.when(has_down)
                def _():
                    copy(owner, k, False, down_sem, me - X).start()
            to_sibling(owner, k, False).start()
        elif not direct:
            for sign in (-1, 1):
                @pl.when((z >= step) if sign < 0 else (z + step < Z))
                def _():
                    owner = across + sign * X * step
                    arrived(owner, k)
                    to_sibling(owner, k, False).start()

    for step in range(1, Z + 1):
        for k in range(chunks):
            if step < Z:
                along(step, k, False)
            crossed(step - 1, k)
            if step < Z and GATHER_CHUNKS[k][3]:
                along(step, k, True)

    own_part.wait()

    @pl.loop(1, group)
    def _(step):
        p = lax.rem(place_in + group - step, group)
        part_copy(step, p, p).wait_recv()
        part_copy(step, p, p).wait_send()

    for source_core in range(2):
        total = arrived_parts[source_core]
        for index in range(1, Z * X):
            total = total + arrived_parts[2 * index + source_core]
        mods_out[source_core] = total

    for k in range(chunks):
        direct = GATHER_CHUNKS[k][3]
        own_copy(k).wait()
        for column in range(2):
            base = me if column == 0 else across
            for step in range(0, Z):
                for sign in (-1, 1) if step else (1,):
                    @pl.when((z >= step) if sign < 0 else (z + step < Z))
                    def _():
                        owner = base + sign * X * step
                        mine = column == 0 and step == 0
                        to_sibling(owner, k, mine).wait_send()
                        pltpu.make_async_remote_copy(
                            src_ref=place(owner, k, 1 - core),
                            dst_ref=place(owner, k, 1 - core),
                            send_sem=sib_sem.at[owner * chunks + k],
                            recv_sem=sib_recv.at[owner * chunks + k],
                            device_id={"section": sibling},
                            device_id_type=MESH,
                        ).wait_recv()
                        runs = column == 0 or direct
                        if runs and (step == 0 or sign < 0):
                            @pl.when(has_up)
                            def _():
                                copy(owner, k, mine, up_sem, me + X).wait_send()
                        if runs and (step == 0 or sign > 0):
                            @pl.when(has_down)
                            def _():
                                copy(owner, k, mine, down_sem, me - X).wait_send()
                        if column == 0 and (step == 0 or not direct):
                            copy(owner, k, mine, x_sem, across).wait_send()


def gather_weights(blk, dn, meta, small, w_two, table, w_mod, w_fm, b_one, b_two):
    n, width = lax.axis_size("dp"), blk.shape[0]
    section = lax.axis_index("section")
    if not ring_fits(n, width):
        both = lambda own, sib: jnp.where(
            lax.rem(section, 2) == 0, jnp.stack([own, sib]), jnp.stack([sib, own])
        )
        blk = lax.all_gather(blk, "dp", axis=0, tiled=True)
        dn = lax.all_gather(dn, "dp", axis=0, tiled=True)
        small = jnp.pad(small, ((0, -width % 16), (0, 0)))
        meta, small = exchange(2, "dp", ("all", "all"), meta, small)
        small = small[:, :width]
        rows = to_half(meta.reshape(-1, META))
        pre = matmul_nt(rows[:, :FREQ], small[:, :, :FREQ].reshape(D, FREQ)) + b_one
        hidden = to_half(jax.nn.silu(pre))
        cond = matmul_nt(hidden, w_two) + b_two + matmul_nt(rows[:, FREQ:], table)
        cond_low = to_half(cond).astype(jnp.float32)
        own_cond = jnp.where(section == 0, cond, cond_low)
        parts = [
            matmul(to_half(jax.nn.silu(own_cond)), w_mod),
            matmul(to_half(jax.nn.silu(cond_low)), w_fm),
        ]
        parts = jnp.pad(jnp.concatenate(parts, axis=1), ((0, 0), (0, 8 * PIECE - 5 * D)))
        parts = parts.reshape(n, 8, 8, PIECE)[:, :2].reshape(2 * n, 8, PIECE)
        (parts,) = exchange(3, "stage", ("each",), parts)
        mods = jnp.sum(parts.reshape(n, 2, 8, PIECE), axis=0)
        return (both(blk, swap(blk, 1)), both(dn, swap(dn, 1)), meta, small, pre, cond, mods)
    units = n * len(GATHER_CHUNKS)
    hbm, vmem = pl.BlockSpec(memory_space=pl.ANY), pl.BlockSpec(memory_space=pltpu.VMEM)
    dma = lambda count: pltpu.SemaphoreType.DMA((count,))
    f32 = jnp.float32
    return pl.pallas_call(
        gather_kernel,
        out_shape=(
            jax.ShapeDtypeStruct((2, D, FF), BF), jax.ShapeDtypeStruct((2, D, HALF), BF),
            jax.ShapeDtypeStruct((n, 8, META), f32), jax.ShapeDtypeStruct((n,) + small.shape, BF),
            jax.ShapeDtypeStruct((n * 8, D), f32), jax.ShapeDtypeStruct((n * 8, width), f32),
            jax.ShapeDtypeStruct((2, 8, PIECE), f32),
        ),
        in_specs=[hbm] * 2 + [vmem] * 8,
        out_specs=(hbm, hbm) + (vmem,) * 5,
        scratch_shapes=[
            pltpu.VMEM((n * 8, 8 * PIECE), f32),
            pltpu.VMEM((2 * n, 8, PIECE), f32), pltpu.VMEM((2 * n, 8, PIECE), f32),
            dma(n), dma(n), dma(n), dma(n), dma(2 * n), dma(2 * n), dma(3),
        ]
        + [dma(units)] * 6
        + [dma(len(GATHER_CHUNKS))],
        compiler_params=pltpu.CompilerParams(
            collective_id=0, has_side_effects=True, vmem_limit_bytes=VMEM_BYTES
        ),
        cost_estimate=pl.CostEstimate(flops=0, bytes_accessed=400_000_000, transcendentals=0),
        name="gather_weights",
    )(blk, dn, meta, small, w_two, table, w_mod, w_fm, b_one, b_two)


VMEM_BYTES = 60 * 1024 * 1024
SUM_CHUNKS = tuple((which,) + chunk for which in range(2) for chunk in CHUNKS)


def sum_kernel(
    g_first, g_second, out, own_b, other_d, xb, xq, up_b, up_o, down_b, down_o, acc,
    load_sem, x_send, x_recv, up_send, up_recv, down_send, down_recv,
):
    me = lax.axis_index("dp")
    z, x = me // X, lax.rem(me, X)
    across = me + 1 - 2 * x
    sources = (g_first, g_second)
    chunks = len(SUM_CHUNKS)
    has_up, has_down = z < Z - 1, z > 0

    barrier = pltpu.get_barrier_semaphore()
    pl.semaphore_signal(barrier, 1, device_id={"dp": across}, device_id_type=MESH)

    @pl.when(has_up)
    def _():
        pl.semaphore_signal(barrier, 1, device_id={"dp": me + X}, device_id_type=MESH)

    @pl.when(has_down)
    def _():
        pl.semaphore_signal(barrier, 1, device_id={"dp": me - X}, device_id_type=MESH)

    def each(distance, run):
        if distance == 0:
            run(z, None)
            return

        @pl.when(z + distance < Z)
        def _():
            run(z + distance, True)

        @pl.when(z >= distance)
        def _():
            run(z - distance, False)

    def part(k):
        return pl.ds(SUM_CHUNKS[k][1], SUM_CHUNKS[k][2])

    def hbm(k, zz, column):
        start = pl.multiple_of((zz * X + column) * 144 + SUM_CHUNKS[k][1], 16)
        return sources[SUM_CHUNKS[k][0]].at[pl.ds(start, SUM_CHUNKS[k][2])]

    def own(k, zz):
        return own_b.at[SUM_CHUNKS[k][0], zz, part(k)]

    def from_x(k, zz):
        return xq.at[SUM_CHUNKS[k][0]] if SUM_CHUNKS[k][3] else xb.at[SUM_CHUNKS[k][0], zz, part(k)]

    def from_z(k, zz, up, other):
        if other:
            return (up_o if up else down_o).at[SUM_CHUNKS[k][0], zz]
        return (up_b if up else down_b).at[SUM_CHUNKS[k][0], zz, part(k)]

    def other_of(k, zz):
        return other_d.at[SUM_CHUNKS[k][0], zz]

    def load(k, zz, other=False):
        index = ((chunks if other else 0) + k) * Z + zz
        return pltpu.make_async_copy(
            hbm(k, zz, (1 - x) if other else x),
            other_of(k, zz) if other else own(k, zz),
            load_sem.at[index],
        )

    def x_copy(k, zz, src):
        unit = k * Z + zz
        return pltpu.make_async_remote_copy(
            src_ref=src, dst_ref=from_x(k, zz), send_sem=x_send.at[unit], recv_sem=x_recv.at[unit],
            device_id={"dp": across}, device_id_type=MESH,
        )

    def z_copy(k, zz, up, other):
        unit = ((chunks if other else 0) + k) * Z + zz
        return pltpu.make_async_remote_copy(
            src_ref=other_of(k, zz) if other else own(k, zz),
            dst_ref=from_z(k, zz, up, other),
            send_sem=(up_send if up else down_send).at[unit],
            recv_sem=(up_recv if up else down_recv).at[unit],
            device_id={"dp": me + X if up else me - X},
            device_id_type=MESH,
        )

    def total(k, dst, srcs):
        @pl.loop(0, SUM_CHUNKS[k][2] // 16)
        def _(step):
            rows = pl.ds(pl.multiple_of(step * 16, 16), 16)
            value = srcs[0][rows].astype(jnp.float32)
            for src in srcs[1:]:
                value = value + src[rows].astype(jnp.float32)
            dst[rows] = value.astype(dst.dtype)

    for distance in (3, 2, 1, 0):
        for k in range(chunks):
            def run(zz, up):
                load(k, zz).start()
                if SUM_CHUNKS[k][3]:
                    load(k, zz, True).start()
            each(distance, run)

    pl.semaphore_wait(barrier, 1 + has_up.astype(jnp.int32) + has_down.astype(jnp.int32))

    for which in range(2):
        for distance in (3, 2, 1, 0):
            for k in range(chunks):
                if SUM_CHUNKS[k][0] == which and not SUM_CHUNKS[k][3]:
                    each(distance, lambda zz, up: x_copy(k, zz, hbm(k, zz, 1 - x)).start())

    def pass_on(k, distance):
        def run(zz, up):
            behind = has_down if up else has_up
            if SUM_CHUNKS[k][3]:
                for other in (False, True):
                    mine = other_of(k, zz) if other else own(k, zz)
                    load(k, zz, other).wait()

                    @pl.when(behind)
                    def _():
                        z_copy(k, zz, up, other).wait_recv()
                        total(k, mine, [mine, from_z(k, zz, up, other)])

                    z_copy(k, zz, up, other).start()
                return
            load(k, zz).wait()
            x_copy(k, zz, hbm(k, zz, 1 - x)).wait_recv()

            @pl.when(behind)
            def _():
                z_copy(k, zz, up, False).wait_recv()
                total(k, own(k, zz), [own(k, zz), from_x(k, zz), from_z(k, zz, up, False)])

            @pl.when(jnp.logical_not(behind))
            def _():
                total(k, own(k, zz), [own(k, zz), from_x(k, zz)])

            z_copy(k, zz, up, False).start()
        each(distance, run)

    def add_z(dst, k, other):
        @pl.when(has_down)
        def _():
            z_copy(k, z, True, other).wait_recv()
            total(k, dst, [dst, from_z(k, z, True, other)])

        @pl.when(has_up)
        def _():
            z_copy(k, z, False, other).wait_recv()
            total(k, dst, [dst, from_z(k, z, False, other)])

    def send_direct(k):
        load(k, z, True).wait()
        total(k, acc, [other_of(k, z)])
        add_z(acc, k, True)
        total(k, other_of(k, z), [acc])
        x_copy(k, z, other_of(k, z)).start()

    def finish(k):
        dst = out.at[SUM_CHUNKS[k][0], part(k)]
        load(k, z).wait()
        if SUM_CHUNKS[k][3]:
            total(k, dst, [own(k, z)])
            add_z(dst, k, False)
            x_copy(k, z, other_of(k, z)).wait_recv()
            total(k, dst, [dst, from_x(k, z)])
        else:
            x_copy(k, z, hbm(k, z, 1 - x)).wait_recv()
            total(k, dst, [own(k, z), from_x(k, z)])
            add_z(dst, k, False)

    straight = [k for k in range(chunks) if not SUM_CHUNKS[k][3]]
    direct = [k for k in range(chunks) if SUM_CHUNKS[k][3]]
    for which in range(2):
        of = lambda group: [k for k in group if SUM_CHUNKS[k][0] == which]
        for distance in (3, 2, 1):
            for k in of(range(chunks)):
                pass_on(k, distance)
        for k in of(direct):
            send_direct(k)
    for k in straight + direct:
        finish(k)

    for k in range(chunks):
        for distance in (3, 2, 1, 0):
            def run(zz, up):
                if not SUM_CHUNKS[k][3]:
                    x_copy(k, zz, hbm(k, zz, 1 - x)).wait_send()
                elif distance == 0:
                    x_copy(k, zz, other_of(k, zz)).wait_send()
                if distance:
                    z_copy(k, zz, up, False).wait_send()
                    if SUM_CHUNKS[k][3]:
                        z_copy(k, zz, up, True).wait_send()
            each(distance, run)


def sum_gradients(first, second):
    n = lax.axis_size("dp")
    if not ring_fits(n, D // n):
        total = lambda grad: lax.psum_scatter(grad, "dp", scatter_dimension=0, tiled=True)
        return jnp.stack([total(first), total(second)]).astype(jnp.float32)
    chunks = len(SUM_CHUNKS)
    dma = lambda count: pltpu.SemaphoreType.DMA((count,))
    ring = pltpu.VMEM((2, Z, 144, HALF), BF)
    short = [rows for start, rows, direct in CHUNKS if direct][0]
    ring_o = pltpu.VMEM((2, Z, short, HALF), BF)
    return pl.pallas_call(
        sum_kernel,
        out_shape=jax.ShapeDtypeStruct((2, 144, HALF), jnp.float32),
        in_specs=[pl.BlockSpec(memory_space=pl.ANY)] * 2,
        out_specs=pl.BlockSpec(memory_space=pltpu.VMEM),
        scratch_shapes=[
            ring, ring_o, ring, pltpu.VMEM((2, short, HALF), BF),
            ring, ring_o, ring, ring_o, pltpu.VMEM((short, HALF), jnp.float32),
            dma(2 * chunks * Z), dma(chunks * Z), dma(chunks * Z),
            dma(2 * chunks * Z), dma(2 * chunks * Z), dma(2 * chunks * Z), dma(2 * chunks * Z),
        ],
        compiler_params=pltpu.CompilerParams(
            collective_id=1, has_side_effects=True, vmem_limit_bytes=VMEM_BYTES
        ),
        cost_estimate=pl.CostEstimate(flops=0, bytes_accessed=300_000_000, transcendentals=0),
        name="sum_gradients",
    )(first, second)


def exchange_kernel(axes, modes, *refs):
    count = len(modes)
    ins, outs = refs[:count], refs[count : 2 * count]
    send_sem, recv_sem, own_sem = refs[2 * count :]
    dp, section = lax.axis_index("dp"), lax.axis_index("section")
    n, sections = lax.axis_size("dp"), lax.axis_size("section")
    if axes == "dp":
        size, me, where = n, dp, lambda p: {"dp": p}
    elif axes == "section":
        size, me, where = sections, section, lambda p: {"section": p}
    elif axes == "stage":
        low = section - lax.rem(section, 2)
        size, me = 2 * n, dp * 2 + lax.rem(section, 2)
        where = lambda p: {"dp": p // 2, "section": low + lax.rem(p, 2)}
    else:
        size, me = n * sections, dp * sections + section
        where = lambda p: {"dp": p // sections, "section": lax.rem(p, sections)}

    def part(k, p):
        if modes[k] == "all":
            return ins[k]
        index = {"each": p, "dp": p // 2, "core": lax.rem(p, 2)}[modes[k]]
        return ins[k].at[index]

    def copy(k, step, src, slot, p):
        return pltpu.make_async_remote_copy(
            src_ref=src, dst_ref=outs[k].at[slot],
            send_sem=send_sem.at[k, step], recv_sem=recv_sem.at[k, step],
            device_id=where(p), device_id_type=MESH,
        )

    barrier = pltpu.get_barrier_semaphore()

    @pl.loop(1, size)
    def _(step):
        pl.semaphore_signal(barrier, 1, device_id=where(lax.rem(me + step, size)), device_id_type=MESH)

    for k in range(count):
        pltpu.make_async_copy(part(k, me), outs[k].at[me], own_sem.at[k]).start()
    pl.semaphore_wait(barrier, size - 1)

    @pl.loop(1, size)
    def _(step):
        p = lax.rem(me + step, size)
        for k in range(count):
            copy(k, step, part(k, p), me, p).start()

    for k in range(count):
        pltpu.make_async_copy(part(k, me), outs[k].at[me], own_sem.at[k]).wait()

    @pl.loop(1, size)
    def _(step):
        p = lax.rem(me + size - step, size)
        for k in range(count):
            copy(k, step, part(k, p), p, p).wait_recv()
            copy(k, step, part(k, p), p, p).wait_send()


def exchange(ident, axes, modes, *arrays):
    n, sections = lax.axis_size("dp"), lax.axis_size("section")
    size = {"dp": n, "section": sections, "stage": 2 * n, "every": n * sections}[axes]
    blocks = [a.shape if mode == "all" else a.shape[1:] for a, mode in zip(arrays, modes)]
    count = len(arrays)
    vmem = pl.BlockSpec(memory_space=pltpu.VMEM)
    return pl.pallas_call(
        partial(exchange_kernel, axes, modes),
        out_shape=tuple(jax.ShapeDtypeStruct((size,) + b, a.dtype) for a, b in zip(arrays, blocks)),
        in_specs=[vmem] * count,
        out_specs=(vmem,) * count,
        scratch_shapes=[
            pltpu.SemaphoreType.DMA((count, size)),
            pltpu.SemaphoreType.DMA((count, size)),
            pltpu.SemaphoreType.DMA((count,)),
        ],
        compiler_params=pltpu.CompilerParams(
            collective_id=ident, has_side_effects=True, vmem_limit_bytes=VMEM_BYTES
        ),
        cost_estimate=pl.CostEstimate(flops=0, bytes_accessed=30_000_000, transcendentals=0),
        name="exchange_" + axes,
    )(*arrays)


def rows_of(value, size):
    value = value.reshape(-1)
    return jnp.pad(value, (0, size * 128 - value.shape[0])).reshape(size, 128)


def row_count(length, unit=8):
    return -(-length // (128 * unit)) * unit


TILE = 768
STEPS = HALF // TILE
GELU_SCALE = math.sqrt(2.0 / math.pi)
SCALE = HEAD_DIM ** (-0.5)


def mean_rows(value):
    return jnp.mean(value, axis=-1, keepdims=True)


def normalized(x):
    centered = x - mean_rows(x)
    inverse = lax.rsqrt(mean_rows(centered * centered) + epsilon_norm)
    return (centered * inverse, inverse)


def modulated_back(normed, inverse, scale, d_xm):
    d_normed = d_xm * (1.0 + scale)
    d_x = inverse * (d_normed - mean_rows(d_normed) - normed * mean_rows(d_normed * normed))
    return (d_x, jnp.sum(d_xm, axis=0), jnp.sum(d_xm * normed, axis=0))


def window(head):
    low = HEAD_DIM * head // 128 * 128
    high = -(-HEAD_DIM * (head + 1) // 128) * 128
    lane = lax.broadcasted_iota(jnp.int32, (PATCHES, high - low), 1) + low
    return slice(low, high), (lane >= HEAD_DIM * head) & (lane < HEAD_DIM * (head + 1))


def own_lanes(mask, value):
    return jnp.where(mask, value, jnp.zeros_like(value))


def softmax_rows(scores):
    shifted = jnp.exp(scores - jnp.max(scores, axis=-1, keepdims=True))
    return shifted / jnp.sum(shifted, axis=-1, keepdims=True)


def half_of(ref, which, side):
    return ref.at[which, :, pl.ds(pl.multiple_of(side * HALF, 128) if which else side * HALF, HALF)]


def weight_copies(sources, targets, sem):
    return [pltpu.make_async_copy(src, dst, sem.at[k]) for k, (src, dst) in enumerate(zip(sources, targets))]


def forward_kernel(
    save, flags, x_ref, mod_a, mod_m, b_attn, b_up, b_down, w_blk, w_dn, out_ref, *refs
):
    if save:
        xm_ref, qkv_ref, att_ref, branch_a_ref, mid_ref, xm2_ref, branch_m_ref, pre_ref, act_ref = refs[:9]
        wa, wu, wd, acc, sem = refs[9:]
    else:
        xm_ref, qkv_ref, att_ref, mid_ref, xm2_ref, wa, wu, wd, acc, sem = refs
    copies = weight_copies(
        [half_of(w_blk, 0, 0), half_of(w_blk, 0, 1)]
        + [ref for side in (flags[0], 1 - flags[0]) for ref in (half_of(w_blk, 1, side), w_dn.at[side])],
        (wa.at[0], wa.at[1], wu.at[0], wd.at[0], wu.at[1], wd.at[1]),
        sem,
    )
    for copy in copies:
        copy.start()
    normed, unused = normalized(x_ref[...])
    xm_ref[...] = to_half(normed * (1.0 + mod_a[1:2]) + mod_a[0:1])
    acc[...] = jnp.zeros_like(acc)
    for k in range(3):
        if k != 1:
            copies[k // 2].wait()
        half, first = (0, D * k) if k < 2 else (1, 0)
        part = slice(D * k, D * (k + 1))
        qkv_ref[:, part] = to_half(
            matmul(xm_ref[...], wa[half, :, first : first + D]) + b_attn[:, part]
        )
    for head in range(HEADS):
        lanes, mask = window(head)
        at = lambda k: slice(D * k + lanes.start, D * k + lanes.stop)
        query = own_lanes(mask, qkv_ref[:, at(0)])
        probs = softmax_rows(matmul_nt(query, qkv_ref[:, at(1)]) * SCALE)
        acc[:, lanes] += own_lanes(mask, matmul(to_half(probs), qkv_ref[:, at(2)]))
    att_ref[...] = to_half(acc[...])
    branch = matmul(att_ref[...], wa[1, :, D:]) + b_attn[:, 3 * D :]
    if save:
        branch_a_ref[...] = branch
    mid_ref[...] = to_half(x_ref[...] + mod_a[2:3] * branch).astype(jnp.float32)
    normed, unused = normalized(mid_ref[...])
    xm2_ref[...] = to_half(normed * (1.0 + mod_m[1:2]) + mod_m[0:1])
    acc[...] = jnp.broadcast_to(b_down[...], acc.shape)
    for half in range(2):
        copies[2 + 2 * half].wait()
        copies[3 + 2 * half].wait()
        for step in range(STEPS):
            own = slice(TILE * step, TILE * (step + 1))
            part = slice(HALF * half + TILE * step, HALF * half + TILE * (step + 1))
            pre = matmul(xm2_ref[...], wu[half, :, own]) + b_up[:, part]
            cube = pre + 0.044715 * (pre * pre * pre)
            act = to_half(pre * (0.5 * (1.0 + jnp.tanh(GELU_SCALE * cube))))
            if save:
                pre_ref[:, part] = pre
                act_ref[:, part] = act
            acc[...] += matmul_nt(act, wd[half, :, own])
    if save:
        branch_m_ref[...] = acc[...]
    out = mid_ref[...] + mod_m[2:3] * acc[...]
    out_ref[...] = out.astype(out_ref.dtype)


def backward_kernel(
    flags, d_ref, x_ref, mid_ref, mod_a, mod_m, branch_a, branch_m, qkv_ref, pre_hbm, w_blk, w_dn,
    d_in_ref, d_mod_a, d_mod_m, grad_a, grad_m, d_pre_ref, d_qkv_ref,
    wa, wu, wd, pre_ref, acc, d_acc, d_att, sem,
):
    copies = weight_copies(
        (
            w_dn.at[flags[0]], pre_hbm, half_of(w_blk, 1, flags[0]),
            w_dn.at[1 - flags[0]], half_of(w_blk, 1, 1 - flags[0]),
            half_of(w_blk, 0, 1), half_of(w_blk, 0, 0),
        ),
        (wd.at[0], pre_ref, wu.at[0], wd.at[1], wu.at[1], wa.at[1], wa.at[0]),
        sem,
    )
    for copy in copies:
        copy.start()
    grad_m[...] = to_half(d_ref[...] * mod_m[2:3])
    d_mod_m[2:3] = jnp.sum(d_ref[...] * branch_m[...], axis=0)[None]
    acc[...] = jnp.zeros_like(acc)
    for half in range(2):
        copies[0 if half == 0 else 3].wait()
        if half == 0:
            copies[1].wait()
        copies[2 if half == 0 else 4].wait()
        for step in range(STEPS):
            own = slice(TILE * step, TILE * (step + 1))
            part = slice(HALF * half + TILE * step, HALF * half + TILE * (step + 1))
            d_act = matmul(grad_m[...], wd[half, :, own])
            pre = pre_ref[:, part]
            square = pre * pre
            tanh = jnp.tanh(GELU_SCALE * (pre + 0.044715 * (square * pre)))
            slope = 0.5 * (1.0 + tanh) + (0.5 * pre) * (1.0 - tanh * tanh) * (
                GELU_SCALE * (1.0 + (3.0 * 0.044715) * square)
            )
            d_pre = to_half(d_act * slope)
            d_pre_ref[:, part] = d_pre
            acc[...] += matmul_nt(d_pre, wu[half, :, own])
    normed, inverse = normalized(mid_ref[...])
    d_x, d_shift, d_scale = modulated_back(normed, inverse, mod_m[1:2], acc[...])
    d_mod_m[0:1] = d_shift[None]
    d_mod_m[1:2] = d_scale[None]
    acc[...] = to_half(d_ref[...] + d_x).astype(jnp.float32)

    d_mod_a[2:3] = jnp.sum(acc[...] * branch_a[...], axis=0)[None]
    grad_a[...] = to_half(acc[...] * mod_a[2:3])
    copies[5].wait()
    d_att[...] = to_half(matmul_nt(grad_a[...], wa[1, :, D:]))
    d_acc[...] = jnp.zeros_like(d_acc)
    for head in range(HEADS):
        lanes, mask = window(head)
        at = lambda k: slice(D * k + lanes.start, D * k + lanes.stop)
        query, key, value = (qkv_ref[:, at(k)] for k in range(3))
        probs = softmax_rows(matmul_nt(own_lanes(mask, query), key) * SCALE)
        outer = d_att[:, lanes]
        d_acc[:, at(2)] += own_lanes(mask, matmul_tn(to_half(probs), outer))
        d_probs = matmul_nt(own_lanes(mask, outer), value)
        d_scores = to_half(probs * (d_probs - jnp.sum(probs * d_probs, axis=-1, keepdims=True)))
        d_acc[:, at(0)] += own_lanes(mask, matmul(d_scores, key) * SCALE)
        d_acc[:, at(1)] += own_lanes(mask, matmul_tn(d_scores, query) * SCALE)
    d_qkv_ref[...] = to_half(d_acc[...])
    copies[6].wait()
    d_xm = matmul_nt(d_qkv_ref[:, 2 * D :], wa[1, :, :D]) + matmul_nt(d_qkv_ref[:, : 2 * D], wa[0])
    normed, inverse = normalized(x_ref[...])
    d_x, d_shift, d_scale = modulated_back(normed, inverse, mod_a[1:2], d_xm)
    d_mod_a[0:1] = d_shift[None]
    d_mod_a[1:2] = d_scale[None]
    d_in_ref[...] = to_half(acc[...] + d_x)


def weight_scratch():
    return [pltpu.VMEM((2, D, HALF), BF)] * 3


def stage_cost():
    flops = 2 * PATCHES * D * 12 * D + 4 * PATCHES * PATCHES * D
    return pl.CostEstimate(flops=2 * flops, bytes_accessed=24 * D * D, transcendentals=2 * PATCHES * FF)


def stage_forward(save, x_in, weights):
    flags, mod_a, mod_m, w_blk, w_dn, b_attn, b_up, b_down = weights
    vmem, hbm = pl.BlockSpec(memory_space=pltpu.VMEM), pl.BlockSpec(memory_space=pl.ANY)
    smem = pl.BlockSpec(memory_space=pltpu.SMEM)
    like = lambda columns, kind: jax.ShapeDtypeStruct((PATCHES, columns), kind)
    tokens, wide = pltpu.VMEM((PATCHES, D), BF), pltpu.VMEM((PATCHES, 3 * D), BF)
    total = pltpu.VMEM((PATCHES, D), jnp.float32)
    f32 = jnp.float32
    if save:
        shapes = [like(D, f32), like(D, BF), like(3 * D, BF), like(D, BF), like(D, f32), like(D, f32)]
        shapes += [like(D, BF), like(D, f32), like(FF, f32), like(FF, BF)]
        scratch = []
    else:
        shapes, scratch = [like(D, BF)], [tokens, wide, tokens, total, tokens]
    return pl.pallas_call(
        partial(forward_kernel, save),
        out_shape=tuple(shapes),
        in_specs=[smem] + [vmem] * 6 + [hbm] * 2,
        out_specs=(vmem,) * len(shapes),
        scratch_shapes=scratch + weight_scratch() + [total, pltpu.SemaphoreType.DMA((6,))],
        compiler_params=pltpu.CompilerParams(vmem_limit_bytes=VMEM_BYTES),
        cost_estimate=stage_cost(),
        name="stage_forward",
    )(flags, x_in, mod_a, mod_m, b_attn, b_up, b_down, w_blk, w_dn)


def stage_backward(d_out, x_in, weights, kept):
    flags, mod_a, mod_m, w_blk, w_dn, b_attn, b_up, b_down = weights
    xm_a, qkv, att, branch_a, x_mid, xm_m, branch_m, pre, act = kept
    vmem, hbm = pl.BlockSpec(memory_space=pltpu.VMEM), pl.BlockSpec(memory_space=pl.ANY)
    smem = pl.BlockSpec(memory_space=pltpu.SMEM)
    like = lambda columns, kind: jax.ShapeDtypeStruct((PATCHES, columns), kind)
    mods = jax.ShapeDtypeStruct((3, D), jnp.float32)
    return pl.pallas_call(
        backward_kernel,
        out_shape=(like(D, BF), mods, mods, like(D, BF), like(D, BF), like(FF, BF), like(3 * D, BF)),
        in_specs=[smem] + [vmem] * 8 + [hbm] * 3,
        out_specs=(vmem,) * 7,
        scratch_shapes=weight_scratch()
        + [
            pltpu.VMEM((PATCHES, FF), jnp.float32),
            pltpu.VMEM((PATCHES, D), jnp.float32),
            pltpu.VMEM((PATCHES, 3 * D), jnp.float32),
            pltpu.VMEM((PATCHES, D), BF),
            pltpu.SemaphoreType.DMA((7,)),
        ],
        compiler_params=pltpu.CompilerParams(vmem_limit_bytes=VMEM_BYTES),
        cost_estimate=stage_cost(),
        name="stage_backward",
    )(flags, d_out, x_in, x_mid, mod_a, mod_m, branch_a, branch_m, qkv, pre, w_blk, w_dn)


SUM_ROWS = 16


def collect_kernel(peers, flags_ref, *refs):
    tokens, d_pre_ref, mods, fm_ref, extra_ref = refs[:4], refs[4], refs[5:7], refs[7], refs[8]
    sums_ref, mods_ref = refs[9:]
    core, stage = flags_ref[0], flags_ref[1]
    ones = jnp.ones((8, PATCHES), BF)
    total = lambda value: matmul(ones, value)[0:1]
    sums_ref[...] = jnp.zeros_like(sums_ref)
    rows = [total(tokens[0][:, D * k : D * (k + 1)]) for k in range(3)]
    rows += [total(ref[...]) for ref in tokens[1:]]
    halves = [[total(d_pre_ref[:, D * k : D * (k + 1)]) for k in range(4)]]
    own = halves[0]
    order = [jnp.where(core == 0, own[k], own[(k + 2) % 4]) for k in range(4)]
    last = jnp.where(stage == 0, rows[5], extra_ref[0:1])
    for place, row in enumerate(rows[:4] + order + [rows[4], last, extra_ref[1:2]]):
        sums_ref[place : place + 1, :D] = row
    for k in range(2):
        block = jnp.concatenate([mods[k][...], fm_ref[...]], axis=0)
        mods_ref[k] = to_half(jnp.concatenate([block, jnp.zeros((16 - 5, D), jnp.float32)], axis=0))


def collect(flags, tokens, d_pre, mods, fm, extra):
    peers = 2 * lax.axis_size("dp")
    vmem = pl.BlockSpec(memory_space=pltpu.VMEM)
    return pl.pallas_call(
        partial(collect_kernel, peers),
        out_shape=(
            jax.ShapeDtypeStruct((SUM_ROWS, 128 * max(peers, 9)), jnp.float32),
            jax.ShapeDtypeStruct((2, 16, D), BF),
        ),
        in_specs=[pl.BlockSpec(memory_space=pltpu.SMEM)] + [vmem] * 9,
        out_specs=(vmem, vmem),
        compiler_params=pltpu.CompilerParams(vmem_limit_bytes=VMEM_BYTES),
        name="collect",
    )(flags, *tokens, d_pre, *mods, fm, extra)


def final_step(x_out, fmod, w_head, b_head, target, counts, loss_scale):
    normed, inverse = normalized(x_out)
    xf_half = to_half(normed * (1.0 + fmod[1:2]) + fmod[0:1])
    error = matmul(xf_half, w_head) + b_head - target
    loss = counts * jnp.sum(error * error)
    d_pred = to_half(2.0 * loss_scale * counts * error)
    g_head = matmul_tn(xf_half, d_pred)
    d_x, d_shift, d_scale = modulated_back(normed, inverse, fmod[1:2], matmul_nt(d_pred, w_head))
    return (loss, d_x, jnp.stack([d_shift, d_scale]), g_head, column_sums(d_pred))


def nesterov(weight, moment, average, grad, factor):
    clipped = grad * factor
    moment_new = momentum_rate * moment + clipped
    weight_new = weight - learn_rate * (clipped + momentum_rate * moment_new)
    average_new = ema_decay * average + (1.0 - ema_decay) * weight_new
    return (weight_new, moment_new, average_new, weight_new.astype(jnp.bfloat16))


def swap(array, by):
    peers = lax.axis_size("section")
    return lax.ppermute(array, "section", [(k, k ^ by) for k in range(peers)])


def pick(parts, index):
    return lax.dynamic_index_in_dim(parts, index, 0, keepdims=False)


def body(
    latents, noise, timesteps, labels, null_mask, valid,
    mod_w, mod_m, mod_e, block_w, block_m, block_e, down_w, down_m, down_e,
    stem_w, stem_m, stem_e, tail_w, tail_m, tail_e, biases, bias_m, bias_e,
):
    place = lax.axis_index("dp")
    section = lax.axis_index("section")
    stage = section // 2
    core = lax.rem(section, 2)
    even = core == 0
    n = lax.axis_size("dp")
    width = D // n

    flags = jnp.stack([core, stage]).astype(jnp.int32)
    downs, stems = jnp.swapaxes(down_w, 1, 2), stem_w.T
    stem_half, tail_half, mod_half_w = to_half(stems), to_half(tail_w), to_half(mod_w[0])
    dn_half = to_half(lax.dynamic_slice(downs, (stage, 0, core * HALF), (1, width, HALF))[0])
    at_one, at_two = NCLS + PATCH_IN, NCLS + PATCH_IN + FREQ
    w_two = stem_half[:, at_two:]
    table = jnp.pad(stem_half[:, :NCLS], ((0, 0), (0, META - FREQ - NCLS)))
    w_fm = tail_half[:, : 2 * D]
    small = jnp.concatenate(
        [stem_half[:, at_one:at_two], stem_half[:, NCLS:at_one], tail_half[:, 2 * D :]], axis=1
    )
    small = jnp.pad(small, ((0, 0), (0, -small.shape[1] % 128)))
    classes = jnp.where(null_mask > 0, NCLS - 1, labels)
    lanes = jnp.arange(META - FREQ, dtype=jnp.int32)[None, :]
    picks = (classes[:, None] == lanes).astype(jnp.float32)
    picks = jnp.where(lanes == META - FREQ - 1, valid.astype(jnp.float32)[:, None], picks)
    freq = to_half(time_features(timesteps.astype(jnp.float32))).astype(jnp.float32)
    meta = jnp.concatenate([freq, picks], axis=1)
    meta = jnp.pad(meta, ((0, 8 - meta.shape[0]), (0, 0)))
    b_two = lax.dynamic_slice_in_dim(biases, 32 * D + place * width, width)
    w_blk, w_dn, meta, small, pre, cond, mods = gather_weights(
        to_half(block_w[0]), dn_half, meta, small, w_two, table, mod_half_w, w_fm,
        biases[None, 31 * D : 32 * D], b_two[None],
    )
    small = small.reshape(D, -1)
    w_patch_all = small[:, FREQ : FREQ + PATCH_IN]
    w_head_all = small[:, FREQ + PATCH_IN : FREQ + PATCH_IN + HEAD_OUT]
    of_images = lambda value: value.reshape(n, 8, -1)[:, :2].reshape(2 * n, -1)
    images = 2 * n
    meta = of_images(meta)
    count = jnp.sum(meta[:, META - 1])
    loss_scale = 1.0 / (count * PATCHES * HEAD_OUT)
    mods = mods.reshape(2, 8 * PIECE)
    bias_of = lambda first, length: lax.dynamic_slice_in_dim(biases, first, length)
    mod_a = (mods[0, : 3 * D] + bias_of(6 * D * stage, 3 * D)).reshape(3, D)
    mod_b = (mods[1, : 3 * D] + bias_of(6 * D * stage + 3 * D, 3 * D)).reshape(3, D)
    fmod = (mods[0, 3 * D : 5 * D] + biases[33 * D : 35 * D]).reshape(2, D)
    weights = (
        flags, mod_a, mod_b, w_blk, w_dn,
        bias_of(12 * D + 8 * D * stage, 4 * D)[None],
        jnp.concatenate(
            [bias_of(16 * D + 8 * D * stage + HALF * half, HALF)[None] for half in (core, 1 - core)], axis=1
        ),
        bias_of(28 * D + D * stage, D)[None],
    )

    freq = to_half(meta[:, :FREQ])
    picks = to_half(meta[:, FREQ : FREQ + NCLS])
    hidden_pre = of_images(pre).T
    hidden_all = to_half(jax.nn.silu(hidden_pre))
    cond = of_images(cond).T
    cond_low = to_half(cond).astype(jnp.float32)
    cond_own = jnp.where(section == 0, cond, cond_low)
    silu_own = to_half(jax.nn.silu(cond_own))
    silu_low = to_half(jax.nn.silu(cond_low))

    step = pick(timesteps, core).astype(jnp.float32)
    signal, spread = noise_levels(step)
    lat, noi = pick(latents, core)[None], pick(noise, core)[None]
    counts = pick(valid, core).astype(jnp.float32)
    tok_half = to_half(patchify(signal * lat + spread * noi))[0]
    target = jnp.concatenate([patchify(signal * noi - spread * lat), patchify(noi)], axis=2)[0]
    x_first = matmul_nt(tok_half, w_patch_all) + biases[30 * D : 31 * D] + position_table(GRID // 2, D)

    x_hop = swap(stage_forward(False, x_first, weights)[0], 2)
    x_in = jnp.where(stage == 0, x_first, x_hop.astype(jnp.float32))
    x_out, *kept = stage_forward(True, x_in, weights)
    loss, d_final, d_fmod, g_head, b_head = final_step(
        x_out, fmod, w_head_all, biases[35 * D :], target, counts, loss_scale
    )
    xm_a, qkv, attended, branch_a, x_mid, xm_b, branch_b, pre, act = kept
    d_hop = swap(stage_backward(d_final, x_in, weights, kept)[0], 2)
    d_out = jnp.where(stage == 1, d_final, d_hop.astype(jnp.float32))
    d_first, d_mod_a, d_mod_b, d_branch_a, d_branch_b, d_pre, d_qkv = stage_backward(
        d_out, x_in, weights, kept
    )
    d_query, d_key, d_value = (d_qkv[:, D * k : D * (k + 1)] for k in range(3))

    act_sib, branch_sib, xm_sib, pre_sib = swap((act[:, HALF:], d_branch_b, xm_b, d_pre[:, HALF:]), 1)
    g_dn = to_half(matmul_tn(d_branch_b, act[:, :HALF]) + matmul_tn(branch_sib, act_sib))
    g_up = to_half(matmul_tn(xm_b, d_pre[:, :HALF]) + matmul_tn(xm_sib, pre_sib))
    g_dn = lax.psum_scatter(g_dn, "dp", scatter_dimension=0, tiled=True)

    xa_sib, last_sib, one_sib, two_sib = swap(
        (
            xm_a,
            jnp.where(even, attended, xm_a),
            jnp.where(even, d_value, d_query),
            jnp.where(even, d_branch_a, d_key),
        ),
        1,
    )
    last = jnp.where(even, xm_a, attended)
    one = jnp.where(even, d_query, d_value)
    two = jnp.where(even, d_key, d_branch_a)
    g_attn = jnp.concatenate(
        [
            to_half(matmul_tn(xm_a, one) + matmul_tn(xa_sib, one_sib)),
            to_half(matmul_tn(last, two) + matmul_tn(last_sib, two_sib)),
        ],
        axis=1,
    )
    g_up, g_attn = sum_gradients(g_up, g_attn)
    crossing = swap(to_half(jnp.where(even, g_up, g_attn)), 1).astype(jnp.float32)
    g_blk = jnp.concatenate(
        [jnp.where(even, g_attn, crossing), jnp.where(even, crossing, g_up)], axis=1
    )
    g_facing = swap(g_dn, 2)
    g_sib, g_corner = swap((g_dn, g_facing), 1)
    in_core = lambda own, sib: jnp.concatenate(
        [jnp.where(even, own, sib), jnp.where(even, sib, own)], axis=1
    ).astype(jnp.float32)
    here, there = in_core(g_dn, g_sib), in_core(g_facing, g_corner)
    down_both = jnp.where(stage == 0, jnp.stack([here, there]), jnp.stack([there, here]))

    extra = jnp.stack([jnp.pad(b_head, (0, D - HEAD_OUT)), jnp.pad(loss[None], (0, D - 1))])
    d_fmod = jnp.where(stage == 1, d_fmod, jnp.zeros_like(d_fmod))
    own_biases, d_mods = collect(
        flags, (d_qkv, d_branch_a, d_branch_b, d_first), d_pre, (d_mod_a, d_mod_b), d_fmod, extra
    )
    g_patch = jnp.pad(matmul_tn(d_first, tok_half), ((0, 0), (0, HEAD_OUT - PATCH_IN)))
    end_rows = row_count(width * HEAD_OUT)
    own_ends = jnp.where(stage == 0, g_patch, g_head).reshape(n, width * HEAD_OUT)
    own_ends = jnp.pad(own_ends, ((0, 0), (0, end_rows * 128 - width * HEAD_OUT))).reshape(n, end_rows, 128)
    own_biases = own_biases.reshape(SUM_ROWS, -1, 128).transpose(1, 0, 2)[: 2 * n]
    d_mods, own_biases, own_ends = exchange(
        4, "stage", ("core", "each", "dp"), d_mods, own_biases, own_ends
    )
    bias_piece = jnp.sum(own_biases, axis=0)
    own_ends = jnp.sum(own_ends, axis=0)
    d_mod_all = d_mods[:, :3].reshape(images, 3 * D)
    d_fm_all = d_mods[:, 3:5].reshape(images, 2 * D)
    g_mod = matmul(silu_own, d_mod_all)
    c_own = matmul_nt(mod_half_w, d_mod_all)
    c_own = c_own + matmul_nt(tail_half[:, : 2 * D], jnp.where(section == 3, d_fm_all, jnp.zeros_like(d_fm_all)))
    c_own = silu_back(cond_own, c_own)
    cond_rows = row_count(width * images)
    c_all, end_pair, d_fm_all = exchange(
        5, "section", ("all", "all", "all"), rows_of(c_own, cond_rows), own_ends, d_fm_all
    )
    d_fm_all = d_fm_all[3]
    ends = [end_pair[k].reshape(-1)[: width * HEAD_OUT].reshape(width, HEAD_OUT) for k in (0, 3)]
    g_fm = matmul(silu_low, d_fm_all)
    c_all = [c_all[k].reshape(-1)[: width * images].reshape(width, images) for k in range(4)]
    d_cond = to_half(c_all[3])
    for slot in (2, 1, 0):
        d_cond = to_half(d_cond.astype(jnp.float32) + c_all[slot])
    part_hidden = matmul_tn(w_two, d_cond).reshape(n, width * images)
    part_hidden = jnp.pad(part_hidden, ((0, 0), (0, cond_rows * 128 - width * images)))
    (d_hidden,) = exchange(6, "dp", ("each",), part_hidden.reshape(n, cond_rows, 128))
    d_hidden = jnp.sum(d_hidden, axis=0).reshape(-1)[: width * images].reshape(width, images)
    pre_own = lax.dynamic_slice_in_dim(hidden_pre, place * width, width)
    d_pre_one = to_half(silu_back(pre_own, d_hidden))
    g_table = matmul(d_cond, picks)
    g_one = matmul(d_pre_one, freq)
    g_two = matmul_nt(d_cond, hidden_all)
    g_stem = jnp.concatenate([g_table, ends[0][:, :PATCH_IN], g_one, g_two], axis=1)
    g_tail = jnp.concatenate([g_fm, ends[1]], axis=1)

    square = lambda value: jnp.sum(value * value)
    once = (section == 0).astype(jnp.float32)
    squares = square(g_mod) + square(g_blk)
    squares = squares + once * (square(down_both) + square(g_stem) + square(g_tail))
    row_sums = lambda value: jnp.sum(value.astype(jnp.float32), axis=1)
    mod_piece = 3 * D // n
    mod_rows, slice_rows = row_count(mod_piece, 1), row_count(2 * width, 1)
    bias_mod = lax.dynamic_slice_in_dim(column_sums(d_mod_all), place * mod_piece, mod_piece)
    slices = jnp.concatenate([row_sums(d_pre_one), row_sums(d_cond)])
    news = jnp.concatenate(
        [bias_piece, rows_of(bias_mod, mod_rows), rows_of(slices, slice_rows), rows_of(squares[None], 1)]
    )
    news = jnp.pad(news, ((0, -news.shape[0] % 8), (0, 0)))
    (news,) = exchange(7, "every", ("all",), news)
    news = news.reshape(n, 4, -1, 128)
    piece = SUM_ROWS
    first, second = piece + mod_rows, piece + mod_rows + slice_rows
    stages = []
    for k in range(2):
        pieces = news[:, 2 * k : 2 * k + 2, :piece].reshape(2 * n, SUM_ROWS, 128)[: D // 128]
        stages.append(pieces.transpose(1, 0, 2).reshape(-1))
    bias_mods = news[:, :, piece:first].reshape(n, 4, mod_rows * 128)[:, :, :mod_piece]
    bias_mods = bias_mods.transpose(1, 0, 2).reshape(-1)
    slices = news[:, 0, first:second].reshape(n, slice_rows * 128)[:, : 2 * width]
    bias_grad = jnp.concatenate(
        [bias_mods]
        + [part[: 8 * D] for part in stages]
        + [part[8 * D : 9 * D] for part in stages]
        + [stages[0][9 * D : 10 * D]]
        + [slices[:, :width].reshape(-1), slices[:, width:].reshape(-1)]
        + [column_sums(d_fm_all), stages[1][9 * D : 9 * D + HEAD_OUT]]
    )
    loss_sum = stages[1][10 * D]
    grad_norm = jnp.sqrt(jnp.sum(news[:, :, second, 0]) + square(bias_grad))
    factor = jnp.minimum(1.0, clip_limit / (grad_norm + 1e-06))
    mod_out = nesterov(mod_w, mod_m, mod_e, g_mod[None], factor)
    block_out = nesterov(block_w, block_m, block_e, g_blk[None], factor)
    flip = lambda value: jnp.swapaxes(value, 1, 2)
    down_out = tuple(map(flip, nesterov(downs, flip(down_m), flip(down_e), down_both, factor)))
    stem_out = tuple(value.T for value in nesterov(stems, stem_m.T, stem_e.T, g_stem, factor))
    tail_out = nesterov(tail_w, tail_m, tail_e, g_tail, factor)
    bias_out = nesterov(biases, bias_m, bias_e, bias_grad, factor)
    return (
        (loss_sum, count, grad_norm)
        + mod_out + block_out + down_out + stem_out + tail_out + bias_out
    )


def solution(mesh):
    images = (P("dp", None, None, None),) * 2 + (P("dp"),) * 4
    owned = P("section", "dp", None)
    states = (owned,) * 6 + (P(None, None, "dp"),) * 3 + (P(None, "dp"),) * 3 + (P("dp", None),) * 3 + (P(),) * 3
    updates = (owned,) * 8 + (P(None, None, "dp"),) * 4 + (P(None, "dp"),) * 4 + (P("dp", None),) * 4 + (P(),) * 4
    return jax.shard_map(
        body,
        mesh=mesh,
        in_specs=images + states,
        out_specs=(P(), P(), P()) + updates,
        check_vma=False,
    )
```

```python
from functools import partial
import math

import jax
import jax.numpy as jnp
from jax import lax
from jax.experimental import pallas as pl
from jax.experimental.pallas import tpu as pltpu
from jax.sharding import PartitionSpec as P

HEADS = 16
HEAD_DIM = 72
D = 1152
FF = 4608
HALF = FF // 2
NCLS = 1001
FREQ = 256
GRID = 32
PATCHES = 256
PATCH_IN = 16
HEAD_OUT = 32
LAYERS = 2
NBIAS = 40352


epsilon_norm = 1e-06
momentum_rate = 0.9
ema_decay = 0.9
learn_rate = 4000.0
clip_limit = 0.02
MESH = pl.DeviceIdType.MESH
BF = jnp.bfloat16


def matmul(left, right):
    return jnp.dot(left, right, preferred_element_type=jnp.float32)


def matmul_nt(left, right):
    return lax.dot_general(
        left, right, (((1,), (1,)), ((), ())), preferred_element_type=jnp.float32
    )


def matmul_tn(left, right):
    return lax.dot_general(
        left, right, (((0,), (0,)), ((), ())), preferred_element_type=jnp.float32
    )


def to_half(value):
    return value.astype(BF)


def column_sums(value):
    return jnp.sum(value.astype(jnp.float32), axis=0)


def silu_back(value, grad):
    return jax.vjp(jax.nn.silu, value)[1](grad)[0]


def patchify(field):
    images, side = (field.shape[0], field.shape[1] // 2)
    return (
        field.reshape(images, side, 2, side, 2, 4)
        .transpose(0, 1, 3, 2, 4, 5)
        .reshape(images, side * side, 16)
    )


def sincos_rows(places, width):
    omega = 1.0 / 10000.0 ** (jnp.arange(width // 2, dtype=jnp.float32) / (width // 2))
    angle = places[:, None] * omega[None, :]
    return jnp.concatenate([jnp.sin(angle), jnp.cos(angle)], axis=1)


def position_table(side, width):
    line = sincos_rows(jnp.arange(side, dtype=jnp.float32), width // 2)
    column = jnp.broadcast_to(line[None], (side, side, width // 2))
    row = jnp.broadcast_to(line[:, None], (side, side, width // 2))
    return jnp.concatenate([column, row], axis=2).reshape(side * side, width)


def time_features(steps):
    half = FREQ // 2
    freqs = jnp.exp(-math.log(10000.0) * jnp.arange(half, dtype=jnp.float32) / half)
    angle = steps[:, None] * freqs[None, :]
    return jnp.concatenate([jnp.cos(angle), jnp.sin(angle)], axis=1)


def noise_levels(steps):
    level = jnp.cos((steps / 1000.0 + 0.008) / 1.008 * (math.pi / 2)) ** 2
    return (jnp.sqrt(level), jnp.sqrt(1.0 - level))


Z, X = 4, 2
GATHER_CHUNKS = (
    (0, 0, 48, False), (0, 48, 48, False), (0, 96, 48, False),
    (1, 0, 48, False), (1, 48, 48, False), (1, 96, 48, False),
)
CHUNKS = ((0, 16, True), (16, 32, False), (48, 32, False), (80, 32, False), (112, 32, False))
META = 384
WIDE = 256
ROWS_END = PATCH_IN + HEAD_OUT
PIECE = 768


def ring_fits(n, rows):
    return n == Z * X and rows == 144


def one_hot(classes, width):
    lane = lax.broadcasted_iota(jnp.int32, (classes.shape[0], width), 1).astype(jnp.float32)
    return to_half(jnp.maximum(1.0 - jnp.abs(lane - classes), 0.0))


def gather_kernel(
    blk_ref, dn_ref, meta_ref, ends_ref, one_ref, two_ref, table_ref, mod_ref, fm_ref, b_one, b_two,
    out_blk, out_dn, meta_out, ends_out, pre_out, hidden_out, cond_out, mods_out,
    metas, hidden, part, parts, arrived_parts,
    meta_send, meta_recv, ends_send, ends_recv, hid_send, hid_recv, part_send, part_recv, local_sem,
    up_sem, down_sem, x_sem, sib_sem, recv_sem, sib_recv, own_sem,
):
    me = lax.axis_index("dp")
    section = lax.axis_index("section")
    z, x = me // X, lax.rem(me, X)
    core = lax.rem(section, 2)
    sibling = section + 1 - 2 * core
    across = me + 1 - 2 * x
    chunks = len(GATHER_CHUNKS)
    low = section - core
    group, place_in = Z * X * 2, me * 2 + core
    where = lambda p: {"dp": p // 2, "section": low + lax.rem(p, 2)}
    has_up, has_down = z < Z - 1, z > 0

    barrier = pltpu.get_barrier_semaphore()

    @pl.loop(1, group)
    def _(step):
        pl.semaphore_signal(
            barrier, 1, device_id=where(lax.rem(place_in + step, group)), device_id_type=MESH
        )

    pl.semaphore_wait(barrier, group - 1)

    def to_dp(src, dst, send, recv, step, p, slot):
        return pltpu.make_async_remote_copy(
            src_ref=src, dst_ref=dst.at[slot], send_sem=send.at[step], recv_sem=recv.at[step],
            device_id={"dp": p}, device_id_type=MESH,
        )

    meta_copy = partial(to_dp, meta_ref, metas, meta_send, meta_recv)
    ends_copy = partial(to_dp, ends_ref, ends_out, ends_send, ends_recv)
    hidden_copy = partial(to_dp, hidden, hidden_out, hid_send, hid_recv)

    def part_copy(step, p, slot):
        return pltpu.make_async_remote_copy(
            src_ref=parts.at[p], dst_ref=arrived_parts.at[slot],
            send_sem=part_send.at[step], recv_sem=part_recv.at[step],
            device_id=where(p), device_id_type=MESH,
        )

    own_meta = pltpu.make_async_copy(meta_ref, metas.at[me], local_sem.at[0])
    own_ends = pltpu.make_async_copy(ends_ref, ends_out.at[me], local_sem.at[1])
    own_hidden = pltpu.make_async_copy(hidden, hidden_out.at[me], local_sem.at[2])
    own_part = pltpu.make_async_copy(parts.at[place_in], arrived_parts.at[place_in], local_sem.at[3])

    def send_all(copy_to, size, index):
        @pl.loop(1, size)
        def _(step):
            copy_to(step, lax.rem(index + step, size), index).start()

    def wait_all(copy_to, size, index):
        @pl.loop(1, size)
        def _(step):
            p = lax.rem(index + size - step, size)
            copy_to(step, p, p).wait_recv()
            copy_to(step, p, p).wait_send()

    own_meta.start()
    own_ends.start()
    send_all(meta_copy, Z * X, me)

    def place(owner, k, side):
        which, first, rows, unused = GATHER_CHUNKS[k]
        return (out_dn if which else out_blk).at[side, pl.ds(pl.multiple_of(owner * 144 + first, 16), rows)]

    def source(owner, k, mine):
        if not mine:
            return place(owner, k, core)
        which, first, rows, unused = GATHER_CHUNKS[k]
        return (dn_ref if which else blk_ref).at[pl.ds(first, rows)]

    def copy(owner, k, mine, sem, target):
        unit = owner * chunks + k
        return pltpu.make_async_remote_copy(
            src_ref=source(owner, k, mine),
            dst_ref=place(owner, k, core),
            send_sem=sem.at[unit],
            recv_sem=recv_sem.at[unit],
            device_id={"dp": target},
            device_id_type=MESH,
        )

    def to_sibling(owner, k, mine):
        unit = owner * chunks + k
        return pltpu.make_async_remote_copy(
            src_ref=source(owner, k, mine),
            dst_ref=place(owner, k, core),
            send_sem=sib_sem.at[unit],
            recv_sem=sib_recv.at[unit],
            device_id={"section": sibling},
            device_id_type=MESH,
        )

    def own_copy(k):
        return pltpu.make_async_copy(source(me, k, True), place(me, k, core), own_sem.at[k])

    def arrived(owner, k):
        copy(owner, k, False, x_sem, across).wait_recv()

    for k in range(chunks):
        @pl.when(has_up)
        def _():
            copy(me, k, True, up_sem, me + X).start()

        @pl.when(has_down)
        def _():
            copy(me, k, True, down_sem, me - X).start()

        copy(me, k, True, x_sem, across).start()
        own_copy(k).start()
        to_sibling(me, k, True).start()

    send_all(ends_copy, Z * X, me)

    def make_hidden():
        own_meta.wait()
        wait_all(meta_copy, Z * X, me)
        for index in range(Z * X):
            meta_out[2 * index : 2 * index + 2] = metas[index]
        pre = matmul_nt(to_half(meta_out[:, :FREQ]), one_ref[...]) + b_one[...]
        pre_out[...] = pre
        hidden[...] = to_half(jax.nn.silu(pre))
        own_hidden.start()
        send_all(hidden_copy, Z * X, me)

    def make_parts():
        own_hidden.wait()
        wait_all(hidden_copy, Z * X, me)
        cond = matmul_nt(one_hot(meta_out[:, FREQ : FREQ + 1], table_ref.shape[1]), table_ref[...]) + b_two[...]
        for index in range(Z * X):
            cond = cond + matmul_nt(hidden_out[index], two_ref[index])
        cond_out[...] = cond
        cond_low = to_half(cond).astype(jnp.float32)
        own_cond = jnp.where(section == 0, cond, cond_low)
        part[:, : 3 * D] = matmul(to_half(jax.nn.silu(own_cond)), mod_ref[...])
        part[:, 3 * D : 5 * D] = matmul(to_half(jax.nn.silu(cond_low)), fm_ref[...])
        part[:, 5 * D :] = jnp.zeros((group, 8 * PIECE - 5 * D), jnp.float32)
        for row in range(group):
            for k in range(8):
                parts[row, k : k + 1] = part[row : row + 1, PIECE * k : PIECE * (k + 1)]
        own_part.start()
        send_all(part_copy, group, place_in)

    def along(step, k, first_across):
        shift = 1 - 2 * x if first_across else 0
        crosses = (not first_across) and (not GATHER_CHUNKS[k][3])

        @pl.when(z >= step)
        def _():
            owner = me - X * step + shift
            arrived(owner, k)

            @pl.when(has_up)
            def _():
                copy(owner, k, False, up_sem, me + X).start()

            if crosses:
                copy(owner, k, False, x_sem, across).start()
            to_sibling(owner, k, False).start()

        @pl.when(z + step < Z)
        def _():
            owner = me + X * step + shift
            arrived(owner, k)

            @pl.when(has_down)
            def _():
                copy(owner, k, False, down_sem, me - X).start()

            if crosses:
                copy(owner, k, False, x_sem, across).start()
            to_sibling(owner, k, False).start()

    def crossed(step, k):
        direct = GATHER_CHUNKS[k][3]
        if step == 0:
            owner = across
            arrived(owner, k)
            if direct:
                @pl.when(has_up)
                def _():
                    copy(owner, k, False, up_sem, me + X).start()

                @pl.when(has_down)
                def _():
                    copy(owner, k, False, down_sem, me - X).start()
            to_sibling(owner, k, False).start()
        elif not direct:
            for sign in (-1, 1):
                @pl.when((z >= step) if sign < 0 else (z + step < Z))
                def _():
                    owner = across + sign * X * step
                    arrived(owner, k)
                    to_sibling(owner, k, False).start()

    for step in range(1, Z + 1):
        for k in range(chunks):
            if step < Z:
                along(step, k, False)
            crossed(step - 1, k)
            if step < Z and GATHER_CHUNKS[k][3]:
                along(step, k, True)
        if step == 1:
            make_hidden()
        if step == 2:
            make_parts()

    own_part.wait()
    wait_all(part_copy, group, place_in)
    own_ends.wait()
    wait_all(ends_copy, Z * X, me)
    for source_core in range(2):
        total = arrived_parts[source_core]
        for index in range(1, Z * X):
            total = total + arrived_parts[2 * index + source_core]
        mods_out[source_core] = total

    for k in range(chunks):
        direct = GATHER_CHUNKS[k][3]
        own_copy(k).wait()
        for column in range(2):
            base = me if column == 0 else across
            for step in range(0, Z):
                for sign in (-1, 1) if step else (1,):
                    @pl.when((z >= step) if sign < 0 else (z + step < Z))
                    def _():
                        owner = base + sign * X * step
                        mine = column == 0 and step == 0
                        to_sibling(owner, k, mine).wait_send()
                        pltpu.make_async_remote_copy(
                            src_ref=place(owner, k, 1 - core),
                            dst_ref=place(owner, k, 1 - core),
                            send_sem=sib_sem.at[owner * chunks + k],
                            recv_sem=sib_recv.at[owner * chunks + k],
                            device_id={"section": sibling},
                            device_id_type=MESH,
                        ).wait_recv()
                        runs = column == 0 or direct
                        if runs and (step == 0 or sign < 0):
                            @pl.when(has_up)
                            def _():
                                copy(owner, k, mine, up_sem, me + X).wait_send()
                        if runs and (step == 0 or sign > 0):
                            @pl.when(has_down)
                            def _():
                                copy(owner, k, mine, down_sem, me - X).wait_send()
                        if column == 0 and (step == 0 or not direct):
                            copy(owner, k, mine, x_sem, across).wait_send()


def gather_weights(blk, dn, meta, ends, w_one, w_two, table, w_mod, w_fm, b_one, b_two):
    n, width = lax.axis_size("dp"), blk.shape[0]
    section = lax.axis_index("section")
    if not ring_fits(n, width):
        both = lambda own, sib: jnp.where(
            lax.rem(section, 2) == 0, jnp.stack([own, sib]), jnp.stack([sib, own])
        )
        blk = lax.all_gather(blk, "dp", axis=0, tiled=True)
        dn = lax.all_gather(dn, "dp", axis=0, tiled=True)
        meta, ends = exchange(2, "dp", ("all", "all"), meta, ends)
        meta = meta.reshape(2 * n, META)
        pre = matmul_nt(to_half(meta[:, :FREQ]), w_one) + b_one
        (hidden,) = exchange(8, "dp", ("all",), to_half(jax.nn.silu(pre)))
        cond = matmul_nt(one_hot(meta[:, FREQ : FREQ + 1], table.shape[1]), table) + b_two
        cond = cond + jnp.einsum("jik,jwk->iw", hidden, w_two, preferred_element_type=jnp.float32)
        cond_low = to_half(cond).astype(jnp.float32)
        own_cond = jnp.where(section == 0, cond, cond_low)
        parts = [
            matmul(to_half(jax.nn.silu(own_cond)), w_mod),
            matmul(to_half(jax.nn.silu(cond_low)), w_fm),
        ]
        parts = jnp.pad(jnp.concatenate(parts, axis=1), ((0, 0), (0, 8 * PIECE - 5 * D)))
        (parts,) = exchange(3, "stage", ("each",), parts.reshape(2 * n, 8, PIECE))
        mods = jnp.sum(parts.reshape(n, 2, 8, PIECE), axis=0)
        return (both(blk, swap(blk, 1)), both(dn, swap(dn, 1)), meta, ends, pre, hidden, cond, mods)
    units, images = n * len(GATHER_CHUNKS), 2 * n
    hbm, vmem = pl.BlockSpec(memory_space=pl.ANY), pl.BlockSpec(memory_space=pltpu.VMEM)
    dma = lambda count: pltpu.SemaphoreType.DMA((count,))
    f32 = jnp.float32
    return pl.pallas_call(
        gather_kernel,
        out_shape=(
            jax.ShapeDtypeStruct((2, D, FF), BF), jax.ShapeDtypeStruct((2, D, HALF), BF),
            jax.ShapeDtypeStruct((images, META), f32), jax.ShapeDtypeStruct((n,) + ends.shape, BF),
            jax.ShapeDtypeStruct((images, WIDE), f32), jax.ShapeDtypeStruct((n, images, WIDE), BF),
            jax.ShapeDtypeStruct((images, width), f32), jax.ShapeDtypeStruct((2, 8, PIECE), f32),
        ),
        in_specs=[hbm] * 2 + [vmem] * 9,
        out_specs=(hbm, hbm) + (vmem,) * 6,
        scratch_shapes=[
            pltpu.VMEM((n, 2, META), f32), pltpu.VMEM((images, WIDE), BF),
            pltpu.VMEM((images, 8 * PIECE), f32),
            pltpu.VMEM((images, 8, PIECE), f32), pltpu.VMEM((images, 8, PIECE), f32),
            dma(n), dma(n), dma(n), dma(n), dma(n), dma(n), dma(images), dma(images), dma(4),
        ]
        + [dma(units)] * 6
        + [dma(len(GATHER_CHUNKS))],
        compiler_params=pltpu.CompilerParams(
            collective_id=0, has_side_effects=True, vmem_limit_bytes=VMEM_BYTES
        ),
        cost_estimate=pl.CostEstimate(flops=0, bytes_accessed=400_000_000, transcendentals=0),
        name="gather_weights",
    )(blk, dn, meta, ends, w_one, w_two, table, w_mod, w_fm, b_one, b_two)


VMEM_BYTES = 60 * 1024 * 1024
SUM_CHUNKS = tuple((which,) + chunk for which in range(3) for chunk in CHUNKS)


def silu_slope(value):
    gate = jax.nn.sigmoid(value)
    return gate * (1.0 + value * (1.0 - gate))


def sum_kernel(
    g_dn, g_up, g_attn, dm_ref, bp_ref, en_ref, mod_ref, fm_ref, two_ref, cond_ref, pre_ref, hid_ref, meta_ref,
    out, cross_out, dn_out, gmod_out, gfm_out, gtab_out, gone_out, gtwo_out,
    ends_all, news_out, cs_all, fmsum_out, sq_all,
    own_b, other_d, xb, xq, up_b, up_o, down_b, down_o, acc, acc_dn,
    dm_in, bp_in, en_in, dmat, ends_src, c_src, c_in, fmd_src, fmd_in, cs_src, dcond, ph, ph_in, news_src,
    sq_src, sq_rows, cross_src,
    load_sem, x_send, x_recv, up_send, up_recv, down_send, down_recv,
    sib_send, sib_recv, y_send, y_recv, group_send, group_recv, sect_send, sect_recv,
    ph_send, ph_recv, news_send, news_recv, sq_send, sq_recv, cross_sem, local_sem,
):
    me = lax.axis_index("dp")
    section = lax.axis_index("section")
    z, x = me // X, lax.rem(me, X)
    core = lax.rem(section, 2)
    low, sibling, facing = section - core, section + 1 - 2 * core, lax.rem(section + 2, 4)
    across = me + 1 - 2 * x
    sources = (g_dn, g_up, g_attn)
    chunks = len(SUM_CHUNKS)
    has_up, has_down = z < Z - 1, z > 0
    devices, group = Z * X * 4, Z * X * 2
    me_all, me_group = me * 4 + section, me * 2 + core
    in_all = lambda p: {"dp": p // 4, "section": lax.rem(p, 4)}
    in_group = lambda p: {"dp": p // 2, "section": low + lax.rem(p, 2)}
    in_section = lambda p: {"section": p}
    in_dp = lambda p: {"dp": p}
    f32 = jnp.float32

    barrier = pltpu.get_barrier_semaphore()

    @pl.loop(1, devices)
    def _(step):
        pl.semaphore_signal(
            barrier, 1, device_id=in_all(lax.rem(me_all + step, devices)), device_id_type=MESH
        )

    def small(src_of, dst, send, recv, where, size, index):
        def copy(step, p, slot):
            return pltpu.make_async_remote_copy(
                src_ref=src_of(p), dst_ref=dst.at[slot], send_sem=send.at[step], recv_sem=recv.at[step],
                device_id=where(p), device_id_type=MESH,
            )
        return (copy, size, index, src_of, dst)

    gradients = [
        small(lambda p: dm_ref.at[lax.rem(p, 2)], dm_in, group_send.at[0], group_recv.at[0], in_group, group, me_group),
        small(lambda p: bp_ref.at[p], bp_in, group_send.at[1], group_recv.at[1], in_group, group, me_group),
        small(lambda p: en_ref.at[p // 2], en_in, group_send.at[2], group_recv.at[2], in_group, group, me_group),
    ]
    conds = [
        small(lambda p, src=src: src, dst, sect_send.at[k], sect_recv.at[k], in_section, 4, section)
        for k, (src, dst) in enumerate(
            ((c_src, c_in), (ends_src, ends_all), (fmd_src, fmd_in), (cs_src, cs_all))
        )
    ]
    hiddens = [small(lambda p: ph.at[p], ph_in, ph_send, ph_recv, in_dp, Z * X, me)]
    news = [small(lambda p: news_src, news_out, news_send, news_recv, in_all, devices, me_all)]
    norms = [small(lambda p: sq_src, sq_all, sq_send, sq_recv, in_all, devices, me_all)]

    def own_copies(batch, first):
        return [
            pltpu.make_async_copy(src_of(index), dst.at[index], local_sem.at[first + k])
            for k, (copy, size, index, src_of, dst) in enumerate(batch)
        ]

    def send_batch(batch, first):
        for copy in own_copies(batch, first):
            copy.start()
        for copy, size, index, src_of, dst in batch:
            @pl.loop(1, size)
            def _(step):
                copy(step, lax.rem(index + step, size), index).start()

    def wait_batch(batch, first):
        for copy in own_copies(batch, first):
            copy.wait()
        for copy, size, index, src_of, dst in batch:
            @pl.loop(1, size)
            def _(step):
                p = lax.rem(index + size - step, size)
                copy(step, p, p).wait_recv()
                copy(step, p, p).wait_send()

    def add_square(value):
        sq_src[...] += jnp.sum(value * value)

    def images_of():
        cond = cond_ref[...]
        cond_low = to_half(cond).astype(f32)
        return jnp.where(section == 0, cond, cond_low), cond_low

    def make_cond():
        wait_batch(gradients, 0)
        flat = dm_in[...].reshape(group * 48, 128)
        row = lax.broadcasted_iota(jnp.int32, (group, group * 48), 0) * 48
        column = lax.broadcasted_iota(jnp.int32, (group, group * 48), 1)
        for k in range(5 * D // 128):
            chosen = jnp.where(column == row + k, 1.0, 0.0).astype(BF)
            dmat[:, 128 * k : 128 * (k + 1)] = to_half(matmul(chosen, flat))
        news_src[...] = jnp.zeros_like(news_src)
        news_src[0:SUM_ROWS] = jnp.sum(bp_in[...], axis=0)
        ends_src[...] = jnp.sum(en_in[...], axis=0)
        own_cond, cond_low = images_of()
        d_mod, d_fm = dmat[:, : 3 * D], dmat[:, 3 * D :]
        fmd_src[...] = d_fm
        cs_src[...] = jnp.sum(d_mod.astype(f32), axis=0, keepdims=True)
        d_silu = matmul_nt(d_mod, mod_ref[...])
        d_silu = d_silu + (section == 3).astype(f32) * matmul_nt(d_fm, fm_ref[...])
        c_src[...] = jnp.zeros_like(c_src)
        c_src[:, :144] = silu_slope(own_cond) * d_silu
        send_batch(conds, 3)
        silu_own = to_half(jax.nn.silu(own_cond))
        for k in range(3):
            part_g = matmul_tn(silu_own, dmat[:, D * k : D * (k + 1)])
            gmod_out[:, D * k : D * (k + 1)] = part_g
            add_square(part_g)

    once = (section == 0).astype(f32)

    def make_hidden():
        wait_batch(conds, 3)
        total = to_half(c_in[3])
        for slot in (2, 1, 0):
            total = to_half(total.astype(f32) + c_in[slot])
        dcond[...] = total
        d_cond = dcond[:, :144]
        for index in range(Z * X):
            ph[index] = matmul(d_cond, two_ref[index])
        send_batch(hiddens, 7)
        own_cond, cond_low = images_of()
        silu_low = to_half(jax.nn.silu(cond_low))
        for k in range(2):
            part_g = matmul_tn(silu_low, fmd_in[3, :, D * k : D * (k + 1)])
            gfm_out[:, D * k : D * (k + 1)] = part_g
            add_square(jnp.sqrt(once) * part_g)
        fmsum_out[...] = jnp.sum(fmd_in[3].astype(f32), axis=0, keepdims=True)
        part_g = matmul_tn(d_cond, one_hot(meta_ref[:, FREQ : FREQ + 1], gtab_out.shape[1]))
        gtab_out[...] = part_g
        add_square(once * part_g)
        for index in range(Z * X):
            part_g = matmul_tn(d_cond, hid_ref[index])
            gtwo_out[index] = part_g
            add_square(once * part_g)

    def make_news():
        wait_batch(hiddens, 7)
        total = ph_in[0]
        for index in range(1, Z * X):
            total = total + ph_in[index]
        d_pre = to_half(silu_slope(pre_ref[...]) * total)
        part_g = matmul_tn(d_pre, to_half(meta_ref[:, :FREQ]))
        gone_out[...] = part_g
        add_square(once * part_g)
        sums = jnp.sum(d_pre.astype(f32), axis=0, keepdims=True)
        sums_cond = jnp.sum(dcond[...].astype(f32), axis=0, keepdims=True)
        for k in range(2):
            news_src[SUM_ROWS + k : SUM_ROWS + k + 1] = sums[:, 128 * k : 128 * (k + 1)]
            news_src[SUM_ROWS + 2 + k : SUM_ROWS + 3 + k] = sums_cond[:, 128 * k : 128 * (k + 1)]
        send_batch(news, 8)
        first = (me == 0).astype(f32)
        add_square(news_src[0:10])
        add_square(once * sums)
        add_square(once * sums_cond)
        add_square(first * cs_src[...])
        add_square(first * once * fmsum_out[...])
        add_square(once * ends_all[0])
        add_square(once * ends_all[3])

    def dn_copy(k, slot, to_sib):
        rows = pl.ds(SUM_CHUNKS[k][1], SUM_CHUNKS[k][2])
        unit = slot * chunks + k
        return pltpu.make_async_remote_copy(
            src_ref=dn_out.at[slot, rows], dst_ref=dn_out.at[slot, rows],
            send_sem=(sib_send if to_sib else y_send).at[unit],
            recv_sem=(sib_recv if to_sib else y_recv).at[unit],
            device_id={"section": sibling if to_sib else facing},
            device_id_type=MESH,
        )

    def each(distance, run):
        if distance == 0:
            run(z, None)
            return

        @pl.when(z + distance < Z)
        def _():
            run(z + distance, True)

        @pl.when(z >= distance)
        def _():
            run(z - distance, False)

    def part(k):
        return pl.ds(SUM_CHUNKS[k][1], SUM_CHUNKS[k][2])

    def hbm(k, zz, column):
        start = pl.multiple_of((zz * X + column) * 144 + SUM_CHUNKS[k][1], 16)
        return sources[SUM_CHUNKS[k][0]].at[pl.ds(start, SUM_CHUNKS[k][2])]

    def own(k, zz):
        return own_b.at[SUM_CHUNKS[k][0], zz, part(k)]

    def from_x(k, zz):
        return xq.at[SUM_CHUNKS[k][0]] if SUM_CHUNKS[k][3] else xb.at[SUM_CHUNKS[k][0], zz, part(k)]

    def from_z(k, zz, up, other):
        if other:
            return (up_o if up else down_o).at[SUM_CHUNKS[k][0], zz]
        return (up_b if up else down_b).at[SUM_CHUNKS[k][0], zz, part(k)]

    def other_of(k, zz):
        return other_d.at[SUM_CHUNKS[k][0], zz]

    def load(k, zz, other=False):
        index = ((chunks if other else 0) + k) * Z + zz
        return pltpu.make_async_copy(
            hbm(k, zz, (1 - x) if other else x),
            other_of(k, zz) if other else own(k, zz),
            load_sem.at[index],
        )

    def x_copy(k, zz, src):
        unit = k * Z + zz
        return pltpu.make_async_remote_copy(
            src_ref=src, dst_ref=from_x(k, zz), send_sem=x_send.at[unit], recv_sem=x_recv.at[unit],
            device_id={"dp": across}, device_id_type=MESH,
        )

    def z_copy(k, zz, up, other):
        unit = ((chunks if other else 0) + k) * Z + zz
        return pltpu.make_async_remote_copy(
            src_ref=other_of(k, zz) if other else own(k, zz),
            dst_ref=from_z(k, zz, up, other),
            send_sem=(up_send if up else down_send).at[unit],
            recv_sem=(up_recv if up else down_recv).at[unit],
            device_id={"dp": me + X if up else me - X},
            device_id_type=MESH,
        )

    def total(k, dst, srcs):
        @pl.loop(0, SUM_CHUNKS[k][2] // 16)
        def _(step):
            rows = pl.ds(pl.multiple_of(step * 16, 16), 16)
            value = srcs[0][rows].astype(jnp.float32)
            for src in srcs[1:]:
                value = value + src[rows].astype(jnp.float32)
            dst[rows] = value.astype(dst.dtype)

    for distance in (3, 2, 1, 0):
        for k in range(chunks):
            def run(zz, up):
                load(k, zz).start()
                if SUM_CHUNKS[k][3]:
                    load(k, zz, True).start()
            each(distance, run)

    sq_src[...] = jnp.zeros_like(sq_src)
    sq_rows[...] = jnp.zeros_like(sq_rows)
    pl.semaphore_wait(barrier, devices - 1)
    send_batch(gradients, 0)

    for which in range(3):
        for distance in (3, 2, 1, 0):
            for k in range(chunks):
                if SUM_CHUNKS[k][0] == which and not SUM_CHUNKS[k][3]:
                    each(distance, lambda zz, up: x_copy(k, zz, hbm(k, zz, 1 - x)).start())

    def pass_on(k, distance):
        def run(zz, up):
            behind = has_down if up else has_up
            if SUM_CHUNKS[k][3]:
                for other in (False, True):
                    mine = other_of(k, zz) if other else own(k, zz)
                    load(k, zz, other).wait()

                    @pl.when(behind)
                    def _():
                        z_copy(k, zz, up, other).wait_recv()
                        total(k, mine, [mine, from_z(k, zz, up, other)])

                    z_copy(k, zz, up, other).start()
                return
            load(k, zz).wait()
            x_copy(k, zz, hbm(k, zz, 1 - x)).wait_recv()

            @pl.when(behind)
            def _():
                z_copy(k, zz, up, False).wait_recv()
                total(k, own(k, zz), [own(k, zz), from_x(k, zz), from_z(k, zz, up, False)])

            @pl.when(jnp.logical_not(behind))
            def _():
                total(k, own(k, zz), [own(k, zz), from_x(k, zz)])

            z_copy(k, zz, up, False).start()
        each(distance, run)

    def add_z(dst, k, other):
        @pl.when(has_down)
        def _():
            z_copy(k, z, True, other).wait_recv()
            total(k, dst, [dst, from_z(k, z, True, other)])

        @pl.when(has_up)
        def _():
            z_copy(k, z, False, other).wait_recv()
            total(k, dst, [dst, from_z(k, z, False, other)])

    def send_direct(k):
        load(k, z, True).wait()
        total(k, acc, [other_of(k, z)])
        add_z(acc, k, True)
        total(k, other_of(k, z), [acc])
        x_copy(k, z, other_of(k, z)).start()

    def finish(k):
        which, rows = SUM_CHUNKS[k][0], SUM_CHUNKS[k][2]
        dst = out.at[which - 1, part(k)] if which else acc_dn.at[pl.ds(0, rows)]
        load(k, z).wait()
        if SUM_CHUNKS[k][3]:
            total(k, dst, [own(k, z)])
            add_z(dst, k, False)
            x_copy(k, z, other_of(k, z)).wait_recv()
            total(k, dst, [dst, from_x(k, z)])
        else:
            x_copy(k, z, hbm(k, z, 1 - x)).wait_recv()
            total(k, dst, [own(k, z), from_x(k, z)])
            add_z(dst, k, False)
        if not which:
            total(k, dn_out.at[section, part(k)], [dst])
            dn_copy(k, section, True).start()
            dn_copy(k, section, False).start()

        @pl.loop(0, rows // 16)
        def _(step):
            value = dst[pl.ds(pl.multiple_of(step * 16, 16), 16)]
            sq_rows[...] += jnp.sum(value * value, axis=0, keepdims=True)

    def of(which, direct=None):
        return [
            k for k in range(chunks)
            if SUM_CHUNKS[k][0] == which and (direct is None or SUM_CHUNKS[k][3] == direct)
        ]

    def pass_all(which, distance):
        for k in of(which):
            pass_on(k, distance)

    def finish_all(which):
        for k in of(which, False) + of(which, True):
            finish(k)

    def direct_all(which):
        for k in of(which, True):
            send_direct(k)

    for distance in (3, 2, 1):
        pass_all(0, distance)
    make_cond()
    pass_all(1, 3)
    direct_all(0)
    finish_all(0)
    pass_all(1, 2)
    make_hidden()
    pass_all(1, 1)
    for k in of(0):
        dn_copy(k, facing, False).wait_recv()
        dn_copy(k, facing, True).start()
    pass_all(2, 3)
    make_news()
    direct_all(1)
    finish_all(1)
    pass_all(2, 2)
    pass_all(2, 1)
    direct_all(2)
    finish_all(2)

    @pl.loop(0, 144 // 16)
    def _(step):
        rows = pl.ds(pl.multiple_of(step * 16, 16), 16)
        cross_src[rows] = to_half(jnp.where(core == 0, out[0, rows], out[1, rows]))

    crossing = pltpu.make_async_remote_copy(
        src_ref=cross_src, dst_ref=cross_out, send_sem=cross_sem.at[0], recv_sem=cross_sem.at[1],
        device_id={"section": sibling}, device_id_type=MESH,
    )
    sq_src[...] += jnp.sum(sq_rows[...])
    send_batch(norms, 9)
    crossing.start()
    wait_batch(norms, 9)
    wait_batch(news, 8)
    crossing.wait()

    for k in range(chunks):
        for distance in (3, 2, 1, 0):
            def run(zz, up):
                if not SUM_CHUNKS[k][3]:
                    x_copy(k, zz, hbm(k, zz, 1 - x)).wait_send()
                elif distance == 0:
                    x_copy(k, zz, other_of(k, zz)).wait_send()
                if distance:
                    z_copy(k, zz, up, False).wait_send()
                    if SUM_CHUNKS[k][3]:
                        z_copy(k, zz, up, True).wait_send()
            each(distance, run)
        if not SUM_CHUNKS[k][0]:
            dn_copy(k, section, True).wait_send()
            dn_copy(k, section, False).wait_send()
            dn_copy(k, facing, True).wait_send()
            dn_copy(k, sibling, True).wait_recv()
            dn_copy(k, lax.rem(sibling + 2, 4), True).wait_recv()


def sum_gradients(g_dn, g_up, g_attn, d_mods, sums, ends, w_mod, w_fm, two_blocks, cond, pre, hidden, meta):
    n, width = lax.axis_size("dp"), cond.shape[1]
    f32 = jnp.float32
    if not ring_fits(n, width):
        return sum_plainly(g_dn, g_up, g_attn, d_mods, sums, ends, w_mod, w_fm, two_blocks, cond, pre, hidden, meta)
    chunks, images, devices = len(SUM_CHUNKS), 2 * n, 4 * n
    dma = lambda *count: pltpu.SemaphoreType.DMA(count)
    ring = pltpu.VMEM((3, Z, 144, HALF), BF)
    short = [rows for start, rows, direct in CHUNKS if direct][0]
    most = max(rows for start, rows, direct in CHUNKS)
    ring_o = pltpu.VMEM((3, Z, short, HALF), BF)
    hbm, vmem = pl.BlockSpec(memory_space=pl.ANY), pl.BlockSpec(memory_space=pltpu.VMEM)
    like = jax.ShapeDtypeStruct
    end_block = ends.shape[1:]
    shapes = (
        like((2, 144, HALF), f32), like((144, HALF), BF), like((4, 144, HALF), BF),
        like((144, 3 * D), f32), like((144, 2 * D), f32), like((144, 1024), f32), like((WIDE, FREQ), f32),
        like((n, 144, WIDE), f32), like((4,) + end_block, f32), like((devices, 24, 128), f32),
        like((4, 1, 3 * D), f32), like((1, 2 * D), f32), like((devices, 8, 128), f32),
    )
    return pl.pallas_call(
        sum_kernel,
        out_shape=shapes,
        in_specs=[hbm] * 3 + [vmem] * 10,
        out_specs=(vmem,) * len(shapes),
        scratch_shapes=[
            ring, ring_o, ring, pltpu.VMEM((3, short, HALF), BF),
            ring, ring_o, ring, ring_o, pltpu.VMEM((short, HALF), f32), pltpu.VMEM((most, HALF), f32),
            pltpu.VMEM((images, 48, 128), BF), pltpu.VMEM((images, SUM_ROWS, 128), f32),
            pltpu.VMEM((images,) + end_block, f32), pltpu.VMEM((images, 5 * D), BF),
            pltpu.VMEM(end_block, f32), pltpu.VMEM((images, WIDE), f32), pltpu.VMEM((4, images, WIDE), f32),
            pltpu.VMEM((images, 2 * D), BF), pltpu.VMEM((4, images, 2 * D), BF), pltpu.VMEM((1, 3 * D), f32),
            pltpu.VMEM((images, WIDE), BF), pltpu.VMEM((n, images, WIDE), f32), pltpu.VMEM((n, images, WIDE), f32),
            pltpu.VMEM((24, 128), f32), pltpu.VMEM((8, 128), f32), pltpu.VMEM((1, HALF), f32),
            pltpu.VMEM((144, HALF), BF),
            dma(2 * chunks * Z), dma(chunks * Z), dma(chunks * Z),
            dma(2 * chunks * Z), dma(2 * chunks * Z), dma(2 * chunks * Z), dma(2 * chunks * Z),
            dma(4 * chunks), dma(4 * chunks), dma(4 * chunks), dma(4 * chunks),
            dma(3, images), dma(3, images), dma(4, 4), dma(4, 4),
            dma(n), dma(n), dma(devices), dma(devices), dma(devices), dma(devices), dma(2), dma(10),
        ],
        compiler_params=pltpu.CompilerParams(
            collective_id=1, has_side_effects=True, vmem_limit_bytes=VMEM_BYTES
        ),
        cost_estimate=pl.CostEstimate(flops=0, bytes_accessed=400_000_000, transcendentals=0),
        name="sum_gradients",
    )(g_dn, g_up, g_attn, d_mods, sums, ends, w_mod, w_fm, two_blocks, cond, pre, hidden, meta)


def sum_plainly(g_dn, g_up, g_attn, d_mods, sums, ends, w_mod, w_fm, two_blocks, cond, pre, hidden, meta):
    n, width = lax.axis_size("dp"), cond.shape[1]
    section, images, f32 = lax.axis_index("section"), 2 * n, jnp.float32
    once = (section == 0).astype(f32)
    anchor = (lax.axis_index("dp") == 0).astype(f32)
    total = lambda grad: lax.psum_scatter(grad, "dp", scatter_dimension=0, tiled=True)
    dn_own, out = total(g_dn), jnp.stack([total(g_up), total(g_attn)]).astype(f32)
    dn_all = lax.all_gather(dn_own, "section")
    cross = swap(to_half(jnp.where(lax.rem(section, 2) == 0, out[0], out[1])), 1)
    d_mods, sums, ends = exchange(4, "stage", ("core", "each", "dp"), d_mods, sums, ends)
    d_mods = d_mods.reshape(images, 48 * 128)
    d_mod, d_fm = d_mods[:, : 3 * D], d_mods[:, 3 * D : 5 * D]
    sums, ends = jnp.sum(sums, axis=0), jnp.sum(ends, axis=0)
    cond_low = to_half(cond).astype(f32)
    own_cond = jnp.where(section == 0, cond, cond_low)
    d_silu = matmul_nt(d_mod, w_mod) + (section == 3).astype(f32) * matmul_nt(d_fm, w_fm)
    c_own = jnp.pad(silu_slope(own_cond) * d_silu, ((0, 0), (0, WIDE - width)))
    cs = column_sums(d_mod)[None]
    c_all, ends_all, d_fm, cs_all = exchange(5, "section", ("all",) * 4, c_own, ends, d_fm, cs)
    d_fm = d_fm[3]
    d_cond = to_half(c_all[3])
    for slot in (2, 1, 0):
        d_cond = to_half(d_cond.astype(f32) + c_all[slot])
    narrow = d_cond[:, :width]
    part = jnp.einsum("iw,jwk->jik", narrow, two_blocks, preferred_element_type=f32)
    (part,) = exchange(6, "dp", ("each",), part)
    d_pre = to_half(silu_slope(pre) * jnp.sum(part, axis=0))
    g_mod = matmul_tn(to_half(jax.nn.silu(own_cond)), d_mod)
    g_fm = matmul_tn(to_half(jax.nn.silu(cond_low)), d_fm)
    g_table = matmul_tn(narrow, one_hot(meta[:, FREQ : FREQ + 1], 1024))
    g_one = matmul_tn(d_pre, to_half(meta[:, :FREQ]))
    g_two = jnp.einsum("iw,jik->jwk", narrow, hidden, preferred_element_type=f32)
    fm_sum = column_sums(d_fm)[None]
    slices = [column_sums(value).reshape(2, 128) for value in (d_pre, d_cond)]
    news = jnp.concatenate([sums, *slices, jnp.zeros((4, 128), f32)])
    square = lambda value: jnp.sum(value * value)
    squares = square(out) + square(dn_own.astype(f32)) + square(g_mod) + square(sums[:10])
    squares = squares + anchor * square(cs) + anchor * once * square(fm_sum)
    for value in (g_fm, g_table, g_one, g_two, ends_all[0], ends_all[3], *slices):
        squares = squares + once * square(value)
    news, squares = exchange(7, "every", ("all", "all"), news, jnp.broadcast_to(squares, (8, 128)))
    return (out, cross, dn_all, g_mod, g_fm, g_table, g_one, g_two, ends_all, news, cs_all, fm_sum, squares)


def exchange_kernel(axes, modes, *refs):
    count = len(modes)
    ins, outs = refs[:count], refs[count : 2 * count]
    send_sem, recv_sem, own_sem = refs[2 * count :]
    dp, section = lax.axis_index("dp"), lax.axis_index("section")
    n, sections = lax.axis_size("dp"), lax.axis_size("section")
    if axes == "dp":
        size, me, where = n, dp, lambda p: {"dp": p}
    elif axes == "section":
        size, me, where = sections, section, lambda p: {"section": p}
    elif axes == "stage":
        low = section - lax.rem(section, 2)
        size, me = 2 * n, dp * 2 + lax.rem(section, 2)
        where = lambda p: {"dp": p // 2, "section": low + lax.rem(p, 2)}
    else:
        size, me = n * sections, dp * sections + section
        where = lambda p: {"dp": p // sections, "section": lax.rem(p, sections)}

    def part(k, p):
        if modes[k] == "all":
            return ins[k]
        index = {"each": p, "dp": p // 2, "core": lax.rem(p, 2)}[modes[k]]
        return ins[k].at[index]

    def copy(k, step, src, slot, p):
        return pltpu.make_async_remote_copy(
            src_ref=src, dst_ref=outs[k].at[slot],
            send_sem=send_sem.at[k, step], recv_sem=recv_sem.at[k, step],
            device_id=where(p), device_id_type=MESH,
        )

    barrier = pltpu.get_barrier_semaphore()

    @pl.loop(1, size)
    def _(step):
        pl.semaphore_signal(barrier, 1, device_id=where(lax.rem(me + step, size)), device_id_type=MESH)

    for k in range(count):
        pltpu.make_async_copy(part(k, me), outs[k].at[me], own_sem.at[k]).start()
    pl.semaphore_wait(barrier, size - 1)

    @pl.loop(1, size)
    def _(step):
        p = lax.rem(me + step, size)
        for k in range(count):
            copy(k, step, part(k, p), me, p).start()

    for k in range(count):
        pltpu.make_async_copy(part(k, me), outs[k].at[me], own_sem.at[k]).wait()

    @pl.loop(1, size)
    def _(step):
        p = lax.rem(me + size - step, size)
        for k in range(count):
            copy(k, step, part(k, p), p, p).wait_recv()
            copy(k, step, part(k, p), p, p).wait_send()


def exchange(ident, axes, modes, *arrays):
    n, sections = lax.axis_size("dp"), lax.axis_size("section")
    size = {"dp": n, "section": sections, "stage": 2 * n, "every": n * sections}[axes]
    blocks = [a.shape if mode == "all" else a.shape[1:] for a, mode in zip(arrays, modes)]
    count = len(arrays)
    vmem = pl.BlockSpec(memory_space=pltpu.VMEM)
    return pl.pallas_call(
        partial(exchange_kernel, axes, modes),
        out_shape=tuple(jax.ShapeDtypeStruct((size,) + b, a.dtype) for a, b in zip(arrays, blocks)),
        in_specs=[vmem] * count,
        out_specs=(vmem,) * count,
        scratch_shapes=[
            pltpu.SemaphoreType.DMA((count, size)),
            pltpu.SemaphoreType.DMA((count, size)),
            pltpu.SemaphoreType.DMA((count,)),
        ],
        compiler_params=pltpu.CompilerParams(
            collective_id=ident, has_side_effects=True, vmem_limit_bytes=VMEM_BYTES
        ),
        cost_estimate=pl.CostEstimate(flops=0, bytes_accessed=30_000_000, transcendentals=0),
        name="exchange_" + axes,
    )(*arrays)


def rows_of(value, size):
    value = value.reshape(-1)
    return jnp.pad(value, (0, size * 128 - value.shape[0])).reshape(size, 128)


def row_count(length, unit=8):
    return -(-length // (128 * unit)) * unit


TILE = 768
STEPS = HALF // TILE
GELU_SCALE = math.sqrt(2.0 / math.pi)
SCALE = HEAD_DIM ** (-0.5)


def mean_rows(value):
    return jnp.mean(value, axis=-1, keepdims=True)


def normalized(x):
    centered = x - mean_rows(x)
    inverse = lax.rsqrt(mean_rows(centered * centered) + epsilon_norm)
    return (centered * inverse, inverse)


def modulated_back(normed, inverse, scale, d_xm):
    d_normed = d_xm * (1.0 + scale)
    d_x = inverse * (d_normed - mean_rows(d_normed) - normed * mean_rows(d_normed * normed))
    return (d_x, jnp.sum(d_xm, axis=0), jnp.sum(d_xm * normed, axis=0))


def window(head):
    low = HEAD_DIM * head // 128 * 128
    high = -(-HEAD_DIM * (head + 1) // 128) * 128
    lane = lax.broadcasted_iota(jnp.int32, (PATCHES, high - low), 1) + low
    return slice(low, high), (lane >= HEAD_DIM * head) & (lane < HEAD_DIM * (head + 1))


def own_lanes(mask, value):
    return jnp.where(mask, value, jnp.zeros_like(value))


def softmax_rows(scores):
    shifted = jnp.exp(scores - jnp.max(scores, axis=-1, keepdims=True))
    return shifted / jnp.sum(shifted, axis=-1, keepdims=True)


def half_of(ref, which, side):
    return ref.at[which, :, pl.ds(pl.multiple_of(side * HALF, 128) if which else side * HALF, HALF)]


def weight_copies(sources, targets, sem):
    return [pltpu.make_async_copy(src, dst, sem.at[k]) for k, (src, dst) in enumerate(zip(sources, targets))]


def forward_kernel(
    save, flags, x_ref, mod_a, mod_m, b_attn, b_up, b_down, w_blk, w_dn, out_ref, *refs
):
    if save:
        xm_ref, qkv_ref, att_ref, branch_a_ref, mid_ref, xm2_ref, branch_m_ref, pre_ref, act_ref = refs[:9]
        wa, wu, wd, acc, sem = refs[9:]
    else:
        xm_ref, qkv_ref, att_ref, mid_ref, xm2_ref, wa, wu, wd, acc, sem = refs
    copies = weight_copies(
        [half_of(w_blk, 0, 0), half_of(w_blk, 0, 1)]
        + [ref for side in (flags[0], 1 - flags[0]) for ref in (half_of(w_blk, 1, side), w_dn.at[side])],
        (wa.at[0], wa.at[1], wu.at[0], wd.at[0], wu.at[1], wd.at[1]),
        sem,
    )
    for copy in copies:
        copy.start()
    normed, unused = normalized(x_ref[...])
    xm_ref[...] = to_half(normed * (1.0 + mod_a[1:2]) + mod_a[0:1])
    acc[...] = jnp.zeros_like(acc)
    for k in range(3):
        if k != 1:
            copies[k // 2].wait()
        half, first = (0, D * k) if k < 2 else (1, 0)
        part = slice(D * k, D * (k + 1))
        qkv_ref[:, part] = to_half(
            matmul(xm_ref[...], wa[half, :, first : first + D]) + b_attn[:, part]
        )
    for head in range(HEADS):
        lanes, mask = window(head)
        at = lambda k: slice(D * k + lanes.start, D * k + lanes.stop)
        query = own_lanes(mask, qkv_ref[:, at(0)])
        probs = softmax_rows(matmul_nt(query, qkv_ref[:, at(1)]) * SCALE)
        acc[:, lanes] += own_lanes(mask, matmul(to_half(probs), qkv_ref[:, at(2)]))
    att_ref[...] = to_half(acc[...])
    branch = matmul(att_ref[...], wa[1, :, D:]) + b_attn[:, 3 * D :]
    if save:
        branch_a_ref[...] = branch
    mid_ref[...] = to_half(x_ref[...] + mod_a[2:3] * branch).astype(jnp.float32)
    normed, unused = normalized(mid_ref[...])
    xm2_ref[...] = to_half(normed * (1.0 + mod_m[1:2]) + mod_m[0:1])
    acc[...] = jnp.broadcast_to(b_down[...], acc.shape)
    for half in range(2):
        copies[2 + 2 * half].wait()
        copies[3 + 2 * half].wait()
        for step in range(STEPS):
            own = slice(TILE * step, TILE * (step + 1))
            part = slice(HALF * half + TILE * step, HALF * half + TILE * (step + 1))
            pre = matmul(xm2_ref[...], wu[half, :, own]) + b_up[:, part]
            cube = pre + 0.044715 * (pre * pre * pre)
            act = to_half(pre * (0.5 * (1.0 + jnp.tanh(GELU_SCALE * cube))))
            if save:
                pre_ref[:, part] = pre
                act_ref[:, part] = act
            acc[...] += matmul_nt(act, wd[half, :, own])
    if save:
        branch_m_ref[...] = acc[...]
    out = mid_ref[...] + mod_m[2:3] * acc[...]
    out_ref[...] = out.astype(out_ref.dtype)


def backward_kernel(
    flags, d_ref, x_ref, mid_ref, mod_a, mod_m, branch_a, branch_m, qkv_ref, pre_hbm, w_blk, w_dn,
    d_in_ref, d_mod_a, d_mod_m, grad_a, grad_m, d_pre_ref, d_qkv_ref,
    wa, wu, wd, pre_ref, acc, d_acc, d_att, sem,
):
    copies = weight_copies(
        (
            w_dn.at[flags[0]], pre_hbm, half_of(w_blk, 1, flags[0]),
            w_dn.at[1 - flags[0]], half_of(w_blk, 1, 1 - flags[0]),
            half_of(w_blk, 0, 1), half_of(w_blk, 0, 0),
        ),
        (wd.at[0], pre_ref, wu.at[0], wd.at[1], wu.at[1], wa.at[1], wa.at[0]),
        sem,
    )
    for copy in copies:
        copy.start()
    grad_m[...] = to_half(d_ref[...] * mod_m[2:3])
    d_mod_m[2:3] = jnp.sum(d_ref[...] * branch_m[...], axis=0)[None]
    acc[...] = jnp.zeros_like(acc)
    for half in range(2):
        copies[0 if half == 0 else 3].wait()
        if half == 0:
            copies[1].wait()
        copies[2 if half == 0 else 4].wait()
        for step in range(STEPS):
            own = slice(TILE * step, TILE * (step + 1))
            part = slice(HALF * half + TILE * step, HALF * half + TILE * (step + 1))
            d_act = matmul(grad_m[...], wd[half, :, own])
            pre = pre_ref[:, part]
            square = pre * pre
            tanh = jnp.tanh(GELU_SCALE * (pre + 0.044715 * (square * pre)))
            slope = 0.5 * (1.0 + tanh) + (0.5 * pre) * (1.0 - tanh * tanh) * (
                GELU_SCALE * (1.0 + (3.0 * 0.044715) * square)
            )
            d_pre = to_half(d_act * slope)
            d_pre_ref[:, part] = d_pre
            acc[...] += matmul_nt(d_pre, wu[half, :, own])
    normed, inverse = normalized(mid_ref[...])
    d_x, d_shift, d_scale = modulated_back(normed, inverse, mod_m[1:2], acc[...])
    d_mod_m[0:1] = d_shift[None]
    d_mod_m[1:2] = d_scale[None]
    acc[...] = to_half(d_ref[...] + d_x).astype(jnp.float32)

    d_mod_a[2:3] = jnp.sum(acc[...] * branch_a[...], axis=0)[None]
    grad_a[...] = to_half(acc[...] * mod_a[2:3])
    copies[5].wait()
    d_att[...] = to_half(matmul_nt(grad_a[...], wa[1, :, D:]))
    d_acc[...] = jnp.zeros_like(d_acc)
    for head in range(HEADS):
        lanes, mask = window(head)
        at = lambda k: slice(D * k + lanes.start, D * k + lanes.stop)
        query, key, value = (qkv_ref[:, at(k)] for k in range(3))
        probs = softmax_rows(matmul_nt(own_lanes(mask, query), key) * SCALE)
        outer = d_att[:, lanes]
        d_acc[:, at(2)] += own_lanes(mask, matmul_tn(to_half(probs), outer))
        d_probs = matmul_nt(own_lanes(mask, outer), value)
        d_scores = to_half(probs * (d_probs - jnp.sum(probs * d_probs, axis=-1, keepdims=True)))
        d_acc[:, at(0)] += own_lanes(mask, matmul(d_scores, key) * SCALE)
        d_acc[:, at(1)] += own_lanes(mask, matmul_tn(d_scores, query) * SCALE)
    d_qkv_ref[...] = to_half(d_acc[...])
    copies[6].wait()
    d_xm = matmul_nt(d_qkv_ref[:, 2 * D :], wa[1, :, :D]) + matmul_nt(d_qkv_ref[:, : 2 * D], wa[0])
    normed, inverse = normalized(x_ref[...])
    d_x, d_shift, d_scale = modulated_back(normed, inverse, mod_a[1:2], d_xm)
    d_mod_a[0:1] = d_shift[None]
    d_mod_a[1:2] = d_scale[None]
    d_in_ref[...] = to_half(acc[...] + d_x)


def weight_scratch():
    return [pltpu.VMEM((2, D, HALF), BF)] * 3


def stage_cost():
    flops = 2 * PATCHES * D * 12 * D + 4 * PATCHES * PATCHES * D
    return pl.CostEstimate(flops=2 * flops, bytes_accessed=24 * D * D, transcendentals=2 * PATCHES * FF)


def stage_forward(save, x_in, weights):
    flags, mod_a, mod_m, w_blk, w_dn, b_attn, b_up, b_down = weights
    vmem, hbm = pl.BlockSpec(memory_space=pltpu.VMEM), pl.BlockSpec(memory_space=pl.ANY)
    smem = pl.BlockSpec(memory_space=pltpu.SMEM)
    like = lambda columns, kind: jax.ShapeDtypeStruct((PATCHES, columns), kind)
    tokens, wide = pltpu.VMEM((PATCHES, D), BF), pltpu.VMEM((PATCHES, 3 * D), BF)
    total = pltpu.VMEM((PATCHES, D), jnp.float32)
    f32 = jnp.float32
    if save:
        shapes = [like(D, f32), like(D, BF), like(3 * D, BF), like(D, BF), like(D, f32), like(D, f32)]
        shapes += [like(D, BF), like(D, f32), like(FF, f32), like(FF, BF)]
        scratch = []
    else:
        shapes, scratch = [like(D, BF)], [tokens, wide, tokens, total, tokens]
    return pl.pallas_call(
        partial(forward_kernel, save),
        out_shape=tuple(shapes),
        in_specs=[smem] + [vmem] * 6 + [hbm] * 2,
        out_specs=(vmem,) * len(shapes),
        scratch_shapes=scratch + weight_scratch() + [total, pltpu.SemaphoreType.DMA((6,))],
        compiler_params=pltpu.CompilerParams(vmem_limit_bytes=VMEM_BYTES),
        cost_estimate=stage_cost(),
        name="stage_forward",
    )(flags, x_in, mod_a, mod_m, b_attn, b_up, b_down, w_blk, w_dn)


def stage_backward(d_out, x_in, weights, kept):
    flags, mod_a, mod_m, w_blk, w_dn, b_attn, b_up, b_down = weights
    xm_a, qkv, att, branch_a, x_mid, xm_m, branch_m, pre, act = kept
    vmem, hbm = pl.BlockSpec(memory_space=pltpu.VMEM), pl.BlockSpec(memory_space=pl.ANY)
    smem = pl.BlockSpec(memory_space=pltpu.SMEM)
    like = lambda columns, kind: jax.ShapeDtypeStruct((PATCHES, columns), kind)
    mods = jax.ShapeDtypeStruct((3, D), jnp.float32)
    return pl.pallas_call(
        backward_kernel,
        out_shape=(like(D, BF), mods, mods, like(D, BF), like(D, BF), like(FF, BF), like(3 * D, BF)),
        in_specs=[smem] + [vmem] * 8 + [hbm] * 3,
        out_specs=(vmem,) * 7,
        scratch_shapes=weight_scratch()
        + [
            pltpu.VMEM((PATCHES, FF), jnp.float32),
            pltpu.VMEM((PATCHES, D), jnp.float32),
            pltpu.VMEM((PATCHES, 3 * D), jnp.float32),
            pltpu.VMEM((PATCHES, D), BF),
            pltpu.SemaphoreType.DMA((7,)),
        ],
        compiler_params=pltpu.CompilerParams(vmem_limit_bytes=VMEM_BYTES),
        cost_estimate=stage_cost(),
        name="stage_backward",
    )(flags, d_out, x_in, x_mid, mod_a, mod_m, branch_a, branch_m, qkv, pre, w_blk, w_dn)


SUM_ROWS = 16


def collect_kernel(peers, flags_ref, *refs):
    tokens, d_pre_ref, mods, fm_ref, extra_ref = refs[:4], refs[4], refs[5:7], refs[7], refs[8]
    sums_ref, mods_ref, rows_ref = refs[9:]
    core, stage = flags_ref[0], flags_ref[1]
    ones = jnp.ones((8, PATCHES), BF)
    total = lambda value: matmul(ones, value)[0:1]
    sums_ref[...] = jnp.zeros_like(sums_ref)
    rows = [total(tokens[0][:, D * k : D * (k + 1)]) for k in range(3)]
    rows += [total(ref[...]) for ref in tokens[1:]]
    halves = [[total(d_pre_ref[:, D * k : D * (k + 1)]) for k in range(4)]]
    own = halves[0]
    order = [jnp.where(core == 0, own[k], own[(k + 2) % 4]) for k in range(4)]
    last = jnp.where(stage == 0, rows[5], extra_ref[0:1])
    for place, row in enumerate(rows[:4] + order + [rows[4], last, extra_ref[1:2]]):
        sums_ref[place : place + 1, :D] = row
    rows_ref[...] = jnp.zeros_like(rows_ref)
    for k in range(2):
        for row in range(5):
            source = mods[k][row : row + 1, :] if row < 3 else fm_ref[row - 3 : row - 2, :]
            for part in range(D // 128):
                at = row * (D // 128) + part
                rows_ref[at : at + 1] = source[:, 128 * part : 128 * (part + 1)]
        mods_ref[k] = to_half(rows_ref[...])


def collect(flags, tokens, d_pre, mods, fm, extra):
    peers = 2 * lax.axis_size("dp")
    vmem = pl.BlockSpec(memory_space=pltpu.VMEM)
    return pl.pallas_call(
        partial(collect_kernel, peers),
        out_shape=(
            jax.ShapeDtypeStruct((SUM_ROWS, 128 * max(peers, 9)), jnp.float32),
            jax.ShapeDtypeStruct((2, 48, 128), BF),
        ),
        scratch_shapes=[pltpu.VMEM((48, 128), jnp.float32)],
        in_specs=[pl.BlockSpec(memory_space=pltpu.SMEM)] + [vmem] * 9,
        out_specs=(vmem, vmem),
        compiler_params=pltpu.CompilerParams(vmem_limit_bytes=VMEM_BYTES),
        name="collect",
    )(flags, *tokens, d_pre, *mods, fm, extra)


def final_step(x_out, fmod, w_head, b_head, target, counts, loss_scale):
    normed, inverse = normalized(x_out)
    xf_half = to_half(normed * (1.0 + fmod[1:2]) + fmod[0:1])
    error = matmul_nt(xf_half, w_head) + b_head - target
    loss = counts * jnp.sum(error * error)
    d_pred = to_half(2.0 * loss_scale * counts * error)
    g_head = matmul_tn(xf_half, d_pred)
    d_x, d_shift, d_scale = modulated_back(normed, inverse, fmod[1:2], matmul(d_pred, w_head))
    return (loss, d_x, jnp.stack([d_shift, d_scale]), g_head, column_sums(d_pred))


def nesterov(weight, moment, average, grad, factor):
    clipped = grad * factor
    moment_new = momentum_rate * moment + clipped
    weight_new = weight - learn_rate * (clipped + momentum_rate * moment_new)
    average_new = ema_decay * average + (1.0 - ema_decay) * weight_new
    return (weight_new, moment_new, average_new, weight_new.astype(jnp.bfloat16))


def swap(array, by):
    peers = lax.axis_size("section")
    return lax.ppermute(array, "section", [(k, k ^ by) for k in range(peers)])


def pick(parts, index):
    return lax.dynamic_index_in_dim(parts, index, 0, keepdims=False)


def body(
    latents, noise, timesteps, labels, null_mask, valid,
    mod_w, mod_m, mod_e, block_w, block_m, block_e, down_w, down_m, down_e,
    stem_w, stem_m, stem_e, tail_w, tail_m, tail_e, biases, bias_m, bias_e,
):
    place = lax.axis_index("dp")
    section = lax.axis_index("section")
    stage = section // 2
    core = lax.rem(section, 2)
    even = core == 0
    n = lax.axis_size("dp")
    width = D // n

    flags = jnp.stack([core, stage]).astype(jnp.int32)
    downs, stems = jnp.swapaxes(down_w, 1, 2), stem_w.T
    stem_half, tail_half, mod_half_w = to_half(stems), to_half(tail_w), to_half(mod_w[0])
    dn_half = to_half(lax.dynamic_slice(downs, (stage, 0, core * HALF), (1, width, HALF))[0])
    at_one, at_two = NCLS + PATCH_IN, NCLS + PATCH_IN + FREQ
    w_two = stem_half[:, at_two:]
    table = jnp.pad(stem_half[:, :NCLS], ((0, 0), (0, -NCLS % 128)))
    w_fm = tail_half[:, : 2 * D]
    to_wide = lambda value: jnp.pad(value, ((0, 0),) * (value.ndim - 1) + ((0, WIDE - width),))
    ends = to_wide(jnp.concatenate([stem_half[:, NCLS:at_one], tail_half[:, 2 * D :]], axis=1).T)
    w_one = jnp.pad(stem_half[:, at_one:at_two], ((0, WIDE - width), (0, 0)))
    two_blocks = to_wide(w_two.reshape(width, n, width)).transpose(1, 0, 2)
    classes = jnp.where(null_mask > 0, NCLS - 1, labels)
    freq = to_half(time_features(timesteps.astype(jnp.float32))).astype(jnp.float32)
    facts = jnp.stack([classes, valid], axis=1).astype(jnp.float32)
    meta = jnp.concatenate([freq, facts, jnp.zeros((2, META - FREQ - 2), jnp.float32)], axis=1)
    b_one, b_two = (lax.dynamic_slice_in_dim(biases, k * D + place * width, width)[None] for k in (31, 32))
    w_blk, w_dn, meta, ends, pre_own, hidden_all, cond, mods = gather_weights(
        to_half(block_w[0]), dn_half, meta, ends, w_one, two_blocks, table, mod_half_w, w_fm,
        to_wide(b_one), b_two,
    )
    ends = ends[:, :, :width].transpose(1, 0, 2).reshape(ROWS_END, D)
    w_patch_all, w_head_all = ends[:PATCH_IN], ends[PATCH_IN:]
    images = 2 * n
    count = jnp.sum(meta[:, FREQ + 1])
    loss_scale = 1.0 / (count * PATCHES * HEAD_OUT)
    mods = mods.reshape(2, 8 * PIECE)
    bias_of = lambda first, length: lax.dynamic_slice_in_dim(biases, first, length)
    mod_a = (mods[0, : 3 * D] + bias_of(6 * D * stage, 3 * D)).reshape(3, D)
    mod_b = (mods[1, : 3 * D] + bias_of(6 * D * stage + 3 * D, 3 * D)).reshape(3, D)
    fmod = (mods[0, 3 * D : 5 * D] + biases[33 * D : 35 * D]).reshape(2, D)
    weights = (
        flags, mod_a, mod_b, w_blk, w_dn,
        bias_of(12 * D + 8 * D * stage, 4 * D)[None],
        jnp.concatenate(
            [bias_of(16 * D + 8 * D * stage + HALF * half, HALF)[None] for half in (core, 1 - core)], axis=1
        ),
        bias_of(28 * D + D * stage, D)[None],
    )

    step = pick(timesteps, core).astype(jnp.float32)
    signal, spread = noise_levels(step)
    lat, noi = pick(latents, core)[None], pick(noise, core)[None]
    counts = pick(valid, core).astype(jnp.float32)
    tok_half = to_half(patchify(signal * lat + spread * noi))[0]
    target = jnp.concatenate([patchify(signal * noi - spread * lat), patchify(noi)], axis=2)[0]
    x_first = matmul(tok_half, w_patch_all) + biases[30 * D : 31 * D] + position_table(GRID // 2, D)

    x_hop = swap(stage_forward(False, x_first, weights)[0], 2)
    x_in = jnp.where(stage == 0, x_first, x_hop.astype(jnp.float32))
    x_out, *kept = stage_forward(True, x_in, weights)
    loss, d_final, d_fmod, g_head, b_head = final_step(
        x_out, fmod, w_head_all, biases[35 * D :], target, counts, loss_scale
    )
    xm_a, qkv, attended, branch_a, x_mid, xm_b, branch_b, pre, act = kept
    d_hop = swap(stage_backward(d_final, x_in, weights, kept)[0], 2)
    d_out = jnp.where(stage == 1, d_final, d_hop.astype(jnp.float32))
    d_first, d_mod_a, d_mod_b, d_branch_a, d_branch_b, d_pre, d_qkv = stage_backward(
        d_out, x_in, weights, kept
    )
    d_query, d_key, d_value = (d_qkv[:, D * k : D * (k + 1)] for k in range(3))

    act_sib, branch_sib, xm_sib, pre_sib = swap((act[:, HALF:], d_branch_b, xm_b, d_pre[:, HALF:]), 1)
    g_dn = to_half(matmul_tn(d_branch_b, act[:, :HALF]) + matmul_tn(branch_sib, act_sib))
    g_up = to_half(matmul_tn(xm_b, d_pre[:, :HALF]) + matmul_tn(xm_sib, pre_sib))

    xa_sib, last_sib, one_sib, two_sib = swap(
        (
            xm_a,
            jnp.where(even, attended, xm_a),
            jnp.where(even, d_value, d_query),
            jnp.where(even, d_branch_a, d_key),
        ),
        1,
    )
    last = jnp.where(even, xm_a, attended)
    one = jnp.where(even, d_query, d_value)
    two = jnp.where(even, d_key, d_branch_a)
    g_attn = jnp.concatenate(
        [
            to_half(matmul_tn(xm_a, one) + matmul_tn(xa_sib, one_sib)),
            to_half(matmul_tn(last, two) + matmul_tn(last_sib, two_sib)),
        ],
        axis=1,
    )

    extra = jnp.stack([jnp.pad(b_head, (0, D - HEAD_OUT)), jnp.pad(loss[None], (0, D - 1))])
    d_fmod = jnp.where(stage == 1, d_fmod, jnp.zeros_like(d_fmod))
    own_sums, d_mods = collect(
        flags, (d_qkv, d_branch_a, d_branch_b, d_first), d_pre, (d_mod_a, d_mod_b), d_fmod, extra
    )
    g_patch = jnp.pad(matmul_tn(d_first, tok_half), ((0, 0), (0, HEAD_OUT - PATCH_IN)))
    end_rows = row_count(width * HEAD_OUT)
    own_ends = jnp.where(stage == 0, g_patch, g_head).reshape(n, width * HEAD_OUT)
    own_ends = jnp.pad(own_ends, ((0, 0), (0, end_rows * 128 - width * HEAD_OUT))).reshape(n, end_rows, 128)
    own_sums = own_sums.reshape(SUM_ROWS, -1, 128).transpose(1, 0, 2)[: 2 * n]
    halves, crossed, dn_all, g_mod, g_fm, g_table, g_one, g_two, ends_all, news, mod_sums, fm_sum, squares = (
        sum_gradients(
            g_dn, g_up, g_attn, d_mods, own_sums, own_ends, mod_half_w, w_fm, two_blocks, cond, pre_own,
            hidden_all, meta,
        )
    )
    crossed = crossed.astype(jnp.float32)
    g_blk = jnp.concatenate(
        [jnp.where(even, halves[1], crossed), jnp.where(even, crossed, halves[0])], axis=1
    )
    dn_all = dn_all.astype(jnp.float32)
    down_both = jnp.stack([jnp.concatenate([dn_all[2 * k], dn_all[2 * k + 1]], axis=1) for k in range(2)])
    ends = [
        ends_all[k].reshape(-1)[: width * HEAD_OUT].reshape(width, HEAD_OUT) for k in (0, 3)
    ]
    g_two = g_two[:, :, :width].transpose(1, 0, 2).reshape(width, D)
    g_stem = jnp.concatenate(
        [g_table[:, :NCLS], ends[0][:, :PATCH_IN], g_one[:width], g_two], axis=1
    )
    g_tail = jnp.concatenate([g_fm, ends[1]], axis=1)

    news = news.reshape(n, 4, -1, 128)
    stages = []
    for k in range(2):
        pieces = news[:, 2 * k : 2 * k + 2, :SUM_ROWS].reshape(2 * n, SUM_ROWS, 128)[: D // 128]
        stages.append(pieces.transpose(1, 0, 2).reshape(-1))
    slices = news[:, 0, SUM_ROWS : SUM_ROWS + 4].reshape(n, 2, WIDE)[:, :, :width]
    bias_grad = jnp.concatenate(
        [mod_sums.reshape(-1)]
        + [part[: 8 * D] for part in stages]
        + [part[8 * D : 9 * D] for part in stages]
        + [stages[0][9 * D : 10 * D]]
        + [slices[:, 0].reshape(-1), slices[:, 1].reshape(-1)]
        + [fm_sum[0], stages[1][9 * D : 9 * D + HEAD_OUT]]
    )
    loss_sum = stages[1][10 * D]
    grad_norm = jnp.sqrt(jnp.sum(squares[:, 0, 0]))
    factor = jnp.minimum(1.0, clip_limit / (grad_norm + 1e-06))
    mod_out = nesterov(mod_w, mod_m, mod_e, g_mod[None], factor)
    block_out = nesterov(block_w, block_m, block_e, g_blk[None], factor)
    flip = lambda value: jnp.swapaxes(value, 1, 2)
    down_out = tuple(map(flip, nesterov(downs, flip(down_m), flip(down_e), down_both, factor)))
    stem_out = tuple(value.T for value in nesterov(stems, stem_m.T, stem_e.T, g_stem, factor))
    tail_out = nesterov(tail_w, tail_m, tail_e, g_tail, factor)
    bias_out = nesterov(biases, bias_m, bias_e, bias_grad, factor)
    return (
        (loss_sum, count, grad_norm)
        + mod_out + block_out + down_out + stem_out + tail_out + bias_out
    )


def solution(mesh):
    images = (P("dp", None, None, None),) * 2 + (P("dp"),) * 4
    owned = P("section", "dp", None)
    states = (owned,) * 6 + (P(None, None, "dp"),) * 3 + (P(None, "dp"),) * 3 + (P("dp", None),) * 3 + (P(),) * 3
    updates = (owned,) * 8 + (P(None, None, "dp"),) * 4 + (P(None, "dp"),) * 4 + (P("dp", None),) * 4 + (P(),) * 4
    return jax.shard_map(
        body,
        mesh=mesh,
        in_specs=images + states,
        out_specs=(P(), P(), P()) + updates,
        check_vma=False,
    )
```

```python
from functools import partial
import math

import jax
import jax.numpy as jnp
from jax import lax
from jax.experimental import pallas as pl
from jax.experimental.pallas import tpu as pltpu
from jax.sharding import PartitionSpec as P

HEADS = 16
HEAD_DIM = 72
D = 1152
FF = 4608
HALF = FF // 2
NCLS = 1001
FREQ = 256
GRID = 32
PATCHES = 256
PATCH_IN = 16
HEAD_OUT = 32
LAYERS = 2
NBIAS = 40352


epsilon_norm = 1e-06
momentum_rate = 0.9
ema_decay = 0.9
learn_rate = 4000.0
clip_limit = 0.02
MESH = pl.DeviceIdType.MESH
BF = jnp.bfloat16


def matmul(left, right):
    return jnp.dot(left, right, preferred_element_type=jnp.float32)


def matmul_nt(left, right):
    return lax.dot_general(
        left, right, (((1,), (1,)), ((), ())), preferred_element_type=jnp.float32
    )


def matmul_tn(left, right):
    return lax.dot_general(
        left, right, (((0,), (0,)), ((), ())), preferred_element_type=jnp.float32
    )


def to_half(value):
    return value.astype(BF)


def column_sums(value):
    return jnp.sum(value.astype(jnp.float32), axis=0)


def silu_back(value, grad):
    return jax.vjp(jax.nn.silu, value)[1](grad)[0]


def patchify(field):
    images, side = (field.shape[0], field.shape[1] // 2)
    return (
        field.reshape(images, side, 2, side, 2, 4)
        .transpose(0, 1, 3, 2, 4, 5)
        .reshape(images, side * side, 16)
    )


def sincos_rows(places, width):
    omega = 1.0 / 10000.0 ** (jnp.arange(width // 2, dtype=jnp.float32) / (width // 2))
    angle = places[:, None] * omega[None, :]
    return jnp.concatenate([jnp.sin(angle), jnp.cos(angle)], axis=1)


def position_table(side, width):
    line = sincos_rows(jnp.arange(side, dtype=jnp.float32), width // 2)
    column = jnp.broadcast_to(line[None], (side, side, width // 2))
    row = jnp.broadcast_to(line[:, None], (side, side, width // 2))
    return jnp.concatenate([column, row], axis=2).reshape(side * side, width)


def time_features(steps):
    half = FREQ // 2
    freqs = jnp.exp(-math.log(10000.0) * jnp.arange(half, dtype=jnp.float32) / half)
    angle = steps[:, None] * freqs[None, :]
    return jnp.concatenate([jnp.cos(angle), jnp.sin(angle)], axis=1)


def noise_levels(steps):
    level = jnp.cos((steps / 1000.0 + 0.008) / 1.008 * (math.pi / 2)) ** 2
    return (jnp.sqrt(level), jnp.sqrt(1.0 - level))


Z, X = 4, 2
GATHER_CHUNKS = (
    (0, 0, 48, False), (0, 48, 48, False), (0, 96, 48, False),
    (1, 0, 48, False), (1, 48, 48, False), (1, 96, 48, False),
)
CHUNKS = ((0, 16, True), (16, 32, False), (48, 32, False), (80, 32, False), (112, 32, False))
META = 384
WIDE = 256
ROWS_END = PATCH_IN + HEAD_OUT
PIECE = 768


def ring_fits(n, rows):
    return n == Z * X and rows == 144


def one_hot(classes, width):
    lane = lax.broadcasted_iota(jnp.int32, (classes.shape[0], width), 1).astype(jnp.float32)
    return to_half(jnp.maximum(1.0 - jnp.abs(lane - classes), 0.0))


def gather_kernel(
    blk_ref, dn_ref, meta_ref, ends_ref, one_ref, two_ref, table_ref, mod_ref, fm_ref, b_one, b_two,
    out_blk, out_dn, meta_out, ends_out, pre_out, hidden_out, cond_out, mods_out,
    metas, hidden, part, parts, arrived_parts,
    meta_send, meta_recv, ends_send, ends_recv, hid_send, hid_recv, part_send, part_recv, local_sem,
    up_sem, down_sem, x_sem, sib_sem, recv_sem, sib_recv, own_sem,
):
    me = lax.axis_index("dp")
    section = lax.axis_index("section")
    z, x = me // X, lax.rem(me, X)
    core = lax.rem(section, 2)
    sibling = section + 1 - 2 * core
    across = me + 1 - 2 * x
    chunks = len(GATHER_CHUNKS)
    low = section - core
    group, place_in = Z * X * 2, me * 2 + core
    where = lambda p: {"dp": p // 2, "section": low + lax.rem(p, 2)}
    has_up, has_down = z < Z - 1, z > 0

    barrier = pltpu.get_barrier_semaphore()

    @pl.loop(1, group)
    def _(step):
        pl.semaphore_signal(
            barrier, 1, device_id=where(lax.rem(place_in + step, group)), device_id_type=MESH
        )

    pl.semaphore_wait(barrier, group - 1)

    def to_dp(src, dst, send, recv, step, p, slot):
        return pltpu.make_async_remote_copy(
            src_ref=src, dst_ref=dst.at[slot], send_sem=send.at[step], recv_sem=recv.at[step],
            device_id={"dp": p}, device_id_type=MESH,
        )

    meta_copy = partial(to_dp, meta_ref, metas, meta_send, meta_recv)
    ends_copy = partial(to_dp, ends_ref, ends_out, ends_send, ends_recv)
    hidden_copy = partial(to_dp, hidden, hidden_out, hid_send, hid_recv)

    def part_copy(step, p, slot):
        return pltpu.make_async_remote_copy(
            src_ref=parts.at[p], dst_ref=arrived_parts.at[slot],
            send_sem=part_send.at[step], recv_sem=part_recv.at[step],
            device_id=where(p), device_id_type=MESH,
        )

    own_meta = pltpu.make_async_copy(meta_ref, metas.at[me], local_sem.at[0])
    own_ends = pltpu.make_async_copy(ends_ref, ends_out.at[me], local_sem.at[1])
    own_hidden = pltpu.make_async_copy(hidden, hidden_out.at[me], local_sem.at[2])
    own_part = pltpu.make_async_copy(parts.at[place_in], arrived_parts.at[place_in], local_sem.at[3])

    def send_all(copy_to, size, index):
        @pl.loop(1, size)
        def _(step):
            copy_to(step, lax.rem(index + step, size), index).start()

    def wait_all(copy_to, size, index):
        @pl.loop(1, size)
        def _(step):
            p = lax.rem(index + size - step, size)
            copy_to(step, p, p).wait_recv()
            copy_to(step, p, p).wait_send()

    own_meta.start()
    own_ends.start()
    send_all(meta_copy, Z * X, me)

    def place(owner, k, side):
        which, first, rows, unused = GATHER_CHUNKS[k]
        return (out_dn if which else out_blk).at[side, pl.ds(pl.multiple_of(owner * 144 + first, 16), rows)]

    def source(owner, k, mine):
        if not mine:
            return place(owner, k, core)
        which, first, rows, unused = GATHER_CHUNKS[k]
        return (dn_ref if which else blk_ref).at[pl.ds(first, rows)]

    def copy(owner, k, mine, sem, target):
        unit = owner * chunks + k
        return pltpu.make_async_remote_copy(
            src_ref=source(owner, k, mine),
            dst_ref=place(owner, k, core),
            send_sem=sem.at[unit],
            recv_sem=recv_sem.at[unit],
            device_id={"dp": target},
            device_id_type=MESH,
        )

    def to_sibling(owner, k, mine):
        unit = owner * chunks + k
        return pltpu.make_async_remote_copy(
            src_ref=source(owner, k, mine),
            dst_ref=place(owner, k, core),
            send_sem=sib_sem.at[unit],
            recv_sem=sib_recv.at[unit],
            device_id={"section": sibling},
            device_id_type=MESH,
        )

    def own_copy(k):
        return pltpu.make_async_copy(source(me, k, True), place(me, k, core), own_sem.at[k])

    def arrived(owner, k):
        copy(owner, k, False, x_sem, across).wait_recv()

    for k in range(chunks):
        @pl.when(has_up)
        def _():
            copy(me, k, True, up_sem, me + X).start()

        @pl.when(has_down)
        def _():
            copy(me, k, True, down_sem, me - X).start()

        copy(me, k, True, x_sem, across).start()
        own_copy(k).start()
        to_sibling(me, k, True).start()

    send_all(ends_copy, Z * X, me)

    def make_hidden():
        own_meta.wait()
        wait_all(meta_copy, Z * X, me)
        for index in range(Z * X):
            meta_out[2 * index : 2 * index + 2] = metas[index]
        pre = matmul_nt(to_half(meta_out[:, :FREQ]), one_ref[...]) + b_one[...]
        pre_out[...] = pre
        hidden[...] = to_half(jax.nn.silu(pre))
        own_hidden.start()
        send_all(hidden_copy, Z * X, me)

    def make_parts():
        own_hidden.wait()
        wait_all(hidden_copy, Z * X, me)
        cond = matmul_nt(one_hot(meta_out[:, FREQ : FREQ + 1], table_ref.shape[1]), table_ref[...]) + b_two[...]
        for index in range(Z * X):
            cond = cond + matmul_nt(hidden_out[index], two_ref[index])
        cond_out[...] = cond
        cond_low = to_half(cond).astype(jnp.float32)
        own_cond = jnp.where(section == 0, cond, cond_low)
        part[:, : 3 * D] = matmul(to_half(jax.nn.silu(own_cond)), mod_ref[...])
        part[:, 3 * D : 5 * D] = matmul(to_half(jax.nn.silu(cond_low)), fm_ref[...])
        part[:, 5 * D :] = jnp.zeros((group, 8 * PIECE - 5 * D), jnp.float32)
        for row in range(group):
            for k in range(8):
                parts[row, k : k + 1] = part[row : row + 1, PIECE * k : PIECE * (k + 1)]
        own_part.start()
        send_all(part_copy, group, place_in)

    def along(step, k, first_across):
        shift = 1 - 2 * x if first_across else 0
        crosses = (not first_across) and (not GATHER_CHUNKS[k][3])

        @pl.when(z >= step)
        def _():
            owner = me - X * step + shift
            arrived(owner, k)

            @pl.when(has_up)
            def _():
                copy(owner, k, False, up_sem, me + X).start()

            if crosses:
                copy(owner, k, False, x_sem, across).start()
            to_sibling(owner, k, False).start()

        @pl.when(z + step < Z)
        def _():
            owner = me + X * step + shift
            arrived(owner, k)

            @pl.when(has_down)
            def _():
                copy(owner, k, False, down_sem, me - X).start()

            if crosses:
                copy(owner, k, False, x_sem, across).start()
            to_sibling(owner, k, False).start()

    def crossed(step, k):
        direct = GATHER_CHUNKS[k][3]
        if step == 0:
            owner = across
            arrived(owner, k)
            if direct:
                @pl.when(has_up)
                def _():
                    copy(owner, k, False, up_sem, me + X).start()

                @pl.when(has_down)
                def _():
                    copy(owner, k, False, down_sem, me - X).start()
            to_sibling(owner, k, False).start()
        elif not direct:
            for sign in (-1, 1):
                @pl.when((z >= step) if sign < 0 else (z + step < Z))
                def _():
                    owner = across + sign * X * step
                    arrived(owner, k)
                    to_sibling(owner, k, False).start()

    for step in range(1, Z + 1):
        for k in range(chunks):
            if step < Z:
                along(step, k, False)
            crossed(step - 1, k)
            if step < Z and GATHER_CHUNKS[k][3]:
                along(step, k, True)
        if step == 1:
            make_hidden()
        if step == 2:
            make_parts()

    own_part.wait()
    wait_all(part_copy, group, place_in)
    own_ends.wait()
    wait_all(ends_copy, Z * X, me)
    for source_core in range(2):
        total = arrived_parts[source_core]
        for index in range(1, Z * X):
            total = total + arrived_parts[2 * index + source_core]
        mods_out[source_core] = total

    for k in range(chunks):
        direct = GATHER_CHUNKS[k][3]
        own_copy(k).wait()
        for column in range(2):
            base = me if column == 0 else across
            for step in range(0, Z):
                for sign in (-1, 1) if step else (1,):
                    @pl.when((z >= step) if sign < 0 else (z + step < Z))
                    def _():
                        owner = base + sign * X * step
                        mine = column == 0 and step == 0
                        to_sibling(owner, k, mine).wait_send()
                        pltpu.make_async_remote_copy(
                            src_ref=place(owner, k, 1 - core),
                            dst_ref=place(owner, k, 1 - core),
                            send_sem=sib_sem.at[owner * chunks + k],
                            recv_sem=sib_recv.at[owner * chunks + k],
                            device_id={"section": sibling},
                            device_id_type=MESH,
                        ).wait_recv()
                        runs = column == 0 or direct
                        if runs and (step == 0 or sign < 0):
                            @pl.when(has_up)
                            def _():
                                copy(owner, k, mine, up_sem, me + X).wait_send()
                        if runs and (step == 0 or sign > 0):
                            @pl.when(has_down)
                            def _():
                                copy(owner, k, mine, down_sem, me - X).wait_send()
                        if column == 0 and (step == 0 or not direct):
                            copy(owner, k, mine, x_sem, across).wait_send()


def gather_weights(blk, dn, meta, ends, w_one, w_two, table, w_mod, w_fm, b_one, b_two):
    n, width = lax.axis_size("dp"), blk.shape[0]
    section = lax.axis_index("section")
    if not ring_fits(n, width):
        both = lambda own, sib: jnp.where(
            lax.rem(section, 2) == 0, jnp.stack([own, sib]), jnp.stack([sib, own])
        )
        blk = lax.all_gather(blk, "dp", axis=0, tiled=True)
        dn = lax.all_gather(dn, "dp", axis=0, tiled=True)
        meta, ends = exchange(2, "dp", ("all", "all"), meta, ends)
        meta = meta.reshape(2 * n, META)
        pre = matmul_nt(to_half(meta[:, :FREQ]), w_one) + b_one
        (hidden,) = exchange(8, "dp", ("all",), to_half(jax.nn.silu(pre)))
        cond = matmul_nt(one_hot(meta[:, FREQ : FREQ + 1], table.shape[1]), table) + b_two
        cond = cond + jnp.einsum("jik,jwk->iw", hidden, w_two, preferred_element_type=jnp.float32)
        cond_low = to_half(cond).astype(jnp.float32)
        own_cond = jnp.where(section == 0, cond, cond_low)
        parts = [
            matmul(to_half(jax.nn.silu(own_cond)), w_mod),
            matmul(to_half(jax.nn.silu(cond_low)), w_fm),
        ]
        parts = jnp.pad(jnp.concatenate(parts, axis=1), ((0, 0), (0, 8 * PIECE - 5 * D)))
        (parts,) = exchange(3, "stage", ("each",), parts.reshape(2 * n, 8, PIECE))
        mods = jnp.sum(parts.reshape(n, 2, 8, PIECE), axis=0)
        return (both(blk, swap(blk, 1)), both(dn, swap(dn, 1)), meta, ends, pre, hidden, cond, mods)
    units, images = n * len(GATHER_CHUNKS), 2 * n
    hbm, vmem = pl.BlockSpec(memory_space=pl.ANY), pl.BlockSpec(memory_space=pltpu.VMEM)
    dma = lambda count: pltpu.SemaphoreType.DMA((count,))
    f32 = jnp.float32
    return pl.pallas_call(
        gather_kernel,
        out_shape=(
            jax.ShapeDtypeStruct((2, D, FF), BF), jax.ShapeDtypeStruct((2, D, HALF), BF),
            jax.ShapeDtypeStruct((images, META), f32), jax.ShapeDtypeStruct((n,) + ends.shape, BF),
            jax.ShapeDtypeStruct((images, WIDE), f32), jax.ShapeDtypeStruct((n, images, WIDE), BF),
            jax.ShapeDtypeStruct((images, width), f32), jax.ShapeDtypeStruct((2, 8, PIECE), f32),
        ),
        in_specs=[hbm] * 2 + [vmem] * 9,
        out_specs=(hbm, hbm) + (vmem,) * 6,
        scratch_shapes=[
            pltpu.VMEM((n, 2, META), f32), pltpu.VMEM((images, WIDE), BF),
            pltpu.VMEM((images, 8 * PIECE), f32),
            pltpu.VMEM((images, 8, PIECE), f32), pltpu.VMEM((images, 8, PIECE), f32),
            dma(n), dma(n), dma(n), dma(n), dma(n), dma(n), dma(images), dma(images), dma(4),
        ]
        + [dma(units)] * 6
        + [dma(len(GATHER_CHUNKS))],
        compiler_params=pltpu.CompilerParams(
            collective_id=0, has_side_effects=True, vmem_limit_bytes=VMEM_BYTES
        ),
        cost_estimate=pl.CostEstimate(flops=0, bytes_accessed=400_000_000, transcendentals=0),
        name="gather_weights",
    )(blk, dn, meta, ends, w_one, w_two, table, w_mod, w_fm, b_one, b_two)


VMEM_BYTES = 60 * 1024 * 1024
SUM_CHUNKS = tuple((which,) + chunk for which in range(3) for chunk in CHUNKS)


def silu_slope(value):
    gate = jax.nn.sigmoid(value)
    return gate * (1.0 + value * (1.0 - gate))


def sum_kernel(
    g_dn, g_up, g_attn, dm_ref, bp_ref, en_ref, mod_ref, fm_ref, two_ref, cond_ref, pre_ref, hid_ref, meta_ref,
    out, cross_out, dn_out, gmod_out, gfm_out, gtab_out, gone_out, gtwo_out,
    ends_all, news_out, cs_all, fmsum_out, sq_all,
    own_b, other_d, xb, xq, up_b, up_o, down_b, down_o, acc, acc_dn,
    dm_in, bp_in, en_in, dmat, ends_src, c_src, c_in, fmd_src, fmd_in, cs_src, dcond, ph, ph_in, news_src,
    sq_src, sq_rows, cross_src,
    load_sem, x_send, x_recv, up_send, up_recv, down_send, down_recv,
    sib_send, sib_recv, y_send, y_recv, group_send, group_recv, sect_send, sect_recv,
    ph_send, ph_recv, news_send, news_recv, sq_send, sq_recv, cross_sem, local_sem,
):
    me = lax.axis_index("dp")
    section = lax.axis_index("section")
    z, x = me // X, lax.rem(me, X)
    core = lax.rem(section, 2)
    low, sibling, facing = section - core, section + 1 - 2 * core, lax.rem(section + 2, 4)
    across = me + 1 - 2 * x
    sources = (g_dn, g_up, g_attn)
    chunks = len(SUM_CHUNKS)
    has_up, has_down = z < Z - 1, z > 0
    devices, group = Z * X * 4, Z * X * 2
    me_all, me_group = me * 4 + section, me * 2 + core
    in_all = lambda p: {"dp": p // 4, "section": lax.rem(p, 4)}
    in_group = lambda p: {"dp": p // 2, "section": low + lax.rem(p, 2)}
    in_section = lambda p: {"section": p}
    in_dp = lambda p: {"dp": p}
    f32 = jnp.float32

    barrier = pltpu.get_barrier_semaphore()

    @pl.loop(1, devices)
    def _(step):
        pl.semaphore_signal(
            barrier, 1, device_id=in_all(lax.rem(me_all + step, devices)), device_id_type=MESH
        )

    def small(src_of, dst, send, recv, where, size, index):
        def copy(step, p, slot):
            return pltpu.make_async_remote_copy(
                src_ref=src_of(p), dst_ref=dst.at[slot], send_sem=send.at[step], recv_sem=recv.at[step],
                device_id=where(p), device_id_type=MESH,
            )
        return (copy, size, index, src_of, dst)

    gradients = [
        small(lambda p: dm_ref.at[lax.rem(p, 2)], dm_in, group_send.at[0], group_recv.at[0], in_group, group, me_group),
        small(lambda p: bp_ref.at[p], bp_in, group_send.at[1], group_recv.at[1], in_group, group, me_group),
        small(lambda p: en_ref.at[p // 2], en_in, group_send.at[2], group_recv.at[2], in_group, group, me_group),
    ]
    conds = [
        small(lambda p, src=src: src, dst, sect_send.at[k], sect_recv.at[k], in_section, 4, section)
        for k, (src, dst) in enumerate(
            ((c_src, c_in), (ends_src, ends_all), (fmd_src, fmd_in), (cs_src, cs_all))
        )
    ]
    hiddens = [small(lambda p: ph.at[p], ph_in, ph_send, ph_recv, in_dp, Z * X, me)]
    news = [small(lambda p: news_src, news_out, news_send, news_recv, in_all, devices, me_all)]
    norms = [small(lambda p: sq_src, sq_all, sq_send, sq_recv, in_all, devices, me_all)]

    def own_copies(batch, first):
        return [
            pltpu.make_async_copy(src_of(index), dst.at[index], local_sem.at[first + k])
            for k, (copy, size, index, src_of, dst) in enumerate(batch)
        ]

    def send_batch(batch, first):
        for copy in own_copies(batch, first):
            copy.start()
        for copy, size, index, src_of, dst in batch:
            @pl.loop(1, size)
            def _(step):
                copy(step, lax.rem(index + step, size), index).start()

    def wait_batch(batch, first):
        for copy in own_copies(batch, first):
            copy.wait()
        for copy, size, index, src_of, dst in batch:
            @pl.loop(1, size)
            def _(step):
                p = lax.rem(index + size - step, size)
                copy(step, p, p).wait_recv()
                copy(step, p, p).wait_send()

    def add_square(value):
        sq_src[...] += jnp.sum(value * value)

    def images_of():
        cond = cond_ref[...]
        cond_low = to_half(cond).astype(f32)
        return jnp.where(section == 0, cond, cond_low), cond_low

    def make_cond():
        wait_batch(gradients, 0)
        flat = dm_in[...].reshape(group * 48, 128)
        row = lax.broadcasted_iota(jnp.int32, (group, group * 48), 0) * 48
        column = lax.broadcasted_iota(jnp.int32, (group, group * 48), 1)
        for k in range(5 * D // 128):
            chosen = jnp.where(column == row + k, 1.0, 0.0).astype(BF)
            dmat[:, 128 * k : 128 * (k + 1)] = to_half(matmul(chosen, flat))
        news_src[...] = jnp.zeros_like(news_src)
        news_src[0:SUM_ROWS] = jnp.sum(bp_in[...], axis=0)
        ends_src[...] = jnp.sum(en_in[...], axis=0)
        own_cond, cond_low = images_of()
        d_mod, d_fm = dmat[:, : 3 * D], dmat[:, 3 * D :]
        fmd_src[...] = d_fm
        cs_src[...] = jnp.sum(d_mod.astype(f32), axis=0, keepdims=True)
        d_silu = matmul_nt(d_mod, mod_ref[...])
        d_silu = d_silu + (section == 3).astype(f32) * matmul_nt(d_fm, fm_ref[...])
        c_src[...] = jnp.zeros_like(c_src)
        c_src[:, :144] = silu_slope(own_cond) * d_silu
        send_batch(conds, 3)
        silu_own = to_half(jax.nn.silu(own_cond))
        for k in range(3):
            part_g = matmul_tn(silu_own, dmat[:, D * k : D * (k + 1)])
            gmod_out[:, D * k : D * (k + 1)] = part_g
            add_square(part_g)

    once = (section == 0).astype(f32)

    def make_hidden():
        wait_batch(conds, 3)
        total = to_half(c_in[3])
        for slot in (2, 1, 0):
            total = to_half(total.astype(f32) + c_in[slot])
        dcond[...] = total
        d_cond = dcond[:, :144]
        for index in range(Z * X):
            ph[index] = matmul(d_cond, two_ref[index])
        send_batch(hiddens, 7)
        own_cond, cond_low = images_of()
        silu_low = to_half(jax.nn.silu(cond_low))
        for k in range(2):
            part_g = matmul_tn(silu_low, fmd_in[3, :, D * k : D * (k + 1)])
            gfm_out[:, D * k : D * (k + 1)] = part_g
            add_square(jnp.sqrt(once) * part_g)
        fmsum_out[...] = jnp.sum(fmd_in[3].astype(f32), axis=0, keepdims=True)
        part_g = matmul_tn(d_cond, one_hot(meta_ref[:, FREQ : FREQ + 1], gtab_out.shape[1]))
        gtab_out[...] = part_g
        add_square(once * part_g)
        for index in range(Z * X):
            part_g = matmul_tn(d_cond, hid_ref[index])
            gtwo_out[index] = part_g
            add_square(once * part_g)

    def make_news():
        wait_batch(hiddens, 7)
        total = ph_in[0]
        for index in range(1, Z * X):
            total = total + ph_in[index]
        d_pre = to_half(silu_slope(pre_ref[...]) * total)
        part_g = matmul_tn(d_pre, to_half(meta_ref[:, :FREQ]))
        gone_out[...] = part_g
        add_square(once * part_g)
        sums = jnp.sum(d_pre.astype(f32), axis=0, keepdims=True)
        sums_cond = jnp.sum(dcond[...].astype(f32), axis=0, keepdims=True)
        for k in range(2):
            news_src[SUM_ROWS + k : SUM_ROWS + k + 1] = sums[:, 128 * k : 128 * (k + 1)]
            news_src[SUM_ROWS + 2 + k : SUM_ROWS + 3 + k] = sums_cond[:, 128 * k : 128 * (k + 1)]
        send_batch(news, 8)
        first = (me == 0).astype(f32)
        add_square(news_src[0:10])
        add_square(once * sums)
        add_square(once * sums_cond)
        add_square(first * cs_src[...])
        add_square(first * once * fmsum_out[...])
        add_square(once * ends_all[0])
        add_square(once * ends_all[3])

    def dn_copy(k, slot, to_sib):
        rows = pl.ds(SUM_CHUNKS[k][1], SUM_CHUNKS[k][2])
        unit = slot * chunks + k
        return pltpu.make_async_remote_copy(
            src_ref=dn_out.at[slot, rows], dst_ref=dn_out.at[slot, rows],
            send_sem=(sib_send if to_sib else y_send).at[unit],
            recv_sem=(sib_recv if to_sib else y_recv).at[unit],
            device_id={"section": sibling if to_sib else facing},
            device_id_type=MESH,
        )

    def each(distance, run):
        if distance == 0:
            run(z, None)
            return

        @pl.when(z + distance < Z)
        def _():
            run(z + distance, True)

        @pl.when(z >= distance)
        def _():
            run(z - distance, False)

    def part(k):
        return pl.ds(SUM_CHUNKS[k][1], SUM_CHUNKS[k][2])

    def hbm(k, zz, column):
        start = pl.multiple_of((zz * X + column) * 144 + SUM_CHUNKS[k][1], 16)
        return sources[SUM_CHUNKS[k][0]].at[pl.ds(start, SUM_CHUNKS[k][2])]

    def own(k, zz):
        return own_b.at[SUM_CHUNKS[k][0], zz, part(k)]

    def from_x(k, zz):
        return xq.at[SUM_CHUNKS[k][0]] if SUM_CHUNKS[k][3] else xb.at[SUM_CHUNKS[k][0], zz, part(k)]

    def from_z(k, zz, up, other):
        if other:
            return (up_o if up else down_o).at[SUM_CHUNKS[k][0], zz]
        return (up_b if up else down_b).at[SUM_CHUNKS[k][0], zz, part(k)]

    def other_of(k, zz):
        return other_d.at[SUM_CHUNKS[k][0], zz]

    def load(k, zz, other=False):
        index = ((chunks if other else 0) + k) * Z + zz
        return pltpu.make_async_copy(
            hbm(k, zz, (1 - x) if other else x),
            other_of(k, zz) if other else own(k, zz),
            load_sem.at[index],
        )

    def x_copy(k, zz, src):
        unit = k * Z + zz
        return pltpu.make_async_remote_copy(
            src_ref=src, dst_ref=from_x(k, zz), send_sem=x_send.at[unit], recv_sem=x_recv.at[unit],
            device_id={"dp": across}, device_id_type=MESH,
        )

    def z_copy(k, zz, up, other):
        unit = ((chunks if other else 0) + k) * Z + zz
        return pltpu.make_async_remote_copy(
            src_ref=other_of(k, zz) if other else own(k, zz),
            dst_ref=from_z(k, zz, up, other),
            send_sem=(up_send if up else down_send).at[unit],
            recv_sem=(up_recv if up else down_recv).at[unit],
            device_id={"dp": me + X if up else me - X},
            device_id_type=MESH,
        )

    def total(k, dst, srcs):
        @pl.loop(0, SUM_CHUNKS[k][2] // 16)
        def _(step):
            rows = pl.ds(pl.multiple_of(step * 16, 16), 16)
            value = srcs[0][rows].astype(jnp.float32)
            for src in srcs[1:]:
                value = value + src[rows].astype(jnp.float32)
            dst[rows] = value.astype(dst.dtype)

    for distance in (3, 2, 1, 0):
        for k in range(chunks):
            def run(zz, up):
                load(k, zz).start()
                if SUM_CHUNKS[k][3]:
                    load(k, zz, True).start()
            each(distance, run)

    sq_src[...] = jnp.zeros_like(sq_src)
    sq_rows[...] = jnp.zeros_like(sq_rows)
    pl.semaphore_wait(barrier, devices - 1)
    send_batch(gradients, 0)

    order = [
        (k, distance) for which, distance in ((0, 3), (0, 2), (0, 1), (1, 3), (0, 0), (1, 2), (1, 1), (2, 3), (1, 0), (2, 2), (2, 1), (2, 0))
        for k in range(chunks) if SUM_CHUNKS[k][0] == which and not SUM_CHUNKS[k][3]
    ]
    sent = []

    def send_x(until):
        while len(sent) < min(until, len(order)):
            k, distance = order[len(sent)]
            sent.append(1)
            each(distance, lambda zz, up: x_copy(k, zz, hbm(k, zz, 1 - x)).start())

    def after(k, distance):
        if not SUM_CHUNKS[k][3]:
            send_x(order.index((k, distance)) + 1 + 6)

    send_x(6)

    def pass_on(k, distance):
        def run(zz, up):
            behind = has_down if up else has_up
            if SUM_CHUNKS[k][3]:
                for other in (False, True):
                    mine = other_of(k, zz) if other else own(k, zz)
                    load(k, zz, other).wait()

                    @pl.when(behind)
                    def _():
                        z_copy(k, zz, up, other).wait_recv()
                        total(k, mine, [mine, from_z(k, zz, up, other)])

                    z_copy(k, zz, up, other).start()
                return
            load(k, zz).wait()
            x_copy(k, zz, hbm(k, zz, 1 - x)).wait_recv()

            @pl.when(behind)
            def _():
                z_copy(k, zz, up, False).wait_recv()
                total(k, own(k, zz), [own(k, zz), from_x(k, zz), from_z(k, zz, up, False)])

            @pl.when(jnp.logical_not(behind))
            def _():
                total(k, own(k, zz), [own(k, zz), from_x(k, zz)])

            z_copy(k, zz, up, False).start()
        each(distance, run)

    def add_z(dst, k, other):
        @pl.when(has_down)
        def _():
            z_copy(k, z, True, other).wait_recv()
            total(k, dst, [dst, from_z(k, z, True, other)])

        @pl.when(has_up)
        def _():
            z_copy(k, z, False, other).wait_recv()
            total(k, dst, [dst, from_z(k, z, False, other)])

    def send_direct(k):
        load(k, z, True).wait()
        total(k, acc, [other_of(k, z)])
        add_z(acc, k, True)
        total(k, other_of(k, z), [acc])
        x_copy(k, z, other_of(k, z)).start()

    def finish(k):
        which, rows = SUM_CHUNKS[k][0], SUM_CHUNKS[k][2]
        dst = out.at[which - 1, part(k)] if which else acc_dn.at[pl.ds(0, rows)]
        load(k, z).wait()
        if SUM_CHUNKS[k][3]:
            total(k, dst, [own(k, z)])
            add_z(dst, k, False)
            x_copy(k, z, other_of(k, z)).wait_recv()
            total(k, dst, [dst, from_x(k, z)])
        else:
            x_copy(k, z, hbm(k, z, 1 - x)).wait_recv()
            total(k, dst, [own(k, z), from_x(k, z)])
            add_z(dst, k, False)
        if not which:
            total(k, dn_out.at[section, part(k)], [dst])
            dn_copy(k, section, True).start()
            dn_copy(k, section, False).start()

        @pl.loop(0, rows // 16)
        def _(step):
            value = dst[pl.ds(pl.multiple_of(step * 16, 16), 16)]
            sq_rows[...] += jnp.sum(value * value, axis=0, keepdims=True)

    def of(which, direct=None):
        return [
            k for k in range(chunks)
            if SUM_CHUNKS[k][0] == which and (direct is None or SUM_CHUNKS[k][3] == direct)
        ]

    def pass_all(which, distance):
        for k in of(which):
            pass_on(k, distance)
            after(k, distance)

    def finish_all(which):
        for k in of(which, False) + of(which, True):
            finish(k)
            after(k, 0)

    def direct_all(which):
        for k in of(which, True):
            send_direct(k)

    for distance in (3, 2, 1):
        pass_all(0, distance)
    make_cond()
    pass_all(1, 3)
    direct_all(0)
    finish_all(0)
    pass_all(1, 2)
    make_hidden()
    pass_all(1, 1)
    for k in of(0):
        dn_copy(k, facing, False).wait_recv()
        dn_copy(k, facing, True).start()
    pass_all(2, 3)
    make_news()
    direct_all(1)
    finish_all(1)
    pass_all(2, 2)
    pass_all(2, 1)
    direct_all(2)
    finish_all(2)

    @pl.loop(0, 144 // 16)
    def _(step):
        rows = pl.ds(pl.multiple_of(step * 16, 16), 16)
        cross_src[rows] = to_half(jnp.where(core == 0, out[0, rows], out[1, rows]))

    crossing = pltpu.make_async_remote_copy(
        src_ref=cross_src, dst_ref=cross_out, send_sem=cross_sem.at[0], recv_sem=cross_sem.at[1],
        device_id={"section": sibling}, device_id_type=MESH,
    )
    sq_src[...] += jnp.sum(sq_rows[...])
    send_batch(norms, 9)
    crossing.start()
    wait_batch(norms, 9)
    wait_batch(news, 8)
    crossing.wait()

    for k in range(chunks):
        for distance in (3, 2, 1, 0):
            def run(zz, up):
                if not SUM_CHUNKS[k][3]:
                    x_copy(k, zz, hbm(k, zz, 1 - x)).wait_send()
                elif distance == 0:
                    x_copy(k, zz, other_of(k, zz)).wait_send()
                if distance:
                    z_copy(k, zz, up, False).wait_send()
                    if SUM_CHUNKS[k][3]:
                        z_copy(k, zz, up, True).wait_send()
            each(distance, run)
        if not SUM_CHUNKS[k][0]:
            dn_copy(k, section, True).wait_send()
            dn_copy(k, section, False).wait_send()
            dn_copy(k, facing, True).wait_send()
            dn_copy(k, sibling, True).wait_recv()
            dn_copy(k, lax.rem(sibling + 2, 4), True).wait_recv()


def sum_gradients(g_dn, g_up, g_attn, d_mods, sums, ends, w_mod, w_fm, two_blocks, cond, pre, hidden, meta):
    n, width = lax.axis_size("dp"), cond.shape[1]
    f32 = jnp.float32
    if not ring_fits(n, width):
        return sum_plainly(g_dn, g_up, g_attn, d_mods, sums, ends, w_mod, w_fm, two_blocks, cond, pre, hidden, meta)
    chunks, images, devices = len(SUM_CHUNKS), 2 * n, 4 * n
    dma = lambda *count: pltpu.SemaphoreType.DMA(count)
    ring = pltpu.VMEM((3, Z, 144, HALF), BF)
    short = [rows for start, rows, direct in CHUNKS if direct][0]
    most = max(rows for start, rows, direct in CHUNKS)
    ring_o = pltpu.VMEM((3, Z, short, HALF), BF)
    hbm, vmem = pl.BlockSpec(memory_space=pl.ANY), pl.BlockSpec(memory_space=pltpu.VMEM)
    like = jax.ShapeDtypeStruct
    end_block = ends.shape[1:]
    shapes = (
        like((2, 144, HALF), f32), like((144, HALF), BF), like((4, 144, HALF), BF),
        like((144, 3 * D), f32), like((144, 2 * D), f32), like((144, 1024), f32), like((WIDE, FREQ), f32),
        like((n, 144, WIDE), f32), like((4,) + end_block, f32), like((devices, 24, 128), f32),
        like((4, 1, 3 * D), f32), like((1, 2 * D), f32), like((devices, 8, 128), f32),
    )
    return pl.pallas_call(
        sum_kernel,
        out_shape=shapes,
        in_specs=[hbm] * 3 + [vmem] * 10,
        out_specs=(vmem,) * len(shapes),
        scratch_shapes=[
            ring, ring_o, ring, pltpu.VMEM((3, short, HALF), BF),
            ring, ring_o, ring, ring_o, pltpu.VMEM((short, HALF), f32), pltpu.VMEM((most, HALF), f32),
            pltpu.VMEM((images, 48, 128), BF), pltpu.VMEM((images, SUM_ROWS, 128), f32),
            pltpu.VMEM((images,) + end_block, f32), pltpu.VMEM((images, 5 * D), BF),
            pltpu.VMEM(end_block, f32), pltpu.VMEM((images, WIDE), f32), pltpu.VMEM((4, images, WIDE), f32),
            pltpu.VMEM((images, 2 * D), BF), pltpu.VMEM((4, images, 2 * D), BF), pltpu.VMEM((1, 3 * D), f32),
            pltpu.VMEM((images, WIDE), BF), pltpu.VMEM((n, images, WIDE), f32), pltpu.VMEM((n, images, WIDE), f32),
            pltpu.VMEM((24, 128), f32), pltpu.VMEM((8, 128), f32), pltpu.VMEM((1, HALF), f32),
            pltpu.VMEM((144, HALF), BF),
            dma(2 * chunks * Z), dma(chunks * Z), dma(chunks * Z),
            dma(2 * chunks * Z), dma(2 * chunks * Z), dma(2 * chunks * Z), dma(2 * chunks * Z),
            dma(4 * chunks), dma(4 * chunks), dma(4 * chunks), dma(4 * chunks),
            dma(3, images), dma(3, images), dma(4, 4), dma(4, 4),
            dma(n), dma(n), dma(devices), dma(devices), dma(devices), dma(devices), dma(2), dma(10),
        ],
        compiler_params=pltpu.CompilerParams(
            collective_id=1, has_side_effects=True, vmem_limit_bytes=VMEM_BYTES
        ),
        cost_estimate=pl.CostEstimate(flops=0, bytes_accessed=400_000_000, transcendentals=0),
        name="sum_gradients",
    )(g_dn, g_up, g_attn, d_mods, sums, ends, w_mod, w_fm, two_blocks, cond, pre, hidden, meta)


def sum_plainly(g_dn, g_up, g_attn, d_mods, sums, ends, w_mod, w_fm, two_blocks, cond, pre, hidden, meta):
    n, width = lax.axis_size("dp"), cond.shape[1]
    section, images, f32 = lax.axis_index("section"), 2 * n, jnp.float32
    once = (section == 0).astype(f32)
    anchor = (lax.axis_index("dp") == 0).astype(f32)
    total = lambda grad: lax.psum_scatter(grad, "dp", scatter_dimension=0, tiled=True)
    dn_own, out = total(g_dn), jnp.stack([total(g_up), total(g_attn)]).astype(f32)
    dn_all = lax.all_gather(dn_own, "section")
    cross = swap(to_half(jnp.where(lax.rem(section, 2) == 0, out[0], out[1])), 1)
    d_mods, sums, ends = exchange(4, "stage", ("core", "each", "dp"), d_mods, sums, ends)
    d_mods = d_mods.reshape(images, 48 * 128)
    d_mod, d_fm = d_mods[:, : 3 * D], d_mods[:, 3 * D : 5 * D]
    sums, ends = jnp.sum(sums, axis=0), jnp.sum(ends, axis=0)
    cond_low = to_half(cond).astype(f32)
    own_cond = jnp.where(section == 0, cond, cond_low)
    d_silu = matmul_nt(d_mod, w_mod) + (section == 3).astype(f32) * matmul_nt(d_fm, w_fm)
    c_own = jnp.pad(silu_slope(own_cond) * d_silu, ((0, 0), (0, WIDE - width)))
    cs = column_sums(d_mod)[None]
    c_all, ends_all, d_fm, cs_all = exchange(5, "section", ("all",) * 4, c_own, ends, d_fm, cs)
    d_fm = d_fm[3]
    d_cond = to_half(c_all[3])
    for slot in (2, 1, 0):
        d_cond = to_half(d_cond.astype(f32) + c_all[slot])
    narrow = d_cond[:, :width]
    part = jnp.einsum("iw,jwk->jik", narrow, two_blocks, preferred_element_type=f32)
    (part,) = exchange(6, "dp", ("each",), part)
    d_pre = to_half(silu_slope(pre) * jnp.sum(part, axis=0))
    g_mod = matmul_tn(to_half(jax.nn.silu(own_cond)), d_mod)
    g_fm = matmul_tn(to_half(jax.nn.silu(cond_low)), d_fm)
    g_table = matmul_tn(narrow, one_hot(meta[:, FREQ : FREQ + 1], 1024))
    g_one = matmul_tn(d_pre, to_half(meta[:, :FREQ]))
    g_two = jnp.einsum("iw,jik->jwk", narrow, hidden, preferred_element_type=f32)
    fm_sum = column_sums(d_fm)[None]
    slices = [column_sums(value).reshape(2, 128) for value in (d_pre, d_cond)]
    news = jnp.concatenate([sums, *slices, jnp.zeros((4, 128), f32)])
    square = lambda value: jnp.sum(value * value)
    squares = square(out) + square(dn_own.astype(f32)) + square(g_mod) + square(sums[:10])
    squares = squares + anchor * square(cs) + anchor * once * square(fm_sum)
    for value in (g_fm, g_table, g_one, g_two, ends_all[0], ends_all[3], *slices):
        squares = squares + once * square(value)
    news, squares = exchange(7, "every", ("all", "all"), news, jnp.broadcast_to(squares, (8, 128)))
    return (out, cross, dn_all, g_mod, g_fm, g_table, g_one, g_two, ends_all, news, cs_all, fm_sum, squares)


def exchange_kernel(axes, modes, *refs):
    count = len(modes)
    ins, outs = refs[:count], refs[count : 2 * count]
    send_sem, recv_sem, own_sem = refs[2 * count :]
    dp, section = lax.axis_index("dp"), lax.axis_index("section")
    n, sections = lax.axis_size("dp"), lax.axis_size("section")
    if axes == "dp":
        size, me, where = n, dp, lambda p: {"dp": p}
    elif axes == "section":
        size, me, where = sections, section, lambda p: {"section": p}
    elif axes == "stage":
        low = section - lax.rem(section, 2)
        size, me = 2 * n, dp * 2 + lax.rem(section, 2)
        where = lambda p: {"dp": p // 2, "section": low + lax.rem(p, 2)}
    else:
        size, me = n * sections, dp * sections + section
        where = lambda p: {"dp": p // sections, "section": lax.rem(p, sections)}

    def part(k, p):
        if modes[k] == "all":
            return ins[k]
        index = {"each": p, "dp": p // 2, "core": lax.rem(p, 2)}[modes[k]]
        return ins[k].at[index]

    def copy(k, step, src, slot, p):
        return pltpu.make_async_remote_copy(
            src_ref=src, dst_ref=outs[k].at[slot],
            send_sem=send_sem.at[k, step], recv_sem=recv_sem.at[k, step],
            device_id=where(p), device_id_type=MESH,
        )

    barrier = pltpu.get_barrier_semaphore()

    @pl.loop(1, size)
    def _(step):
        pl.semaphore_signal(barrier, 1, device_id=where(lax.rem(me + step, size)), device_id_type=MESH)

    for k in range(count):
        pltpu.make_async_copy(part(k, me), outs[k].at[me], own_sem.at[k]).start()
    pl.semaphore_wait(barrier, size - 1)

    @pl.loop(1, size)
    def _(step):
        p = lax.rem(me + step, size)
        for k in range(count):
            copy(k, step, part(k, p), me, p).start()

    for k in range(count):
        pltpu.make_async_copy(part(k, me), outs[k].at[me], own_sem.at[k]).wait()

    @pl.loop(1, size)
    def _(step):
        p = lax.rem(me + size - step, size)
        for k in range(count):
            copy(k, step, part(k, p), p, p).wait_recv()
            copy(k, step, part(k, p), p, p).wait_send()


def exchange(ident, axes, modes, *arrays):
    n, sections = lax.axis_size("dp"), lax.axis_size("section")
    size = {"dp": n, "section": sections, "stage": 2 * n, "every": n * sections}[axes]
    blocks = [a.shape if mode == "all" else a.shape[1:] for a, mode in zip(arrays, modes)]
    count = len(arrays)
    vmem = pl.BlockSpec(memory_space=pltpu.VMEM)
    return pl.pallas_call(
        partial(exchange_kernel, axes, modes),
        out_shape=tuple(jax.ShapeDtypeStruct((size,) + b, a.dtype) for a, b in zip(arrays, blocks)),
        in_specs=[vmem] * count,
        out_specs=(vmem,) * count,
        scratch_shapes=[
            pltpu.SemaphoreType.DMA((count, size)),
            pltpu.SemaphoreType.DMA((count, size)),
            pltpu.SemaphoreType.DMA((count,)),
        ],
        compiler_params=pltpu.CompilerParams(
            collective_id=ident, has_side_effects=True, vmem_limit_bytes=VMEM_BYTES
        ),
        cost_estimate=pl.CostEstimate(flops=0, bytes_accessed=30_000_000, transcendentals=0),
        name="exchange_" + axes,
    )(*arrays)


def rows_of(value, size):
    value = value.reshape(-1)
    return jnp.pad(value, (0, size * 128 - value.shape[0])).reshape(size, 128)


def row_count(length, unit=8):
    return -(-length // (128 * unit)) * unit


TILE = 768
STEPS = HALF // TILE
GELU_SCALE = math.sqrt(2.0 / math.pi)
SCALE = HEAD_DIM ** (-0.5)


def mean_rows(value):
    return jnp.mean(value, axis=-1, keepdims=True)


def normalized(x):
    centered = x - mean_rows(x)
    inverse = lax.rsqrt(mean_rows(centered * centered) + epsilon_norm)
    return (centered * inverse, inverse)


def modulated_back(normed, inverse, scale, d_xm):
    d_normed = d_xm * (1.0 + scale)
    d_x = inverse * (d_normed - mean_rows(d_normed) - normed * mean_rows(d_normed * normed))
    return (d_x, jnp.sum(d_xm, axis=0), jnp.sum(d_xm * normed, axis=0))


def window(head):
    low = HEAD_DIM * head // 128 * 128
    high = -(-HEAD_DIM * (head + 1) // 128) * 128
    lane = lax.broadcasted_iota(jnp.int32, (PATCHES, high - low), 1) + low
    return slice(low, high), (lane >= HEAD_DIM * head) & (lane < HEAD_DIM * (head + 1))


def own_lanes(mask, value):
    return jnp.where(mask, value, jnp.zeros_like(value))


def softmax_rows(scores):
    shifted = jnp.exp(scores - jnp.max(scores, axis=-1, keepdims=True))
    return shifted / jnp.sum(shifted, axis=-1, keepdims=True)


def half_of(ref, which, side):
    return ref.at[which, :, pl.ds(pl.multiple_of(side * HALF, 128) if which else side * HALF, HALF)]


def weight_copies(sources, targets, sem):
    return [pltpu.make_async_copy(src, dst, sem.at[k]) for k, (src, dst) in enumerate(zip(sources, targets))]


def forward_kernel(
    save, flags, x_ref, mod_a, mod_m, b_attn, b_up, b_down, w_blk, w_dn, out_ref, *refs
):
    if save:
        xm_ref, qkv_ref, att_ref, branch_a_ref, mid_ref, xm2_ref, branch_m_ref, pre_ref, act_ref = refs[:9]
        wa, wu, wd, acc, sem = refs[9:]
    else:
        xm_ref, qkv_ref, att_ref, mid_ref, xm2_ref, wa, wu, wd, acc, sem = refs
    copies = weight_copies(
        [half_of(w_blk, 0, 0), half_of(w_blk, 0, 1)]
        + [ref for side in (flags[0], 1 - flags[0]) for ref in (half_of(w_blk, 1, side), w_dn.at[side])],
        (wa.at[0], wa.at[1], wu.at[0], wd.at[0], wu.at[1], wd.at[1]),
        sem,
    )
    for copy in copies:
        copy.start()
    normed, unused = normalized(x_ref[...])
    xm_ref[...] = to_half(normed * (1.0 + mod_a[1:2]) + mod_a[0:1])
    acc[...] = jnp.zeros_like(acc)
    for k in range(3):
        if k != 1:
            copies[k // 2].wait()
        half, first = (0, D * k) if k < 2 else (1, 0)
        part = slice(D * k, D * (k + 1))
        qkv_ref[:, part] = to_half(
            matmul(xm_ref[...], wa[half, :, first : first + D]) + b_attn[:, part]
        )
    for head in range(HEADS):
        lanes, mask = window(head)
        at = lambda k: slice(D * k + lanes.start, D * k + lanes.stop)
        query = own_lanes(mask, qkv_ref[:, at(0)])
        probs = softmax_rows(matmul_nt(query, qkv_ref[:, at(1)]) * SCALE)
        acc[:, lanes] += own_lanes(mask, matmul(to_half(probs), qkv_ref[:, at(2)]))
    att_ref[...] = to_half(acc[...])
    branch = matmul(att_ref[...], wa[1, :, D:]) + b_attn[:, 3 * D :]
    if save:
        branch_a_ref[...] = branch
    mid_ref[...] = to_half(x_ref[...] + mod_a[2:3] * branch).astype(jnp.float32)
    normed, unused = normalized(mid_ref[...])
    xm2_ref[...] = to_half(normed * (1.0 + mod_m[1:2]) + mod_m[0:1])
    acc[...] = jnp.broadcast_to(b_down[...], acc.shape)
    for half in range(2):
        copies[2 + 2 * half].wait()
        copies[3 + 2 * half].wait()
        for step in range(STEPS):
            own = slice(TILE * step, TILE * (step + 1))
            part = slice(HALF * half + TILE * step, HALF * half + TILE * (step + 1))
            pre = matmul(xm2_ref[...], wu[half, :, own]) + b_up[:, part]
            cube = pre + 0.044715 * (pre * pre * pre)
            act = to_half(pre * (0.5 * (1.0 + jnp.tanh(GELU_SCALE * cube))))
            if save:
                pre_ref[:, part] = pre
                act_ref[:, part] = act
            acc[...] += matmul_nt(act, wd[half, :, own])
    if save:
        branch_m_ref[...] = acc[...]
    out = mid_ref[...] + mod_m[2:3] * acc[...]
    out_ref[...] = out.astype(out_ref.dtype)


def backward_kernel(
    flags, d_ref, x_ref, mid_ref, mod_a, mod_m, branch_a, branch_m, qkv_ref, pre_hbm, w_blk, w_dn,
    d_in_ref, d_mod_a, d_mod_m, grad_a, grad_m, d_pre_ref, d_qkv_ref,
    wa, wu, wd, pre_ref, acc, d_acc, d_att, sem,
):
    copies = weight_copies(
        (
            w_dn.at[flags[0]], pre_hbm, half_of(w_blk, 1, flags[0]),
            w_dn.at[1 - flags[0]], half_of(w_blk, 1, 1 - flags[0]),
            half_of(w_blk, 0, 1), half_of(w_blk, 0, 0),
        ),
        (wd.at[0], pre_ref, wu.at[0], wd.at[1], wu.at[1], wa.at[1], wa.at[0]),
        sem,
    )
    for copy in copies:
        copy.start()
    grad_m[...] = to_half(d_ref[...] * mod_m[2:3])
    d_mod_m[2:3] = jnp.sum(d_ref[...] * branch_m[...], axis=0)[None]
    acc[...] = jnp.zeros_like(acc)
    for half in range(2):
        copies[0 if half == 0 else 3].wait()
        if half == 0:
            copies[1].wait()
        copies[2 if half == 0 else 4].wait()
        for step in range(STEPS):
            own = slice(TILE * step, TILE * (step + 1))
            part = slice(HALF * half + TILE * step, HALF * half + TILE * (step + 1))
            d_act = matmul(grad_m[...], wd[half, :, own])
            pre = pre_ref[:, part]
            square = pre * pre
            tanh = jnp.tanh(GELU_SCALE * (pre + 0.044715 * (square * pre)))
            slope = 0.5 * (1.0 + tanh) + (0.5 * pre) * (1.0 - tanh * tanh) * (
                GELU_SCALE * (1.0 + (3.0 * 0.044715) * square)
            )
            d_pre = to_half(d_act * slope)
            d_pre_ref[:, part] = d_pre
            acc[...] += matmul_nt(d_pre, wu[half, :, own])
    normed, inverse = normalized(mid_ref[...])
    d_x, d_shift, d_scale = modulated_back(normed, inverse, mod_m[1:2], acc[...])
    d_mod_m[0:1] = d_shift[None]
    d_mod_m[1:2] = d_scale[None]
    acc[...] = to_half(d_ref[...] + d_x).astype(jnp.float32)

    d_mod_a[2:3] = jnp.sum(acc[...] * branch_a[...], axis=0)[None]
    grad_a[...] = to_half(acc[...] * mod_a[2:3])
    copies[5].wait()
    d_att[...] = to_half(matmul_nt(grad_a[...], wa[1, :, D:]))
    d_acc[...] = jnp.zeros_like(d_acc)
    for head in range(HEADS):
        lanes, mask = window(head)
        at = lambda k: slice(D * k + lanes.start, D * k + lanes.stop)
        query, key, value = (qkv_ref[:, at(k)] for k in range(3))
        probs = softmax_rows(matmul_nt(own_lanes(mask, query), key) * SCALE)
        outer = d_att[:, lanes]
        d_acc[:, at(2)] += own_lanes(mask, matmul_tn(to_half(probs), outer))
        d_probs = matmul_nt(own_lanes(mask, outer), value)
        d_scores = to_half(probs * (d_probs - jnp.sum(probs * d_probs, axis=-1, keepdims=True)))
        d_acc[:, at(0)] += own_lanes(mask, matmul(d_scores, key) * SCALE)
        d_acc[:, at(1)] += own_lanes(mask, matmul_tn(d_scores, query) * SCALE)
    d_qkv_ref[...] = to_half(d_acc[...])
    copies[6].wait()
    d_xm = matmul_nt(d_qkv_ref[:, 2 * D :], wa[1, :, :D]) + matmul_nt(d_qkv_ref[:, : 2 * D], wa[0])
    normed, inverse = normalized(x_ref[...])
    d_x, d_shift, d_scale = modulated_back(normed, inverse, mod_a[1:2], d_xm)
    d_mod_a[0:1] = d_shift[None]
    d_mod_a[1:2] = d_scale[None]
    d_in_ref[...] = to_half(acc[...] + d_x)


def weight_scratch():
    return [pltpu.VMEM((2, D, HALF), BF)] * 3


def stage_cost():
    flops = 2 * PATCHES * D * 12 * D + 4 * PATCHES * PATCHES * D
    return pl.CostEstimate(flops=2 * flops, bytes_accessed=24 * D * D, transcendentals=2 * PATCHES * FF)


def stage_forward(save, x_in, weights):
    flags, mod_a, mod_m, w_blk, w_dn, b_attn, b_up, b_down = weights
    vmem, hbm = pl.BlockSpec(memory_space=pltpu.VMEM), pl.BlockSpec(memory_space=pl.ANY)
    smem = pl.BlockSpec(memory_space=pltpu.SMEM)
    like = lambda columns, kind: jax.ShapeDtypeStruct((PATCHES, columns), kind)
    tokens, wide = pltpu.VMEM((PATCHES, D), BF), pltpu.VMEM((PATCHES, 3 * D), BF)
    total = pltpu.VMEM((PATCHES, D), jnp.float32)
    f32 = jnp.float32
    if save:
        shapes = [like(D, f32), like(D, BF), like(3 * D, BF), like(D, BF), like(D, f32), like(D, f32)]
        shapes += [like(D, BF), like(D, f32), like(FF, f32), like(FF, BF)]
        scratch = []
    else:
        shapes, scratch = [like(D, BF)], [tokens, wide, tokens, total, tokens]
    return pl.pallas_call(
        partial(forward_kernel, save),
        out_shape=tuple(shapes),
        in_specs=[smem] + [vmem] * 6 + [hbm] * 2,
        out_specs=(vmem,) * len(shapes),
        scratch_shapes=scratch + weight_scratch() + [total, pltpu.SemaphoreType.DMA((6,))],
        compiler_params=pltpu.CompilerParams(vmem_limit_bytes=VMEM_BYTES),
        cost_estimate=stage_cost(),
        name="stage_forward",
    )(flags, x_in, mod_a, mod_m, b_attn, b_up, b_down, w_blk, w_dn)


def stage_backward(d_out, x_in, weights, kept):
    flags, mod_a, mod_m, w_blk, w_dn, b_attn, b_up, b_down = weights
    xm_a, qkv, att, branch_a, x_mid, xm_m, branch_m, pre, act = kept
    vmem, hbm = pl.BlockSpec(memory_space=pltpu.VMEM), pl.BlockSpec(memory_space=pl.ANY)
    smem = pl.BlockSpec(memory_space=pltpu.SMEM)
    like = lambda columns, kind: jax.ShapeDtypeStruct((PATCHES, columns), kind)
    mods = jax.ShapeDtypeStruct((3, D), jnp.float32)
    return pl.pallas_call(
        backward_kernel,
        out_shape=(like(D, BF), mods, mods, like(D, BF), like(D, BF), like(FF, BF), like(3 * D, BF)),
        in_specs=[smem] + [vmem] * 8 + [hbm] * 3,
        out_specs=(vmem,) * 7,
        scratch_shapes=weight_scratch()
        + [
            pltpu.VMEM((PATCHES, FF), jnp.float32),
            pltpu.VMEM((PATCHES, D), jnp.float32),
            pltpu.VMEM((PATCHES, 3 * D), jnp.float32),
            pltpu.VMEM((PATCHES, D), BF),
            pltpu.SemaphoreType.DMA((7,)),
        ],
        compiler_params=pltpu.CompilerParams(vmem_limit_bytes=VMEM_BYTES),
        cost_estimate=stage_cost(),
        name="stage_backward",
    )(flags, d_out, x_in, x_mid, mod_a, mod_m, branch_a, branch_m, qkv, pre, w_blk, w_dn)


SUM_ROWS = 16


def collect_kernel(peers, flags_ref, *refs):
    tokens, d_pre_ref, mods, fm_ref, extra_ref = refs[:4], refs[4], refs[5:7], refs[7], refs[8]
    sums_ref, mods_ref, rows_ref = refs[9:]
    core, stage = flags_ref[0], flags_ref[1]
    ones = jnp.ones((8, PATCHES), BF)
    total = lambda value: matmul(ones, value)[0:1]
    sums_ref[...] = jnp.zeros_like(sums_ref)
    rows = [total(tokens[0][:, D * k : D * (k + 1)]) for k in range(3)]
    rows += [total(ref[...]) for ref in tokens[1:]]
    halves = [[total(d_pre_ref[:, D * k : D * (k + 1)]) for k in range(4)]]
    own = halves[0]
    order = [jnp.where(core == 0, own[k], own[(k + 2) % 4]) for k in range(4)]
    last = jnp.where(stage == 0, rows[5], extra_ref[0:1])
    for place, row in enumerate(rows[:4] + order + [rows[4], last, extra_ref[1:2]]):
        sums_ref[place : place + 1, :D] = row
    rows_ref[...] = jnp.zeros_like(rows_ref)
    for k in range(2):
        for row in range(5):
            source = mods[k][row : row + 1, :] if row < 3 else fm_ref[row - 3 : row - 2, :]
            for part in range(D // 128):
                at = row * (D // 128) + part
                rows_ref[at : at + 1] = source[:, 128 * part : 128 * (part + 1)]
        mods_ref[k] = to_half(rows_ref[...])


def collect(flags, tokens, d_pre, mods, fm, extra):
    peers = 2 * lax.axis_size("dp")
    vmem = pl.BlockSpec(memory_space=pltpu.VMEM)
    return pl.pallas_call(
        partial(collect_kernel, peers),
        out_shape=(
            jax.ShapeDtypeStruct((SUM_ROWS, 128 * max(peers, 9)), jnp.float32),
            jax.ShapeDtypeStruct((2, 48, 128), BF),
        ),
        scratch_shapes=[pltpu.VMEM((48, 128), jnp.float32)],
        in_specs=[pl.BlockSpec(memory_space=pltpu.SMEM)] + [vmem] * 9,
        out_specs=(vmem, vmem),
        compiler_params=pltpu.CompilerParams(vmem_limit_bytes=VMEM_BYTES),
        name="collect",
    )(flags, *tokens, d_pre, *mods, fm, extra)


def final_step(x_out, fmod, w_head, b_head, target, counts, loss_scale):
    normed, inverse = normalized(x_out)
    xf_half = to_half(normed * (1.0 + fmod[1:2]) + fmod[0:1])
    error = matmul_nt(xf_half, w_head) + b_head - target
    loss = counts * jnp.sum(error * error)
    d_pred = to_half(2.0 * loss_scale * counts * error)
    g_head = matmul_tn(xf_half, d_pred)
    d_x, d_shift, d_scale = modulated_back(normed, inverse, fmod[1:2], matmul(d_pred, w_head))
    return (loss, d_x, jnp.stack([d_shift, d_scale]), g_head, column_sums(d_pred))


def nesterov(weight, moment, average, grad, factor):
    clipped = grad * factor
    moment_new = momentum_rate * moment + clipped
    weight_new = weight - learn_rate * (clipped + momentum_rate * moment_new)
    average_new = ema_decay * average + (1.0 - ema_decay) * weight_new
    return (weight_new, moment_new, average_new, weight_new.astype(jnp.bfloat16))


def swap(array, by):
    peers = lax.axis_size("section")
    return lax.ppermute(array, "section", [(k, k ^ by) for k in range(peers)])


def pick(parts, index):
    return lax.dynamic_index_in_dim(parts, index, 0, keepdims=False)


def body(
    latents, noise, timesteps, labels, null_mask, valid,
    mod_w, mod_m, mod_e, block_w, block_m, block_e, down_w, down_m, down_e,
    stem_w, stem_m, stem_e, tail_w, tail_m, tail_e, biases, bias_m, bias_e,
):
    place = lax.axis_index("dp")
    section = lax.axis_index("section")
    stage = section // 2
    core = lax.rem(section, 2)
    even = core == 0
    n = lax.axis_size("dp")
    width = D // n

    flags = jnp.stack([core, stage]).astype(jnp.int32)
    downs, stems = jnp.swapaxes(down_w, 1, 2), stem_w.T
    stem_half, tail_half, mod_half_w = to_half(stems), to_half(tail_w), to_half(mod_w[0])
    dn_half = to_half(lax.dynamic_slice(downs, (stage, 0, core * HALF), (1, width, HALF))[0])
    at_one, at_two = NCLS + PATCH_IN, NCLS + PATCH_IN + FREQ
    w_two = stem_half[:, at_two:]
    table = jnp.pad(stem_half[:, :NCLS], ((0, 0), (0, -NCLS % 128)))
    w_fm = tail_half[:, : 2 * D]
    to_wide = lambda value: jnp.pad(value, ((0, 0),) * (value.ndim - 1) + ((0, WIDE - width),))
    ends = to_wide(jnp.concatenate([stem_half[:, NCLS:at_one], tail_half[:, 2 * D :]], axis=1).T)
    w_one = jnp.pad(stem_half[:, at_one:at_two], ((0, WIDE - width), (0, 0)))
    two_blocks = to_wide(w_two.reshape(width, n, width)).transpose(1, 0, 2)
    classes = jnp.where(null_mask > 0, NCLS - 1, labels)
    freq = to_half(time_features(timesteps.astype(jnp.float32))).astype(jnp.float32)
    facts = jnp.stack([classes, valid], axis=1).astype(jnp.float32)
    meta = jnp.concatenate([freq, facts, jnp.zeros((2, META - FREQ - 2), jnp.float32)], axis=1)
    b_one, b_two = (lax.dynamic_slice_in_dim(biases, k * D + place * width, width)[None] for k in (31, 32))
    w_blk, w_dn, meta, ends, pre_own, hidden_all, cond, mods = gather_weights(
        to_half(block_w[0]), dn_half, meta, ends, w_one, two_blocks, table, mod_half_w, w_fm,
        to_wide(b_one), b_two,
    )
    ends = ends[:, :, :width].transpose(1, 0, 2).reshape(ROWS_END, D)
    w_patch_all, w_head_all = ends[:PATCH_IN], ends[PATCH_IN:]
    images = 2 * n
    count = jnp.sum(meta[:, FREQ + 1])
    loss_scale = 1.0 / (count * PATCHES * HEAD_OUT)
    mods = mods.reshape(2, 8 * PIECE)
    bias_of = lambda first, length: lax.dynamic_slice_in_dim(biases, first, length)
    mod_a = (mods[0, : 3 * D] + bias_of(6 * D * stage, 3 * D)).reshape(3, D)
    mod_b = (mods[1, : 3 * D] + bias_of(6 * D * stage + 3 * D, 3 * D)).reshape(3, D)
    fmod = (mods[0, 3 * D : 5 * D] + biases[33 * D : 35 * D]).reshape(2, D)
    weights = (
        flags, mod_a, mod_b, w_blk, w_dn,
        bias_of(12 * D + 8 * D * stage, 4 * D)[None],
        jnp.concatenate(
            [bias_of(16 * D + 8 * D * stage + HALF * half, HALF)[None] for half in (core, 1 - core)], axis=1
        ),
        bias_of(28 * D + D * stage, D)[None],
    )

    step = pick(timesteps, core).astype(jnp.float32)
    signal, spread = noise_levels(step)
    lat, noi = pick(latents, core)[None], pick(noise, core)[None]
    counts = pick(valid, core).astype(jnp.float32)
    tok_half = to_half(patchify(signal * lat + spread * noi))[0]
    target = jnp.concatenate([patchify(signal * noi - spread * lat), patchify(noi)], axis=2)[0]
    x_first = matmul(tok_half, w_patch_all) + biases[30 * D : 31 * D] + position_table(GRID // 2, D)

    x_hop = swap(stage_forward(False, x_first, weights)[0], 2)
    x_in = jnp.where(stage == 0, x_first, x_hop.astype(jnp.float32))
    x_out, *kept = stage_forward(True, x_in, weights)
    loss, d_final, d_fmod, g_head, b_head = final_step(
        x_out, fmod, w_head_all, biases[35 * D :], target, counts, loss_scale
    )
    xm_a, qkv, attended, branch_a, x_mid, xm_b, branch_b, pre, act = kept
    d_hop = swap(stage_backward(d_final, x_in, weights, kept)[0], 2)
    d_out = jnp.where(stage == 1, d_final, d_hop.astype(jnp.float32))
    d_first, d_mod_a, d_mod_b, d_branch_a, d_branch_b, d_pre, d_qkv = stage_backward(
        d_out, x_in, weights, kept
    )
    d_query, d_key, d_value = (d_qkv[:, D * k : D * (k + 1)] for k in range(3))

    act_sib, branch_sib, xm_sib, pre_sib = swap((act[:, HALF:], d_branch_b, xm_b, d_pre[:, HALF:]), 1)
    g_dn = to_half(matmul_tn(d_branch_b, act[:, :HALF]) + matmul_tn(branch_sib, act_sib))
    g_up = to_half(matmul_tn(xm_b, d_pre[:, :HALF]) + matmul_tn(xm_sib, pre_sib))

    xa_sib, last_sib, one_sib, two_sib = swap(
        (
            xm_a,
            jnp.where(even, attended, xm_a),
            jnp.where(even, d_value, d_query),
            jnp.where(even, d_branch_a, d_key),
        ),
        1,
    )
    last = jnp.where(even, xm_a, attended)
    one = jnp.where(even, d_query, d_value)
    two = jnp.where(even, d_key, d_branch_a)
    g_attn = jnp.concatenate(
        [
            to_half(matmul_tn(xm_a, one) + matmul_tn(xa_sib, one_sib)),
            to_half(matmul_tn(last, two) + matmul_tn(last_sib, two_sib)),
        ],
        axis=1,
    )

    extra = jnp.stack([jnp.pad(b_head, (0, D - HEAD_OUT)), jnp.pad(loss[None], (0, D - 1))])
    d_fmod = jnp.where(stage == 1, d_fmod, jnp.zeros_like(d_fmod))
    own_sums, d_mods = collect(
        flags, (d_qkv, d_branch_a, d_branch_b, d_first), d_pre, (d_mod_a, d_mod_b), d_fmod, extra
    )
    g_patch = jnp.pad(matmul_tn(d_first, tok_half), ((0, 0), (0, HEAD_OUT - PATCH_IN)))
    end_rows = row_count(width * HEAD_OUT)
    own_ends = jnp.where(stage == 0, g_patch, g_head).reshape(n, width * HEAD_OUT)
    own_ends = jnp.pad(own_ends, ((0, 0), (0, end_rows * 128 - width * HEAD_OUT))).reshape(n, end_rows, 128)
    own_sums = own_sums.reshape(SUM_ROWS, -1, 128).transpose(1, 0, 2)[: 2 * n]
    halves, crossed, dn_all, g_mod, g_fm, g_table, g_one, g_two, ends_all, news, mod_sums, fm_sum, squares = (
        sum_gradients(
            g_dn, g_up, g_attn, d_mods, own_sums, own_ends, mod_half_w, w_fm, two_blocks, cond, pre_own,
            hidden_all, meta,
        )
    )
    crossed = crossed.astype(jnp.float32)
    g_blk = jnp.concatenate(
        [jnp.where(even, halves[1], crossed), jnp.where(even, crossed, halves[0])], axis=1
    )
    dn_all = dn_all.astype(jnp.float32)
    down_both = jnp.stack([jnp.concatenate([dn_all[2 * k], dn_all[2 * k + 1]], axis=1) for k in range(2)])
    ends = [
        ends_all[k].reshape(-1)[: width * HEAD_OUT].reshape(width, HEAD_OUT) for k in (0, 3)
    ]
    g_two = g_two[:, :, :width].transpose(1, 0, 2).reshape(width, D)
    g_stem = jnp.concatenate(
        [g_table[:, :NCLS], ends[0][:, :PATCH_IN], g_one[:width], g_two], axis=1
    )
    g_tail = jnp.concatenate([g_fm, ends[1]], axis=1)

    news = news.reshape(n, 4, -1, 128)
    stages = []
    for k in range(2):
        pieces = news[:, 2 * k : 2 * k + 2, :SUM_ROWS].reshape(2 * n, SUM_ROWS, 128)[: D // 128]
        stages.append(pieces.transpose(1, 0, 2).reshape(-1))
    slices = news[:, 0, SUM_ROWS : SUM_ROWS + 4].reshape(n, 2, WIDE)[:, :, :width]
    bias_grad = jnp.concatenate(
        [mod_sums.reshape(-1)]
        + [part[: 8 * D] for part in stages]
        + [part[8 * D : 9 * D] for part in stages]
        + [stages[0][9 * D : 10 * D]]
        + [slices[:, 0].reshape(-1), slices[:, 1].reshape(-1)]
        + [fm_sum[0], stages[1][9 * D : 9 * D + HEAD_OUT]]
    )
    loss_sum = stages[1][10 * D]
    grad_norm = jnp.sqrt(jnp.sum(squares[:, 0, 0]))
    factor = jnp.minimum(1.0, clip_limit / (grad_norm + 1e-06))
    mod_out = nesterov(mod_w, mod_m, mod_e, g_mod[None], factor)
    block_out = nesterov(block_w, block_m, block_e, g_blk[None], factor)
    flip = lambda value: jnp.swapaxes(value, 1, 2)
    down_out = tuple(map(flip, nesterov(downs, flip(down_m), flip(down_e), down_both, factor)))
    stem_out = tuple(value.T for value in nesterov(stems, stem_m.T, stem_e.T, g_stem, factor))
    tail_out = nesterov(tail_w, tail_m, tail_e, g_tail, factor)
    bias_out = nesterov(biases, bias_m, bias_e, bias_grad, factor)
    return (
        (loss_sum, count, grad_norm)
        + mod_out + block_out + down_out + stem_out + tail_out + bias_out
    )


def solution(mesh):
    images = (P("dp", None, None, None),) * 2 + (P("dp"),) * 4
    owned = P("section", "dp", None)
    states = (owned,) * 6 + (P(None, None, "dp"),) * 3 + (P(None, "dp"),) * 3 + (P("dp", None),) * 3 + (P(),) * 3
    updates = (owned,) * 8 + (P(None, None, "dp"),) * 4 + (P(None, "dp"),) * 4 + (P("dp", None),) * 4 + (P(),) * 4
    return jax.shard_map(
        body,
        mesh=mesh,
        in_specs=images + states,
        out_specs=(P(), P(), P()) + updates,
        check_vma=False,
    )
```

```python
from functools import partial
import math

import jax
import jax.numpy as jnp
from jax import lax
from jax.experimental import pallas as pl
from jax.experimental.pallas import tpu as pltpu
from jax.sharding import PartitionSpec as P

HEADS = 16
HEAD_DIM = 72
D = 1152
FF = 4608
HALF = FF // 2
NCLS = 1001
FREQ = 256
GRID = 32
PATCHES = 256
PATCH_IN = 16
HEAD_OUT = 32
LAYERS = 2
NBIAS = 40352


epsilon_norm = 1e-06
momentum_rate = 0.9
ema_decay = 0.9
learn_rate = 4000.0
clip_limit = 0.02
MESH = pl.DeviceIdType.MESH
BF = jnp.bfloat16


def matmul(left, right):
    return jnp.dot(left, right, preferred_element_type=jnp.float32)


def matmul_nt(left, right):
    return lax.dot_general(
        left, right, (((1,), (1,)), ((), ())), preferred_element_type=jnp.float32
    )


def matmul_tn(left, right):
    return lax.dot_general(
        left, right, (((0,), (0,)), ((), ())), preferred_element_type=jnp.float32
    )


def to_half(value):
    return value.astype(BF)


def column_sums(value):
    return jnp.sum(value.astype(jnp.float32), axis=0)


def silu_back(value, grad):
    return jax.vjp(jax.nn.silu, value)[1](grad)[0]


def patchify(field):
    images, side = (field.shape[0], field.shape[1] // 2)
    return (
        field.reshape(images, side, 2, side, 2, 4)
        .transpose(0, 1, 3, 2, 4, 5)
        .reshape(images, side * side, 16)
    )


def sincos_rows(places, width):
    omega = 1.0 / 10000.0 ** (jnp.arange(width // 2, dtype=jnp.float32) / (width // 2))
    angle = places[:, None] * omega[None, :]
    return jnp.concatenate([jnp.sin(angle), jnp.cos(angle)], axis=1)


def position_table(side, width):
    line = sincos_rows(jnp.arange(side, dtype=jnp.float32), width // 2)
    column = jnp.broadcast_to(line[None], (side, side, width // 2))
    row = jnp.broadcast_to(line[:, None], (side, side, width // 2))
    return jnp.concatenate([column, row], axis=2).reshape(side * side, width)


def time_features(steps):
    half = FREQ // 2
    freqs = jnp.exp(-math.log(10000.0) * jnp.arange(half, dtype=jnp.float32) / half)
    angle = steps[:, None] * freqs[None, :]
    return jnp.concatenate([jnp.cos(angle), jnp.sin(angle)], axis=1)


def noise_levels(steps):
    level = jnp.cos((steps / 1000.0 + 0.008) / 1.008 * (math.pi / 2)) ** 2
    return (jnp.sqrt(level), jnp.sqrt(1.0 - level))


Z, X = 4, 2
GATHER_CHUNKS = (
    (0, 0, 48, True), (0, 48, 48, True), (0, 96, 48, False),
    (1, 0, 48, False), (1, 48, 48, False), (1, 96, 48, False),
)
CHUNKS = ((0, 16, True), (16, 32, False), (48, 32, False), (80, 32, False), (112, 32, False))
META = 384
WIDE = 256
ROWS_END = PATCH_IN + HEAD_OUT
PIECE = 768


def ring_fits(n, rows):
    return n == Z * X and rows == 144


def one_hot(classes, width):
    lane = lax.broadcasted_iota(jnp.int32, (classes.shape[0], width), 1).astype(jnp.float32)
    return to_half(jnp.maximum(1.0 - jnp.abs(lane - classes), 0.0))


def gather_kernel(
    blk_ref, dn_ref, meta_ref, ends_ref, one_ref, two_ref, table_ref, mod_ref, fm_ref, b_one, b_two,
    out_blk, out_dn, meta_out, ends_out, pre_out, hidden_out, cond_out, mods_out,
    metas, hidden, part, parts, arrived_parts,
    meta_send, meta_recv, ends_send, ends_recv, hid_send, hid_recv, part_send, part_recv, local_sem,
    up_sem, down_sem, x_sem, sib_sem, recv_sem, sib_recv, own_sem,
):
    me = lax.axis_index("dp")
    section = lax.axis_index("section")
    z, x = me // X, lax.rem(me, X)
    core = lax.rem(section, 2)
    sibling = section + 1 - 2 * core
    across = me + 1 - 2 * x
    chunks = len(GATHER_CHUNKS)
    low = section - core
    group, place_in = Z * X * 2, me * 2 + core
    where = lambda p: {"dp": p // 2, "section": low + lax.rem(p, 2)}
    has_up, has_down = z < Z - 1, z > 0

    barrier = pltpu.get_barrier_semaphore()

    @pl.loop(1, group)
    def _(step):
        pl.semaphore_signal(
            barrier, 1, device_id=where(lax.rem(place_in + step, group)), device_id_type=MESH
        )

    pl.semaphore_wait(barrier, group - 1)

    def to_dp(src, dst, send, recv, step, p, slot):
        return pltpu.make_async_remote_copy(
            src_ref=src, dst_ref=dst.at[slot], send_sem=send.at[step], recv_sem=recv.at[step],
            device_id={"dp": p}, device_id_type=MESH,
        )

    meta_copy = partial(to_dp, meta_ref, metas, meta_send, meta_recv)
    ends_copy = partial(to_dp, ends_ref, ends_out, ends_send, ends_recv)
    hidden_copy = partial(to_dp, hidden, hidden_out, hid_send, hid_recv)

    def part_copy(step, p, slot):
        return pltpu.make_async_remote_copy(
            src_ref=parts.at[p], dst_ref=arrived_parts.at[slot],
            send_sem=part_send.at[step], recv_sem=part_recv.at[step],
            device_id=where(p), device_id_type=MESH,
        )

    own_meta = pltpu.make_async_copy(meta_ref, metas.at[me], local_sem.at[0])
    own_ends = pltpu.make_async_copy(ends_ref, ends_out.at[me], local_sem.at[1])
    own_hidden = pltpu.make_async_copy(hidden, hidden_out.at[me], local_sem.at[2])
    own_part = pltpu.make_async_copy(parts.at[place_in], arrived_parts.at[place_in], local_sem.at[3])

    def send_all(copy_to, size, index):
        @pl.loop(1, size)
        def _(step):
            copy_to(step, lax.rem(index + step, size), index).start()

    def wait_all(copy_to, size, index):
        @pl.loop(1, size)
        def _(step):
            p = lax.rem(index + size - step, size)
            copy_to(step, p, p).wait_recv()
            copy_to(step, p, p).wait_send()

    own_meta.start()
    own_ends.start()
    send_all(meta_copy, Z * X, me)

    def place(owner, k, side):
        which, first, rows, unused = GATHER_CHUNKS[k]
        return (out_dn if which else out_blk).at[side, pl.ds(pl.multiple_of(owner * 144 + first, 16), rows)]

    def source(owner, k, mine):
        if not mine:
            return place(owner, k, core)
        which, first, rows, unused = GATHER_CHUNKS[k]
        return (dn_ref if which else blk_ref).at[pl.ds(first, rows)]

    def copy(owner, k, mine, sem, target):
        unit = owner * chunks + k
        return pltpu.make_async_remote_copy(
            src_ref=source(owner, k, mine),
            dst_ref=place(owner, k, core),
            send_sem=sem.at[unit],
            recv_sem=recv_sem.at[unit],
            device_id={"dp": target},
            device_id_type=MESH,
        )

    def to_sibling(owner, k, mine):
        unit = owner * chunks + k
        return pltpu.make_async_remote_copy(
            src_ref=source(owner, k, mine),
            dst_ref=place(owner, k, core),
            send_sem=sib_sem.at[unit],
            recv_sem=sib_recv.at[unit],
            device_id={"section": sibling},
            device_id_type=MESH,
        )

    def own_copy(k):
        return pltpu.make_async_copy(source(me, k, True), place(me, k, core), own_sem.at[k])

    def arrived(owner, k):
        copy(owner, k, False, x_sem, across).wait_recv()

    for k in range(chunks):
        @pl.when(has_up)
        def _():
            copy(me, k, True, up_sem, me + X).start()

        @pl.when(has_down)
        def _():
            copy(me, k, True, down_sem, me - X).start()

        copy(me, k, True, x_sem, across).start()
        own_copy(k).start()
        to_sibling(me, k, True).start()

    send_all(ends_copy, Z * X, me)

    def make_hidden():
        own_meta.wait()
        wait_all(meta_copy, Z * X, me)
        for index in range(Z * X):
            meta_out[2 * index : 2 * index + 2] = metas[index]
        pre = matmul_nt(to_half(meta_out[:, :FREQ]), one_ref[...]) + b_one[...]
        pre_out[...] = pre
        hidden[...] = to_half(jax.nn.silu(pre))
        own_hidden.start()
        send_all(hidden_copy, Z * X, me)

    def make_parts():
        own_hidden.wait()
        wait_all(hidden_copy, Z * X, me)
        cond = matmul_nt(one_hot(meta_out[:, FREQ : FREQ + 1], table_ref.shape[1]), table_ref[...]) + b_two[...]
        for index in range(Z * X):
            cond = cond + matmul_nt(hidden_out[index], two_ref[index])
        cond_out[...] = cond
        cond_low = to_half(cond).astype(jnp.float32)
        own_cond = jnp.where(section == 0, cond, cond_low)
        part[:, : 3 * D] = matmul(to_half(jax.nn.silu(own_cond)), mod_ref[...])
        part[:, 3 * D : 5 * D] = matmul(to_half(jax.nn.silu(cond_low)), fm_ref[...])
        part[:, 5 * D :] = jnp.zeros((group, 8 * PIECE - 5 * D), jnp.float32)
        for row in range(group):
            for k in range(8):
                parts[row, k : k + 1] = part[row : row + 1, PIECE * k : PIECE * (k + 1)]
        own_part.start()
        send_all(part_copy, group, place_in)

    def along(step, k):
        crosses = not (step == 1 and GATHER_CHUNKS[k][3])
        for sign in (-1, 1):
            @pl.when((z >= step) if sign < 0 else (z + step < Z))
            def _():
                owner = me + sign * X * step
                arrived(owner, k)

                @pl.when(has_up if sign < 0 else has_down)
                def _():
                    copy(owner, k, False, up_sem if sign < 0 else down_sem, me - sign * X).start()

                if crosses:
                    copy(owner, k, False, x_sem, across).start()
                to_sibling(owner, k, False).start()

    def crossed(step, k):
        if step == 0:
            arrived(across, k)
            if GATHER_CHUNKS[k][3]:
                @pl.when(has_up)
                def _():
                    copy(across, k, False, up_sem, me + X).start()

                @pl.when(has_down)
                def _():
                    copy(across, k, False, down_sem, me - X).start()
            to_sibling(across, k, False).start()
            return
        for sign in (-1, 1):
            @pl.when((z >= step) if sign < 0 else (z + step < Z))
            def _():
                owner = across + sign * X * step
                arrived(owner, k)
                to_sibling(owner, k, False).start()

    for step in range(1, Z + 1):
        for k in range(chunks):
            if step < Z:
                along(step, k)
            crossed(step - 1, k)
        if step == 1:
            make_hidden()
        if step == 2:
            make_parts()

    own_part.wait()
    wait_all(part_copy, group, place_in)
    own_ends.wait()
    wait_all(ends_copy, Z * X, me)
    for source_core in range(2):
        total = arrived_parts[source_core]
        for index in range(1, Z * X):
            total = total + arrived_parts[2 * index + source_core]
        mods_out[source_core] = total

    for k in range(chunks):
        near = GATHER_CHUNKS[k][3]
        own_copy(k).wait()
        for column in range(2):
            base = me if column == 0 else across
            for step in range(0, Z):
                for sign in (-1, 1) if step else (1,):
                    @pl.when((z >= step) if sign < 0 else (z + step < Z))
                    def _():
                        owner = base + sign * X * step
                        mine = column == 0 and step == 0
                        to_sibling(owner, k, mine).wait_send()
                        pltpu.make_async_remote_copy(
                            src_ref=place(owner, k, 1 - core),
                            dst_ref=place(owner, k, 1 - core),
                            send_sem=sib_sem.at[owner * chunks + k],
                            recv_sem=sib_recv.at[owner * chunks + k],
                            device_id={"section": sibling},
                            device_id_type=MESH,
                        ).wait_recv()
                        runs = column == 0 or (near and step == 0)
                        if runs and (step == 0 or sign < 0):
                            @pl.when(has_up)
                            def _():
                                copy(owner, k, mine, up_sem, me + X).wait_send()
                        if runs and (step == 0 or sign > 0):
                            @pl.when(has_down)
                            def _():
                                copy(owner, k, mine, down_sem, me - X).wait_send()
                        if column == 0 and not (step == 1 and near):
                            copy(owner, k, mine, x_sem, across).wait_send()


def gather_weights(blk, dn, meta, ends, w_one, w_two, table, w_mod, w_fm, b_one, b_two):
    n, width = lax.axis_size("dp"), blk.shape[0]
    section = lax.axis_index("section")
    if not ring_fits(n, width):
        both = lambda own, sib: jnp.where(
            lax.rem(section, 2) == 0, jnp.stack([own, sib]), jnp.stack([sib, own])
        )
        blk = lax.all_gather(blk, "dp", axis=0, tiled=True)
        dn = lax.all_gather(dn, "dp", axis=0, tiled=True)
        meta, ends = exchange(2, "dp", ("all", "all"), meta, ends)
        meta = meta.reshape(2 * n, META)
        pre = matmul_nt(to_half(meta[:, :FREQ]), w_one) + b_one
        (hidden,) = exchange(8, "dp", ("all",), to_half(jax.nn.silu(pre)))
        cond = matmul_nt(one_hot(meta[:, FREQ : FREQ + 1], table.shape[1]), table) + b_two
        cond = cond + jnp.einsum("jik,jwk->iw", hidden, w_two, preferred_element_type=jnp.float32)
        cond_low = to_half(cond).astype(jnp.float32)
        own_cond = jnp.where(section == 0, cond, cond_low)
        parts = [
            matmul(to_half(jax.nn.silu(own_cond)), w_mod),
            matmul(to_half(jax.nn.silu(cond_low)), w_fm),
        ]
        parts = jnp.pad(jnp.concatenate(parts, axis=1), ((0, 0), (0, 8 * PIECE - 5 * D)))
        (parts,) = exchange(3, "stage", ("each",), parts.reshape(2 * n, 8, PIECE))
        mods = jnp.sum(parts.reshape(n, 2, 8, PIECE), axis=0)
        return (both(blk, swap(blk, 1)), both(dn, swap(dn, 1)), meta, ends, pre, hidden, cond, mods)
    units, images = n * len(GATHER_CHUNKS), 2 * n
    hbm, vmem = pl.BlockSpec(memory_space=pl.ANY), pl.BlockSpec(memory_space=pltpu.VMEM)
    dma = lambda count: pltpu.SemaphoreType.DMA((count,))
    f32 = jnp.float32
    return pl.pallas_call(
        gather_kernel,
        out_shape=(
            jax.ShapeDtypeStruct((2, D, FF), BF), jax.ShapeDtypeStruct((2, D, HALF), BF),
            jax.ShapeDtypeStruct((images, META), f32), jax.ShapeDtypeStruct((n,) + ends.shape, BF),
            jax.ShapeDtypeStruct((images, WIDE), f32), jax.ShapeDtypeStruct((n, images, WIDE), BF),
            jax.ShapeDtypeStruct((images, width), f32), jax.ShapeDtypeStruct((2, 8, PIECE), f32),
        ),
        in_specs=[hbm] * 2 + [vmem] * 9,
        out_specs=(hbm, hbm) + (vmem,) * 6,
        scratch_shapes=[
            pltpu.VMEM((n, 2, META), f32), pltpu.VMEM((images, WIDE), BF),
            pltpu.VMEM((images, 8 * PIECE), f32),
            pltpu.VMEM((images, 8, PIECE), f32), pltpu.VMEM((images, 8, PIECE), f32),
            dma(n), dma(n), dma(n), dma(n), dma(n), dma(n), dma(images), dma(images), dma(4),
        ]
        + [dma(units)] * 6
        + [dma(len(GATHER_CHUNKS))],
        compiler_params=pltpu.CompilerParams(
            collective_id=0, has_side_effects=True, vmem_limit_bytes=VMEM_BYTES
        ),
        cost_estimate=pl.CostEstimate(flops=0, bytes_accessed=400_000_000, transcendentals=0),
        name="gather_weights",
    )(blk, dn, meta, ends, w_one, w_two, table, w_mod, w_fm, b_one, b_two)


VMEM_BYTES = 60 * 1024 * 1024
SUM_CHUNKS = tuple((which,) + chunk for which in range(3) for chunk in CHUNKS)


def silu_slope(value):
    gate = jax.nn.sigmoid(value)
    return gate * (1.0 + value * (1.0 - gate))


def sum_kernel(
    g_dn, g_up, g_attn, dm_ref, bp_ref, en_ref, mod_ref, fm_ref, two_ref, cond_ref, pre_ref, hid_ref, meta_ref,
    out, cross_out, dn_out, gmod_out, gfm_out, gtab_out, gone_out, gtwo_out,
    ends_all, news_out, cs_all, fmsum_out, sq_out,
    own_b, other_d, xb, xq, up_b, up_o, down_b, down_o, acc, acc_dn,
    dm_in, bp_in, en_in, dmat, ends_src, c_src, c_in, fmd_src, fmd_in, cs_src, dcond, ph, ph_in, news_src,
    sq_src, sq_all, sq_rows, cross_src,
    load_sem, x_send, x_recv, up_send, up_recv, down_send, down_recv,
    sib_send, sib_recv, y_send, y_recv, group_send, group_recv, sect_send, sect_recv,
    ph_send, ph_recv, news_send, news_recv, sq_send, sq_recv, cross_sem, local_sem,
):
    me = lax.axis_index("dp")
    section = lax.axis_index("section")
    z, x = me // X, lax.rem(me, X)
    core = lax.rem(section, 2)
    low, sibling, facing = section - core, section + 1 - 2 * core, lax.rem(section + 2, 4)
    across = me + 1 - 2 * x
    sources = (g_dn, g_up, g_attn)
    chunks = len(SUM_CHUNKS)
    has_up, has_down = z < Z - 1, z > 0
    devices, group = Z * X * 4, Z * X * 2
    me_all, me_group = me * 4 + section, me * 2 + core
    in_all = lambda p: {"dp": p // 4, "section": lax.rem(p, 4)}
    in_group = lambda p: {"dp": p // 2, "section": low + lax.rem(p, 2)}
    in_section = lambda p: {"section": p}
    in_dp = lambda p: {"dp": p}
    f32 = jnp.float32

    barrier = pltpu.get_barrier_semaphore()

    @pl.loop(1, devices)
    def _(step):
        pl.semaphore_signal(
            barrier, 1, device_id=in_all(lax.rem(me_all + step, devices)), device_id_type=MESH
        )

    def small(src_of, dst, send, recv, where, size, index):
        def copy(step, p, slot):
            return pltpu.make_async_remote_copy(
                src_ref=src_of(p), dst_ref=dst.at[slot], send_sem=send.at[step], recv_sem=recv.at[step],
                device_id=where(p), device_id_type=MESH,
            )
        return (copy, size, index, src_of, dst)

    gradients = [
        small(lambda p: dm_ref.at[lax.rem(p, 2)], dm_in, group_send.at[0], group_recv.at[0], in_group, group, me_group),
        small(lambda p: bp_ref.at[p], bp_in, group_send.at[1], group_recv.at[1], in_group, group, me_group),
        small(lambda p: en_ref.at[p // 2], en_in, group_send.at[2], group_recv.at[2], in_group, group, me_group),
    ]
    conds = [
        small(lambda p, src=src: src, dst, sect_send.at[k], sect_recv.at[k], in_section, 4, section)
        for k, (src, dst) in enumerate(
            ((c_src, c_in), (ends_src, ends_all), (fmd_src, fmd_in), (cs_src, cs_all))
        )
    ]
    hiddens = [small(lambda p: ph.at[p], ph_in, ph_send, ph_recv, in_dp, Z * X, me)]
    news = [small(lambda p: news_src, news_out, news_send, news_recv, in_all, devices, me_all)]
    norms = [small(lambda p: sq_src, sq_all, sq_send, sq_recv, in_all, devices, me_all)]

    def own_copies(batch, first):
        return [
            pltpu.make_async_copy(src_of(index), dst.at[index], local_sem.at[first + k])
            for k, (copy, size, index, src_of, dst) in enumerate(batch)
        ]

    def send_batch(batch, first):
        for copy in own_copies(batch, first):
            copy.start()
        for copy, size, index, src_of, dst in batch:
            @pl.loop(1, size)
            def _(step):
                copy(step, lax.rem(index + step, size), index).start()

    def wait_batch(batch, first):
        for copy in own_copies(batch, first):
            copy.wait()
        for copy, size, index, src_of, dst in batch:
            @pl.loop(1, size)
            def _(step):
                p = lax.rem(index + size - step, size)
                copy(step, p, p).wait_recv()
                copy(step, p, p).wait_send()

    def add_square(value):
        sq_src[...] += jnp.sum(value * value)

    def images_of():
        cond = cond_ref[...]
        cond_low = to_half(cond).astype(f32)
        return jnp.where(section == 0, cond, cond_low), cond_low

    def make_cond():
        wait_batch(gradients, 0)
        flat = dm_in[...].reshape(group * 48, 128)
        row = lax.broadcasted_iota(jnp.int32, (group, group * 48), 0) * 48
        column = lax.broadcasted_iota(jnp.int32, (group, group * 48), 1)
        for k in range(5 * D // 128):
            chosen = jnp.where(column == row + k, 1.0, 0.0).astype(BF)
            dmat[:, 128 * k : 128 * (k + 1)] = to_half(matmul(chosen, flat))
        news_src[...] = jnp.zeros_like(news_src)
        news_src[0:SUM_ROWS] = jnp.sum(bp_in[...], axis=0)
        ends_src[...] = jnp.sum(en_in[...], axis=0)
        own_cond, cond_low = images_of()
        d_mod, d_fm = dmat[:, : 3 * D], dmat[:, 3 * D :]
        fmd_src[...] = d_fm
        cs_src[...] = jnp.sum(d_mod.astype(f32), axis=0, keepdims=True)
        d_silu = matmul_nt(d_mod, mod_ref[...])
        d_silu = d_silu + (section == 3).astype(f32) * matmul_nt(d_fm, fm_ref[...])
        c_src[...] = jnp.zeros_like(c_src)
        c_src[:, :144] = silu_slope(own_cond) * d_silu
        send_batch(conds, 3)
        silu_own = to_half(jax.nn.silu(own_cond))
        for k in range(3):
            part_g = matmul_tn(silu_own, dmat[:, D * k : D * (k + 1)])
            gmod_out[:, D * k : D * (k + 1)] = part_g
            add_square(part_g)

    once = (section == 0).astype(f32)

    def make_hidden():
        wait_batch(conds, 3)
        total = to_half(c_in[3])
        for slot in (2, 1, 0):
            total = to_half(total.astype(f32) + c_in[slot])
        dcond[...] = total
        d_cond = dcond[:, :144]
        for index in range(Z * X):
            ph[index] = matmul(d_cond, two_ref[index])
        send_batch(hiddens, 7)
        own_cond, cond_low = images_of()
        silu_low = to_half(jax.nn.silu(cond_low))
        for k in range(2):
            part_g = matmul_tn(silu_low, fmd_in[3, :, D * k : D * (k + 1)])
            gfm_out[:, D * k : D * (k + 1)] = part_g
            add_square(jnp.sqrt(once) * part_g)
        fmsum_out[...] = jnp.sum(fmd_in[3].astype(f32), axis=0, keepdims=True)
        part_g = matmul_tn(d_cond, one_hot(meta_ref[:, FREQ : FREQ + 1], gtab_out.shape[1]))
        gtab_out[...] = part_g
        add_square(once * part_g)
        for index in range(Z * X):
            part_g = matmul_tn(d_cond, hid_ref[index])
            gtwo_out[:, 144 * index : 144 * (index + 1)] = part_g[:, :144]
            add_square(once * part_g)

    def make_news():
        wait_batch(hiddens, 7)
        total = ph_in[0]
        for index in range(1, Z * X):
            total = total + ph_in[index]
        d_pre = to_half(silu_slope(pre_ref[...]) * total)
        part_g = matmul_tn(d_pre, to_half(meta_ref[:, :FREQ]))
        gone_out[...] = part_g
        add_square(once * part_g)
        sums = jnp.sum(d_pre.astype(f32), axis=0, keepdims=True)
        sums_cond = jnp.sum(dcond[...].astype(f32), axis=0, keepdims=True)
        for k in range(2):
            news_src[SUM_ROWS + k : SUM_ROWS + k + 1] = sums[:, 128 * k : 128 * (k + 1)]
            news_src[SUM_ROWS + 2 + k : SUM_ROWS + 3 + k] = sums_cond[:, 128 * k : 128 * (k + 1)]
        send_batch(news, 8)
        first = (me == 0).astype(f32)
        add_square(news_src[0:10])
        add_square(once * sums)
        add_square(once * sums_cond)
        add_square(first * cs_src[...])
        add_square(first * once * fmsum_out[...])
        add_square(once * ends_all[0])
        add_square(once * ends_all[3])

    def dn_copy(k, slot, to_sib):
        rows = pl.ds(SUM_CHUNKS[k][1], SUM_CHUNKS[k][2])
        unit = slot * chunks + k
        return pltpu.make_async_remote_copy(
            src_ref=dn_out.at[slot, rows], dst_ref=dn_out.at[slot, rows],
            send_sem=(sib_send if to_sib else y_send).at[unit],
            recv_sem=(sib_recv if to_sib else y_recv).at[unit],
            device_id={"section": sibling if to_sib else facing},
            device_id_type=MESH,
        )

    def each(distance, run):
        if distance == 0:
            run(z, None)
            return

        @pl.when(z + distance < Z)
        def _():
            run(z + distance, True)

        @pl.when(z >= distance)
        def _():
            run(z - distance, False)

    def part(k):
        return pl.ds(SUM_CHUNKS[k][1], SUM_CHUNKS[k][2])

    def hbm(k, zz, column):
        start = pl.multiple_of((zz * X + column) * 144 + SUM_CHUNKS[k][1], 16)
        return sources[SUM_CHUNKS[k][0]].at[pl.ds(start, SUM_CHUNKS[k][2])]

    def own(k, zz):
        return own_b.at[SUM_CHUNKS[k][0], zz, part(k)]

    def from_x(k, zz):
        return xq.at[SUM_CHUNKS[k][0]] if SUM_CHUNKS[k][3] else xb.at[SUM_CHUNKS[k][0], zz, part(k)]

    def from_z(k, zz, up, other):
        if other:
            return (up_o if up else down_o).at[SUM_CHUNKS[k][0], zz]
        return (up_b if up else down_b).at[SUM_CHUNKS[k][0], zz, part(k)]

    def other_of(k, zz):
        return other_d.at[SUM_CHUNKS[k][0], zz]

    def load(k, zz, other=False):
        index = ((chunks if other else 0) + k) * Z + zz
        return pltpu.make_async_copy(
            hbm(k, zz, (1 - x) if other else x),
            other_of(k, zz) if other else own(k, zz),
            load_sem.at[index],
        )

    def x_copy(k, zz, src):
        unit = k * Z + zz
        return pltpu.make_async_remote_copy(
            src_ref=src, dst_ref=from_x(k, zz), send_sem=x_send.at[unit], recv_sem=x_recv.at[unit],
            device_id={"dp": across}, device_id_type=MESH,
        )

    def z_copy(k, zz, up, other):
        unit = ((chunks if other else 0) + k) * Z + zz
        return pltpu.make_async_remote_copy(
            src_ref=other_of(k, zz) if other else own(k, zz),
            dst_ref=from_z(k, zz, up, other),
            send_sem=(up_send if up else down_send).at[unit],
            recv_sem=(up_recv if up else down_recv).at[unit],
            device_id={"dp": me + X if up else me - X},
            device_id_type=MESH,
        )

    def total(k, dst, srcs):
        @pl.loop(0, SUM_CHUNKS[k][2] // 16)
        def _(step):
            rows = pl.ds(pl.multiple_of(step * 16, 16), 16)
            value = srcs[0][rows].astype(jnp.float32)
            for src in srcs[1:]:
                value = value + src[rows].astype(jnp.float32)
            dst[rows] = value.astype(dst.dtype)

    for distance in (3, 2, 1, 0):
        for k in range(chunks):
            def run(zz, up):
                load(k, zz).start()
                if SUM_CHUNKS[k][3]:
                    load(k, zz, True).start()
            each(distance, run)

    sq_src[...] = jnp.zeros_like(sq_src)
    sq_rows[...] = jnp.zeros_like(sq_rows)
    pl.semaphore_wait(barrier, devices - 1)
    send_batch(gradients, 0)

    order = [
        (k, distance) for which, distance in ((0, 3), (0, 2), (0, 1), (1, 3), (0, 0), (1, 2), (1, 1), (2, 3), (1, 0), (2, 2), (2, 1), (2, 0))
        for k in range(chunks) if SUM_CHUNKS[k][0] == which and not SUM_CHUNKS[k][3]
    ]
    sent = []

    def send_x(until):
        while len(sent) < min(until, len(order)):
            k, distance = order[len(sent)]
            sent.append(1)
            each(distance, lambda zz, up: x_copy(k, zz, hbm(k, zz, 1 - x)).start())

    def after(k, distance):
        if not SUM_CHUNKS[k][3]:
            send_x(order.index((k, distance)) + 1 + 6)

    send_x(6)

    def pass_on(k, distance):
        def run(zz, up):
            behind = has_down if up else has_up
            if SUM_CHUNKS[k][3]:
                for other in (False, True):
                    mine = other_of(k, zz) if other else own(k, zz)
                    load(k, zz, other).wait()

                    @pl.when(behind)
                    def _():
                        z_copy(k, zz, up, other).wait_recv()
                        total(k, mine, [mine, from_z(k, zz, up, other)])

                    z_copy(k, zz, up, other).start()
                return
            load(k, zz).wait()
            x_copy(k, zz, hbm(k, zz, 1 - x)).wait_recv()

            @pl.when(behind)
            def _():
                z_copy(k, zz, up, False).wait_recv()
                total(k, own(k, zz), [own(k, zz), from_x(k, zz), from_z(k, zz, up, False)])

            @pl.when(jnp.logical_not(behind))
            def _():
                total(k, own(k, zz), [own(k, zz), from_x(k, zz)])

            z_copy(k, zz, up, False).start()
        each(distance, run)

    def add_z(dst, k, other):
        @pl.when(has_down)
        def _():
            z_copy(k, z, True, other).wait_recv()
            total(k, dst, [dst, from_z(k, z, True, other)])

        @pl.when(has_up)
        def _():
            z_copy(k, z, False, other).wait_recv()
            total(k, dst, [dst, from_z(k, z, False, other)])

    def send_direct(k):
        load(k, z, True).wait()
        total(k, acc, [other_of(k, z)])
        add_z(acc, k, True)
        total(k, other_of(k, z), [acc])
        x_copy(k, z, other_of(k, z)).start()

    def finish(k):
        which, rows = SUM_CHUNKS[k][0], SUM_CHUNKS[k][2]
        dst = out.at[which - 1, part(k)] if which else acc_dn.at[pl.ds(0, rows)]
        load(k, z).wait()
        if SUM_CHUNKS[k][3]:
            total(k, dst, [own(k, z)])
            add_z(dst, k, False)
            x_copy(k, z, other_of(k, z)).wait_recv()
            total(k, dst, [dst, from_x(k, z)])
        else:
            x_copy(k, z, hbm(k, z, 1 - x)).wait_recv()
            total(k, dst, [own(k, z), from_x(k, z)])
            add_z(dst, k, False)
        if not which:
            total(k, dn_out.at[section, part(k)], [dst])
            dn_copy(k, section, True).start()
            dn_copy(k, section, False).start()

        @pl.loop(0, rows // 16)
        def _(step):
            value = dst[pl.ds(pl.multiple_of(step * 16, 16), 16)]
            sq_rows[...] += jnp.sum(value * value, axis=0, keepdims=True)

    def of(which, direct=None):
        return [
            k for k in range(chunks)
            if SUM_CHUNKS[k][0] == which and (direct is None or SUM_CHUNKS[k][3] == direct)
        ]

    def pass_all(which, distance):
        for k in of(which):
            pass_on(k, distance)
            after(k, distance)

    def finish_all(which):
        for k in of(which, False) + of(which, True):
            finish(k)
            after(k, 0)

    def direct_all(which):
        for k in of(which, True):
            send_direct(k)

    for distance in (3, 2, 1):
        pass_all(0, distance)
    make_cond()
    pass_all(1, 3)
    direct_all(0)
    finish_all(0)
    pass_all(1, 2)
    make_hidden()
    pass_all(1, 1)
    for k in of(0):
        dn_copy(k, facing, False).wait_recv()
        dn_copy(k, facing, True).start()
    pass_all(2, 3)
    make_news()
    direct_all(1)
    finish_all(1)
    pass_all(2, 2)
    pass_all(2, 1)
    direct_all(2)
    finish_all(2)

    @pl.loop(0, 144 // 16)
    def _(step):
        rows = pl.ds(pl.multiple_of(step * 16, 16), 16)
        cross_src[rows] = to_half(jnp.where(core == 0, out[0, rows], out[1, rows]))

    crossing = pltpu.make_async_remote_copy(
        src_ref=cross_src, dst_ref=cross_out, send_sem=cross_sem.at[0], recv_sem=cross_sem.at[1],
        device_id={"section": sibling}, device_id_type=MESH,
    )
    sq_src[...] += jnp.sum(sq_rows[...])
    send_batch(norms, 9)
    crossing.start()
    wait_batch(norms, 9)
    sq_out[...] = jnp.sum(sq_all[...], axis=0)
    wait_batch(news, 8)
    crossing.wait()

    for k in range(chunks):
        for distance in (3, 2, 1, 0):
            def run(zz, up):
                if not SUM_CHUNKS[k][3]:
                    x_copy(k, zz, hbm(k, zz, 1 - x)).wait_send()
                elif distance == 0:
                    x_copy(k, zz, other_of(k, zz)).wait_send()
                if distance:
                    z_copy(k, zz, up, False).wait_send()
                    if SUM_CHUNKS[k][3]:
                        z_copy(k, zz, up, True).wait_send()
            each(distance, run)
        if not SUM_CHUNKS[k][0]:
            dn_copy(k, section, True).wait_send()
            dn_copy(k, section, False).wait_send()
            dn_copy(k, facing, True).wait_send()
            dn_copy(k, sibling, True).wait_recv()
            dn_copy(k, lax.rem(sibling + 2, 4), True).wait_recv()


def sum_gradients(g_dn, g_up, g_attn, d_mods, sums, ends, w_mod, w_fm, two_blocks, cond, pre, hidden, meta):
    n, width = lax.axis_size("dp"), cond.shape[1]
    f32 = jnp.float32
    if not ring_fits(n, width):
        return sum_plainly(g_dn, g_up, g_attn, d_mods, sums, ends, w_mod, w_fm, two_blocks, cond, pre, hidden, meta)
    chunks, images, devices = len(SUM_CHUNKS), 2 * n, 4 * n
    dma = lambda *count: pltpu.SemaphoreType.DMA(count)
    ring = pltpu.VMEM((3, Z, 144, HALF), BF)
    short = [rows for start, rows, direct in CHUNKS if direct][0]
    most = max(rows for start, rows, direct in CHUNKS)
    ring_o = pltpu.VMEM((3, Z, short, HALF), BF)
    hbm, vmem = pl.BlockSpec(memory_space=pl.ANY), pl.BlockSpec(memory_space=pltpu.VMEM)
    like = jax.ShapeDtypeStruct
    end_block = ends.shape[1:]
    shapes = (
        like((2, 144, HALF), f32), like((144, HALF), BF), like((4, 144, HALF), BF),
        like((144, 3 * D), f32), like((144, 2 * D), f32), like((144, 1024), f32), like((WIDE, FREQ), f32),
        like((144, D), f32), like((4,) + end_block, f32), like((devices, 24, 128), f32),
        like((4, 1, 3 * D), f32), like((1, 2 * D), f32), like((8, 128), f32),
    )
    return pl.pallas_call(
        sum_kernel,
        out_shape=shapes,
        in_specs=[hbm] * 3 + [vmem] * 10,
        out_specs=(vmem,) * len(shapes),
        scratch_shapes=[
            ring, ring_o, ring, pltpu.VMEM((3, short, HALF), BF),
            ring, ring_o, ring, ring_o, pltpu.VMEM((short, HALF), f32), pltpu.VMEM((most, HALF), f32),
            pltpu.VMEM((images, 48, 128), BF), pltpu.VMEM((images, SUM_ROWS, 128), f32),
            pltpu.VMEM((images,) + end_block, f32), pltpu.VMEM((images, 5 * D), BF),
            pltpu.VMEM(end_block, f32), pltpu.VMEM((images, WIDE), f32), pltpu.VMEM((4, images, WIDE), f32),
            pltpu.VMEM((images, 2 * D), BF), pltpu.VMEM((4, images, 2 * D), BF), pltpu.VMEM((1, 3 * D), f32),
            pltpu.VMEM((images, WIDE), BF), pltpu.VMEM((n, images, WIDE), f32), pltpu.VMEM((n, images, WIDE), f32),
            pltpu.VMEM((24, 128), f32), pltpu.VMEM((8, 128), f32), pltpu.VMEM((devices, 8, 128), f32),
            pltpu.VMEM((1, HALF), f32),
            pltpu.VMEM((144, HALF), BF),
            dma(2 * chunks * Z), dma(chunks * Z), dma(chunks * Z),
            dma(2 * chunks * Z), dma(2 * chunks * Z), dma(2 * chunks * Z), dma(2 * chunks * Z),
            dma(4 * chunks), dma(4 * chunks), dma(4 * chunks), dma(4 * chunks),
            dma(3, images), dma(3, images), dma(4, 4), dma(4, 4),
            dma(n), dma(n), dma(devices), dma(devices), dma(devices), dma(devices), dma(2), dma(10),
        ],
        compiler_params=pltpu.CompilerParams(
            collective_id=1, has_side_effects=True, vmem_limit_bytes=VMEM_BYTES
        ),
        cost_estimate=pl.CostEstimate(flops=0, bytes_accessed=400_000_000, transcendentals=0),
        name="sum_gradients",
    )(g_dn, g_up, g_attn, d_mods, sums, ends, w_mod, w_fm, two_blocks, cond, pre, hidden, meta)


def sum_plainly(g_dn, g_up, g_attn, d_mods, sums, ends, w_mod, w_fm, two_blocks, cond, pre, hidden, meta):
    n, width = lax.axis_size("dp"), cond.shape[1]
    section, images, f32 = lax.axis_index("section"), 2 * n, jnp.float32
    once = (section == 0).astype(f32)
    anchor = (lax.axis_index("dp") == 0).astype(f32)
    total = lambda grad: lax.psum_scatter(grad, "dp", scatter_dimension=0, tiled=True)
    dn_own, out = total(g_dn), jnp.stack([total(g_up), total(g_attn)]).astype(f32)
    dn_all = lax.all_gather(dn_own, "section")
    cross = swap(to_half(jnp.where(lax.rem(section, 2) == 0, out[0], out[1])), 1)
    d_mods, sums, ends = exchange(4, "stage", ("core", "each", "dp"), d_mods, sums, ends)
    d_mods = d_mods.reshape(images, 48 * 128)
    d_mod, d_fm = d_mods[:, : 3 * D], d_mods[:, 3 * D : 5 * D]
    sums, ends = jnp.sum(sums, axis=0), jnp.sum(ends, axis=0)
    cond_low = to_half(cond).astype(f32)
    own_cond = jnp.where(section == 0, cond, cond_low)
    d_silu = matmul_nt(d_mod, w_mod) + (section == 3).astype(f32) * matmul_nt(d_fm, w_fm)
    c_own = jnp.pad(silu_slope(own_cond) * d_silu, ((0, 0), (0, WIDE - width)))
    cs = column_sums(d_mod)[None]
    c_all, ends_all, d_fm, cs_all = exchange(5, "section", ("all",) * 4, c_own, ends, d_fm, cs)
    d_fm = d_fm[3]
    d_cond = to_half(c_all[3])
    for slot in (2, 1, 0):
        d_cond = to_half(d_cond.astype(f32) + c_all[slot])
    narrow = d_cond[:, :width]
    part = jnp.einsum("iw,jwk->jik", narrow, two_blocks, preferred_element_type=f32)
    (part,) = exchange(6, "dp", ("each",), part)
    d_pre = to_half(silu_slope(pre) * jnp.sum(part, axis=0))
    g_mod = matmul_tn(to_half(jax.nn.silu(own_cond)), d_mod)
    g_fm = matmul_tn(to_half(jax.nn.silu(cond_low)), d_fm)
    g_table = matmul_tn(narrow, one_hot(meta[:, FREQ : FREQ + 1], 1024))
    g_one = matmul_tn(d_pre, to_half(meta[:, :FREQ]))
    g_two = jnp.einsum("iw,jik->wjk", narrow, hidden, preferred_element_type=f32)
    g_two = g_two[:, :, :width].reshape(width, D)
    fm_sum = column_sums(d_fm)[None]
    slices = [column_sums(value).reshape(2, 128) for value in (d_pre, d_cond)]
    news = jnp.concatenate([sums, *slices, jnp.zeros((4, 128), f32)])
    square = lambda value: jnp.sum(value * value)
    squares = square(out) + square(dn_own.astype(f32)) + square(g_mod) + square(sums[:10])
    squares = squares + anchor * square(cs) + anchor * once * square(fm_sum)
    for value in (g_fm, g_table, g_one, g_two, ends_all[0], ends_all[3], *slices):
        squares = squares + once * square(value)
    news, squares = exchange(7, "every", ("all", "all"), news, jnp.broadcast_to(squares, (8, 128)))
    squares = jnp.sum(squares, axis=0)
    return (out, cross, dn_all, g_mod, g_fm, g_table, g_one, g_two, ends_all, news, cs_all, fm_sum, squares)


def exchange_kernel(axes, modes, *refs):
    count = len(modes)
    ins, outs = refs[:count], refs[count : 2 * count]
    send_sem, recv_sem, own_sem = refs[2 * count :]
    dp, section = lax.axis_index("dp"), lax.axis_index("section")
    n, sections = lax.axis_size("dp"), lax.axis_size("section")
    if axes == "dp":
        size, me, where = n, dp, lambda p: {"dp": p}
    elif axes == "section":
        size, me, where = sections, section, lambda p: {"section": p}
    elif axes == "stage":
        low = section - lax.rem(section, 2)
        size, me = 2 * n, dp * 2 + lax.rem(section, 2)
        where = lambda p: {"dp": p // 2, "section": low + lax.rem(p, 2)}
    else:
        size, me = n * sections, dp * sections + section
        where = lambda p: {"dp": p // sections, "section": lax.rem(p, sections)}

    def part(k, p):
        if modes[k] == "all":
            return ins[k]
        index = {"each": p, "dp": p // 2, "core": lax.rem(p, 2)}[modes[k]]
        return ins[k].at[index]

    def copy(k, step, src, slot, p):
        return pltpu.make_async_remote_copy(
            src_ref=src, dst_ref=outs[k].at[slot],
            send_sem=send_sem.at[k, step], recv_sem=recv_sem.at[k, step],
            device_id=where(p), device_id_type=MESH,
        )

    barrier = pltpu.get_barrier_semaphore()

    @pl.loop(1, size)
    def _(step):
        pl.semaphore_signal(barrier, 1, device_id=where(lax.rem(me + step, size)), device_id_type=MESH)

    for k in range(count):
        pltpu.make_async_copy(part(k, me), outs[k].at[me], own_sem.at[k]).start()
    pl.semaphore_wait(barrier, size - 1)

    @pl.loop(1, size)
    def _(step):
        p = lax.rem(me + step, size)
        for k in range(count):
            copy(k, step, part(k, p), me, p).start()

    for k in range(count):
        pltpu.make_async_copy(part(k, me), outs[k].at[me], own_sem.at[k]).wait()

    @pl.loop(1, size)
    def _(step):
        p = lax.rem(me + size - step, size)
        for k in range(count):
            copy(k, step, part(k, p), p, p).wait_recv()
            copy(k, step, part(k, p), p, p).wait_send()


def exchange(ident, axes, modes, *arrays):
    n, sections = lax.axis_size("dp"), lax.axis_size("section")
    size = {"dp": n, "section": sections, "stage": 2 * n, "every": n * sections}[axes]
    blocks = [a.shape if mode == "all" else a.shape[1:] for a, mode in zip(arrays, modes)]
    count = len(arrays)
    vmem = pl.BlockSpec(memory_space=pltpu.VMEM)
    return pl.pallas_call(
        partial(exchange_kernel, axes, modes),
        out_shape=tuple(jax.ShapeDtypeStruct((size,) + b, a.dtype) for a, b in zip(arrays, blocks)),
        in_specs=[vmem] * count,
        out_specs=(vmem,) * count,
        scratch_shapes=[
            pltpu.SemaphoreType.DMA((count, size)),
            pltpu.SemaphoreType.DMA((count, size)),
            pltpu.SemaphoreType.DMA((count,)),
        ],
        compiler_params=pltpu.CompilerParams(
            collective_id=ident, has_side_effects=True, vmem_limit_bytes=VMEM_BYTES
        ),
        cost_estimate=pl.CostEstimate(flops=0, bytes_accessed=30_000_000, transcendentals=0),
        name="exchange_" + axes,
    )(*arrays)


def rows_of(value, size):
    value = value.reshape(-1)
    return jnp.pad(value, (0, size * 128 - value.shape[0])).reshape(size, 128)


def row_count(length, unit=8):
    return -(-length // (128 * unit)) * unit


TILE = 768
STEPS = HALF // TILE
GELU_SCALE = math.sqrt(2.0 / math.pi)
SCALE = HEAD_DIM ** (-0.5)


def mean_rows(value):
    return jnp.mean(value, axis=-1, keepdims=True)


def normalized(x):
    centered = x - mean_rows(x)
    inverse = lax.rsqrt(mean_rows(centered * centered) + epsilon_norm)
    return (centered * inverse, inverse)


def modulated_back(normed, inverse, scale, d_xm):
    d_normed = d_xm * (1.0 + scale)
    d_x = inverse * (d_normed - mean_rows(d_normed) - normed * mean_rows(d_normed * normed))
    return (d_x, jnp.sum(d_xm, axis=0), jnp.sum(d_xm * normed, axis=0))


def window(head):
    low = HEAD_DIM * head // 128 * 128
    high = -(-HEAD_DIM * (head + 1) // 128) * 128
    lane = lax.broadcasted_iota(jnp.int32, (PATCHES, high - low), 1) + low
    return slice(low, high), (lane >= HEAD_DIM * head) & (lane < HEAD_DIM * (head + 1))


def own_lanes(mask, value):
    return jnp.where(mask, value, jnp.zeros_like(value))


def softmax_rows(scores):
    shifted = jnp.exp(scores - jnp.max(scores, axis=-1, keepdims=True))
    return shifted / jnp.sum(shifted, axis=-1, keepdims=True)


def half_of(ref, which, side):
    return ref.at[which, :, pl.ds(pl.multiple_of(side * HALF, 128) if which else side * HALF, HALF)]


def weight_copies(sources, targets, sem):
    return [pltpu.make_async_copy(src, dst, sem.at[k]) for k, (src, dst) in enumerate(zip(sources, targets))]


def forward_kernel(
    save, flags, x_ref, mod_a, mod_m, b_attn, b_up, b_down, w_blk, w_dn, out_ref, *refs
):
    if save:
        xm_ref, qkv_ref, att_ref, last_ref, branch_a_ref, mid_ref, xm2_ref, branch_m_ref, pre_ref = refs[:9]
        act_refs = refs[9:11]
        wa, wu, wd, acc, sem = refs[11:]
    else:
        xm_ref, qkv_ref, att_ref, mid_ref, xm2_ref, wa, wu, wd, acc, sem = refs
    copies = weight_copies(
        [half_of(w_blk, 0, 0), half_of(w_blk, 0, 1)]
        + [ref for side in (flags[0], 1 - flags[0]) for ref in (half_of(w_blk, 1, side), w_dn.at[side])],
        (wa.at[0], wa.at[1], wu.at[0], wd.at[0], wu.at[1], wd.at[1]),
        sem,
    )
    for copy in copies:
        copy.start()
    normed, unused = normalized(x_ref[...])
    xm_ref[...] = to_half(normed * (1.0 + mod_a[1:2]) + mod_a[0:1])
    acc[...] = jnp.zeros_like(acc)
    for k in range(3):
        if k != 1:
            copies[k // 2].wait()
        half, first = (0, D * k) if k < 2 else (1, 0)
        part = slice(D * k, D * (k + 1))
        qkv_ref[:, part] = to_half(
            matmul(xm_ref[...], wa[half, :, first : first + D]) + b_attn[:, part]
        )
    for head in range(HEADS):
        lanes, mask = window(head)
        at = lambda k: slice(D * k + lanes.start, D * k + lanes.stop)
        query = own_lanes(mask, qkv_ref[:, at(0)])
        probs = softmax_rows(matmul_nt(query, qkv_ref[:, at(1)]) * SCALE)
        acc[:, lanes] += own_lanes(mask, matmul(to_half(probs), qkv_ref[:, at(2)]))
    att_ref[...] = to_half(acc[...])
    branch = matmul(att_ref[...], wa[1, :, D:]) + b_attn[:, 3 * D :]
    if save:
        branch_a_ref[...] = branch
        last_ref[...] = jnp.where(flags[0] == 0, att_ref[...], xm_ref[...])
    mid_ref[...] = to_half(x_ref[...] + mod_a[2:3] * branch).astype(jnp.float32)
    normed, unused = normalized(mid_ref[...])
    xm2_ref[...] = to_half(normed * (1.0 + mod_m[1:2]) + mod_m[0:1])
    acc[...] = jnp.broadcast_to(b_down[...], acc.shape)
    for half in range(2):
        copies[2 + 2 * half].wait()
        copies[3 + 2 * half].wait()
        for step in range(STEPS):
            own = slice(TILE * step, TILE * (step + 1))
            part = slice(HALF * half + TILE * step, HALF * half + TILE * (step + 1))
            pre = matmul(xm2_ref[...], wu[half, :, own]) + b_up[:, part]
            cube = pre + 0.044715 * (pre * pre * pre)
            act = to_half(pre * (0.5 * (1.0 + jnp.tanh(GELU_SCALE * cube))))
            if save:
                pre_ref[:, part] = pre
                act_refs[half][:, own] = act
            acc[...] += matmul_nt(act, wd[half, :, own])
    if save:
        branch_m_ref[...] = acc[...]
    out = mid_ref[...] + mod_m[2:3] * acc[...]
    out_ref[...] = out.astype(out_ref.dtype)


def backward_kernel(
    flags, d_ref, x_ref, mid_ref, mod_a, mod_m, branch_a, branch_m, qkv_ref, pre_hbm, w_blk, w_dn,
    d_in_ref, d_mod_a, d_mod_m, grad_a, grad_m, d_pre_own, d_pre_sib, d_qkv_ref, right_own, right_sib,
    wa, wu, wd, pre_ref, acc, d_acc, d_att, sem,
):
    copies = weight_copies(
        (
            w_dn.at[flags[0]], pre_hbm, half_of(w_blk, 1, flags[0]),
            w_dn.at[1 - flags[0]], half_of(w_blk, 1, 1 - flags[0]),
            half_of(w_blk, 0, 1), half_of(w_blk, 0, 0),
        ),
        (wd.at[0], pre_ref, wu.at[0], wd.at[1], wu.at[1], wa.at[1], wa.at[0]),
        sem,
    )
    for copy in copies:
        copy.start()
    grad_m[...] = to_half(d_ref[...] * mod_m[2:3])
    d_mod_m[2:3] = jnp.sum(d_ref[...] * branch_m[...], axis=0)[None]
    acc[...] = jnp.zeros_like(acc)
    for half in range(2):
        copies[0 if half == 0 else 3].wait()
        if half == 0:
            copies[1].wait()
        copies[2 if half == 0 else 4].wait()
        for step in range(STEPS):
            own = slice(TILE * step, TILE * (step + 1))
            part = slice(HALF * half + TILE * step, HALF * half + TILE * (step + 1))
            d_act = matmul(grad_m[...], wd[half, :, own])
            pre = pre_ref[:, part]
            square = pre * pre
            tanh = jnp.tanh(GELU_SCALE * (pre + 0.044715 * (square * pre)))
            slope = 0.5 * (1.0 + tanh) + (0.5 * pre) * (1.0 - tanh * tanh) * (
                GELU_SCALE * (1.0 + (3.0 * 0.044715) * square)
            )
            d_pre = to_half(d_act * slope)
            (d_pre_sib if half else d_pre_own)[:, own] = d_pre
            acc[...] += matmul_nt(d_pre, wu[half, :, own])
    normed, inverse = normalized(mid_ref[...])
    d_x, d_shift, d_scale = modulated_back(normed, inverse, mod_m[1:2], acc[...])
    d_mod_m[0:1] = d_shift[None]
    d_mod_m[1:2] = d_scale[None]
    acc[...] = to_half(d_ref[...] + d_x).astype(jnp.float32)

    d_mod_a[2:3] = jnp.sum(acc[...] * branch_a[...], axis=0)[None]
    grad_a[...] = to_half(acc[...] * mod_a[2:3])
    copies[5].wait()
    d_att[...] = to_half(matmul_nt(grad_a[...], wa[1, :, D:]))
    d_acc[...] = jnp.zeros_like(d_acc)
    for head in range(HEADS):
        lanes, mask = window(head)
        at = lambda k: slice(D * k + lanes.start, D * k + lanes.stop)
        query, key, value = (qkv_ref[:, at(k)] for k in range(3))
        probs = softmax_rows(matmul_nt(own_lanes(mask, query), key) * SCALE)
        outer = d_att[:, lanes]
        d_acc[:, at(2)] += own_lanes(mask, matmul_tn(to_half(probs), outer))
        d_probs = matmul_nt(own_lanes(mask, outer), value)
        d_scores = to_half(probs * (d_probs - jnp.sum(probs * d_probs, axis=-1, keepdims=True)))
        d_acc[:, at(0)] += own_lanes(mask, matmul(d_scores, key) * SCALE)
        d_acc[:, at(1)] += own_lanes(mask, matmul_tn(d_scores, query) * SCALE)
    d_qkv_ref[...] = to_half(d_acc[...])
    first = flags[0] == 0
    pairs = ((d_qkv_ref[:, :D], d_qkv_ref[:, 2 * D :]), (d_qkv_ref[:, D : 2 * D], grad_a[...]))
    for k, (one, two) in enumerate(pairs):
        right_own[:, D * k : D * (k + 1)] = jnp.where(first, one, two)
        right_sib[:, D * k : D * (k + 1)] = jnp.where(first, two, one)
    copies[6].wait()
    d_xm = matmul_nt(d_qkv_ref[:, 2 * D :], wa[1, :, :D]) + matmul_nt(d_qkv_ref[:, : 2 * D], wa[0])
    normed, inverse = normalized(x_ref[...])
    d_x, d_shift, d_scale = modulated_back(normed, inverse, mod_a[1:2], d_xm)
    d_mod_a[0:1] = d_shift[None]
    d_mod_a[1:2] = d_scale[None]
    d_in_ref[...] = to_half(acc[...] + d_x)


def weight_scratch():
    return [pltpu.VMEM((2, D, HALF), BF)] * 3


def stage_cost():
    flops = 2 * PATCHES * D * 12 * D + 4 * PATCHES * PATCHES * D
    return pl.CostEstimate(flops=2 * flops, bytes_accessed=24 * D * D, transcendentals=2 * PATCHES * FF)


def stage_forward(save, x_in, weights):
    flags, mod_a, mod_m, w_blk, w_dn, b_attn, b_up, b_down = weights
    vmem, hbm = pl.BlockSpec(memory_space=pltpu.VMEM), pl.BlockSpec(memory_space=pl.ANY)
    smem = pl.BlockSpec(memory_space=pltpu.SMEM)
    like = lambda columns, kind: jax.ShapeDtypeStruct((PATCHES, columns), kind)
    tokens, wide = pltpu.VMEM((PATCHES, D), BF), pltpu.VMEM((PATCHES, 3 * D), BF)
    total = pltpu.VMEM((PATCHES, D), jnp.float32)
    f32 = jnp.float32
    if save:
        shapes = [like(D, f32), like(D, BF), like(3 * D, BF), like(D, BF), like(D, BF), like(D, f32), like(D, f32)]
        shapes += [like(D, BF), like(D, f32), like(FF, f32), like(HALF, BF), like(HALF, BF)]
        scratch = []
    else:
        shapes, scratch = [like(D, BF)], [tokens, wide, tokens, total, tokens]
    return pl.pallas_call(
        partial(forward_kernel, save),
        out_shape=tuple(shapes),
        in_specs=[smem] + [vmem] * 6 + [hbm] * 2,
        out_specs=(vmem,) * len(shapes),
        scratch_shapes=scratch + weight_scratch() + [total, pltpu.SemaphoreType.DMA((6,))],
        compiler_params=pltpu.CompilerParams(vmem_limit_bytes=VMEM_BYTES),
        cost_estimate=stage_cost(),
        name="stage_forward",
    )(flags, x_in, mod_a, mod_m, b_attn, b_up, b_down, w_blk, w_dn)


def stage_backward(d_out, x_in, weights, kept):
    flags, mod_a, mod_m, w_blk, w_dn, b_attn, b_up, b_down = weights
    xm_a, qkv, att, last, branch_a, x_mid, xm_m, branch_m, pre, act_own, act_sib = kept
    vmem, hbm = pl.BlockSpec(memory_space=pltpu.VMEM), pl.BlockSpec(memory_space=pl.ANY)
    smem = pl.BlockSpec(memory_space=pltpu.SMEM)
    like = lambda columns, kind: jax.ShapeDtypeStruct((PATCHES, columns), kind)
    mods = jax.ShapeDtypeStruct((3, D), jnp.float32)
    return pl.pallas_call(
        backward_kernel,
        out_shape=(like(D, BF), mods, mods, like(D, BF), like(D, BF))
        + (like(HALF, BF), like(HALF, BF), like(3 * D, BF), like(HALF, BF), like(HALF, BF)),
        in_specs=[smem] + [vmem] * 8 + [hbm] * 3,
        out_specs=(vmem,) * 10,
        scratch_shapes=weight_scratch()
        + [
            pltpu.VMEM((PATCHES, FF), jnp.float32),
            pltpu.VMEM((PATCHES, D), jnp.float32),
            pltpu.VMEM((PATCHES, 3 * D), jnp.float32),
            pltpu.VMEM((PATCHES, D), BF),
            pltpu.SemaphoreType.DMA((7,)),
        ],
        compiler_params=pltpu.CompilerParams(vmem_limit_bytes=VMEM_BYTES),
        cost_estimate=stage_cost(),
        name="stage_backward",
    )(flags, d_out, x_in, x_mid, mod_a, mod_m, branch_a, branch_m, qkv, pre, w_blk, w_dn)


COLUMNS = 384


def products_kernel(
    flags, dn_own, dn_sib, up_own, up_sib, xa_own, xa_sib, att_own, last_sib,
    act_own, act_sib, pre_own, pre_sib, right_own, right_sib,
    g_dn, g_up, g_attn, t_dn, t_up, t_one, t_two,
):
    step = pl.program_id(0)

    @pl.when(step == 0)
    def _():
        last_own = jnp.where(flags[0] == 0, xa_own[...], att_own[...])
        for target, own, sib in (
            (t_dn, dn_own[...], dn_sib), (t_up, up_own[...], up_sib),
            (t_one, xa_own[...], xa_sib), (t_two, last_own, last_sib),
        ):
            target[:, :PATCHES] = own.T
            target[:, PATCHES:] = sib[...].T

    def product(left, own, sib):
        return to_half(
            matmul(left[:, :PATCHES], own[...]) + matmul(left[:, PATCHES:], sib[...])
        )

    g_dn[...] = product(t_dn, act_own, act_sib)
    g_up[...] = product(t_up, pre_own, pre_sib)

    @pl.when(step < D // COLUMNS)
    def _():
        g_attn[...] = product(t_one, right_own, right_sib)

    @pl.when(step >= D // COLUMNS)
    def _():
        g_attn[...] = product(t_two, right_own, right_sib)


def products(flags, lefts, rights):
    left = whole_spec((PATCHES, D))
    right = pl.BlockSpec((PATCHES, COLUMNS), lambda step: (0, step))
    out = pl.BlockSpec((D, COLUMNS), lambda step: (0, step))
    return pl.pallas_call(
        products_kernel,
        grid=(HALF // COLUMNS,),
        out_shape=(jax.ShapeDtypeStruct((D, HALF), BF),) * 3,
        in_specs=[pl.BlockSpec(memory_space=pltpu.SMEM)] + [left] * 8 + [right] * 6,
        out_specs=(out,) * 3,
        scratch_shapes=[pltpu.VMEM((D, 2 * PATCHES), BF)] * 4,
        compiler_params=pltpu.CompilerParams(vmem_limit_bytes=VMEM_BYTES),
        cost_estimate=pl.CostEstimate(
            flops=12 * PATCHES * D * HALF, bytes_accessed=10 * D * HALF, transcendentals=0
        ),
        name="products",
    )(flags, *lefts, *rights)


def whole_spec(shape):
    return pl.BlockSpec(shape, lambda step: (0,) * len(shape))


SUM_ROWS = 16


def collect_kernel(flags_ref, *refs):
    tokens, d_pres, mods, fm_ref, extra_ref, tok_ref, head_ref = refs[:4], refs[4:6], refs[6:8], *refs[8:12]
    sums_ref, mods_ref, ends_ref, rows_ref = refs[12:]
    core, stage = flags_ref[0], flags_ref[1]
    ones = jnp.ones((8, PATCHES), BF)
    total = lambda value: matmul(ones, value)[0:1]
    sums_ref[...] = jnp.zeros_like(sums_ref)
    rows = [total(tokens[0][:, D * k : D * (k + 1)]) for k in range(3)]
    rows += [total(ref[...]) for ref in tokens[1:]]
    halves = [[total(ref[:, D * k : D * (k + 1)]) for k in range(2)] for ref in d_pres]
    own = halves[0] + halves[1]
    order = [jnp.where(core == 0, own[k], own[(k + 2) % 4]) for k in range(4)]
    last = jnp.where(stage == 0, rows[5], extra_ref[0:1])
    for place, row in enumerate(rows[:4] + order + [rows[4], last, extra_ref[1:2]]):
        sums_ref[place : place + 1, :D] = row
    ends = jnp.where(stage == 0, matmul_tn(tok_ref[...], tokens[3][...]), head_ref[...])
    ends_ref[...] = jnp.zeros_like(ends_ref)
    width = D // ends_ref.shape[0]
    for index in range(ends_ref.shape[0]):
        ends_ref[index, :, :width] = ends[:, width * index : width * (index + 1)]
    rows_ref[...] = jnp.zeros_like(rows_ref)
    for k in range(2):
        for row in range(5):
            source = mods[k][row : row + 1, :] if row < 3 else fm_ref[row - 3 : row - 2, :]
            for part in range(D // 128):
                at = row * (D // 128) + part
                rows_ref[at : at + 1] = source[:, 128 * part : 128 * (part + 1)]
        mods_ref[k] = to_half(rows_ref[...])


def collect(flags, tokens, d_pres, mods, fm, extra, tok, g_head):
    n = lax.axis_size("dp")
    vmem = pl.BlockSpec(memory_space=pltpu.VMEM)
    return pl.pallas_call(
        collect_kernel,
        out_shape=(
            jax.ShapeDtypeStruct((SUM_ROWS, 128 * max(2 * n, 9)), jnp.float32),
            jax.ShapeDtypeStruct((2, 48, 128), BF),
            jax.ShapeDtypeStruct((n, HEAD_OUT, WIDE), jnp.float32),
        ),
        scratch_shapes=[pltpu.VMEM((48, 128), jnp.float32)],
        in_specs=[pl.BlockSpec(memory_space=pltpu.SMEM)] + [vmem] * 12,
        out_specs=(vmem,) * 3,
        compiler_params=pltpu.CompilerParams(vmem_limit_bytes=VMEM_BYTES),
        name="collect",
    )(flags, *tokens, *d_pres, *mods, fm, extra, tok, g_head)


def final_step(x_out, fmod, w_head, b_head, target, counts, loss_scale):
    normed, inverse = normalized(x_out)
    xf_half = to_half(normed * (1.0 + fmod[1:2]) + fmod[0:1])
    error = matmul_nt(xf_half, w_head) + b_head - target
    loss = counts * jnp.sum(error * error)
    d_pred = to_half(2.0 * loss_scale * counts * error)
    g_head = matmul_tn(d_pred, xf_half)
    d_x, d_shift, d_scale = modulated_back(normed, inverse, fmod[1:2], matmul(d_pred, w_head))
    return (loss, d_x, jnp.stack([d_shift, d_scale]), g_head, column_sums(d_pred))


def nesterov(weight, moment, average, grad, factor):
    clipped = grad * factor
    moment_new = momentum_rate * moment + clipped
    weight_new = weight - learn_rate * (clipped + momentum_rate * moment_new)
    average_new = ema_decay * average + (1.0 - ema_decay) * weight_new
    return (weight_new, moment_new, average_new, weight_new.astype(jnp.bfloat16))


def swap(array, by):
    peers = lax.axis_size("section")
    return lax.ppermute(array, "section", [(k, k ^ by) for k in range(peers)])


def pick(parts, index):
    return lax.dynamic_index_in_dim(parts, index, 0, keepdims=False)


def body(
    latents, noise, timesteps, labels, null_mask, valid,
    mod_w, mod_m, mod_e, block_w, block_m, block_e, down_w, down_m, down_e,
    stem_w, stem_m, stem_e, tail_w, tail_m, tail_e, biases, bias_m, bias_e,
):
    place = lax.axis_index("dp")
    section = lax.axis_index("section")
    stage = section // 2
    core = lax.rem(section, 2)
    even = core == 0
    n = lax.axis_size("dp")
    width = D // n

    flags = jnp.stack([core, stage]).astype(jnp.int32)
    downs, stems = jnp.swapaxes(down_w, 1, 2), stem_w.T
    stem_half, tail_half, mod_half_w = to_half(stems), to_half(tail_w), to_half(mod_w[0])
    dn_half = to_half(lax.dynamic_slice(downs, (stage, 0, core * HALF), (1, width, HALF))[0])
    at_one, at_two = NCLS + PATCH_IN, NCLS + PATCH_IN + FREQ
    w_two = stem_half[:, at_two:]
    table = jnp.pad(stem_half[:, :NCLS], ((0, 0), (0, -NCLS % 128)))
    w_fm = tail_half[:, : 2 * D]
    to_wide = lambda value: jnp.pad(value, ((0, 0),) * (value.ndim - 1) + ((0, WIDE - width),))
    ends = to_wide(jnp.concatenate([stem_half[:, NCLS:at_one], tail_half[:, 2 * D :]], axis=1).T)
    w_one = jnp.pad(stem_half[:, at_one:at_two], ((0, WIDE - width), (0, 0)))
    two_blocks = to_wide(w_two.reshape(width, n, width)).transpose(1, 0, 2)
    classes = jnp.where(null_mask > 0, NCLS - 1, labels)
    freq = to_half(time_features(timesteps.astype(jnp.float32))).astype(jnp.float32)
    facts = jnp.stack([classes, valid], axis=1).astype(jnp.float32)
    meta = jnp.concatenate([freq, facts, jnp.zeros((2, META - FREQ - 2), jnp.float32)], axis=1)
    b_one, b_two = (lax.dynamic_slice_in_dim(biases, k * D + place * width, width)[None] for k in (31, 32))
    w_blk, w_dn, meta, ends, pre_own, hidden_all, cond, mods = gather_weights(
        to_half(block_w[0]), dn_half, meta, ends, w_one, two_blocks, table, mod_half_w, w_fm,
        to_wide(b_one), b_two,
    )
    ends = ends[:, :, :width].transpose(1, 0, 2).reshape(ROWS_END, D)
    w_patch_all, w_head_all = ends[:PATCH_IN], ends[PATCH_IN:]
    images = 2 * n
    count = jnp.sum(meta[:, FREQ + 1])
    loss_scale = 1.0 / (count * PATCHES * HEAD_OUT)
    mods = mods.reshape(2, 8 * PIECE)
    bias_of = lambda first, length: lax.dynamic_slice_in_dim(biases, first, length)
    mod_a = (mods[0, : 3 * D] + bias_of(6 * D * stage, 3 * D)).reshape(3, D)
    mod_b = (mods[1, : 3 * D] + bias_of(6 * D * stage + 3 * D, 3 * D)).reshape(3, D)
    fmod = (mods[0, 3 * D : 5 * D] + biases[33 * D : 35 * D]).reshape(2, D)
    weights = (
        flags, mod_a, mod_b, w_blk, w_dn,
        bias_of(12 * D + 8 * D * stage, 4 * D)[None],
        jnp.concatenate(
            [bias_of(16 * D + 8 * D * stage + HALF * half, HALF)[None] for half in (core, 1 - core)], axis=1
        ),
        bias_of(28 * D + D * stage, D)[None],
    )

    step = pick(timesteps, core).astype(jnp.float32)
    signal, spread = noise_levels(step)
    lat, noi = pick(latents, core)[None], pick(noise, core)[None]
    counts = pick(valid, core).astype(jnp.float32)
    tok_half = to_half(patchify(signal * lat + spread * noi))[0]
    target = jnp.concatenate([patchify(signal * noi - spread * lat), patchify(noi)], axis=2)[0]
    x_first = matmul(tok_half, w_patch_all) + biases[30 * D : 31 * D] + position_table(GRID // 2, D)

    x_hop = swap(stage_forward(False, x_first, weights)[0], 2)
    x_in = jnp.where(stage == 0, x_first, x_hop.astype(jnp.float32))
    x_out, *kept = stage_forward(True, x_in, weights)
    loss, d_final, d_fmod, g_head, b_head = final_step(
        x_out, fmod, w_head_all, biases[35 * D :], target, counts, loss_scale
    )
    xm_a, qkv, attended, last_sib, branch_a, x_mid, xm_b, branch_b, pre, act_own, act_sib = kept
    d_hop = swap(stage_backward(d_final, x_in, weights, kept)[0], 2)
    d_out = jnp.where(stage == 1, d_final, d_hop.astype(jnp.float32))
    d_first, d_mod_a, d_mod_b, d_branch_a, d_branch_b, d_pre_own, d_pre_sib, d_qkv, right_own, right_sib = (
        stage_backward(d_out, x_in, weights, kept)
    )

    act_come, xb_come, xa_come, last_come = swap((act_sib, xm_b, xm_a, last_sib), 1)
    branch_come, pre_come, right_come = swap((d_branch_b, d_pre_sib, right_sib), 1)
    g_dn, g_up, g_attn = products(
        flags,
        (d_branch_b, branch_come, xm_b, xb_come, xm_a, xa_come, attended, last_come),
        (act_own, act_come, d_pre_own, pre_come, right_own, right_come),
    )

    extra = jnp.stack([jnp.pad(b_head, (0, D - HEAD_OUT)), jnp.pad(loss[None], (0, D - 1))])
    d_fmod = jnp.where(stage == 1, d_fmod, jnp.zeros_like(d_fmod))
    tok_wide = jnp.pad(tok_half, ((0, 0), (0, HEAD_OUT - PATCH_IN)))
    own_sums, d_mods, own_ends = collect(
        flags, (d_qkv, d_branch_a, d_branch_b, d_first), (d_pre_own, d_pre_sib), (d_mod_a, d_mod_b), d_fmod,
        extra, tok_wide, g_head,
    )
    own_sums = own_sums.reshape(SUM_ROWS, -1, 128).transpose(1, 0, 2)[: 2 * n]
    halves, crossed, dn_all, g_mod, g_fm, g_table, g_one, g_two, ends_all, news, mod_sums, fm_sum, squares = (
        sum_gradients(
            g_dn, g_up, g_attn, d_mods, own_sums, own_ends, mod_half_w, w_fm, two_blocks, cond, pre_own,
            hidden_all, meta,
        )
    )
    crossed = crossed.astype(jnp.float32)
    g_blk = jnp.concatenate(
        [jnp.where(even, halves[1], crossed), jnp.where(even, crossed, halves[0])], axis=1
    )
    dn_all = dn_all.astype(jnp.float32)
    down_both = jnp.stack([jnp.concatenate([dn_all[2 * k], dn_all[2 * k + 1]], axis=1) for k in range(2)])
    ends = [ends_all[k, :, :width].T for k in (0, 3)]
    g_stem = jnp.concatenate(
        [g_table[:, :NCLS], ends[0][:, :PATCH_IN], g_one[:width], g_two], axis=1
    )
    g_tail = jnp.concatenate([g_fm, ends[1]], axis=1)

    news = news.reshape(n, 4, -1, 128)
    stages = []
    for k in range(2):
        pieces = news[:, 2 * k : 2 * k + 2, :SUM_ROWS].reshape(2 * n, SUM_ROWS, 128)[: D // 128]
        stages.append(pieces.transpose(1, 0, 2).reshape(-1))
    slices = news[:, 0, SUM_ROWS : SUM_ROWS + 4].reshape(n, 2, WIDE)[:, :, :width]
    bias_grad = jnp.concatenate(
        [mod_sums.reshape(-1)]
        + [part[: 8 * D] for part in stages]
        + [part[8 * D : 9 * D] for part in stages]
        + [stages[0][9 * D : 10 * D]]
        + [slices[:, 0].reshape(-1), slices[:, 1].reshape(-1)]
        + [fm_sum[0], stages[1][9 * D : 9 * D + HEAD_OUT]]
    )
    loss_sum = stages[1][10 * D]
    grad_norm = jnp.sqrt(squares[0, 0])
    factor = jnp.minimum(1.0, clip_limit / (grad_norm + 1e-06))
    mod_out = nesterov(mod_w, mod_m, mod_e, g_mod[None], factor)
    block_out = nesterov(block_w, block_m, block_e, g_blk[None], factor)
    flip = lambda value: jnp.swapaxes(value, 1, 2)
    down_out = tuple(map(flip, nesterov(downs, flip(down_m), flip(down_e), down_both, factor)))
    stem_out = tuple(value.T for value in nesterov(stems, stem_m.T, stem_e.T, g_stem, factor))
    tail_out = nesterov(tail_w, tail_m, tail_e, g_tail, factor)
    bias_out = nesterov(biases, bias_m, bias_e, bias_grad, factor)
    return (
        (loss_sum, count, grad_norm)
        + mod_out + block_out + down_out + stem_out + tail_out + bias_out
    )


def solution(mesh):
    images = (P("dp", None, None, None),) * 2 + (P("dp"),) * 4
    owned = P("section", "dp", None)
    states = (owned,) * 6 + (P(None, None, "dp"),) * 3 + (P(None, "dp"),) * 3 + (P("dp", None),) * 3 + (P(),) * 3
    updates = (owned,) * 8 + (P(None, None, "dp"),) * 4 + (P(None, "dp"),) * 4 + (P("dp", None),) * 4 + (P(),) * 4
    return jax.shard_map(
        body,
        mesh=mesh,
        in_specs=images + states,
        out_specs=(P(), P(), P()) + updates,
        check_vma=False,
    )
```

```python
from functools import partial
import math

import jax
import jax.numpy as jnp
from jax import lax
from jax.experimental import pallas as pl
from jax.experimental.pallas import tpu as pltpu
from jax.sharding import PartitionSpec as P

HEADS = 16
HEAD_DIM = 72
D = 1152
FF = 4608
HALF = FF // 2
NCLS = 1001
FREQ = 256
GRID = 32
PATCHES = 256
PATCH_IN = 16
HEAD_OUT = 32
LAYERS = 2
NBIAS = 40352


epsilon_norm = 1e-06
momentum_rate = 0.9
ema_decay = 0.9
learn_rate = 4000.0
clip_limit = 0.02
MESH = pl.DeviceIdType.MESH
BF = jnp.bfloat16


def matmul(left, right):
    return jnp.dot(left, right, preferred_element_type=jnp.float32)


def matmul_nt(left, right):
    return lax.dot_general(
        left, right, (((1,), (1,)), ((), ())), preferred_element_type=jnp.float32
    )


def matmul_tn(left, right):
    return lax.dot_general(
        left, right, (((0,), (0,)), ((), ())), preferred_element_type=jnp.float32
    )


def to_half(value):
    return value.astype(BF)


def column_sums(value):
    return jnp.sum(value.astype(jnp.float32), axis=0)


def silu_back(value, grad):
    return jax.vjp(jax.nn.silu, value)[1](grad)[0]


def patchify(field):
    images, side = (field.shape[0], field.shape[1] // 2)
    return (
        field.reshape(images, side, 2, side, 2, 4)
        .transpose(0, 1, 3, 2, 4, 5)
        .reshape(images, side * side, 16)
    )


def sincos_rows(places, width):
    omega = 1.0 / 10000.0 ** (jnp.arange(width // 2, dtype=jnp.float32) / (width // 2))
    angle = places[:, None] * omega[None, :]
    return jnp.concatenate([jnp.sin(angle), jnp.cos(angle)], axis=1)


def position_table(side, width):
    line = sincos_rows(jnp.arange(side, dtype=jnp.float32), width // 2)
    column = jnp.broadcast_to(line[None], (side, side, width // 2))
    row = jnp.broadcast_to(line[:, None], (side, side, width // 2))
    return jnp.concatenate([column, row], axis=2).reshape(side * side, width)


def time_features(steps):
    half = FREQ // 2
    freqs = jnp.exp(-math.log(10000.0) * jnp.arange(half, dtype=jnp.float32) / half)
    angle = steps[:, None] * freqs[None, :]
    return jnp.concatenate([jnp.cos(angle), jnp.sin(angle)], axis=1)


def noise_levels(steps):
    level = jnp.cos((steps / 1000.0 + 0.008) / 1.008 * (math.pi / 2)) ** 2
    return (jnp.sqrt(level), jnp.sqrt(1.0 - level))


Z, X = 4, 2
GATHER_CHUNKS = (
    (0, 0, 48, True), (0, 48, 48, True), (0, 96, 48, False),
    (1, 0, 48, False), (1, 48, 48, False), (1, 96, 48, False),
)
CHUNKS = ((0, 16, True), (16, 32, False), (48, 32, False), (80, 32, False), (112, 32, False))
META = 384
WIDE = 256
ROWS_END = PATCH_IN + HEAD_OUT
PIECE = 768


def ring_fits(n, rows):
    return n == Z * X and rows == 144


def one_hot(classes, width):
    lane = lax.broadcasted_iota(jnp.int32, (classes.shape[0], width), 1).astype(jnp.float32)
    return to_half(jnp.maximum(1.0 - jnp.abs(lane - classes), 0.0))


def gather_kernel(
    blk_hbm, dn_hbm, stem_hbm, mod_hbm, tail_hbm, meta_ref, ends_ref, b_one, b_two,
    out_blk, out_dn, meta_out, ends_out, pre_out, hidden_out, cond_out, mods_out, mod_ref, fm_ref, two_ref,
    blk_f, dn_f, stem_f, mod_f, tail_f, blk_ref, dn_ref, one_ref, table_ref, load_sem, metas, hidden, part, parts, arrived_parts,
    meta_send, meta_recv, ends_send, ends_recv, hid_send, hid_recv, part_send, part_recv, local_sem,
    up_sem, down_sem, x_sem, sib_sem, recv_sem, sib_recv, own_sem,
):
    me = lax.axis_index("dp")
    section = lax.axis_index("section")
    z, x = me // X, lax.rem(me, X)
    core = lax.rem(section, 2)
    sibling = section + 1 - 2 * core
    across = me + 1 - 2 * x
    chunks = len(GATHER_CHUNKS)
    low = section - core
    group, place_in = Z * X * 2, me * 2 + core
    where = lambda p: {"dp": p // 2, "section": low + lax.rem(p, 2)}
    has_up, has_down = z < Z - 1, z > 0

    stage_rows = dn_hbm.at[section // 2, :, pl.ds(pl.multiple_of(core * HALF, 128), HALF)]
    loads = [
        pltpu.make_async_copy(src, dst, load_sem.at[k])
        for k, (src, dst) in enumerate(
            ((blk_hbm, blk_f), (stage_rows, dn_f), (stem_hbm, stem_f), (mod_hbm, mod_f), (tail_hbm, tail_f))
        )
    ]
    for copy_in in loads:
        copy_in.start()
    barrier = pltpu.get_barrier_semaphore()

    @pl.loop(1, group)
    def _(step):
        pl.semaphore_signal(
            barrier, 1, device_id=where(lax.rem(place_in + step, group)), device_id_type=MESH
        )

    pl.semaphore_wait(barrier, group - 1)

    def to_dp(src, dst, send, recv, step, p, slot):
        return pltpu.make_async_remote_copy(
            src_ref=src, dst_ref=dst.at[slot], send_sem=send.at[step], recv_sem=recv.at[step],
            device_id={"dp": p}, device_id_type=MESH,
        )

    meta_copy = partial(to_dp, meta_ref, metas, meta_send, meta_recv)
    ends_copy = partial(to_dp, ends_ref, ends_out, ends_send, ends_recv)
    hidden_copy = partial(to_dp, hidden, hidden_out, hid_send, hid_recv)

    def part_copy(step, p, slot):
        return pltpu.make_async_remote_copy(
            src_ref=parts.at[p], dst_ref=arrived_parts.at[slot],
            send_sem=part_send.at[step], recv_sem=part_recv.at[step],
            device_id=where(p), device_id_type=MESH,
        )

    own_meta = pltpu.make_async_copy(meta_ref, metas.at[me], local_sem.at[0])
    own_ends = pltpu.make_async_copy(ends_ref, ends_out.at[me], local_sem.at[1])
    own_hidden = pltpu.make_async_copy(hidden, hidden_out.at[me], local_sem.at[2])
    own_part = pltpu.make_async_copy(parts.at[place_in], arrived_parts.at[place_in], local_sem.at[3])

    def send_all(copy_to, size, index):
        @pl.loop(1, size)
        def _(step):
            copy_to(step, lax.rem(index + step, size), index).start()

    def wait_all(copy_to, size, index):
        @pl.loop(1, size)
        def _(step):
            p = lax.rem(index + size - step, size)
            copy_to(step, p, p).wait_recv()
            copy_to(step, p, p).wait_send()

    own_meta.start()
    own_ends.start()
    send_all(meta_copy, Z * X, me)

    def place(owner, k, side):
        which, first, rows, unused = GATHER_CHUNKS[k]
        return (out_dn if which else out_blk).at[side, pl.ds(pl.multiple_of(owner * 144 + first, 16), rows)]

    def source(owner, k, mine):
        if not mine:
            return place(owner, k, core)
        which, first, rows, unused = GATHER_CHUNKS[k]
        return (dn_ref if which else blk_ref).at[pl.ds(first, rows)]

    def copy(owner, k, mine, sem, target):
        unit = owner * chunks + k
        return pltpu.make_async_remote_copy(
            src_ref=source(owner, k, mine),
            dst_ref=place(owner, k, core),
            send_sem=sem.at[unit],
            recv_sem=recv_sem.at[unit],
            device_id={"dp": target},
            device_id_type=MESH,
        )

    def to_sibling(owner, k, mine):
        unit = owner * chunks + k
        return pltpu.make_async_remote_copy(
            src_ref=source(owner, k, mine),
            dst_ref=place(owner, k, core),
            send_sem=sib_sem.at[unit],
            recv_sem=sib_recv.at[unit],
            device_id={"section": sibling},
            device_id_type=MESH,
        )

    def own_copy(k):
        return pltpu.make_async_copy(source(me, k, True), place(me, k, core), own_sem.at[k])

    def arrived(owner, k):
        copy(owner, k, False, x_sem, across).wait_recv()

    for which in range(2):
        loads[which].wait()

        @pl.loop(0, 144 // 16)
        def _(step):
            rows = pl.ds(pl.multiple_of(step * 16, 16), 16)
            if which:
                dn_ref[rows] = to_half(dn_f[rows])
            else:
                blk_ref[rows] = to_half(blk_f[rows])

    for k in range(chunks):
        @pl.when(has_up)
        def _():
            copy(me, k, True, up_sem, me + X).start()

        @pl.when(has_down)
        def _():
            copy(me, k, True, down_sem, me - X).start()

        copy(me, k, True, x_sem, across).start()
        own_copy(k).start()
        to_sibling(me, k, True).start()

    send_all(ends_copy, Z * X, me)

    at_one, at_two = NCLS + PATCH_IN, NCLS + PATCH_IN + FREQ
    for copy_in in loads[2:]:
        copy_in.wait()
    for ref in (table_ref, one_ref, two_ref):
        ref[...] = jnp.zeros_like(ref)
    table_ref[:, :NCLS] = to_half(stem_f[:, :NCLS])
    one_ref[:144] = to_half(stem_f[:, at_one:at_two])
    for index in range(Z * X):
        two_ref[index, :, :144] = to_half(stem_f[:, at_two + 144 * index : at_two + 144 * (index + 1)])
    mod_ref[...] = to_half(mod_f[...])
    fm_ref[...] = to_half(tail_f[:, : 2 * D])

    def make_hidden():
        own_meta.wait()
        wait_all(meta_copy, Z * X, me)
        for index in range(Z * X):
            meta_out[2 * index : 2 * index + 2] = metas[index]
        pre = matmul_nt(to_half(meta_out[:, :FREQ]), one_ref[...]) + b_one[...]
        pre_out[...] = pre
        hidden[...] = to_half(jax.nn.silu(pre))
        own_hidden.start()
        send_all(hidden_copy, Z * X, me)

    def make_parts():
        own_hidden.wait()
        wait_all(hidden_copy, Z * X, me)
        cond = matmul_nt(one_hot(meta_out[:, FREQ : FREQ + 1], table_ref.shape[1]), table_ref[...]) + b_two[...]
        for index in range(Z * X):
            cond = cond + matmul_nt(hidden_out[index], two_ref[index])
        cond_out[...] = cond
        cond_low = to_half(cond).astype(jnp.float32)
        own_cond = jnp.where(section == 0, cond, cond_low)
        part[:, : 3 * D] = matmul(to_half(jax.nn.silu(own_cond)), mod_ref[...])
        part[:, 3 * D : 5 * D] = matmul(to_half(jax.nn.silu(cond_low)), fm_ref[...])
        part[:, 5 * D :] = jnp.zeros((group, 8 * PIECE - 5 * D), jnp.float32)
        for row in range(group):
            for k in range(8):
                parts[row, k : k + 1] = part[row : row + 1, PIECE * k : PIECE * (k + 1)]
        own_part.start()
        send_all(part_copy, group, place_in)

    def along(step, k):
        crosses = not (step == 1 and GATHER_CHUNKS[k][3])
        for sign in (-1, 1):
            @pl.when((z >= step) if sign < 0 else (z + step < Z))
            def _():
                owner = me + sign * X * step
                arrived(owner, k)

                @pl.when(has_up if sign < 0 else has_down)
                def _():
                    copy(owner, k, False, up_sem if sign < 0 else down_sem, me - sign * X).start()

                if crosses:
                    copy(owner, k, False, x_sem, across).start()
                to_sibling(owner, k, False).start()

    def crossed(step, k):
        if step == 0:
            arrived(across, k)
            if GATHER_CHUNKS[k][3]:
                @pl.when(has_up)
                def _():
                    copy(across, k, False, up_sem, me + X).start()

                @pl.when(has_down)
                def _():
                    copy(across, k, False, down_sem, me - X).start()
            to_sibling(across, k, False).start()
            return
        for sign in (-1, 1):
            @pl.when((z >= step) if sign < 0 else (z + step < Z))
            def _():
                owner = across + sign * X * step
                arrived(owner, k)
                to_sibling(owner, k, False).start()

    for step in range(1, Z + 1):
        for k in range(chunks):
            if step < Z:
                along(step, k)
            crossed(step - 1, k)
        if step == 1:
            make_hidden()
        if step == 2:
            make_parts()

    own_part.wait()
    wait_all(part_copy, group, place_in)
    own_ends.wait()
    wait_all(ends_copy, Z * X, me)
    for source_core in range(2):
        total = arrived_parts[source_core]
        for index in range(1, Z * X):
            total = total + arrived_parts[2 * index + source_core]
        mods_out[source_core] = total

    for k in range(chunks):
        near = GATHER_CHUNKS[k][3]
        own_copy(k).wait()
        for column in range(2):
            base = me if column == 0 else across
            for step in range(0, Z):
                for sign in (-1, 1) if step else (1,):
                    @pl.when((z >= step) if sign < 0 else (z + step < Z))
                    def _():
                        owner = base + sign * X * step
                        mine = column == 0 and step == 0
                        to_sibling(owner, k, mine).wait_send()
                        pltpu.make_async_remote_copy(
                            src_ref=place(owner, k, 1 - core),
                            dst_ref=place(owner, k, 1 - core),
                            send_sem=sib_sem.at[owner * chunks + k],
                            recv_sem=sib_recv.at[owner * chunks + k],
                            device_id={"section": sibling},
                            device_id_type=MESH,
                        ).wait_recv()
                        runs = column == 0 or (near and step == 0)
                        if runs and (step == 0 or sign < 0):
                            @pl.when(has_up)
                            def _():
                                copy(owner, k, mine, up_sem, me + X).wait_send()
                        if runs and (step == 0 or sign > 0):
                            @pl.when(has_down)
                            def _():
                                copy(owner, k, mine, down_sem, me - X).wait_send()
                        if column == 0 and not (step == 1 and near):
                            copy(owner, k, mine, x_sem, across).wait_send()


def gather_weights(block, downs, stems, mod, tail, meta, ends, b_one, b_two):
    n, width = lax.axis_size("dp"), block.shape[0]
    section = lax.axis_index("section")
    if not ring_fits(n, width):
        both = lambda own, sib: jnp.where(
            lax.rem(section, 2) == 0, jnp.stack([own, sib]), jnp.stack([sib, own])
        )
        core = lax.rem(section, 2)
        dn = lax.dynamic_slice(downs, (section // 2, 0, core * HALF), (1, width, HALF))[0]
        blk = lax.all_gather(to_half(block), "dp", axis=0, tiled=True)
        dn = lax.all_gather(to_half(dn), "dp", axis=0, tiled=True)
        at_one, at_two = NCLS + PATCH_IN, NCLS + PATCH_IN + FREQ
        stem, w_mod, w_fm = to_half(stems), to_half(mod), to_half(tail[:, : 2 * D])
        table = jnp.pad(stem[:, :NCLS], ((0, 0), (0, -NCLS % 128)))
        w_one = jnp.pad(stem[:, at_one:at_two], ((0, WIDE - width), (0, 0)))
        w_two = stem[:, at_two:].reshape(width, n, width).transpose(1, 0, 2)
        w_two = jnp.pad(w_two, ((0, 0), (0, 0), (0, WIDE - width)))
        meta, ends = exchange(2, "dp", ("all", "all"), meta, ends)
        meta = meta.reshape(2 * n, META)
        pre = matmul_nt(to_half(meta[:, :FREQ]), w_one) + b_one
        (hidden,) = exchange(8, "dp", ("all",), to_half(jax.nn.silu(pre)))
        cond = matmul_nt(one_hot(meta[:, FREQ : FREQ + 1], table.shape[1]), table) + b_two
        cond = cond + jnp.einsum("jik,jwk->iw", hidden, w_two, preferred_element_type=jnp.float32)
        cond_low = to_half(cond).astype(jnp.float32)
        own_cond = jnp.where(section == 0, cond, cond_low)
        parts = [
            matmul(to_half(jax.nn.silu(own_cond)), w_mod),
            matmul(to_half(jax.nn.silu(cond_low)), w_fm),
        ]
        parts = jnp.pad(jnp.concatenate(parts, axis=1), ((0, 0), (0, 8 * PIECE - 5 * D)))
        (parts,) = exchange(3, "stage", ("each",), parts.reshape(2 * n, 8, PIECE))
        mods = jnp.sum(parts.reshape(n, 2, 8, PIECE), axis=0)
        own = (both(blk, swap(blk, 1)), both(dn, swap(dn, 1)), meta, ends, pre, hidden, cond, mods)
        return own + (w_mod, w_fm, w_two)
    units, images = n * len(GATHER_CHUNKS), 2 * n
    hbm, vmem = pl.BlockSpec(memory_space=pl.ANY), pl.BlockSpec(memory_space=pltpu.VMEM)
    dma = lambda count: pltpu.SemaphoreType.DMA((count,))
    f32 = jnp.float32
    return pl.pallas_call(
        gather_kernel,
        out_shape=(
            jax.ShapeDtypeStruct((2, D, FF), BF), jax.ShapeDtypeStruct((2, D, HALF), BF),
            jax.ShapeDtypeStruct((images, META), f32), jax.ShapeDtypeStruct((n,) + ends.shape, BF),
            jax.ShapeDtypeStruct((images, WIDE), f32), jax.ShapeDtypeStruct((n, images, WIDE), BF),
            jax.ShapeDtypeStruct((images, width), f32), jax.ShapeDtypeStruct((2, 8, PIECE), f32),
            jax.ShapeDtypeStruct((width, 3 * D), BF), jax.ShapeDtypeStruct((width, 2 * D), BF),
            jax.ShapeDtypeStruct((n, width, WIDE), BF),
        ),
        in_specs=[hbm] * 5 + [vmem] * 4,
        out_specs=(hbm, hbm) + (vmem,) * 9,
        scratch_shapes=[
            pltpu.VMEM((width, FF), f32), pltpu.VMEM((width, HALF), f32), pltpu.VMEM(stems.shape, f32),
            pltpu.VMEM((width, 3 * D), f32), pltpu.VMEM(tail.shape, f32),
            pltpu.VMEM((width, FF), BF), pltpu.VMEM((width, HALF), BF), pltpu.VMEM((WIDE, FREQ), BF),
            pltpu.VMEM((width, 1024), BF), dma(5),
            pltpu.VMEM((n, 2, META), f32), pltpu.VMEM((images, WIDE), BF),
            pltpu.VMEM((images, 8 * PIECE), f32),
            pltpu.VMEM((images, 8, PIECE), f32), pltpu.VMEM((images, 8, PIECE), f32),
            dma(n), dma(n), dma(n), dma(n), dma(n), dma(n), dma(images), dma(images), dma(4),
        ]
        + [dma(units)] * 6
        + [dma(len(GATHER_CHUNKS))],
        compiler_params=pltpu.CompilerParams(
            collective_id=0, has_side_effects=True, vmem_limit_bytes=VMEM_BYTES
        ),
        cost_estimate=pl.CostEstimate(flops=0, bytes_accessed=400_000_000, transcendentals=0),
        name="gather_weights",
    )(block, downs, stems, mod, tail, meta, ends, b_one, b_two)


VMEM_BYTES = 60 * 1024 * 1024
SUM_CHUNKS = tuple((which,) + chunk for which in range(3) for chunk in CHUNKS)


def silu_slope(value):
    gate = jax.nn.sigmoid(value)
    return gate * (1.0 + value * (1.0 - gate))


def sum_kernel(
    g_dn, g_up, g_attn, dm_ref, bp_ref, en_ref, mod_ref, fm_ref, two_ref, cond_ref, pre_ref, hid_ref, meta_ref,
    out, cross_out, dn_out, gmod_out, gfm_out, gtab_out, gone_out, gtwo_out,
    ends_all, news_out, cs_all, fmsum_out, sq_out,
    own_b, other_d, xb, xq, up_b, up_o, down_b, down_o, acc, acc_dn,
    dm_in, bp_in, en_in, dmat, ends_src, c_src, c_in, fmd_src, fmd_in, cs_src, dcond, ph, ph_in, news_src,
    sq_src, sq_all, sq_rows, cross_src,
    load_sem, x_send, x_recv, up_send, up_recv, down_send, down_recv,
    sib_send, sib_recv, y_send, y_recv, group_send, group_recv, sect_send, sect_recv,
    ph_send, ph_recv, news_send, news_recv, sq_send, sq_recv, cross_sem, local_sem,
):
    me = lax.axis_index("dp")
    section = lax.axis_index("section")
    z, x = me // X, lax.rem(me, X)
    core = lax.rem(section, 2)
    low, sibling, facing = section - core, section + 1 - 2 * core, lax.rem(section + 2, 4)
    across = me + 1 - 2 * x
    sources = (g_dn, g_up, g_attn)
    chunks = len(SUM_CHUNKS)
    has_up, has_down = z < Z - 1, z > 0
    devices, group = Z * X * 4, Z * X * 2
    me_all, me_group = me * 4 + section, me * 2 + core
    in_all = lambda p: {"dp": p // 4, "section": lax.rem(p, 4)}
    in_group = lambda p: {"dp": p // 2, "section": low + lax.rem(p, 2)}
    in_section = lambda p: {"section": p}
    in_dp = lambda p: {"dp": p}
    f32 = jnp.float32

    barrier = pltpu.get_barrier_semaphore()

    @pl.loop(1, devices)
    def _(step):
        pl.semaphore_signal(
            barrier, 1, device_id=in_all(lax.rem(me_all + step, devices)), device_id_type=MESH
        )

    def small(src_of, dst, send, recv, where, size, index):
        def copy(step, p, slot):
            return pltpu.make_async_remote_copy(
                src_ref=src_of(p), dst_ref=dst.at[slot], send_sem=send.at[step], recv_sem=recv.at[step],
                device_id=where(p), device_id_type=MESH,
            )
        return (copy, size, index, src_of, dst)

    gradients = [
        small(lambda p: dm_ref.at[lax.rem(p, 2)], dm_in, group_send.at[0], group_recv.at[0], in_group, group, me_group),
        small(lambda p: bp_ref.at[p], bp_in, group_send.at[1], group_recv.at[1], in_group, group, me_group),
        small(lambda p: en_ref.at[p // 2], en_in, group_send.at[2], group_recv.at[2], in_group, group, me_group),
    ]
    conds = [
        small(lambda p, src=src: src, dst, sect_send.at[k], sect_recv.at[k], in_section, 4, section)
        for k, (src, dst) in enumerate(
            ((c_src, c_in), (ends_src, ends_all), (fmd_src, fmd_in), (cs_src, cs_all))
        )
    ]
    hiddens = [small(lambda p: ph.at[p], ph_in, ph_send, ph_recv, in_dp, Z * X, me)]
    news = [small(lambda p: news_src, news_out, news_send, news_recv, in_all, devices, me_all)]
    norms = [small(lambda p: sq_src, sq_all, sq_send, sq_recv, in_all, devices, me_all)]

    def own_copies(batch, first):
        return [
            pltpu.make_async_copy(src_of(index), dst.at[index], local_sem.at[first + k])
            for k, (copy, size, index, src_of, dst) in enumerate(batch)
        ]

    def send_batch(batch, first):
        for copy in own_copies(batch, first):
            copy.start()
        for copy, size, index, src_of, dst in batch:
            @pl.loop(1, size)
            def _(step):
                copy(step, lax.rem(index + step, size), index).start()

    def wait_batch(batch, first):
        for copy in own_copies(batch, first):
            copy.wait()
        for copy, size, index, src_of, dst in batch:
            @pl.loop(1, size)
            def _(step):
                p = lax.rem(index + size - step, size)
                copy(step, p, p).wait_recv()
                copy(step, p, p).wait_send()

    def add_square(value):
        sq_src[...] += jnp.sum(value * value)

    def images_of():
        cond = cond_ref[...]
        cond_low = to_half(cond).astype(f32)
        return jnp.where(section == 0, cond, cond_low), cond_low

    def make_cond():
        wait_batch(gradients, 0)
        flat = dm_in[...].reshape(group * 48, 128)
        row = lax.broadcasted_iota(jnp.int32, (group, group * 48), 0) * 48
        column = lax.broadcasted_iota(jnp.int32, (group, group * 48), 1)
        for k in range(5 * D // 128):
            chosen = jnp.where(column == row + k, 1.0, 0.0).astype(BF)
            dmat[:, 128 * k : 128 * (k + 1)] = to_half(matmul(chosen, flat))
        news_src[...] = jnp.zeros_like(news_src)
        news_src[0:SUM_ROWS] = jnp.sum(bp_in[...], axis=0)
        ends_src[...] = jnp.sum(en_in[...], axis=0)
        own_cond, cond_low = images_of()
        d_mod, d_fm = dmat[:, : 3 * D], dmat[:, 3 * D :]
        fmd_src[...] = d_fm
        cs_src[...] = jnp.sum(d_mod.astype(f32), axis=0, keepdims=True)
        d_silu = matmul_nt(d_mod, mod_ref[...])
        d_silu = d_silu + (section == 3).astype(f32) * matmul_nt(d_fm, fm_ref[...])
        c_src[...] = jnp.zeros_like(c_src)
        c_src[:, :144] = silu_slope(own_cond) * d_silu
        send_batch(conds, 3)
        silu_own = to_half(jax.nn.silu(own_cond))
        for k in range(3):
            part_g = matmul_tn(silu_own, dmat[:, D * k : D * (k + 1)])
            gmod_out[:, D * k : D * (k + 1)] = part_g
            add_square(part_g)

    once = (section == 0).astype(f32)

    def make_hidden():
        wait_batch(conds, 3)
        total = to_half(c_in[3])
        for slot in (2, 1, 0):
            total = to_half(total.astype(f32) + c_in[slot])
        dcond[...] = total
        d_cond = dcond[:, :144]
        for index in range(Z * X):
            ph[index] = matmul(d_cond, two_ref[index])
        send_batch(hiddens, 7)
        own_cond, cond_low = images_of()
        silu_low = to_half(jax.nn.silu(cond_low))
        for k in range(2):
            part_g = matmul_tn(silu_low, fmd_in[3, :, D * k : D * (k + 1)])
            gfm_out[:, D * k : D * (k + 1)] = part_g
            add_square(jnp.sqrt(once) * part_g)
        fmsum_out[...] = jnp.sum(fmd_in[3].astype(f32), axis=0, keepdims=True)
        part_g = matmul_tn(d_cond, one_hot(meta_ref[:, FREQ : FREQ + 1], gtab_out.shape[1]))
        gtab_out[...] = part_g
        add_square(once * part_g)
        for index in range(Z * X):
            part_g = matmul_tn(d_cond, hid_ref[index])
            gtwo_out[:, 144 * index : 144 * (index + 1)] = part_g[:, :144]
            add_square(once * part_g)

    def make_news():
        wait_batch(hiddens, 7)
        total = ph_in[0]
        for index in range(1, Z * X):
            total = total + ph_in[index]
        d_pre = to_half(silu_slope(pre_ref[...]) * total)
        part_g = matmul_tn(d_pre, to_half(meta_ref[:, :FREQ]))
        gone_out[...] = part_g
        add_square(once * part_g)
        sums = jnp.sum(d_pre.astype(f32), axis=0, keepdims=True)
        sums_cond = jnp.sum(dcond[...].astype(f32), axis=0, keepdims=True)
        for k in range(2):
            news_src[SUM_ROWS + k : SUM_ROWS + k + 1] = sums[:, 128 * k : 128 * (k + 1)]
            news_src[SUM_ROWS + 2 + k : SUM_ROWS + 3 + k] = sums_cond[:, 128 * k : 128 * (k + 1)]
        send_batch(news, 8)
        first = (me == 0).astype(f32)
        add_square(news_src[0:10])
        add_square(once * sums)
        add_square(once * sums_cond)
        add_square(first * cs_src[...])
        add_square(first * once * fmsum_out[...])
        add_square(once * ends_all[0])
        add_square(once * ends_all[3])

    def dn_copy(k, slot, to_sib):
        rows = pl.ds(SUM_CHUNKS[k][1], SUM_CHUNKS[k][2])
        unit = slot * chunks + k
        return pltpu.make_async_remote_copy(
            src_ref=dn_out.at[slot, rows], dst_ref=dn_out.at[slot, rows],
            send_sem=(sib_send if to_sib else y_send).at[unit],
            recv_sem=(sib_recv if to_sib else y_recv).at[unit],
            device_id={"section": sibling if to_sib else facing},
            device_id_type=MESH,
        )

    def each(distance, run):
        if distance == 0:
            run(z, None)
            return

        @pl.when(z + distance < Z)
        def _():
            run(z + distance, True)

        @pl.when(z >= distance)
        def _():
            run(z - distance, False)

    def part(k):
        return pl.ds(SUM_CHUNKS[k][1], SUM_CHUNKS[k][2])

    def hbm(k, zz, column):
        start = pl.multiple_of((zz * X + column) * 144 + SUM_CHUNKS[k][1], 16)
        return sources[SUM_CHUNKS[k][0]].at[pl.ds(start, SUM_CHUNKS[k][2])]

    def own(k, zz):
        return own_b.at[SUM_CHUNKS[k][0], zz, part(k)]

    def from_x(k, zz):
        return xq.at[SUM_CHUNKS[k][0]] if SUM_CHUNKS[k][3] else xb.at[SUM_CHUNKS[k][0], zz, part(k)]

    def from_z(k, zz, up, other):
        if other:
            return (up_o if up else down_o).at[SUM_CHUNKS[k][0], zz]
        return (up_b if up else down_b).at[SUM_CHUNKS[k][0], zz, part(k)]

    def other_of(k, zz):
        return other_d.at[SUM_CHUNKS[k][0], zz]

    def load(k, zz, other=False):
        index = ((chunks if other else 0) + k) * Z + zz
        return pltpu.make_async_copy(
            hbm(k, zz, (1 - x) if other else x),
            other_of(k, zz) if other else own(k, zz),
            load_sem.at[index],
        )

    def x_copy(k, zz, src):
        unit = k * Z + zz
        return pltpu.make_async_remote_copy(
            src_ref=src, dst_ref=from_x(k, zz), send_sem=x_send.at[unit], recv_sem=x_recv.at[unit],
            device_id={"dp": across}, device_id_type=MESH,
        )

    def z_copy(k, zz, up, other):
        unit = ((chunks if other else 0) + k) * Z + zz
        return pltpu.make_async_remote_copy(
            src_ref=other_of(k, zz) if other else own(k, zz),
            dst_ref=from_z(k, zz, up, other),
            send_sem=(up_send if up else down_send).at[unit],
            recv_sem=(up_recv if up else down_recv).at[unit],
            device_id={"dp": me + X if up else me - X},
            device_id_type=MESH,
        )

    def total(k, dst, srcs):
        @pl.loop(0, SUM_CHUNKS[k][2] // 16)
        def _(step):
            rows = pl.ds(pl.multiple_of(step * 16, 16), 16)
            value = srcs[0][rows].astype(jnp.float32)
            for src in srcs[1:]:
                value = value + src[rows].astype(jnp.float32)
            dst[rows] = value.astype(dst.dtype)

    for distance in (3, 2, 1, 0):
        for k in range(chunks):
            def run(zz, up):
                load(k, zz).start()
                if SUM_CHUNKS[k][3]:
                    load(k, zz, True).start()
            each(distance, run)

    sq_src[...] = jnp.zeros_like(sq_src)
    sq_rows[...] = jnp.zeros_like(sq_rows)
    pl.semaphore_wait(barrier, devices - 1)
    send_batch(gradients, 0)

    order = [
        (k, distance) for which, distance in ((0, 3), (0, 2), (0, 1), (1, 3), (0, 0), (1, 2), (1, 1), (2, 3), (1, 0), (2, 2), (2, 1), (2, 0))
        for k in range(chunks) if SUM_CHUNKS[k][0] == which and not SUM_CHUNKS[k][3]
    ]
    sent = []

    def send_x(until):
        while len(sent) < min(until, len(order)):
            k, distance = order[len(sent)]
            sent.append(1)
            each(distance, lambda zz, up: x_copy(k, zz, hbm(k, zz, 1 - x)).start())

    def after(k, distance):
        if not SUM_CHUNKS[k][3]:
            send_x(order.index((k, distance)) + 1 + 6)

    send_x(6)

    def pass_on(k, distance):
        def run(zz, up):
            behind = has_down if up else has_up
            if SUM_CHUNKS[k][3]:
                for other in (False, True):
                    mine = other_of(k, zz) if other else own(k, zz)
                    load(k, zz, other).wait()

                    @pl.when(behind)
                    def _():
                        z_copy(k, zz, up, other).wait_recv()
                        total(k, mine, [mine, from_z(k, zz, up, other)])

                    z_copy(k, zz, up, other).start()
                return
            load(k, zz).wait()
            x_copy(k, zz, hbm(k, zz, 1 - x)).wait_recv()

            @pl.when(behind)
            def _():
                z_copy(k, zz, up, False).wait_recv()
                total(k, own(k, zz), [own(k, zz), from_x(k, zz), from_z(k, zz, up, False)])

            @pl.when(jnp.logical_not(behind))
            def _():
                total(k, own(k, zz), [own(k, zz), from_x(k, zz)])

            z_copy(k, zz, up, False).start()
        each(distance, run)

    def add_z(dst, k, other):
        @pl.when(has_down)
        def _():
            z_copy(k, z, True, other).wait_recv()
            total(k, dst, [dst, from_z(k, z, True, other)])

        @pl.when(has_up)
        def _():
            z_copy(k, z, False, other).wait_recv()
            total(k, dst, [dst, from_z(k, z, False, other)])

    def send_direct(k):
        load(k, z, True).wait()
        total(k, acc, [other_of(k, z)])
        add_z(acc, k, True)
        total(k, other_of(k, z), [acc])
        x_copy(k, z, other_of(k, z)).start()

    def finish(k):
        which, rows = SUM_CHUNKS[k][0], SUM_CHUNKS[k][2]
        dst = out.at[which - 1, part(k)] if which else acc_dn.at[pl.ds(0, rows)]
        load(k, z).wait()
        if SUM_CHUNKS[k][3]:
            total(k, dst, [own(k, z)])
            add_z(dst, k, False)
            x_copy(k, z, other_of(k, z)).wait_recv()
            total(k, dst, [dst, from_x(k, z)])
        else:
            x_copy(k, z, hbm(k, z, 1 - x)).wait_recv()
            total(k, dst, [own(k, z), from_x(k, z)])
            add_z(dst, k, False)
        if not which:
            total(k, dn_out.at[section, part(k)], [dst])
            dn_copy(k, section, True).start()
            dn_copy(k, section, False).start()

        @pl.loop(0, rows // 16)
        def _(step):
            value = dst[pl.ds(pl.multiple_of(step * 16, 16), 16)]
            sq_rows[...] += jnp.sum(value * value, axis=0, keepdims=True)

    def of(which, direct=None):
        return [
            k for k in range(chunks)
            if SUM_CHUNKS[k][0] == which and (direct is None or SUM_CHUNKS[k][3] == direct)
        ]

    def pass_all(which, distance):
        for k in of(which):
            pass_on(k, distance)
            after(k, distance)

    def finish_all(which):
        for k in of(which, False) + of(which, True):
            finish(k)
            after(k, 0)

    def direct_all(which):
        for k in of(which, True):
            send_direct(k)

    for distance in (3, 2, 1):
        pass_all(0, distance)
    make_cond()
    pass_all(1, 3)
    direct_all(0)
    finish_all(0)
    pass_all(1, 2)
    make_hidden()
    pass_all(1, 1)
    for k in of(0):
        dn_copy(k, facing, False).wait_recv()
        dn_copy(k, facing, True).start()
    pass_all(2, 3)
    make_news()
    direct_all(1)
    finish_all(1)
    pass_all(2, 2)
    pass_all(2, 1)
    direct_all(2)
    finish_all(2)

    @pl.loop(0, 144 // 16)
    def _(step):
        rows = pl.ds(pl.multiple_of(step * 16, 16), 16)
        cross_src[rows] = to_half(jnp.where(core == 0, out[0, rows], out[1, rows]))

    crossing = pltpu.make_async_remote_copy(
        src_ref=cross_src, dst_ref=cross_out, send_sem=cross_sem.at[0], recv_sem=cross_sem.at[1],
        device_id={"section": sibling}, device_id_type=MESH,
    )
    sq_src[...] += jnp.sum(sq_rows[...])
    send_batch(norms, 9)
    crossing.start()
    wait_batch(norms, 9)
    sq_out[...] = jnp.sum(sq_all[...], axis=0)
    wait_batch(news, 8)
    crossing.wait()

    for k in range(chunks):
        for distance in (3, 2, 1, 0):
            def run(zz, up):
                if not SUM_CHUNKS[k][3]:
                    x_copy(k, zz, hbm(k, zz, 1 - x)).wait_send()
                elif distance == 0:
                    x_copy(k, zz, other_of(k, zz)).wait_send()
                if distance:
                    z_copy(k, zz, up, False).wait_send()
                    if SUM_CHUNKS[k][3]:
                        z_copy(k, zz, up, True).wait_send()
            each(distance, run)
        if not SUM_CHUNKS[k][0]:
            dn_copy(k, section, True).wait_send()
            dn_copy(k, section, False).wait_send()
            dn_copy(k, facing, True).wait_send()
            dn_copy(k, sibling, True).wait_recv()
            dn_copy(k, lax.rem(sibling + 2, 4), True).wait_recv()


def sum_gradients(g_dn, g_up, g_attn, d_mods, sums, ends, w_mod, w_fm, two_blocks, cond, pre, hidden, meta):
    n, width = lax.axis_size("dp"), cond.shape[1]
    f32 = jnp.float32
    if not ring_fits(n, width):
        return sum_plainly(g_dn, g_up, g_attn, d_mods, sums, ends, w_mod, w_fm, two_blocks, cond, pre, hidden, meta)
    chunks, images, devices = len(SUM_CHUNKS), 2 * n, 4 * n
    dma = lambda *count: pltpu.SemaphoreType.DMA(count)
    ring = pltpu.VMEM((3, Z, 144, HALF), BF)
    short = [rows for start, rows, direct in CHUNKS if direct][0]
    most = max(rows for start, rows, direct in CHUNKS)
    ring_o = pltpu.VMEM((3, Z, short, HALF), BF)
    hbm, vmem = pl.BlockSpec(memory_space=pl.ANY), pl.BlockSpec(memory_space=pltpu.VMEM)
    like = jax.ShapeDtypeStruct
    end_block = ends.shape[1:]
    shapes = (
        like((2, 144, HALF), f32), like((144, HALF), BF), like((4, 144, HALF), BF),
        like((144, 3 * D), f32), like((144, 2 * D), f32), like((144, 1024), f32), like((WIDE, FREQ), f32),
        like((144, D), f32), like((4,) + end_block, f32), like((devices, 24, 128), f32),
        like((4, 1, 3 * D), f32), like((1, 2 * D), f32), like((8, 128), f32),
    )
    return pl.pallas_call(
        sum_kernel,
        out_shape=shapes,
        in_specs=[hbm] * 3 + [vmem] * 10,
        out_specs=(vmem,) * len(shapes),
        scratch_shapes=[
            ring, ring_o, ring, pltpu.VMEM((3, short, HALF), BF),
            ring, ring_o, ring, ring_o, pltpu.VMEM((short, HALF), f32), pltpu.VMEM((most, HALF), f32),
            pltpu.VMEM((images, 48, 128), BF), pltpu.VMEM((images, SUM_ROWS, 128), f32),
            pltpu.VMEM((images,) + end_block, f32), pltpu.VMEM((images, 5 * D), BF),
            pltpu.VMEM(end_block, f32), pltpu.VMEM((images, WIDE), f32), pltpu.VMEM((4, images, WIDE), f32),
            pltpu.VMEM((images, 2 * D), BF), pltpu.VMEM((4, images, 2 * D), BF), pltpu.VMEM((1, 3 * D), f32),
            pltpu.VMEM((images, WIDE), BF), pltpu.VMEM((n, images, WIDE), f32), pltpu.VMEM((n, images, WIDE), f32),
            pltpu.VMEM((24, 128), f32), pltpu.VMEM((8, 128), f32), pltpu.VMEM((devices, 8, 128), f32),
            pltpu.VMEM((1, HALF), f32),
            pltpu.VMEM((144, HALF), BF),
            dma(2 * chunks * Z), dma(chunks * Z), dma(chunks * Z),
            dma(2 * chunks * Z), dma(2 * chunks * Z), dma(2 * chunks * Z), dma(2 * chunks * Z),
            dma(4 * chunks), dma(4 * chunks), dma(4 * chunks), dma(4 * chunks),
            dma(3, images), dma(3, images), dma(4, 4), dma(4, 4),
            dma(n), dma(n), dma(devices), dma(devices), dma(devices), dma(devices), dma(2), dma(10),
        ],
        compiler_params=pltpu.CompilerParams(
            collective_id=1, has_side_effects=True, vmem_limit_bytes=VMEM_BYTES
        ),
        cost_estimate=pl.CostEstimate(flops=0, bytes_accessed=400_000_000, transcendentals=0),
        name="sum_gradients",
    )(g_dn, g_up, g_attn, d_mods, sums, ends, w_mod, w_fm, two_blocks, cond, pre, hidden, meta)


def sum_plainly(g_dn, g_up, g_attn, d_mods, sums, ends, w_mod, w_fm, two_blocks, cond, pre, hidden, meta):
    n, width = lax.axis_size("dp"), cond.shape[1]
    section, images, f32 = lax.axis_index("section"), 2 * n, jnp.float32
    once = (section == 0).astype(f32)
    anchor = (lax.axis_index("dp") == 0).astype(f32)
    total = lambda grad: lax.psum_scatter(grad, "dp", scatter_dimension=0, tiled=True)
    dn_own, out = total(g_dn), jnp.stack([total(g_up), total(g_attn)]).astype(f32)
    dn_all = lax.all_gather(dn_own, "section")
    cross = swap(to_half(jnp.where(lax.rem(section, 2) == 0, out[0], out[1])), 1)
    d_mods, sums, ends = exchange(4, "stage", ("core", "each", "dp"), d_mods, sums, ends)
    d_mods = d_mods.reshape(images, 48 * 128)
    d_mod, d_fm = d_mods[:, : 3 * D], d_mods[:, 3 * D : 5 * D]
    sums, ends = jnp.sum(sums, axis=0), jnp.sum(ends, axis=0)
    cond_low = to_half(cond).astype(f32)
    own_cond = jnp.where(section == 0, cond, cond_low)
    d_silu = matmul_nt(d_mod, w_mod) + (section == 3).astype(f32) * matmul_nt(d_fm, w_fm)
    c_own = jnp.pad(silu_slope(own_cond) * d_silu, ((0, 0), (0, WIDE - width)))
    cs = column_sums(d_mod)[None]
    c_all, ends_all, d_fm, cs_all = exchange(5, "section", ("all",) * 4, c_own, ends, d_fm, cs)
    d_fm = d_fm[3]
    d_cond = to_half(c_all[3])
    for slot in (2, 1, 0):
        d_cond = to_half(d_cond.astype(f32) + c_all[slot])
    narrow = d_cond[:, :width]
    part = jnp.einsum("iw,jwk->jik", narrow, two_blocks, preferred_element_type=f32)
    (part,) = exchange(6, "dp", ("each",), part)
    d_pre = to_half(silu_slope(pre) * jnp.sum(part, axis=0))
    g_mod = matmul_tn(to_half(jax.nn.silu(own_cond)), d_mod)
    g_fm = matmul_tn(to_half(jax.nn.silu(cond_low)), d_fm)
    g_table = matmul_tn(narrow, one_hot(meta[:, FREQ : FREQ + 1], 1024))
    g_one = matmul_tn(d_pre, to_half(meta[:, :FREQ]))
    g_two = jnp.einsum("iw,jik->wjk", narrow, hidden, preferred_element_type=f32)
    g_two = g_two[:, :, :width].reshape(width, D)
    fm_sum = column_sums(d_fm)[None]
    slices = [column_sums(value).reshape(2, 128) for value in (d_pre, d_cond)]
    news = jnp.concatenate([sums, *slices, jnp.zeros((4, 128), f32)])
    square = lambda value: jnp.sum(value * value)
    squares = square(out) + square(dn_own.astype(f32)) + square(g_mod) + square(sums[:10])
    squares = squares + anchor * square(cs) + anchor * once * square(fm_sum)
    for value in (g_fm, g_table, g_one, g_two, ends_all[0], ends_all[3], *slices):
        squares = squares + once * square(value)
    news, squares = exchange(7, "every", ("all", "all"), news, jnp.broadcast_to(squares, (8, 128)))
    squares = jnp.sum(squares, axis=0)
    return (out, cross, dn_all, g_mod, g_fm, g_table, g_one, g_two, ends_all, news, cs_all, fm_sum, squares)


def exchange_kernel(axes, modes, *refs):
    count = len(modes)
    ins, outs = refs[:count], refs[count : 2 * count]
    send_sem, recv_sem, own_sem = refs[2 * count :]
    dp, section = lax.axis_index("dp"), lax.axis_index("section")
    n, sections = lax.axis_size("dp"), lax.axis_size("section")
    if axes == "dp":
        size, me, where = n, dp, lambda p: {"dp": p}
    elif axes == "section":
        size, me, where = sections, section, lambda p: {"section": p}
    elif axes == "stage":
        low = section - lax.rem(section, 2)
        size, me = 2 * n, dp * 2 + lax.rem(section, 2)
        where = lambda p: {"dp": p // 2, "section": low + lax.rem(p, 2)}
    else:
        size, me = n * sections, dp * sections + section
        where = lambda p: {"dp": p // sections, "section": lax.rem(p, sections)}

    def part(k, p):
        if modes[k] == "all":
            return ins[k]
        index = {"each": p, "dp": p // 2, "core": lax.rem(p, 2)}[modes[k]]
        return ins[k].at[index]

    def copy(k, step, src, slot, p):
        return pltpu.make_async_remote_copy(
            src_ref=src, dst_ref=outs[k].at[slot],
            send_sem=send_sem.at[k, step], recv_sem=recv_sem.at[k, step],
            device_id=where(p), device_id_type=MESH,
        )

    barrier = pltpu.get_barrier_semaphore()

    @pl.loop(1, size)
    def _(step):
        pl.semaphore_signal(barrier, 1, device_id=where(lax.rem(me + step, size)), device_id_type=MESH)

    for k in range(count):
        pltpu.make_async_copy(part(k, me), outs[k].at[me], own_sem.at[k]).start()
    pl.semaphore_wait(barrier, size - 1)

    @pl.loop(1, size)
    def _(step):
        p = lax.rem(me + step, size)
        for k in range(count):
            copy(k, step, part(k, p), me, p).start()

    for k in range(count):
        pltpu.make_async_copy(part(k, me), outs[k].at[me], own_sem.at[k]).wait()

    @pl.loop(1, size)
    def _(step):
        p = lax.rem(me + size - step, size)
        for k in range(count):
            copy(k, step, part(k, p), p, p).wait_recv()
            copy(k, step, part(k, p), p, p).wait_send()


def exchange(ident, axes, modes, *arrays):
    n, sections = lax.axis_size("dp"), lax.axis_size("section")
    size = {"dp": n, "section": sections, "stage": 2 * n, "every": n * sections}[axes]
    blocks = [a.shape if mode == "all" else a.shape[1:] for a, mode in zip(arrays, modes)]
    count = len(arrays)
    vmem = pl.BlockSpec(memory_space=pltpu.VMEM)
    return pl.pallas_call(
        partial(exchange_kernel, axes, modes),
        out_shape=tuple(jax.ShapeDtypeStruct((size,) + b, a.dtype) for a, b in zip(arrays, blocks)),
        in_specs=[vmem] * count,
        out_specs=(vmem,) * count,
        scratch_shapes=[
            pltpu.SemaphoreType.DMA((count, size)),
            pltpu.SemaphoreType.DMA((count, size)),
            pltpu.SemaphoreType.DMA((count,)),
        ],
        compiler_params=pltpu.CompilerParams(
            collective_id=ident, has_side_effects=True, vmem_limit_bytes=VMEM_BYTES
        ),
        cost_estimate=pl.CostEstimate(flops=0, bytes_accessed=30_000_000, transcendentals=0),
        name="exchange_" + axes,
    )(*arrays)


def rows_of(value, size):
    value = value.reshape(-1)
    return jnp.pad(value, (0, size * 128 - value.shape[0])).reshape(size, 128)


def row_count(length, unit=8):
    return -(-length // (128 * unit)) * unit


TILE = 768
STEPS = HALF // TILE
GELU_SCALE = math.sqrt(2.0 / math.pi)
SCALE = HEAD_DIM ** (-0.5)


def mean_rows(value):
    return jnp.mean(value, axis=-1, keepdims=True)


def normalized(x):
    centered = x - mean_rows(x)
    inverse = lax.rsqrt(mean_rows(centered * centered) + epsilon_norm)
    return (centered * inverse, inverse)


def modulated_back(normed, inverse, scale, d_xm):
    d_normed = d_xm * (1.0 + scale)
    d_x = inverse * (d_normed - mean_rows(d_normed) - normed * mean_rows(d_normed * normed))
    return (d_x, jnp.sum(d_xm, axis=0), jnp.sum(d_xm * normed, axis=0))


def window(head):
    low = HEAD_DIM * head // 128 * 128
    high = -(-HEAD_DIM * (head + 1) // 128) * 128
    lane = lax.broadcasted_iota(jnp.int32, (PATCHES, high - low), 1) + low
    return slice(low, high), (lane >= HEAD_DIM * head) & (lane < HEAD_DIM * (head + 1))


def own_lanes(mask, value):
    return jnp.where(mask, value, jnp.zeros_like(value))


def softmax_rows(scores):
    shifted = jnp.exp(scores - jnp.max(scores, axis=-1, keepdims=True))
    return shifted / jnp.sum(shifted, axis=-1, keepdims=True)


def half_of(ref, which, side):
    return ref.at[which, :, pl.ds(pl.multiple_of(side * HALF, 128) if which else side * HALF, HALF)]


def weight_copies(sources, targets, sem):
    return [pltpu.make_async_copy(src, dst, sem.at[k]) for k, (src, dst) in enumerate(zip(sources, targets))]


def forward_kernel(
    save, flags, x_ref, mod_a, mod_m, b_attn, b_up, b_down, w_blk, w_dn, out_ref, *refs
):
    if save:
        xm_ref, qkv_ref, att_ref, last_ref, branch_a_ref, mid_ref, xm2_ref, branch_m_ref, pre_ref = refs[:9]
        act_refs = refs[9:11]
        wa, wu, wd, acc, sem = refs[11:]
    else:
        xm_ref, qkv_ref, att_ref, mid_ref, xm2_ref, wa, wu, wd, acc, sem = refs
    copies = weight_copies(
        [half_of(w_blk, 0, 0), half_of(w_blk, 0, 1)]
        + [ref for side in (flags[0], 1 - flags[0]) for ref in (half_of(w_blk, 1, side), w_dn.at[side])],
        (wa.at[0], wa.at[1], wu.at[0], wd.at[0], wu.at[1], wd.at[1]),
        sem,
    )
    for copy in copies:
        copy.start()
    normed, unused = normalized(x_ref[...])
    xm_ref[...] = to_half(normed * (1.0 + mod_a[1:2]) + mod_a[0:1])
    acc[...] = jnp.zeros_like(acc)
    for k in range(3):
        if k != 1:
            copies[k // 2].wait()
        half, first = (0, D * k) if k < 2 else (1, 0)
        part = slice(D * k, D * (k + 1))
        qkv_ref[:, part] = to_half(
            matmul(xm_ref[...], wa[half, :, first : first + D]) + b_attn[:, part]
        )
    for head in range(HEADS):
        lanes, mask = window(head)
        at = lambda k: slice(D * k + lanes.start, D * k + lanes.stop)
        query = own_lanes(mask, qkv_ref[:, at(0)])
        probs = softmax_rows(matmul_nt(query, qkv_ref[:, at(1)]) * SCALE)
        acc[:, lanes] += own_lanes(mask, matmul(to_half(probs), qkv_ref[:, at(2)]))
    att_ref[...] = to_half(acc[...])
    branch = matmul(att_ref[...], wa[1, :, D:]) + b_attn[:, 3 * D :]
    if save:
        branch_a_ref[...] = branch
        last_ref[...] = jnp.where(flags[0] == 0, att_ref[...], xm_ref[...])
    mid_ref[...] = to_half(x_ref[...] + mod_a[2:3] * branch).astype(jnp.float32)
    normed, unused = normalized(mid_ref[...])
    xm2_ref[...] = to_half(normed * (1.0 + mod_m[1:2]) + mod_m[0:1])
    acc[...] = jnp.broadcast_to(b_down[...], acc.shape)
    for half in range(2):
        copies[2 + 2 * half].wait()
        copies[3 + 2 * half].wait()
        for step in range(STEPS):
            own = slice(TILE * step, TILE * (step + 1))
            part = slice(HALF * half + TILE * step, HALF * half + TILE * (step + 1))
            pre = matmul(xm2_ref[...], wu[half, :, own]) + b_up[:, part]
            cube = pre + 0.044715 * (pre * pre * pre)
            act = to_half(pre * (0.5 * (1.0 + jnp.tanh(GELU_SCALE * cube))))
            if save:
                pre_ref[:, part] = pre
                act_refs[half][:, own] = act
            acc[...] += matmul_nt(act, wd[half, :, own])
    if save:
        branch_m_ref[...] = acc[...]
    out = mid_ref[...] + mod_m[2:3] * acc[...]
    out_ref[...] = out.astype(out_ref.dtype)


def backward_kernel(
    flags, d_ref, x_ref, mid_ref, mod_a, mod_m, branch_a, branch_m, qkv_ref, pre_hbm, w_blk, w_dn,
    d_in_ref, d_mod_a, d_mod_m, grad_a, grad_m, d_pre_own, d_pre_sib, d_qkv_ref, right_own, right_sib,
    wa, wu, wd, pre_ref, acc, d_acc, d_att, sem,
):
    copies = weight_copies(
        (
            w_dn.at[flags[0]], pre_hbm, half_of(w_blk, 1, flags[0]),
            w_dn.at[1 - flags[0]], half_of(w_blk, 1, 1 - flags[0]),
            half_of(w_blk, 0, 1), half_of(w_blk, 0, 0),
        ),
        (wd.at[0], pre_ref, wu.at[0], wd.at[1], wu.at[1], wa.at[1], wa.at[0]),
        sem,
    )
    for copy in copies:
        copy.start()
    grad_m[...] = to_half(d_ref[...] * mod_m[2:3])
    d_mod_m[2:3] = jnp.sum(d_ref[...] * branch_m[...], axis=0)[None]
    acc[...] = jnp.zeros_like(acc)
    for half in range(2):
        copies[0 if half == 0 else 3].wait()
        if half == 0:
            copies[1].wait()
        copies[2 if half == 0 else 4].wait()
        for step in range(STEPS):
            own = slice(TILE * step, TILE * (step + 1))
            part = slice(HALF * half + TILE * step, HALF * half + TILE * (step + 1))
            d_act = matmul(grad_m[...], wd[half, :, own])
            pre = pre_ref[:, part]
            square = pre * pre
            tanh = jnp.tanh(GELU_SCALE * (pre + 0.044715 * (square * pre)))
            slope = 0.5 * (1.0 + tanh) + (0.5 * pre) * (1.0 - tanh * tanh) * (
                GELU_SCALE * (1.0 + (3.0 * 0.044715) * square)
            )
            d_pre = to_half(d_act * slope)
            (d_pre_sib if half else d_pre_own)[:, own] = d_pre
            acc[...] += matmul_nt(d_pre, wu[half, :, own])
    normed, inverse = normalized(mid_ref[...])
    d_x, d_shift, d_scale = modulated_back(normed, inverse, mod_m[1:2], acc[...])
    d_mod_m[0:1] = d_shift[None]
    d_mod_m[1:2] = d_scale[None]
    acc[...] = to_half(d_ref[...] + d_x).astype(jnp.float32)

    d_mod_a[2:3] = jnp.sum(acc[...] * branch_a[...], axis=0)[None]
    grad_a[...] = to_half(acc[...] * mod_a[2:3])
    copies[5].wait()
    d_att[...] = to_half(matmul_nt(grad_a[...], wa[1, :, D:]))
    d_acc[...] = jnp.zeros_like(d_acc)
    for head in range(HEADS):
        lanes, mask = window(head)
        at = lambda k: slice(D * k + lanes.start, D * k + lanes.stop)
        query, key, value = (qkv_ref[:, at(k)] for k in range(3))
        probs = softmax_rows(matmul_nt(own_lanes(mask, query), key) * SCALE)
        outer = d_att[:, lanes]
        d_acc[:, at(2)] += own_lanes(mask, matmul_tn(to_half(probs), outer))
        d_probs = matmul_nt(own_lanes(mask, outer), value)
        d_scores = to_half(probs * (d_probs - jnp.sum(probs * d_probs, axis=-1, keepdims=True)))
        d_acc[:, at(0)] += own_lanes(mask, matmul(d_scores, key) * SCALE)
        d_acc[:, at(1)] += own_lanes(mask, matmul_tn(d_scores, query) * SCALE)
    d_qkv_ref[...] = to_half(d_acc[...])
    first = flags[0] == 0
    pairs = ((d_qkv_ref[:, :D], d_qkv_ref[:, 2 * D :]), (d_qkv_ref[:, D : 2 * D], grad_a[...]))
    for k, (one, two) in enumerate(pairs):
        right_own[:, D * k : D * (k + 1)] = jnp.where(first, one, two)
        right_sib[:, D * k : D * (k + 1)] = jnp.where(first, two, one)
    copies[6].wait()
    d_xm = matmul_nt(d_qkv_ref[:, 2 * D :], wa[1, :, :D]) + matmul_nt(d_qkv_ref[:, : 2 * D], wa[0])
    normed, inverse = normalized(x_ref[...])
    d_x, d_shift, d_scale = modulated_back(normed, inverse, mod_a[1:2], d_xm)
    d_mod_a[0:1] = d_shift[None]
    d_mod_a[1:2] = d_scale[None]
    d_in_ref[...] = to_half(acc[...] + d_x)


def weight_scratch():
    return [pltpu.VMEM((2, D, HALF), BF)] * 3


def stage_cost():
    flops = 2 * PATCHES * D * 12 * D + 4 * PATCHES * PATCHES * D
    return pl.CostEstimate(flops=2 * flops, bytes_accessed=24 * D * D, transcendentals=2 * PATCHES * FF)


def stage_forward(save, x_in, weights):
    flags, mod_a, mod_m, w_blk, w_dn, b_attn, b_up, b_down = weights
    vmem, hbm = pl.BlockSpec(memory_space=pltpu.VMEM), pl.BlockSpec(memory_space=pl.ANY)
    smem = pl.BlockSpec(memory_space=pltpu.SMEM)
    like = lambda columns, kind: jax.ShapeDtypeStruct((PATCHES, columns), kind)
    tokens, wide = pltpu.VMEM((PATCHES, D), BF), pltpu.VMEM((PATCHES, 3 * D), BF)
    total = pltpu.VMEM((PATCHES, D), jnp.float32)
    f32 = jnp.float32
    if save:
        shapes = [like(D, f32), like(D, BF), like(3 * D, BF), like(D, BF), like(D, BF), like(D, f32), like(D, f32)]
        shapes += [like(D, BF), like(D, f32), like(FF, f32), like(HALF, BF), like(HALF, BF)]
        scratch = []
    else:
        shapes, scratch = [like(D, BF)], [tokens, wide, tokens, total, tokens]
    return pl.pallas_call(
        partial(forward_kernel, save),
        out_shape=tuple(shapes),
        in_specs=[smem] + [vmem] * 6 + [hbm] * 2,
        out_specs=(vmem,) * len(shapes),
        scratch_shapes=scratch + weight_scratch() + [total, pltpu.SemaphoreType.DMA((6,))],
        compiler_params=pltpu.CompilerParams(vmem_limit_bytes=VMEM_BYTES),
        cost_estimate=stage_cost(),
        name="stage_forward",
    )(flags, x_in, mod_a, mod_m, b_attn, b_up, b_down, w_blk, w_dn)


def stage_backward(d_out, x_in, weights, kept):
    flags, mod_a, mod_m, w_blk, w_dn, b_attn, b_up, b_down = weights
    xm_a, qkv, att, last, branch_a, x_mid, xm_m, branch_m, pre, act_own, act_sib = kept
    vmem, hbm = pl.BlockSpec(memory_space=pltpu.VMEM), pl.BlockSpec(memory_space=pl.ANY)
    smem = pl.BlockSpec(memory_space=pltpu.SMEM)
    like = lambda columns, kind: jax.ShapeDtypeStruct((PATCHES, columns), kind)
    mods = jax.ShapeDtypeStruct((3, D), jnp.float32)
    return pl.pallas_call(
        backward_kernel,
        out_shape=(like(D, BF), mods, mods, like(D, BF), like(D, BF))
        + (like(HALF, BF), like(HALF, BF), like(3 * D, BF), like(HALF, BF), like(HALF, BF)),
        in_specs=[smem] + [vmem] * 8 + [hbm] * 3,
        out_specs=(vmem,) * 10,
        scratch_shapes=weight_scratch()
        + [
            pltpu.VMEM((PATCHES, FF), jnp.float32),
            pltpu.VMEM((PATCHES, D), jnp.float32),
            pltpu.VMEM((PATCHES, 3 * D), jnp.float32),
            pltpu.VMEM((PATCHES, D), BF),
            pltpu.SemaphoreType.DMA((7,)),
        ],
        compiler_params=pltpu.CompilerParams(vmem_limit_bytes=VMEM_BYTES),
        cost_estimate=stage_cost(),
        name="stage_backward",
    )(flags, d_out, x_in, x_mid, mod_a, mod_m, branch_a, branch_m, qkv, pre, w_blk, w_dn)


COLUMNS = 384


def products_kernel(
    flags, dn_own, dn_sib, up_own, up_sib, xa_own, xa_sib, att_own, last_sib,
    act_own, act_sib, pre_own, pre_sib, right_own, right_sib,
    g_dn, g_up, g_attn, t_dn, t_up, t_one, t_two,
):
    step = pl.program_id(0)

    @pl.when(step == 0)
    def _():
        last_own = jnp.where(flags[0] == 0, xa_own[...], att_own[...])
        for target, own, sib in (
            (t_dn, dn_own[...], dn_sib), (t_up, up_own[...], up_sib),
            (t_one, xa_own[...], xa_sib), (t_two, last_own, last_sib),
        ):
            target[:, :PATCHES] = own.T
            target[:, PATCHES:] = sib[...].T

    def product(left, own, sib):
        return to_half(
            matmul(left[:, :PATCHES], own[...]) + matmul(left[:, PATCHES:], sib[...])
        )

    g_dn[...] = product(t_dn, act_own, act_sib)
    g_up[...] = product(t_up, pre_own, pre_sib)

    @pl.when(step < D // COLUMNS)
    def _():
        g_attn[...] = product(t_one, right_own, right_sib)

    @pl.when(step >= D // COLUMNS)
    def _():
        g_attn[...] = product(t_two, right_own, right_sib)


def products(flags, lefts, rights):
    left = whole_spec((PATCHES, D))
    right = pl.BlockSpec((PATCHES, COLUMNS), lambda step: (0, step))
    out = pl.BlockSpec((D, COLUMNS), lambda step: (0, step))
    return pl.pallas_call(
        products_kernel,
        grid=(HALF // COLUMNS,),
        out_shape=(jax.ShapeDtypeStruct((D, HALF), BF),) * 3,
        in_specs=[pl.BlockSpec(memory_space=pltpu.SMEM)] + [left] * 8 + [right] * 6,
        out_specs=(out,) * 3,
        scratch_shapes=[pltpu.VMEM((D, 2 * PATCHES), BF)] * 4,
        compiler_params=pltpu.CompilerParams(vmem_limit_bytes=VMEM_BYTES),
        cost_estimate=pl.CostEstimate(
            flops=12 * PATCHES * D * HALF, bytes_accessed=10 * D * HALF, transcendentals=0
        ),
        name="products",
    )(flags, *lefts, *rights)


def whole_spec(shape):
    return pl.BlockSpec(shape, lambda step: (0,) * len(shape))


SUM_ROWS = 16


def collect_kernel(flags_ref, *refs):
    tokens, d_pres, mods, fm_ref, extra_ref, tok_ref, head_ref = refs[:4], refs[4:6], refs[6:8], *refs[8:12]
    sums_ref, mods_ref, ends_ref, rows_ref = refs[12:]
    core, stage = flags_ref[0], flags_ref[1]
    ones = jnp.ones((8, PATCHES), BF)
    total = lambda value: matmul(ones, value)[0:1]
    sums_ref[...] = jnp.zeros_like(sums_ref)
    rows = [total(tokens[0][:, D * k : D * (k + 1)]) for k in range(3)]
    rows += [total(ref[...]) for ref in tokens[1:]]
    halves = [[total(ref[:, D * k : D * (k + 1)]) for k in range(2)] for ref in d_pres]
    own = halves[0] + halves[1]
    order = [jnp.where(core == 0, own[k], own[(k + 2) % 4]) for k in range(4)]
    last = jnp.where(stage == 0, rows[5], extra_ref[0:1])
    for place, row in enumerate(rows[:4] + order + [rows[4], last, extra_ref[1:2]]):
        sums_ref[place : place + 1, :D] = row
    ends = jnp.where(stage == 0, matmul_tn(tok_ref[...], tokens[3][...]), head_ref[...])
    ends_ref[...] = jnp.zeros_like(ends_ref)
    width = D // ends_ref.shape[0]
    for index in range(ends_ref.shape[0]):
        ends_ref[index, :, :width] = ends[:, width * index : width * (index + 1)]
    rows_ref[...] = jnp.zeros_like(rows_ref)
    for k in range(2):
        for row in range(5):
            source = mods[k][row : row + 1, :] if row < 3 else fm_ref[row - 3 : row - 2, :]
            for part in range(D // 128):
                at = row * (D // 128) + part
                rows_ref[at : at + 1] = source[:, 128 * part : 128 * (part + 1)]
        mods_ref[k] = to_half(rows_ref[...])


def collect(flags, tokens, d_pres, mods, fm, extra, tok, g_head):
    n = lax.axis_size("dp")
    vmem = pl.BlockSpec(memory_space=pltpu.VMEM)
    return pl.pallas_call(
        collect_kernel,
        out_shape=(
            jax.ShapeDtypeStruct((SUM_ROWS, 128 * max(2 * n, 9)), jnp.float32),
            jax.ShapeDtypeStruct((2, 48, 128), BF),
            jax.ShapeDtypeStruct((n, HEAD_OUT, WIDE), jnp.float32),
        ),
        scratch_shapes=[pltpu.VMEM((48, 128), jnp.float32)],
        in_specs=[pl.BlockSpec(memory_space=pltpu.SMEM)] + [vmem] * 12,
        out_specs=(vmem,) * 3,
        compiler_params=pltpu.CompilerParams(vmem_limit_bytes=VMEM_BYTES),
        name="collect",
    )(flags, *tokens, *d_pres, *mods, fm, extra, tok, g_head)


def final_step(x_out, fmod, w_head, b_head, target, counts, loss_scale):
    normed, inverse = normalized(x_out)
    xf_half = to_half(normed * (1.0 + fmod[1:2]) + fmod[0:1])
    error = matmul_nt(xf_half, w_head) + b_head - target
    loss = counts * jnp.sum(error * error)
    d_pred = to_half(2.0 * loss_scale * counts * error)
    g_head = matmul_tn(d_pred, xf_half)
    d_x, d_shift, d_scale = modulated_back(normed, inverse, fmod[1:2], matmul(d_pred, w_head))
    return (loss, d_x, jnp.stack([d_shift, d_scale]), g_head, column_sums(d_pred))


def nesterov(weight, moment, average, grad, factor):
    clipped = grad * factor
    moment_new = momentum_rate * moment + clipped
    weight_new = weight - learn_rate * (clipped + momentum_rate * moment_new)
    average_new = ema_decay * average + (1.0 - ema_decay) * weight_new
    return (weight_new, moment_new, average_new, weight_new.astype(jnp.bfloat16))


def down_update_kernel(factor, weight, moment, average, grad, *outs):
    values = nesterov(
        weight[...], moment[...], average[...], grad[...].astype(jnp.float32), factor[0]
    )
    for out, value in zip(outs, values):
        out[...] = value


def updated(like):
    f32 = jax.ShapeDtypeStruct(like.shape, jnp.float32)
    return (f32, f32, f32, jax.ShapeDtypeStruct(like.shape, BF))


def down_update(factor, weight, moment, average, grads):
    width = weight.shape[1]
    rows = width
    state = pl.BlockSpec((1, rows, HALF), lambda l, h, r: (l, r, h))
    return pl.pallas_call(
        down_update_kernel,
        grid=(LAYERS, 2, width // rows),
        out_shape=updated(weight),
        in_specs=[pl.BlockSpec(memory_space=pltpu.SMEM), state, state, state]
        + [pl.BlockSpec((1, rows, HALF), lambda l, h, r: (2 * l + h, r, 0))],
        out_specs=(state,) * 4,
        compiler_params=pltpu.CompilerParams(vmem_limit_bytes=VMEM_BYTES),
        cost_estimate=pl.CostEstimate(flops=10 * weight.size, bytes_accessed=28 * weight.size, transcendentals=0),
        name="down_update",
    )(factor, weight, moment, average, grads)


def stem_update_kernel(factor, weight, moment, average, g_table, g_patch, g_one, g_two, *outs):
    width, first = weight.shape[0], 0
    for grad, length in ((g_table, NCLS), (g_patch, PATCH_IN), (g_one, FREQ), (g_two, D)):
        part = slice(first, first + length)
        values = nesterov(
            weight[:, part], moment[:, part], average[:, part], grad[:width, :length], factor[0]
        )
        for out, value in zip(outs, values):
            out[:, part] = value
        first += length


def stem_update(factor, weight, moment, average, *grads):
    vmem = pl.BlockSpec(memory_space=pltpu.VMEM)
    return pl.pallas_call(
        stem_update_kernel,
        out_shape=updated(weight),
        in_specs=[pl.BlockSpec(memory_space=pltpu.SMEM)] + [vmem] * 7,
        out_specs=(vmem,) * 4,
        compiler_params=pltpu.CompilerParams(vmem_limit_bytes=VMEM_BYTES),
        cost_estimate=pl.CostEstimate(flops=10 * weight.size, bytes_accessed=30 * weight.size, transcendentals=0),
        name="stem_update",
    )(factor, weight, moment, average, *grads)


def swap(array, by):
    peers = lax.axis_size("section")
    return lax.ppermute(array, "section", [(k, k ^ by) for k in range(peers)])


def pick(parts, index):
    return lax.dynamic_index_in_dim(parts, index, 0, keepdims=False)


def body(
    latents, noise, timesteps, labels, null_mask, valid,
    mod_w, mod_m, mod_e, block_w, block_m, block_e, down_w, down_m, down_e,
    stem_w, stem_m, stem_e, tail_w, tail_m, tail_e, biases, bias_m, bias_e,
):
    place = lax.axis_index("dp")
    section = lax.axis_index("section")
    stage = section // 2
    core = lax.rem(section, 2)
    even = core == 0
    n = lax.axis_size("dp")
    width = D // n

    flags = jnp.stack([core, stage]).astype(jnp.int32)
    downs, stems = jnp.swapaxes(down_w, 1, 2), stem_w.T
    to_wide = lambda value: jnp.pad(value, ((0, 0),) * (value.ndim - 1) + ((0, WIDE - width),))
    ends = jnp.concatenate([stems[:, NCLS : NCLS + PATCH_IN], tail_w[:, 2 * D :]], axis=1)
    ends = to_wide(to_half(ends).T)
    classes = jnp.where(null_mask > 0, NCLS - 1, labels)
    freq = to_half(time_features(timesteps.astype(jnp.float32))).astype(jnp.float32)
    facts = jnp.stack([classes, valid], axis=1).astype(jnp.float32)
    meta = jnp.concatenate([freq, facts, jnp.zeros((2, META - FREQ - 2), jnp.float32)], axis=1)
    b_one, b_two = (lax.dynamic_slice_in_dim(biases, k * D + place * width, width)[None] for k in (31, 32))
    w_blk, w_dn, meta, ends, pre_own, hidden_all, cond, mods, mod_half_w, w_fm, two_blocks = gather_weights(
        block_w[0], downs, stems, mod_w[0], tail_w, meta, ends, to_wide(b_one), b_two
    )
    ends = ends[:, :, :width].transpose(1, 0, 2).reshape(ROWS_END, D)
    w_patch_all, w_head_all = ends[:PATCH_IN], ends[PATCH_IN:]
    images = 2 * n
    count = jnp.sum(meta[:, FREQ + 1])
    loss_scale = 1.0 / (count * PATCHES * HEAD_OUT)
    mods = mods.reshape(2, 8 * PIECE)
    bias_of = lambda first, length: lax.dynamic_slice_in_dim(biases, first, length)
    mod_a = (mods[0, : 3 * D] + bias_of(6 * D * stage, 3 * D)).reshape(3, D)
    mod_b = (mods[1, : 3 * D] + bias_of(6 * D * stage + 3 * D, 3 * D)).reshape(3, D)
    fmod = (mods[0, 3 * D : 5 * D] + biases[33 * D : 35 * D]).reshape(2, D)
    weights = (
        flags, mod_a, mod_b, w_blk, w_dn,
        bias_of(12 * D + 8 * D * stage, 4 * D)[None],
        jnp.concatenate(
            [bias_of(16 * D + 8 * D * stage + HALF * half, HALF)[None] for half in (core, 1 - core)], axis=1
        ),
        bias_of(28 * D + D * stage, D)[None],
    )

    step = pick(timesteps, core).astype(jnp.float32)
    signal, spread = noise_levels(step)
    lat, noi = pick(latents, core)[None], pick(noise, core)[None]
    counts = pick(valid, core).astype(jnp.float32)
    tok_half = to_half(patchify(signal * lat + spread * noi))[0]
    target = jnp.concatenate([patchify(signal * noi - spread * lat), patchify(noi)], axis=2)[0]
    x_first = matmul(tok_half, w_patch_all) + biases[30 * D : 31 * D] + position_table(GRID // 2, D)

    x_hop = swap(stage_forward(False, x_first, weights)[0], 2)
    x_in = jnp.where(stage == 0, x_first, x_hop.astype(jnp.float32))
    x_out, *kept = stage_forward(True, x_in, weights)
    loss, d_final, d_fmod, g_head, b_head = final_step(
        x_out, fmod, w_head_all, biases[35 * D :], target, counts, loss_scale
    )
    xm_a, qkv, attended, last_sib, branch_a, x_mid, xm_b, branch_b, pre, act_own, act_sib = kept
    d_hop = swap(stage_backward(d_final, x_in, weights, kept)[0], 2)
    d_out = jnp.where(stage == 1, d_final, d_hop.astype(jnp.float32))
    d_first, d_mod_a, d_mod_b, d_branch_a, d_branch_b, d_pre_own, d_pre_sib, d_qkv, right_own, right_sib = (
        stage_backward(d_out, x_in, weights, kept)
    )

    act_come, xb_come, xa_come, last_come = swap((act_sib, xm_b, xm_a, last_sib), 1)
    branch_come, pre_come, right_come = swap((d_branch_b, d_pre_sib, right_sib), 1)
    g_dn, g_up, g_attn = products(
        flags,
        (d_branch_b, branch_come, xm_b, xb_come, xm_a, xa_come, attended, last_come),
        (act_own, act_come, d_pre_own, pre_come, right_own, right_come),
    )

    extra = jnp.stack([jnp.pad(b_head, (0, D - HEAD_OUT)), jnp.pad(loss[None], (0, D - 1))])
    d_fmod = jnp.where(stage == 1, d_fmod, jnp.zeros_like(d_fmod))
    tok_wide = jnp.pad(tok_half, ((0, 0), (0, HEAD_OUT - PATCH_IN)))
    own_sums, d_mods, own_ends = collect(
        flags, (d_qkv, d_branch_a, d_branch_b, d_first), (d_pre_own, d_pre_sib), (d_mod_a, d_mod_b), d_fmod,
        extra, tok_wide, g_head,
    )
    own_sums = own_sums.reshape(SUM_ROWS, -1, 128).transpose(1, 0, 2)[: 2 * n]
    halves, crossed, dn_all, g_mod, g_fm, g_table, g_one, g_two, ends_all, news, mod_sums, fm_sum, squares = (
        sum_gradients(
            g_dn, g_up, g_attn, d_mods, own_sums, own_ends, mod_half_w, w_fm, two_blocks, cond, pre_own,
            hidden_all, meta,
        )
    )
    crossed = crossed.astype(jnp.float32)
    g_blk = jnp.concatenate(
        [jnp.where(even, halves[1], crossed), jnp.where(even, crossed, halves[0])], axis=1
    )
    ends = [ends_all[k, :, :width].T for k in (0, 3)]
    g_tail = jnp.concatenate([g_fm, ends[1]], axis=1)

    news = news.reshape(n, 4, -1, 128)
    stages = []
    for k in range(2):
        pieces = news[:, 2 * k : 2 * k + 2, :SUM_ROWS].reshape(2 * n, SUM_ROWS, 128)[: D // 128]
        stages.append(pieces.transpose(1, 0, 2).reshape(-1))
    slices = news[:, 0, SUM_ROWS : SUM_ROWS + 4].reshape(n, 2, WIDE)[:, :, :width]
    bias_grad = jnp.concatenate(
        [mod_sums.reshape(-1)]
        + [part[: 8 * D] for part in stages]
        + [part[8 * D : 9 * D] for part in stages]
        + [stages[0][9 * D : 10 * D]]
        + [slices[:, 0].reshape(-1), slices[:, 1].reshape(-1)]
        + [fm_sum[0], stages[1][9 * D : 9 * D + HEAD_OUT]]
    )
    loss_sum = stages[1][10 * D]
    grad_norm = jnp.sqrt(squares[0, 0])
    factor = jnp.minimum(1.0, clip_limit / (grad_norm + 1e-06))
    mod_out = nesterov(mod_w, mod_m, mod_e, g_mod[None], factor)
    block_out = nesterov(block_w, block_m, block_e, g_blk[None], factor)
    flip = lambda value: jnp.swapaxes(value, 1, 2)
    scalar = factor.reshape(1)
    down_out = tuple(map(flip, down_update(scalar, downs, flip(down_m), flip(down_e), dn_all)))
    stem_out = stem_update(
        scalar, stems, stem_m.T, stem_e.T, g_table, ends[0][:, :PATCH_IN], g_one, g_two
    )
    stem_out = tuple(value.T for value in stem_out)
    tail_out = nesterov(tail_w, tail_m, tail_e, g_tail, factor)
    bias_out = nesterov(biases, bias_m, bias_e, bias_grad, factor)
    return (
        (loss_sum, count, grad_norm)
        + mod_out + block_out + down_out + stem_out + tail_out + bias_out
    )


def solution(mesh):
    images = (P("dp", None, None, None),) * 2 + (P("dp"),) * 4
    owned = P("section", "dp", None)
    states = (owned,) * 6 + (P(None, None, "dp"),) * 3 + (P(None, "dp"),) * 3 + (P("dp", None),) * 3 + (P(),) * 3
    updates = (owned,) * 8 + (P(None, None, "dp"),) * 4 + (P(None, "dp"),) * 4 + (P("dp", None),) * 4 + (P(),) * 4
    return jax.shard_map(
        body,
        mesh=mesh,
        in_specs=images + states,
        out_specs=(P(), P(), P()) + updates,
        check_vma=False,
    )
```

```python
from functools import partial
import math

import jax
import jax.numpy as jnp
from jax import lax
from jax.experimental import pallas as pl
from jax.experimental.pallas import tpu as pltpu
from jax.sharding import PartitionSpec as P

HEADS = 16
HEAD_DIM = 72
D = 1152
FF = 4608
HALF = FF // 2
NCLS = 1001
FREQ = 256
GRID = 32
PATCHES = 256
PATCH_IN = 16
HEAD_OUT = 32
LAYERS = 2
NBIAS = 40352


epsilon_norm = 1e-06
momentum_rate = 0.9
ema_decay = 0.9
learn_rate = 4000.0
clip_limit = 0.02
MESH = pl.DeviceIdType.MESH
BF = jnp.bfloat16


def matmul(left, right):
    return jnp.dot(left, right, preferred_element_type=jnp.float32)


def matmul_nt(left, right):
    return lax.dot_general(
        left, right, (((1,), (1,)), ((), ())), preferred_element_type=jnp.float32
    )


def matmul_tn(left, right):
    return lax.dot_general(
        left, right, (((0,), (0,)), ((), ())), preferred_element_type=jnp.float32
    )


def to_half(value):
    return value.astype(BF)


def column_sums(value):
    return jnp.sum(value.astype(jnp.float32), axis=0)


def silu_back(value, grad):
    return jax.vjp(jax.nn.silu, value)[1](grad)[0]


def patchify(field):
    images, side = (field.shape[0], field.shape[1] // 2)
    return (
        field.reshape(images, side, 2, side, 2, 4)
        .transpose(0, 1, 3, 2, 4, 5)
        .reshape(images, side * side, 16)
    )


def sincos_rows(places, width):
    omega = 1.0 / 10000.0 ** (jnp.arange(width // 2, dtype=jnp.float32) / (width // 2))
    angle = places[:, None] * omega[None, :]
    return jnp.concatenate([jnp.sin(angle), jnp.cos(angle)], axis=1)


def position_table(side, width):
    line = sincos_rows(jnp.arange(side, dtype=jnp.float32), width // 2)
    column = jnp.broadcast_to(line[None], (side, side, width // 2))
    row = jnp.broadcast_to(line[:, None], (side, side, width // 2))
    return jnp.concatenate([column, row], axis=2).reshape(side * side, width)


def time_features(steps):
    half = FREQ // 2
    freqs = jnp.exp(-math.log(10000.0) * jnp.arange(half, dtype=jnp.float32) / half)
    angle = steps[:, None] * freqs[None, :]
    return jnp.concatenate([jnp.cos(angle), jnp.sin(angle)], axis=1)


def noise_levels(steps):
    level = jnp.cos((steps / 1000.0 + 0.008) / 1.008 * (math.pi / 2)) ** 2
    return (jnp.sqrt(level), jnp.sqrt(1.0 - level))


Z, X = 4, 2
GATHER_CHUNKS = (
    (0, 0, 48, True), (0, 48, 48, True), (0, 96, 48, False),
    (1, 0, 48, False), (1, 48, 48, False), (1, 96, 48, False),
)
CHUNKS = ((0, 16, True), (16, 32, False), (48, 32, False), (80, 32, False), (112, 32, False))
META = 384
WIDE = 256
ROWS_END = PATCH_IN + HEAD_OUT
PIECE = 768


def ring_fits(n, rows):
    return n == Z * X and rows == 144


def one_hot(classes, width):
    lane = lax.broadcasted_iota(jnp.int32, (classes.shape[0], width), 1).astype(jnp.float32)
    return to_half(jnp.maximum(1.0 - jnp.abs(lane - classes), 0.0))


def gather_kernel(
    blk_hbm, dn_hbm, stem_hbm, mod_hbm, tail_hbm, meta_ref, ends_ref, b_one, b_two,
    out_blk, out_dn, meta_out, ends_out, pre_out, hidden_out, cond_out, mods_out, mod_ref, fm_ref, two_ref,
    blk_f, dn_f, stem_f, mod_f, tail_f, blk_ref, dn_ref, one_ref, table_ref, load_sem, metas, hidden, part, parts, arrived_parts,
    meta_send, meta_recv, ends_send, ends_recv, hid_send, hid_recv, part_send, part_recv, local_sem,
    up_sem, down_sem, x_sem, sib_sem, recv_sem, sib_recv, own_sem,
):
    me = lax.axis_index("dp")
    section = lax.axis_index("section")
    z, x = me // X, lax.rem(me, X)
    core = lax.rem(section, 2)
    sibling = section + 1 - 2 * core
    across = me + 1 - 2 * x
    chunks = len(GATHER_CHUNKS)
    low = section - core
    group, place_in = Z * X * 2, me * 2 + core
    where = lambda p: {"dp": p // 2, "section": low + lax.rem(p, 2)}
    has_up, has_down = z < Z - 1, z > 0

    stage_rows = dn_hbm.at[section // 2, :, pl.ds(pl.multiple_of(core * HALF, 128), HALF)]
    loads = [
        pltpu.make_async_copy(src, dst, load_sem.at[k])
        for k, (src, dst) in enumerate(
            ((blk_hbm, blk_f), (stage_rows, dn_f), (stem_hbm, stem_f), (mod_hbm, mod_f), (tail_hbm, tail_f))
        )
    ]
    for copy_in in loads:
        copy_in.start()
    barrier = pltpu.get_barrier_semaphore()

    @pl.loop(1, group)
    def _(step):
        pl.semaphore_signal(
            barrier, 1, device_id=where(lax.rem(place_in + step, group)), device_id_type=MESH
        )

    pl.semaphore_wait(barrier, group - 1)

    def to_dp(src, dst, send, recv, step, p, slot):
        return pltpu.make_async_remote_copy(
            src_ref=src, dst_ref=dst.at[slot], send_sem=send.at[step], recv_sem=recv.at[step],
            device_id={"dp": p}, device_id_type=MESH,
        )

    meta_copy = partial(to_dp, meta_ref, metas, meta_send, meta_recv)
    ends_copy = partial(to_dp, ends_ref, ends_out, ends_send, ends_recv)
    hidden_copy = partial(to_dp, hidden, hidden_out, hid_send, hid_recv)

    def part_copy(step, p, slot):
        return pltpu.make_async_remote_copy(
            src_ref=parts.at[p], dst_ref=arrived_parts.at[slot],
            send_sem=part_send.at[step], recv_sem=part_recv.at[step],
            device_id=where(p), device_id_type=MESH,
        )

    own_meta = pltpu.make_async_copy(meta_ref, metas.at[me], local_sem.at[0])
    own_ends = pltpu.make_async_copy(ends_ref, ends_out.at[me], local_sem.at[1])
    own_hidden = pltpu.make_async_copy(hidden, hidden_out.at[me], local_sem.at[2])
    own_part = pltpu.make_async_copy(parts.at[place_in], arrived_parts.at[place_in], local_sem.at[3])

    def send_all(copy_to, size, index):
        @pl.loop(1, size)
        def _(step):
            copy_to(step, lax.rem(index + step, size), index).start()

    def wait_all(copy_to, size, index):
        @pl.loop(1, size)
        def _(step):
            p = lax.rem(index + size - step, size)
            copy_to(step, p, p).wait_recv()
            copy_to(step, p, p).wait_send()

    own_meta.start()
    own_ends.start()
    send_all(meta_copy, Z * X, me)

    def place(owner, k, side):
        which, first, rows, unused = GATHER_CHUNKS[k]
        return (out_dn if which else out_blk).at[side, pl.ds(pl.multiple_of(owner * 144 + first, 16), rows)]

    def source(owner, k, mine):
        if not mine:
            return place(owner, k, core)
        which, first, rows, unused = GATHER_CHUNKS[k]
        return (dn_ref if which else blk_ref).at[pl.ds(first, rows)]

    def copy(owner, k, mine, sem, target):
        unit = owner * chunks + k
        return pltpu.make_async_remote_copy(
            src_ref=source(owner, k, mine),
            dst_ref=place(owner, k, core),
            send_sem=sem.at[unit],
            recv_sem=recv_sem.at[unit],
            device_id={"dp": target},
            device_id_type=MESH,
        )

    def to_sibling(owner, k, mine):
        unit = owner * chunks + k
        return pltpu.make_async_remote_copy(
            src_ref=source(owner, k, mine),
            dst_ref=place(owner, k, core),
            send_sem=sib_sem.at[unit],
            recv_sem=sib_recv.at[unit],
            device_id={"section": sibling},
            device_id_type=MESH,
        )

    def own_copy(k):
        return pltpu.make_async_copy(source(me, k, True), place(me, k, core), own_sem.at[k])

    def arrived(owner, k):
        copy(owner, k, False, x_sem, across).wait_recv()

    for which in range(2):
        loads[which].wait()

        @pl.loop(0, 144 // 16)
        def _(step):
            rows = pl.ds(pl.multiple_of(step * 16, 16), 16)
            if which:
                dn_ref[rows] = to_half(dn_f[rows])
            else:
                blk_ref[rows] = to_half(blk_f[rows])

    for k in range(chunks):
        @pl.when(has_up)
        def _():
            copy(me, k, True, up_sem, me + X).start()

        @pl.when(has_down)
        def _():
            copy(me, k, True, down_sem, me - X).start()

        copy(me, k, True, x_sem, across).start()
        own_copy(k).start()
        to_sibling(me, k, True).start()

    send_all(ends_copy, Z * X, me)

    at_one, at_two = NCLS + PATCH_IN, NCLS + PATCH_IN + FREQ
    for copy_in in loads[2:]:
        copy_in.wait()
    for ref in (table_ref, one_ref, two_ref):
        ref[...] = jnp.zeros_like(ref)
    table_ref[:, :NCLS] = to_half(stem_f[:, :NCLS])
    one_ref[:144] = to_half(stem_f[:, at_one:at_two])
    for index in range(Z * X):
        two_ref[index, :, :144] = to_half(stem_f[:, at_two + 144 * index : at_two + 144 * (index + 1)])
    mod_ref[...] = to_half(mod_f[...])
    fm_ref[...] = to_half(tail_f[:, : 2 * D])

    def make_hidden():
        own_meta.wait()
        wait_all(meta_copy, Z * X, me)
        for index in range(Z * X):
            meta_out[2 * index : 2 * index + 2] = metas[index]
        pre = matmul_nt(to_half(meta_out[:, :FREQ]), one_ref[...]) + b_one[...]
        pre_out[...] = pre
        hidden[...] = to_half(jax.nn.silu(pre))
        own_hidden.start()
        send_all(hidden_copy, Z * X, me)

    def make_parts():
        own_hidden.wait()
        wait_all(hidden_copy, Z * X, me)
        cond = matmul_nt(one_hot(meta_out[:, FREQ : FREQ + 1], table_ref.shape[1]), table_ref[...]) + b_two[...]
        for index in range(Z * X):
            cond = cond + matmul_nt(hidden_out[index], two_ref[index])
        cond_out[...] = cond
        cond_low = to_half(cond).astype(jnp.float32)
        own_cond = jnp.where(section == 0, cond, cond_low)
        part[:, : 3 * D] = matmul(to_half(jax.nn.silu(own_cond)), mod_ref[...])
        part[:, 3 * D : 5 * D] = matmul(to_half(jax.nn.silu(cond_low)), fm_ref[...])
        part[:, 5 * D :] = jnp.zeros((group, 8 * PIECE - 5 * D), jnp.float32)
        for row in range(group):
            for k in range(8):
                parts[row, k : k + 1] = part[row : row + 1, PIECE * k : PIECE * (k + 1)]
        own_part.start()
        send_all(part_copy, group, place_in)

    def along(step, k):
        crosses = not (step == 1 and GATHER_CHUNKS[k][3])
        for sign in (-1, 1):
            @pl.when((z >= step) if sign < 0 else (z + step < Z))
            def _():
                owner = me + sign * X * step
                arrived(owner, k)

                @pl.when(has_up if sign < 0 else has_down)
                def _():
                    copy(owner, k, False, up_sem if sign < 0 else down_sem, me - sign * X).start()

                if crosses:
                    copy(owner, k, False, x_sem, across).start()
                to_sibling(owner, k, False).start()

    def crossed(step, k):
        if step == 0:
            arrived(across, k)
            if GATHER_CHUNKS[k][3]:
                @pl.when(has_up)
                def _():
                    copy(across, k, False, up_sem, me + X).start()

                @pl.when(has_down)
                def _():
                    copy(across, k, False, down_sem, me - X).start()
            to_sibling(across, k, False).start()
            return
        for sign in (-1, 1):
            @pl.when((z >= step) if sign < 0 else (z + step < Z))
            def _():
                owner = across + sign * X * step
                arrived(owner, k)
                to_sibling(owner, k, False).start()

    for step in range(1, Z + 1):
        for k in range(chunks):
            if step < Z:
                along(step, k)
            crossed(step - 1, k)
        if step == 1:
            make_hidden()
        if step == 2:
            make_parts()

    own_part.wait()
    wait_all(part_copy, group, place_in)
    own_ends.wait()
    wait_all(ends_copy, Z * X, me)
    for source_core in range(2):
        total = arrived_parts[source_core]
        for index in range(1, Z * X):
            total = total + arrived_parts[2 * index + source_core]
        mods_out[source_core] = total

    for k in range(chunks):
        near = GATHER_CHUNKS[k][3]
        own_copy(k).wait()
        for column in range(2):
            base = me if column == 0 else across
            for step in range(0, Z):
                for sign in (-1, 1) if step else (1,):
                    @pl.when((z >= step) if sign < 0 else (z + step < Z))
                    def _():
                        owner = base + sign * X * step
                        mine = column == 0 and step == 0
                        to_sibling(owner, k, mine).wait_send()
                        pltpu.make_async_remote_copy(
                            src_ref=place(owner, k, 1 - core),
                            dst_ref=place(owner, k, 1 - core),
                            send_sem=sib_sem.at[owner * chunks + k],
                            recv_sem=sib_recv.at[owner * chunks + k],
                            device_id={"section": sibling},
                            device_id_type=MESH,
                        ).wait_recv()
                        runs = column == 0 or (near and step == 0)
                        if runs and (step == 0 or sign < 0):
                            @pl.when(has_up)
                            def _():
                                copy(owner, k, mine, up_sem, me + X).wait_send()
                        if runs and (step == 0 or sign > 0):
                            @pl.when(has_down)
                            def _():
                                copy(owner, k, mine, down_sem, me - X).wait_send()
                        if column == 0 and not (step == 1 and near):
                            copy(owner, k, mine, x_sem, across).wait_send()


def gather_weights(block, downs, stems, mod, tail, meta, ends, b_one, b_two):
    n, width = lax.axis_size("dp"), block.shape[0]
    section = lax.axis_index("section")
    if not ring_fits(n, width):
        both = lambda own, sib: jnp.where(
            lax.rem(section, 2) == 0, jnp.stack([own, sib]), jnp.stack([sib, own])
        )
        core = lax.rem(section, 2)
        dn = lax.dynamic_slice(downs, (section // 2, 0, core * HALF), (1, width, HALF))[0]
        blk = lax.all_gather(to_half(block), "dp", axis=0, tiled=True)
        dn = lax.all_gather(to_half(dn), "dp", axis=0, tiled=True)
        at_one, at_two = NCLS + PATCH_IN, NCLS + PATCH_IN + FREQ
        stem, w_mod, w_fm = to_half(stems), to_half(mod), to_half(tail[:, : 2 * D])
        table = jnp.pad(stem[:, :NCLS], ((0, 0), (0, -NCLS % 128)))
        w_one = jnp.pad(stem[:, at_one:at_two], ((0, WIDE - width), (0, 0)))
        w_two = stem[:, at_two:].reshape(width, n, width).transpose(1, 0, 2)
        w_two = jnp.pad(w_two, ((0, 0), (0, 0), (0, WIDE - width)))
        meta, ends = exchange(2, "dp", ("all", "all"), meta, ends)
        meta = meta.reshape(2 * n, META)
        pre = matmul_nt(to_half(meta[:, :FREQ]), w_one) + b_one
        (hidden,) = exchange(8, "dp", ("all",), to_half(jax.nn.silu(pre)))
        cond = matmul_nt(one_hot(meta[:, FREQ : FREQ + 1], table.shape[1]), table) + b_two
        cond = cond + jnp.einsum("jik,jwk->iw", hidden, w_two, preferred_element_type=jnp.float32)
        cond_low = to_half(cond).astype(jnp.float32)
        own_cond = jnp.where(section == 0, cond, cond_low)
        parts = [
            matmul(to_half(jax.nn.silu(own_cond)), w_mod),
            matmul(to_half(jax.nn.silu(cond_low)), w_fm),
        ]
        parts = jnp.pad(jnp.concatenate(parts, axis=1), ((0, 0), (0, 8 * PIECE - 5 * D)))
        (parts,) = exchange(3, "stage", ("each",), parts.reshape(2 * n, 8, PIECE))
        mods = jnp.sum(parts.reshape(n, 2, 8, PIECE), axis=0)
        own = (both(blk, swap(blk, 1)), both(dn, swap(dn, 1)), meta, ends, pre, hidden, cond, mods)
        return own + (w_mod, w_fm, w_two)
    units, images = n * len(GATHER_CHUNKS), 2 * n
    hbm, vmem = pl.BlockSpec(memory_space=pl.ANY), pl.BlockSpec(memory_space=pltpu.VMEM)
    dma = lambda count: pltpu.SemaphoreType.DMA((count,))
    f32 = jnp.float32
    return pl.pallas_call(
        gather_kernel,
        out_shape=(
            jax.ShapeDtypeStruct((2, D, FF), BF), jax.ShapeDtypeStruct((2, D, HALF), BF),
            jax.ShapeDtypeStruct((images, META), f32), jax.ShapeDtypeStruct((n,) + ends.shape, BF),
            jax.ShapeDtypeStruct((images, WIDE), f32), jax.ShapeDtypeStruct((n, images, WIDE), BF),
            jax.ShapeDtypeStruct((images, width), f32), jax.ShapeDtypeStruct((2, 8, PIECE), f32),
            jax.ShapeDtypeStruct((width, 3 * D), BF), jax.ShapeDtypeStruct((width, 2 * D), BF),
            jax.ShapeDtypeStruct((n, width, WIDE), BF),
        ),
        in_specs=[hbm] * 5 + [vmem] * 4,
        out_specs=(hbm, hbm) + (vmem,) * 9,
        scratch_shapes=[
            pltpu.VMEM((width, FF), f32), pltpu.VMEM((width, HALF), f32), pltpu.VMEM(stems.shape, f32),
            pltpu.VMEM((width, 3 * D), f32), pltpu.VMEM(tail.shape, f32),
            pltpu.VMEM((width, FF), BF), pltpu.VMEM((width, HALF), BF), pltpu.VMEM((WIDE, FREQ), BF),
            pltpu.VMEM((width, 1024), BF), dma(5),
            pltpu.VMEM((n, 2, META), f32), pltpu.VMEM((images, WIDE), BF),
            pltpu.VMEM((images, 8 * PIECE), f32),
            pltpu.VMEM((images, 8, PIECE), f32), pltpu.VMEM((images, 8, PIECE), f32),
            dma(n), dma(n), dma(n), dma(n), dma(n), dma(n), dma(images), dma(images), dma(4),
        ]
        + [dma(units)] * 6
        + [dma(len(GATHER_CHUNKS))],
        compiler_params=pltpu.CompilerParams(
            collective_id=0, has_side_effects=True, vmem_limit_bytes=VMEM_BYTES
        ),
        cost_estimate=pl.CostEstimate(flops=0, bytes_accessed=400_000_000, transcendentals=0),
        name="gather_weights",
    )(block, downs, stems, mod, tail, meta, ends, b_one, b_two)


VMEM_BYTES = 60 * 1024 * 1024
SUM_CHUNKS = tuple((which,) + chunk for which in range(3) for chunk in CHUNKS)


def silu_slope(value):
    gate = jax.nn.sigmoid(value)
    return gate * (1.0 + value * (1.0 - gate))


def sum_kernel(
    g_dn, g_up, g_attn, dm_ref, bp_ref, en_ref, mod_ref, fm_ref, two_ref, cond_ref, pre_ref, hid_ref, meta_ref,
    out, cross_out, dn_out, gmod_out, gfm_out, gtab_out, gone_out, gtwo_out,
    ends_all, bias_out, sq_out,
    own_b, other_d, xb, xq, up_b, up_o, down_b, down_o, acc, acc_dn,
    dm_in, bp_in, en_in, dmat, ends_src, c_src, c_in, fmd_src, fmd_in, cs_src, dcond, ph, ph_in, news_src,
    sq_src, sq_all, sq_rows, cross_src, news_out, cs_all, fmsum_out,
    load_sem, x_send, x_recv, up_send, up_recv, down_send, down_recv,
    sib_send, sib_recv, y_send, y_recv, group_send, group_recv, sect_send, sect_recv,
    ph_send, ph_recv, news_send, news_recv, sq_send, sq_recv, cross_sem, local_sem,
):
    me = lax.axis_index("dp")
    section = lax.axis_index("section")
    z, x = me // X, lax.rem(me, X)
    core = lax.rem(section, 2)
    low, sibling, facing = section - core, section + 1 - 2 * core, lax.rem(section + 2, 4)
    across = me + 1 - 2 * x
    sources = (g_dn, g_up, g_attn)
    chunks = len(SUM_CHUNKS)
    has_up, has_down = z < Z - 1, z > 0
    devices, group = Z * X * 4, Z * X * 2
    me_all, me_group = me * 4 + section, me * 2 + core
    in_all = lambda p: {"dp": p // 4, "section": lax.rem(p, 4)}
    in_group = lambda p: {"dp": p // 2, "section": low + lax.rem(p, 2)}
    in_section = lambda p: {"section": p}
    in_dp = lambda p: {"dp": p}
    f32 = jnp.float32

    barrier = pltpu.get_barrier_semaphore()

    @pl.loop(1, devices)
    def _(step):
        pl.semaphore_signal(
            barrier, 1, device_id=in_all(lax.rem(me_all + step, devices)), device_id_type=MESH
        )

    def small(src_of, dst, send, recv, where, size, index):
        def copy(step, p, slot):
            return pltpu.make_async_remote_copy(
                src_ref=src_of(p), dst_ref=dst.at[slot], send_sem=send.at[step], recv_sem=recv.at[step],
                device_id=where(p), device_id_type=MESH,
            )
        return (copy, size, index, src_of, dst)

    gradients = [
        small(lambda p: dm_ref.at[lax.rem(p, 2)], dm_in, group_send.at[0], group_recv.at[0], in_group, group, me_group),
        small(lambda p: bp_ref.at[p], bp_in, group_send.at[1], group_recv.at[1], in_group, group, me_group),
        small(lambda p: en_ref.at[p // 2], en_in, group_send.at[2], group_recv.at[2], in_group, group, me_group),
    ]
    conds = [
        small(lambda p, src=src: src, dst, sect_send.at[k], sect_recv.at[k], in_section, 4, section)
        for k, (src, dst) in enumerate(
            ((c_src, c_in), (ends_src, ends_all), (fmd_src, fmd_in), (cs_src, cs_all))
        )
    ]
    hiddens = [small(lambda p: ph.at[p], ph_in, ph_send, ph_recv, in_dp, Z * X, me)]
    news = [small(lambda p: news_src, news_out, news_send, news_recv, in_all, devices, me_all)]
    norms = [small(lambda p: sq_src, sq_all, sq_send, sq_recv, in_all, devices, me_all)]

    def own_copies(batch, first):
        return [
            pltpu.make_async_copy(src_of(index), dst.at[index], local_sem.at[first + k])
            for k, (copy, size, index, src_of, dst) in enumerate(batch)
        ]

    def send_batch(batch, first):
        for copy in own_copies(batch, first):
            copy.start()
        for copy, size, index, src_of, dst in batch:
            @pl.loop(1, size)
            def _(step):
                copy(step, lax.rem(index + step, size), index).start()

    def wait_batch(batch, first):
        for copy in own_copies(batch, first):
            copy.wait()
        for copy, size, index, src_of, dst in batch:
            @pl.loop(1, size)
            def _(step):
                p = lax.rem(index + size - step, size)
                copy(step, p, p).wait_recv()
                copy(step, p, p).wait_send()

    def add_square(value):
        sq_src[...] += jnp.sum(value * value)

    def images_of():
        cond = cond_ref[...]
        cond_low = to_half(cond).astype(f32)
        return jnp.where(section == 0, cond, cond_low), cond_low

    def make_cond():
        wait_batch(gradients, 0)
        flat = dm_in[...].reshape(group * 48, 128)
        row = lax.broadcasted_iota(jnp.int32, (group, group * 48), 0) * 48
        column = lax.broadcasted_iota(jnp.int32, (group, group * 48), 1)
        for k in range(5 * D // 128):
            chosen = jnp.where(column == row + k, 1.0, 0.0).astype(BF)
            dmat[:, 128 * k : 128 * (k + 1)] = to_half(matmul(chosen, flat))
        news_src[...] = jnp.zeros_like(news_src)
        news_src[0:SUM_ROWS] = jnp.sum(bp_in[...], axis=0)
        ends_src[...] = jnp.sum(en_in[...], axis=0)
        own_cond, cond_low = images_of()
        d_mod, d_fm = dmat[:, : 3 * D], dmat[:, 3 * D :]
        fmd_src[...] = d_fm
        cs_src[...] = jnp.sum(d_mod.astype(f32), axis=0, keepdims=True)
        d_silu = matmul_nt(d_mod, mod_ref[...])
        d_silu = d_silu + (section == 3).astype(f32) * matmul_nt(d_fm, fm_ref[...])
        c_src[...] = jnp.zeros_like(c_src)
        c_src[:, :144] = silu_slope(own_cond) * d_silu
        send_batch(conds, 3)
        silu_own = to_half(jax.nn.silu(own_cond))
        for k in range(3):
            part_g = matmul_tn(silu_own, dmat[:, D * k : D * (k + 1)])
            gmod_out[:, D * k : D * (k + 1)] = part_g
            add_square(part_g)

    once = (section == 0).astype(f32)

    def make_hidden():
        wait_batch(conds, 3)
        total = to_half(c_in[3])
        for slot in (2, 1, 0):
            total = to_half(total.astype(f32) + c_in[slot])
        dcond[...] = total
        d_cond = dcond[:, :144]
        for index in range(Z * X):
            ph[index] = matmul(d_cond, two_ref[index])
        send_batch(hiddens, 7)
        own_cond, cond_low = images_of()
        silu_low = to_half(jax.nn.silu(cond_low))
        for k in range(2):
            part_g = matmul_tn(silu_low, fmd_in[3, :, D * k : D * (k + 1)])
            gfm_out[:, D * k : D * (k + 1)] = part_g
            add_square(jnp.sqrt(once) * part_g)
        fmsum_out[...] = jnp.sum(fmd_in[3].astype(f32), axis=0, keepdims=True)
        part_g = matmul_tn(d_cond, one_hot(meta_ref[:, FREQ : FREQ + 1], gtab_out.shape[1]))
        gtab_out[...] = part_g
        add_square(once * part_g)
        for index in range(Z * X):
            part_g = matmul_tn(d_cond, hid_ref[index])
            gtwo_out[:, 144 * index : 144 * (index + 1)] = part_g[:, :144]
            add_square(once * part_g)

    def make_news():
        wait_batch(hiddens, 7)
        total = ph_in[0]
        for index in range(1, Z * X):
            total = total + ph_in[index]
        d_pre = to_half(silu_slope(pre_ref[...]) * total)
        part_g = matmul_tn(d_pre, to_half(meta_ref[:, :FREQ]))
        gone_out[...] = part_g
        add_square(once * part_g)
        sums = jnp.sum(d_pre.astype(f32), axis=0, keepdims=True)
        sums_cond = jnp.sum(dcond[...].astype(f32), axis=0, keepdims=True)
        for k in range(2):
            news_src[SUM_ROWS + k : SUM_ROWS + k + 1] = sums[:, 128 * k : 128 * (k + 1)]
            news_src[SUM_ROWS + 2 + k : SUM_ROWS + 3 + k] = sums_cond[:, 128 * k : 128 * (k + 1)]
        send_batch(news, 8)
        first = (me == 0).astype(f32)
        add_square(news_src[0:10])
        add_square(once * sums)
        add_square(once * sums_cond)
        add_square(first * cs_src[...])
        add_square(first * once * fmsum_out[...])
        add_square(once * ends_all[0])
        add_square(once * ends_all[3])

    def make_biases():
        wait_batch(news, 8)
        bias_out[...] = jnp.zeros_like(bias_out)
        for slot in range(4):
            for k in range(3):
                row = 3 * slot + k
                bias_out[row : row + 1] = cs_all[slot, :, D * k : D * (k + 1)]
        for side in range(2):
            for block in range(D // 128):
                part = slice(128 * block, 128 * (block + 1))
                device = (block // 2) * 4 + 2 * side + block % 2
                bias_out[12 + 8 * side : 20 + 8 * side, part] = news_out[device, 0:8]
                bias_out[28 + side : 29 + side, part] = news_out[device, 8:9]
                row = 35 if side else 30
                bias_out[row : row + 1, part] = news_out[device, 9:10]
                if side:
                    bias_out[36:37, part] = news_out[device, 10:11]
        for index in range(Z * X):
            first = 144 * index
            for k in range(2):
                at = SUM_ROWS + 2 * k
                bias_out[31 + k : 32 + k, first : first + 128] = news_out[4 * index, at : at + 1]
                bias_out[31 + k : 32 + k, first + 128 : first + 144] = news_out[4 * index, at + 1 : at + 2, :16]
        for k in range(2):
            bias_out[33 + k : 34 + k] = fmsum_out[:, D * k : D * (k + 1)]

    def dn_copy(k, slot, to_sib):
        rows = pl.ds(SUM_CHUNKS[k][1], SUM_CHUNKS[k][2])
        unit = slot * chunks + k
        return pltpu.make_async_remote_copy(
            src_ref=dn_out.at[slot, rows], dst_ref=dn_out.at[slot, rows],
            send_sem=(sib_send if to_sib else y_send).at[unit],
            recv_sem=(sib_recv if to_sib else y_recv).at[unit],
            device_id={"section": sibling if to_sib else facing},
            device_id_type=MESH,
        )

    def each(distance, run):
        if distance == 0:
            run(z, None)
            return

        @pl.when(z + distance < Z)
        def _():
            run(z + distance, True)

        @pl.when(z >= distance)
        def _():
            run(z - distance, False)

    def part(k):
        return pl.ds(SUM_CHUNKS[k][1], SUM_CHUNKS[k][2])

    def hbm(k, zz, column):
        start = pl.multiple_of((zz * X + column) * 144 + SUM_CHUNKS[k][1], 16)
        return sources[SUM_CHUNKS[k][0]].at[pl.ds(start, SUM_CHUNKS[k][2])]

    def own(k, zz):
        return own_b.at[SUM_CHUNKS[k][0], zz, part(k)]

    def from_x(k, zz):
        return xq.at[SUM_CHUNKS[k][0]] if SUM_CHUNKS[k][3] else xb.at[SUM_CHUNKS[k][0], zz, part(k)]

    def from_z(k, zz, up, other):
        if other:
            return (up_o if up else down_o).at[SUM_CHUNKS[k][0], zz]
        return (up_b if up else down_b).at[SUM_CHUNKS[k][0], zz, part(k)]

    def other_of(k, zz):
        return other_d.at[SUM_CHUNKS[k][0], zz]

    def load(k, zz, other=False):
        index = ((chunks if other else 0) + k) * Z + zz
        return pltpu.make_async_copy(
            hbm(k, zz, (1 - x) if other else x),
            other_of(k, zz) if other else own(k, zz),
            load_sem.at[index],
        )

    def x_copy(k, zz, src):
        unit = k * Z + zz
        return pltpu.make_async_remote_copy(
            src_ref=src, dst_ref=from_x(k, zz), send_sem=x_send.at[unit], recv_sem=x_recv.at[unit],
            device_id={"dp": across}, device_id_type=MESH,
        )

    def z_copy(k, zz, up, other):
        unit = ((chunks if other else 0) + k) * Z + zz
        return pltpu.make_async_remote_copy(
            src_ref=other_of(k, zz) if other else own(k, zz),
            dst_ref=from_z(k, zz, up, other),
            send_sem=(up_send if up else down_send).at[unit],
            recv_sem=(up_recv if up else down_recv).at[unit],
            device_id={"dp": me + X if up else me - X},
            device_id_type=MESH,
        )

    def total(k, dst, srcs):
        @pl.loop(0, SUM_CHUNKS[k][2] // 16)
        def _(step):
            rows = pl.ds(pl.multiple_of(step * 16, 16), 16)
            value = srcs[0][rows].astype(jnp.float32)
            for src in srcs[1:]:
                value = value + src[rows].astype(jnp.float32)
            dst[rows] = value.astype(dst.dtype)

    for distance in (3, 2, 1, 0):
        for k in range(chunks):
            def run(zz, up):
                load(k, zz).start()
                if SUM_CHUNKS[k][3]:
                    load(k, zz, True).start()
            each(distance, run)

    sq_src[...] = jnp.zeros_like(sq_src)
    sq_rows[...] = jnp.zeros_like(sq_rows)
    pl.semaphore_wait(barrier, devices - 1)
    send_batch(gradients, 0)

    order = [
        (k, distance) for which, distance in ((0, 3), (0, 2), (0, 1), (1, 3), (0, 0), (1, 2), (1, 1), (2, 3), (1, 0), (2, 2), (2, 1), (2, 0))
        for k in range(chunks) if SUM_CHUNKS[k][0] == which and not SUM_CHUNKS[k][3]
    ]
    sent = []

    def send_x(until):
        while len(sent) < min(until, len(order)):
            k, distance = order[len(sent)]
            sent.append(1)
            each(distance, lambda zz, up: x_copy(k, zz, hbm(k, zz, 1 - x)).start())

    def after(k, distance):
        if not SUM_CHUNKS[k][3]:
            send_x(order.index((k, distance)) + 1 + 6)

    send_x(6)

    def pass_on(k, distance):
        def run(zz, up):
            behind = has_down if up else has_up
            if SUM_CHUNKS[k][3]:
                for other in (False, True):
                    mine = other_of(k, zz) if other else own(k, zz)
                    load(k, zz, other).wait()

                    @pl.when(behind)
                    def _():
                        z_copy(k, zz, up, other).wait_recv()
                        total(k, mine, [mine, from_z(k, zz, up, other)])

                    z_copy(k, zz, up, other).start()
                return
            load(k, zz).wait()
            x_copy(k, zz, hbm(k, zz, 1 - x)).wait_recv()

            @pl.when(behind)
            def _():
                z_copy(k, zz, up, False).wait_recv()
                total(k, own(k, zz), [own(k, zz), from_x(k, zz), from_z(k, zz, up, False)])

            @pl.when(jnp.logical_not(behind))
            def _():
                total(k, own(k, zz), [own(k, zz), from_x(k, zz)])

            z_copy(k, zz, up, False).start()
        each(distance, run)

    def add_z(dst, k, other):
        @pl.when(has_down)
        def _():
            z_copy(k, z, True, other).wait_recv()
            total(k, dst, [dst, from_z(k, z, True, other)])

        @pl.when(has_up)
        def _():
            z_copy(k, z, False, other).wait_recv()
            total(k, dst, [dst, from_z(k, z, False, other)])

    def send_direct(k):
        load(k, z, True).wait()
        total(k, acc, [other_of(k, z)])
        add_z(acc, k, True)
        total(k, other_of(k, z), [acc])
        x_copy(k, z, other_of(k, z)).start()

    def finish(k):
        which, rows = SUM_CHUNKS[k][0], SUM_CHUNKS[k][2]
        dst = out.at[which - 1, part(k)] if which else acc_dn.at[pl.ds(0, rows)]
        load(k, z).wait()
        if SUM_CHUNKS[k][3]:
            total(k, dst, [own(k, z)])
            add_z(dst, k, False)
            x_copy(k, z, other_of(k, z)).wait_recv()
            total(k, dst, [dst, from_x(k, z)])
        else:
            x_copy(k, z, hbm(k, z, 1 - x)).wait_recv()
            total(k, dst, [own(k, z), from_x(k, z)])
            add_z(dst, k, False)
        if not which:
            total(k, dn_out.at[section, part(k)], [dst])
            dn_copy(k, section, True).start()
            dn_copy(k, section, False).start()

        @pl.loop(0, rows // 16)
        def _(step):
            value = dst[pl.ds(pl.multiple_of(step * 16, 16), 16)]
            sq_rows[...] += jnp.sum(value * value, axis=0, keepdims=True)

    def of(which, direct=None):
        return [
            k for k in range(chunks)
            if SUM_CHUNKS[k][0] == which and (direct is None or SUM_CHUNKS[k][3] == direct)
        ]

    def pass_all(which, distance):
        for k in of(which):
            pass_on(k, distance)
            after(k, distance)

    def finish_all(which):
        for k in of(which, False) + of(which, True):
            finish(k)
            after(k, 0)

    def direct_all(which):
        for k in of(which, True):
            send_direct(k)

    for distance in (3, 2, 1):
        pass_all(0, distance)
    make_cond()
    pass_all(1, 3)
    direct_all(0)
    finish_all(0)
    pass_all(1, 2)
    make_hidden()
    pass_all(1, 1)
    for k in of(0):
        dn_copy(k, facing, False).wait_recv()
        dn_copy(k, facing, True).start()
    pass_all(2, 3)
    make_news()
    direct_all(1)
    finish_all(1)
    pass_all(2, 2)
    pass_all(2, 1)
    make_biases()
    direct_all(2)
    finish_all(2)

    @pl.loop(0, 144 // 16)
    def _(step):
        rows = pl.ds(pl.multiple_of(step * 16, 16), 16)
        cross_src[rows] = to_half(jnp.where(core == 0, out[0, rows], out[1, rows]))

    crossing = pltpu.make_async_remote_copy(
        src_ref=cross_src, dst_ref=cross_out, send_sem=cross_sem.at[0], recv_sem=cross_sem.at[1],
        device_id={"section": sibling}, device_id_type=MESH,
    )
    sq_src[...] += jnp.sum(sq_rows[...])
    send_batch(norms, 9)
    crossing.start()
    wait_batch(norms, 9)
    sq_out[...] = jnp.sum(sq_all[...], axis=0)
    crossing.wait()

    for k in range(chunks):
        for distance in (3, 2, 1, 0):
            def run(zz, up):
                if not SUM_CHUNKS[k][3]:
                    x_copy(k, zz, hbm(k, zz, 1 - x)).wait_send()
                elif distance == 0:
                    x_copy(k, zz, other_of(k, zz)).wait_send()
                if distance:
                    z_copy(k, zz, up, False).wait_send()
                    if SUM_CHUNKS[k][3]:
                        z_copy(k, zz, up, True).wait_send()
            each(distance, run)
        if not SUM_CHUNKS[k][0]:
            dn_copy(k, section, True).wait_send()
            dn_copy(k, section, False).wait_send()
            dn_copy(k, facing, True).wait_send()
            dn_copy(k, sibling, True).wait_recv()
            dn_copy(k, lax.rem(sibling + 2, 4), True).wait_recv()


def sum_gradients(g_dn, g_up, g_attn, d_mods, sums, ends, w_mod, w_fm, two_blocks, cond, pre, hidden, meta):
    n, width = lax.axis_size("dp"), cond.shape[1]
    f32 = jnp.float32
    if not ring_fits(n, width):
        return sum_plainly(g_dn, g_up, g_attn, d_mods, sums, ends, w_mod, w_fm, two_blocks, cond, pre, hidden, meta)
    chunks, images, devices = len(SUM_CHUNKS), 2 * n, 4 * n
    dma = lambda *count: pltpu.SemaphoreType.DMA(count)
    ring = pltpu.VMEM((3, Z, 144, HALF), BF)
    short = [rows for start, rows, direct in CHUNKS if direct][0]
    most = max(rows for start, rows, direct in CHUNKS)
    ring_o = pltpu.VMEM((3, Z, short, HALF), BF)
    hbm, vmem = pl.BlockSpec(memory_space=pl.ANY), pl.BlockSpec(memory_space=pltpu.VMEM)
    like = jax.ShapeDtypeStruct
    end_block = ends.shape[1:]
    shapes = (
        like((2, 144, HALF), f32), like((144, HALF), BF), like((4, 144, HALF), BF),
        like((144, 3 * D), f32), like((144, 2 * D), f32), like((144, 1024), f32), like((WIDE, FREQ), f32),
        like((144, D), f32), like((4,) + end_block, f32), like((40, D), f32), like((8, 128), f32),
    )
    return pl.pallas_call(
        sum_kernel,
        out_shape=shapes,
        in_specs=[hbm] * 3 + [vmem] * 10,
        out_specs=(vmem,) * len(shapes),
        scratch_shapes=[
            ring, ring_o, ring, pltpu.VMEM((3, short, HALF), BF),
            ring, ring_o, ring, ring_o, pltpu.VMEM((short, HALF), f32), pltpu.VMEM((most, HALF), f32),
            pltpu.VMEM((images, 48, 128), BF), pltpu.VMEM((images, SUM_ROWS, 128), f32),
            pltpu.VMEM((images,) + end_block, f32), pltpu.VMEM((images, 5 * D), BF),
            pltpu.VMEM(end_block, f32), pltpu.VMEM((images, WIDE), f32), pltpu.VMEM((4, images, WIDE), f32),
            pltpu.VMEM((images, 2 * D), BF), pltpu.VMEM((4, images, 2 * D), BF), pltpu.VMEM((1, 3 * D), f32),
            pltpu.VMEM((images, WIDE), BF), pltpu.VMEM((n, images, WIDE), f32), pltpu.VMEM((n, images, WIDE), f32),
            pltpu.VMEM((24, 128), f32), pltpu.VMEM((8, 128), f32), pltpu.VMEM((devices, 8, 128), f32),
            pltpu.VMEM((1, HALF), f32),
            pltpu.VMEM((144, HALF), BF), pltpu.VMEM((devices, 24, 128), f32), pltpu.VMEM((4, 1, 3 * D), f32),
            pltpu.VMEM((1, 2 * D), f32),
            dma(2 * chunks * Z), dma(chunks * Z), dma(chunks * Z),
            dma(2 * chunks * Z), dma(2 * chunks * Z), dma(2 * chunks * Z), dma(2 * chunks * Z),
            dma(4 * chunks), dma(4 * chunks), dma(4 * chunks), dma(4 * chunks),
            dma(3, images), dma(3, images), dma(4, 4), dma(4, 4),
            dma(n), dma(n), dma(devices), dma(devices), dma(devices), dma(devices), dma(2), dma(10),
        ],
        compiler_params=pltpu.CompilerParams(
            collective_id=1, has_side_effects=True, vmem_limit_bytes=VMEM_BYTES
        ),
        cost_estimate=pl.CostEstimate(flops=0, bytes_accessed=400_000_000, transcendentals=0),
        name="sum_gradients",
    )(g_dn, g_up, g_attn, d_mods, sums, ends, w_mod, w_fm, two_blocks, cond, pre, hidden, meta)


def sum_plainly(g_dn, g_up, g_attn, d_mods, sums, ends, w_mod, w_fm, two_blocks, cond, pre, hidden, meta):
    n, width = lax.axis_size("dp"), cond.shape[1]
    section, images, f32 = lax.axis_index("section"), 2 * n, jnp.float32
    once = (section == 0).astype(f32)
    anchor = (lax.axis_index("dp") == 0).astype(f32)
    total = lambda grad: lax.psum_scatter(grad, "dp", scatter_dimension=0, tiled=True)
    dn_own, out = total(g_dn), jnp.stack([total(g_up), total(g_attn)]).astype(f32)
    dn_all = lax.all_gather(dn_own, "section")
    cross = swap(to_half(jnp.where(lax.rem(section, 2) == 0, out[0], out[1])), 1)
    d_mods, sums, ends = exchange(4, "stage", ("core", "each", "dp"), d_mods, sums, ends)
    d_mods = d_mods.reshape(images, 48 * 128)
    d_mod, d_fm = d_mods[:, : 3 * D], d_mods[:, 3 * D : 5 * D]
    sums, ends = jnp.sum(sums, axis=0), jnp.sum(ends, axis=0)
    cond_low = to_half(cond).astype(f32)
    own_cond = jnp.where(section == 0, cond, cond_low)
    d_silu = matmul_nt(d_mod, w_mod) + (section == 3).astype(f32) * matmul_nt(d_fm, w_fm)
    c_own = jnp.pad(silu_slope(own_cond) * d_silu, ((0, 0), (0, WIDE - width)))
    cs = column_sums(d_mod)[None]
    c_all, ends_all, d_fm, cs_all = exchange(5, "section", ("all",) * 4, c_own, ends, d_fm, cs)
    d_fm = d_fm[3]
    d_cond = to_half(c_all[3])
    for slot in (2, 1, 0):
        d_cond = to_half(d_cond.astype(f32) + c_all[slot])
    narrow = d_cond[:, :width]
    part = jnp.einsum("iw,jwk->jik", narrow, two_blocks, preferred_element_type=f32)
    (part,) = exchange(6, "dp", ("each",), part)
    d_pre = to_half(silu_slope(pre) * jnp.sum(part, axis=0))
    g_mod = matmul_tn(to_half(jax.nn.silu(own_cond)), d_mod)
    g_fm = matmul_tn(to_half(jax.nn.silu(cond_low)), d_fm)
    g_table = matmul_tn(narrow, one_hot(meta[:, FREQ : FREQ + 1], 1024))
    g_one = matmul_tn(d_pre, to_half(meta[:, :FREQ]))
    g_two = jnp.einsum("iw,jik->wjk", narrow, hidden, preferred_element_type=f32)
    g_two = g_two[:, :, :width].reshape(width, D)
    fm_sum = column_sums(d_fm)[None]
    slices = [column_sums(value).reshape(2, 128) for value in (d_pre, d_cond)]
    news = jnp.concatenate([sums, *slices, jnp.zeros((4, 128), f32)])
    square = lambda value: jnp.sum(value * value)
    squares = square(out) + square(dn_own.astype(f32)) + square(g_mod) + square(sums[:10])
    squares = squares + anchor * square(cs) + anchor * once * square(fm_sum)
    for value in (g_fm, g_table, g_one, g_two, ends_all[0], ends_all[3], *slices):
        squares = squares + once * square(value)
    news, squares = exchange(7, "every", ("all", "all"), news, jnp.broadcast_to(squares, (8, 128)))
    squares = jnp.sum(squares, axis=0)
    news = news.reshape(n, 4, -1, 128)
    stages = []
    for k in range(2):
        pieces = news[:, 2 * k : 2 * k + 2, :SUM_ROWS].reshape(2 * n, SUM_ROWS, 128)[: D // 128]
        stages.append(pieces.transpose(1, 0, 2).reshape(-1))
    slices = news[:, 0, SUM_ROWS : SUM_ROWS + 4].reshape(n, 2, WIDE)[:, :, :width]
    bias_rows = jnp.concatenate(
        [cs_all.reshape(-1)]
        + [part[: 8 * D] for part in stages]
        + [part[8 * D : 9 * D] for part in stages]
        + [stages[0][9 * D : 10 * D]]
        + [slices[:, 0].reshape(-1), slices[:, 1].reshape(-1)]
        + [fm_sum[0], stages[1][9 * D : 11 * D], jnp.zeros((3 * D,), f32)]
    ).reshape(40, D)
    return (out, cross, dn_all, g_mod, g_fm, g_table, g_one, g_two, ends_all, bias_rows, squares)


def exchange_kernel(axes, modes, *refs):
    count = len(modes)
    ins, outs = refs[:count], refs[count : 2 * count]
    send_sem, recv_sem, own_sem = refs[2 * count :]
    dp, section = lax.axis_index("dp"), lax.axis_index("section")
    n, sections = lax.axis_size("dp"), lax.axis_size("section")
    if axes == "dp":
        size, me, where = n, dp, lambda p: {"dp": p}
    elif axes == "section":
        size, me, where = sections, section, lambda p: {"section": p}
    elif axes == "stage":
        low = section - lax.rem(section, 2)
        size, me = 2 * n, dp * 2 + lax.rem(section, 2)
        where = lambda p: {"dp": p // 2, "section": low + lax.rem(p, 2)}
    else:
        size, me = n * sections, dp * sections + section
        where = lambda p: {"dp": p // sections, "section": lax.rem(p, sections)}

    def part(k, p):
        if modes[k] == "all":
            return ins[k]
        index = {"each": p, "dp": p // 2, "core": lax.rem(p, 2)}[modes[k]]
        return ins[k].at[index]

    def copy(k, step, src, slot, p):
        return pltpu.make_async_remote_copy(
            src_ref=src, dst_ref=outs[k].at[slot],
            send_sem=send_sem.at[k, step], recv_sem=recv_sem.at[k, step],
            device_id=where(p), device_id_type=MESH,
        )

    barrier = pltpu.get_barrier_semaphore()

    @pl.loop(1, size)
    def _(step):
        pl.semaphore_signal(barrier, 1, device_id=where(lax.rem(me + step, size)), device_id_type=MESH)

    for k in range(count):
        pltpu.make_async_copy(part(k, me), outs[k].at[me], own_sem.at[k]).start()
    pl.semaphore_wait(barrier, size - 1)

    @pl.loop(1, size)
    def _(step):
        p = lax.rem(me + step, size)
        for k in range(count):
            copy(k, step, part(k, p), me, p).start()

    for k in range(count):
        pltpu.make_async_copy(part(k, me), outs[k].at[me], own_sem.at[k]).wait()

    @pl.loop(1, size)
    def _(step):
        p = lax.rem(me + size - step, size)
        for k in range(count):
            copy(k, step, part(k, p), p, p).wait_recv()
            copy(k, step, part(k, p), p, p).wait_send()


def exchange(ident, axes, modes, *arrays):
    n, sections = lax.axis_size("dp"), lax.axis_size("section")
    size = {"dp": n, "section": sections, "stage": 2 * n, "every": n * sections}[axes]
    blocks = [a.shape if mode == "all" else a.shape[1:] for a, mode in zip(arrays, modes)]
    count = len(arrays)
    vmem = pl.BlockSpec(memory_space=pltpu.VMEM)
    return pl.pallas_call(
        partial(exchange_kernel, axes, modes),
        out_shape=tuple(jax.ShapeDtypeStruct((size,) + b, a.dtype) for a, b in zip(arrays, blocks)),
        in_specs=[vmem] * count,
        out_specs=(vmem,) * count,
        scratch_shapes=[
            pltpu.SemaphoreType.DMA((count, size)),
            pltpu.SemaphoreType.DMA((count, size)),
            pltpu.SemaphoreType.DMA((count,)),
        ],
        compiler_params=pltpu.CompilerParams(
            collective_id=ident, has_side_effects=True, vmem_limit_bytes=VMEM_BYTES
        ),
        cost_estimate=pl.CostEstimate(flops=0, bytes_accessed=30_000_000, transcendentals=0),
        name="exchange_" + axes,
    )(*arrays)


def rows_of(value, size):
    value = value.reshape(-1)
    return jnp.pad(value, (0, size * 128 - value.shape[0])).reshape(size, 128)


def row_count(length, unit=8):
    return -(-length // (128 * unit)) * unit


TILE = 768
STEPS = HALF // TILE
GELU_SCALE = math.sqrt(2.0 / math.pi)
SCALE = HEAD_DIM ** (-0.5)


def mean_rows(value):
    return jnp.mean(value, axis=-1, keepdims=True)


def normalized(x):
    centered = x - mean_rows(x)
    inverse = lax.rsqrt(mean_rows(centered * centered) + epsilon_norm)
    return (centered * inverse, inverse)


def modulated_back(normed, inverse, scale, d_xm):
    d_normed = d_xm * (1.0 + scale)
    d_x = inverse * (d_normed - mean_rows(d_normed) - normed * mean_rows(d_normed * normed))
    return (d_x, jnp.sum(d_xm, axis=0), jnp.sum(d_xm * normed, axis=0))


def window(head):
    low = HEAD_DIM * head // 128 * 128
    high = -(-HEAD_DIM * (head + 1) // 128) * 128
    lane = lax.broadcasted_iota(jnp.int32, (PATCHES, high - low), 1) + low
    return slice(low, high), (lane >= HEAD_DIM * head) & (lane < HEAD_DIM * (head + 1))


def own_lanes(mask, value):
    return jnp.where(mask, value, jnp.zeros_like(value))


def softmax_rows(scores):
    shifted = jnp.exp(scores - jnp.max(scores, axis=-1, keepdims=True))
    return shifted / jnp.sum(shifted, axis=-1, keepdims=True)


def half_of(ref, which, side):
    return ref.at[which, :, pl.ds(pl.multiple_of(side * HALF, 128) if which else side * HALF, HALF)]


def weight_copies(sources, targets, sem):
    return [pltpu.make_async_copy(src, dst, sem.at[k]) for k, (src, dst) in enumerate(zip(sources, targets))]


def forward_kernel(
    save, flags, x_ref, mod_a, mod_m, b_attn, b_up, b_down, w_blk, w_dn, out_ref, *refs
):
    if save:
        xm_ref, qkv_ref, att_ref, last_ref, branch_a_ref, mid_ref, xm2_ref, branch_m_ref, pre_ref = refs[:9]
        act_refs = refs[9:11]
        wa, wu, wd, acc, sem = refs[11:]
    else:
        xm_ref, qkv_ref, att_ref, mid_ref, xm2_ref, wa, wu, wd, acc, sem = refs
    copies = weight_copies(
        [half_of(w_blk, 0, 0), half_of(w_blk, 0, 1)]
        + [ref for side in (flags[0], 1 - flags[0]) for ref in (half_of(w_blk, 1, side), w_dn.at[side])],
        (wa.at[0], wa.at[1], wu.at[0], wd.at[0], wu.at[1], wd.at[1]),
        sem,
    )
    for copy in copies:
        copy.start()
    normed, unused = normalized(x_ref[...])
    xm_ref[...] = to_half(normed * (1.0 + mod_a[1:2]) + mod_a[0:1])
    acc[...] = jnp.zeros_like(acc)
    for k in range(3):
        if k != 1:
            copies[k // 2].wait()
        half, first = (0, D * k) if k < 2 else (1, 0)
        part = slice(D * k, D * (k + 1))
        qkv_ref[:, part] = to_half(
            matmul(xm_ref[...], wa[half, :, first : first + D]) + b_attn[:, part]
        )
    for head in range(HEADS):
        lanes, mask = window(head)
        at = lambda k: slice(D * k + lanes.start, D * k + lanes.stop)
        query = own_lanes(mask, qkv_ref[:, at(0)])
        probs = softmax_rows(matmul_nt(query, qkv_ref[:, at(1)]) * SCALE)
        acc[:, lanes] += own_lanes(mask, matmul(to_half(probs), qkv_ref[:, at(2)]))
    att_ref[...] = to_half(acc[...])
    branch = matmul(att_ref[...], wa[1, :, D:]) + b_attn[:, 3 * D :]
    if save:
        branch_a_ref[...] = branch
        last_ref[...] = jnp.where(flags[0] == 0, att_ref[...], xm_ref[...])
    mid_ref[...] = to_half(x_ref[...] + mod_a[2:3] * branch).astype(jnp.float32)
    normed, unused = normalized(mid_ref[...])
    xm2_ref[...] = to_half(normed * (1.0 + mod_m[1:2]) + mod_m[0:1])
    acc[...] = jnp.broadcast_to(b_down[...], acc.shape)
    for half in range(2):
        copies[2 + 2 * half].wait()
        copies[3 + 2 * half].wait()
        for step in range(STEPS):
            own = slice(TILE * step, TILE * (step + 1))
            part = slice(HALF * half + TILE * step, HALF * half + TILE * (step + 1))
            pre = matmul(xm2_ref[...], wu[half, :, own]) + b_up[:, part]
            cube = pre + 0.044715 * (pre * pre * pre)
            act = to_half(pre * (0.5 * (1.0 + jnp.tanh(GELU_SCALE * cube))))
            if save:
                pre_ref[:, part] = pre
                act_refs[half][:, own] = act
            acc[...] += matmul_nt(act, wd[half, :, own])
    if save:
        branch_m_ref[...] = acc[...]
    out = mid_ref[...] + mod_m[2:3] * acc[...]
    out_ref[...] = out.astype(out_ref.dtype)


def backward_kernel(
    flags, d_ref, x_ref, mid_ref, mod_a, mod_m, branch_a, branch_m, qkv_ref, pre_hbm, w_blk, w_dn,
    d_in_ref, d_mod_a, d_mod_m, grad_a, grad_m, d_pre_own, d_pre_sib, d_qkv_ref, right_own, right_sib,
    wa, wu, wd, pre_ref, acc, d_acc, d_att, sem,
):
    copies = weight_copies(
        (
            w_dn.at[flags[0]], pre_hbm, half_of(w_blk, 1, flags[0]),
            w_dn.at[1 - flags[0]], half_of(w_blk, 1, 1 - flags[0]),
            half_of(w_blk, 0, 1), half_of(w_blk, 0, 0),
        ),
        (wd.at[0], pre_ref, wu.at[0], wd.at[1], wu.at[1], wa.at[1], wa.at[0]),
        sem,
    )
    for copy in copies:
        copy.start()
    grad_m[...] = to_half(d_ref[...] * mod_m[2:3])
    d_mod_m[2:3] = jnp.sum(d_ref[...] * branch_m[...], axis=0)[None]
    acc[...] = jnp.zeros_like(acc)
    for half in range(2):
        copies[0 if half == 0 else 3].wait()
        if half == 0:
            copies[1].wait()
        copies[2 if half == 0 else 4].wait()
        for step in range(STEPS):
            own = slice(TILE * step, TILE * (step + 1))
            part = slice(HALF * half + TILE * step, HALF * half + TILE * (step + 1))
            d_act = matmul(grad_m[...], wd[half, :, own])
            pre = pre_ref[:, part]
            square = pre * pre
            tanh = jnp.tanh(GELU_SCALE * (pre + 0.044715 * (square * pre)))
            slope = 0.5 * (1.0 + tanh) + (0.5 * pre) * (1.0 - tanh * tanh) * (
                GELU_SCALE * (1.0 + (3.0 * 0.044715) * square)
            )
            d_pre = to_half(d_act * slope)
            (d_pre_sib if half else d_pre_own)[:, own] = d_pre
            acc[...] += matmul_nt(d_pre, wu[half, :, own])
    normed, inverse = normalized(mid_ref[...])
    d_x, d_shift, d_scale = modulated_back(normed, inverse, mod_m[1:2], acc[...])
    d_mod_m[0:1] = d_shift[None]
    d_mod_m[1:2] = d_scale[None]
    acc[...] = to_half(d_ref[...] + d_x).astype(jnp.float32)

    d_mod_a[2:3] = jnp.sum(acc[...] * branch_a[...], axis=0)[None]
    grad_a[...] = to_half(acc[...] * mod_a[2:3])
    copies[5].wait()
    d_att[...] = to_half(matmul_nt(grad_a[...], wa[1, :, D:]))
    d_acc[...] = jnp.zeros_like(d_acc)
    for head in range(HEADS):
        lanes, mask = window(head)
        at = lambda k: slice(D * k + lanes.start, D * k + lanes.stop)
        query, key, value = (qkv_ref[:, at(k)] for k in range(3))
        probs = softmax_rows(matmul_nt(own_lanes(mask, query), key) * SCALE)
        outer = d_att[:, lanes]
        d_acc[:, at(2)] += own_lanes(mask, matmul_tn(to_half(probs), outer))
        d_probs = matmul_nt(own_lanes(mask, outer), value)
        d_scores = to_half(probs * (d_probs - jnp.sum(probs * d_probs, axis=-1, keepdims=True)))
        d_acc[:, at(0)] += own_lanes(mask, matmul(d_scores, key) * SCALE)
        d_acc[:, at(1)] += own_lanes(mask, matmul_tn(d_scores, query) * SCALE)
    d_qkv_ref[...] = to_half(d_acc[...])
    first = flags[0] == 0
    pairs = ((d_qkv_ref[:, :D], d_qkv_ref[:, 2 * D :]), (d_qkv_ref[:, D : 2 * D], grad_a[...]))
    for k, (one, two) in enumerate(pairs):
        right_own[:, D * k : D * (k + 1)] = jnp.where(first, one, two)
        right_sib[:, D * k : D * (k + 1)] = jnp.where(first, two, one)
    copies[6].wait()
    d_xm = matmul_nt(d_qkv_ref[:, 2 * D :], wa[1, :, :D]) + matmul_nt(d_qkv_ref[:, : 2 * D], wa[0])
    normed, inverse = normalized(x_ref[...])
    d_x, d_shift, d_scale = modulated_back(normed, inverse, mod_a[1:2], d_xm)
    d_mod_a[0:1] = d_shift[None]
    d_mod_a[1:2] = d_scale[None]
    d_in_ref[...] = to_half(acc[...] + d_x)


def weight_scratch():
    return [pltpu.VMEM((2, D, HALF), BF)] * 3


def stage_cost():
    flops = 2 * PATCHES * D * 12 * D + 4 * PATCHES * PATCHES * D
    return pl.CostEstimate(flops=2 * flops, bytes_accessed=24 * D * D, transcendentals=2 * PATCHES * FF)


def stage_forward(save, x_in, weights):
    flags, mod_a, mod_m, w_blk, w_dn, b_attn, b_up, b_down = weights
    vmem, hbm = pl.BlockSpec(memory_space=pltpu.VMEM), pl.BlockSpec(memory_space=pl.ANY)
    smem = pl.BlockSpec(memory_space=pltpu.SMEM)
    like = lambda columns, kind: jax.ShapeDtypeStruct((PATCHES, columns), kind)
    tokens, wide = pltpu.VMEM((PATCHES, D), BF), pltpu.VMEM((PATCHES, 3 * D), BF)
    total = pltpu.VMEM((PATCHES, D), jnp.float32)
    f32 = jnp.float32
    if save:
        shapes = [like(D, f32), like(D, BF), like(3 * D, BF), like(D, BF), like(D, BF), like(D, f32), like(D, f32)]
        shapes += [like(D, BF), like(D, f32), like(FF, f32), like(HALF, BF), like(HALF, BF)]
        scratch = []
    else:
        shapes, scratch = [like(D, BF)], [tokens, wide, tokens, total, tokens]
    return pl.pallas_call(
        partial(forward_kernel, save),
        out_shape=tuple(shapes),
        in_specs=[smem] + [vmem] * 6 + [hbm] * 2,
        out_specs=(vmem,) * len(shapes),
        scratch_shapes=scratch + weight_scratch() + [total, pltpu.SemaphoreType.DMA((6,))],
        compiler_params=pltpu.CompilerParams(vmem_limit_bytes=VMEM_BYTES),
        cost_estimate=stage_cost(),
        name="stage_forward",
    )(flags, x_in, mod_a, mod_m, b_attn, b_up, b_down, w_blk, w_dn)


def stage_backward(d_out, x_in, weights, kept):
    flags, mod_a, mod_m, w_blk, w_dn, b_attn, b_up, b_down = weights
    xm_a, qkv, att, last, branch_a, x_mid, xm_m, branch_m, pre, act_own, act_sib = kept
    vmem, hbm = pl.BlockSpec(memory_space=pltpu.VMEM), pl.BlockSpec(memory_space=pl.ANY)
    smem = pl.BlockSpec(memory_space=pltpu.SMEM)
    like = lambda columns, kind: jax.ShapeDtypeStruct((PATCHES, columns), kind)
    mods = jax.ShapeDtypeStruct((3, D), jnp.float32)
    return pl.pallas_call(
        backward_kernel,
        out_shape=(like(D, BF), mods, mods, like(D, BF), like(D, BF))
        + (like(HALF, BF), like(HALF, BF), like(3 * D, BF), like(HALF, BF), like(HALF, BF)),
        in_specs=[smem] + [vmem] * 8 + [hbm] * 3,
        out_specs=(vmem,) * 10,
        scratch_shapes=weight_scratch()
        + [
            pltpu.VMEM((PATCHES, FF), jnp.float32),
            pltpu.VMEM((PATCHES, D), jnp.float32),
            pltpu.VMEM((PATCHES, 3 * D), jnp.float32),
            pltpu.VMEM((PATCHES, D), BF),
            pltpu.SemaphoreType.DMA((7,)),
        ],
        compiler_params=pltpu.CompilerParams(vmem_limit_bytes=VMEM_BYTES),
        cost_estimate=stage_cost(),
        name="stage_backward",
    )(flags, d_out, x_in, x_mid, mod_a, mod_m, branch_a, branch_m, qkv, pre, w_blk, w_dn)


COLUMNS = 384


def products_kernel(
    flags, dn_own, dn_sib, up_own, up_sib, xa_own, xa_sib, att_own, last_sib,
    act_own, act_sib, pre_own, pre_sib, right_own, right_sib,
    g_dn, g_up, g_attn, t_dn, t_up, t_one, t_two,
):
    step = pl.program_id(0)

    @pl.when(step == 0)
    def _():
        last_own = jnp.where(flags[0] == 0, xa_own[...], att_own[...])
        for target, own, sib in (
            (t_dn, dn_own[...], dn_sib), (t_up, up_own[...], up_sib),
            (t_one, xa_own[...], xa_sib), (t_two, last_own, last_sib),
        ):
            target[:, :PATCHES] = own.T
            target[:, PATCHES:] = sib[...].T

    def product(left, own, sib):
        return to_half(
            matmul(left[:, :PATCHES], own[...]) + matmul(left[:, PATCHES:], sib[...])
        )

    g_dn[...] = product(t_dn, act_own, act_sib)
    g_up[...] = product(t_up, pre_own, pre_sib)

    @pl.when(step < D // COLUMNS)
    def _():
        g_attn[...] = product(t_one, right_own, right_sib)

    @pl.when(step >= D // COLUMNS)
    def _():
        g_attn[...] = product(t_two, right_own, right_sib)


def products(flags, lefts, rights):
    left = whole_spec((PATCHES, D))
    right = pl.BlockSpec((PATCHES, COLUMNS), lambda step: (0, step))
    out = pl.BlockSpec((D, COLUMNS), lambda step: (0, step))
    return pl.pallas_call(
        products_kernel,
        grid=(HALF // COLUMNS,),
        out_shape=(jax.ShapeDtypeStruct((D, HALF), BF),) * 3,
        in_specs=[pl.BlockSpec(memory_space=pltpu.SMEM)] + [left] * 8 + [right] * 6,
        out_specs=(out,) * 3,
        scratch_shapes=[pltpu.VMEM((D, 2 * PATCHES), BF)] * 4,
        compiler_params=pltpu.CompilerParams(vmem_limit_bytes=VMEM_BYTES),
        cost_estimate=pl.CostEstimate(
            flops=12 * PATCHES * D * HALF, bytes_accessed=10 * D * HALF, transcendentals=0
        ),
        name="products",
    )(flags, *lefts, *rights)


def whole_spec(shape):
    return pl.BlockSpec(shape, lambda step: (0,) * len(shape))


SUM_ROWS = 16


def collect_kernel(flags_ref, *refs):
    tokens, d_pres, mods, fm_ref, extra_ref, tok_ref, head_ref = refs[:4], refs[4:6], refs[6:8], *refs[8:12]
    sums_ref, mods_ref, ends_ref, rows_ref = refs[12:]
    core, stage = flags_ref[0], flags_ref[1]
    ones = jnp.ones((8, PATCHES), BF)
    total = lambda value: matmul(ones, value)[0:1]
    sums_ref[...] = jnp.zeros_like(sums_ref)
    rows = [total(tokens[0][:, D * k : D * (k + 1)]) for k in range(3)]
    rows += [total(ref[...]) for ref in tokens[1:]]
    halves = [[total(ref[:, D * k : D * (k + 1)]) for k in range(2)] for ref in d_pres]
    own = halves[0] + halves[1]
    order = [jnp.where(core == 0, own[k], own[(k + 2) % 4]) for k in range(4)]
    last = jnp.where(stage == 0, rows[5], extra_ref[0:1])
    for place, row in enumerate(rows[:4] + order + [rows[4], last, extra_ref[1:2]]):
        sums_ref[place : place + 1, :D] = row
    ends = jnp.where(stage == 0, matmul_tn(tok_ref[...], tokens[3][...]), head_ref[...])
    ends_ref[...] = jnp.zeros_like(ends_ref)
    width = D // ends_ref.shape[0]
    for index in range(ends_ref.shape[0]):
        ends_ref[index, :, :width] = ends[:, width * index : width * (index + 1)]
    rows_ref[...] = jnp.zeros_like(rows_ref)
    for k in range(2):
        for row in range(5):
            source = mods[k][row : row + 1, :] if row < 3 else fm_ref[row - 3 : row - 2, :]
            for part in range(D // 128):
                at = row * (D // 128) + part
                rows_ref[at : at + 1] = source[:, 128 * part : 128 * (part + 1)]
        mods_ref[k] = to_half(rows_ref[...])


def collect(flags, tokens, d_pres, mods, fm, extra, tok, g_head):
    n = lax.axis_size("dp")
    vmem = pl.BlockSpec(memory_space=pltpu.VMEM)
    return pl.pallas_call(
        collect_kernel,
        out_shape=(
            jax.ShapeDtypeStruct((SUM_ROWS, 128 * max(2 * n, 9)), jnp.float32),
            jax.ShapeDtypeStruct((2, 48, 128), BF),
            jax.ShapeDtypeStruct((n, HEAD_OUT, WIDE), jnp.float32),
        ),
        scratch_shapes=[pltpu.VMEM((48, 128), jnp.float32)],
        in_specs=[pl.BlockSpec(memory_space=pltpu.SMEM)] + [vmem] * 12,
        out_specs=(vmem,) * 3,
        compiler_params=pltpu.CompilerParams(vmem_limit_bytes=VMEM_BYTES),
        name="collect",
    )(flags, *tokens, *d_pres, *mods, fm, extra, tok, g_head)


def final_step(x_out, fmod, w_head, b_head, target, counts, loss_scale):
    normed, inverse = normalized(x_out)
    xf_half = to_half(normed * (1.0 + fmod[1:2]) + fmod[0:1])
    error = matmul_nt(xf_half, w_head) + b_head - target
    loss = counts * jnp.sum(error * error)
    d_pred = to_half(2.0 * loss_scale * counts * error)
    g_head = matmul_tn(d_pred, xf_half)
    d_x, d_shift, d_scale = modulated_back(normed, inverse, fmod[1:2], matmul(d_pred, w_head))
    return (loss, d_x, jnp.stack([d_shift, d_scale]), g_head, column_sums(d_pred))


def nesterov(weight, moment, average, grad, factor):
    clipped = grad * factor
    moment_new = momentum_rate * moment + clipped
    weight_new = weight - learn_rate * (clipped + momentum_rate * moment_new)
    average_new = ema_decay * average + (1.0 - ema_decay) * weight_new
    return (weight_new, moment_new, average_new, weight_new.astype(jnp.bfloat16))


def down_update_kernel(factor, weight, moment, average, grad, *outs):
    values = nesterov(
        weight[...], moment[...], average[...], grad[...].astype(jnp.float32), factor[0]
    )
    for out, value in zip(outs, values):
        out[...] = value


def updated(like):
    f32 = jax.ShapeDtypeStruct(like.shape, jnp.float32)
    return (f32, f32, f32, jax.ShapeDtypeStruct(like.shape, BF))


def down_update(factor, weight, moment, average, grads):
    width = weight.shape[1]
    rows = width
    state = pl.BlockSpec((1, rows, HALF), lambda l, h, r: (l, r, h))
    return pl.pallas_call(
        down_update_kernel,
        grid=(LAYERS, 2, width // rows),
        out_shape=updated(weight),
        in_specs=[pl.BlockSpec(memory_space=pltpu.SMEM), state, state, state]
        + [pl.BlockSpec((1, rows, HALF), lambda l, h, r: (2 * l + h, r, 0))],
        out_specs=(state,) * 4,
        compiler_params=pltpu.CompilerParams(vmem_limit_bytes=VMEM_BYTES),
        cost_estimate=pl.CostEstimate(flops=10 * weight.size, bytes_accessed=28 * weight.size, transcendentals=0),
        name="down_update",
    )(factor, weight, moment, average, grads)


def stem_update_kernel(factor, weight, moment, average, g_table, g_patch, g_one, g_two, *outs):
    width, first = weight.shape[0], 0
    for grad, length in ((g_table, NCLS), (g_patch, PATCH_IN), (g_one, FREQ), (g_two, D)):
        part = slice(first, first + length)
        values = nesterov(
            weight[:, part], moment[:, part], average[:, part], grad[:width, :length], factor[0]
        )
        for out, value in zip(outs, values):
            out[:, part] = value
        first += length


def stem_update(factor, weight, moment, average, *grads):
    vmem = pl.BlockSpec(memory_space=pltpu.VMEM)
    return pl.pallas_call(
        stem_update_kernel,
        out_shape=updated(weight),
        in_specs=[pl.BlockSpec(memory_space=pltpu.SMEM)] + [vmem] * 7,
        out_specs=(vmem,) * 4,
        compiler_params=pltpu.CompilerParams(vmem_limit_bytes=VMEM_BYTES),
        cost_estimate=pl.CostEstimate(flops=10 * weight.size, bytes_accessed=30 * weight.size, transcendentals=0),
        name="stem_update",
    )(factor, weight, moment, average, *grads)


def swap(array, by):
    peers = lax.axis_size("section")
    return lax.ppermute(array, "section", [(k, k ^ by) for k in range(peers)])


def pick(parts, index):
    return lax.dynamic_index_in_dim(parts, index, 0, keepdims=False)


def body(
    latents, noise, timesteps, labels, null_mask, valid,
    mod_w, mod_m, mod_e, block_w, block_m, block_e, down_w, down_m, down_e,
    stem_w, stem_m, stem_e, tail_w, tail_m, tail_e, biases, bias_m, bias_e,
):
    place = lax.axis_index("dp")
    section = lax.axis_index("section")
    stage = section // 2
    core = lax.rem(section, 2)
    even = core == 0
    n = lax.axis_size("dp")
    width = D // n

    flags = jnp.stack([core, stage]).astype(jnp.int32)
    downs, stems = jnp.swapaxes(down_w, 1, 2), stem_w.T
    to_wide = lambda value: jnp.pad(value, ((0, 0),) * (value.ndim - 1) + ((0, WIDE - width),))
    ends = jnp.concatenate([stems[:, NCLS : NCLS + PATCH_IN], tail_w[:, 2 * D :]], axis=1)
    ends = to_wide(to_half(ends).T)
    classes = jnp.where(null_mask > 0, NCLS - 1, labels)
    freq = to_half(time_features(timesteps.astype(jnp.float32))).astype(jnp.float32)
    facts = jnp.stack([classes, valid], axis=1).astype(jnp.float32)
    meta = jnp.concatenate([freq, facts, jnp.zeros((2, META - FREQ - 2), jnp.float32)], axis=1)
    b_one, b_two = (lax.dynamic_slice_in_dim(biases, k * D + place * width, width)[None] for k in (31, 32))
    w_blk, w_dn, meta, ends, pre_own, hidden_all, cond, mods, mod_half_w, w_fm, two_blocks = gather_weights(
        block_w[0], downs, stems, mod_w[0], tail_w, meta, ends, to_wide(b_one), b_two
    )
    ends = ends[:, :, :width].transpose(1, 0, 2).reshape(ROWS_END, D)
    w_patch_all, w_head_all = ends[:PATCH_IN], ends[PATCH_IN:]
    images = 2 * n
    count = jnp.sum(meta[:, FREQ + 1])
    loss_scale = 1.0 / (count * PATCHES * HEAD_OUT)
    mods = mods.reshape(2, 8 * PIECE)
    bias_of = lambda first, length: lax.dynamic_slice_in_dim(biases, first, length)
    mod_a = (mods[0, : 3 * D] + bias_of(6 * D * stage, 3 * D)).reshape(3, D)
    mod_b = (mods[1, : 3 * D] + bias_of(6 * D * stage + 3 * D, 3 * D)).reshape(3, D)
    fmod = (mods[0, 3 * D : 5 * D] + biases[33 * D : 35 * D]).reshape(2, D)
    weights = (
        flags, mod_a, mod_b, w_blk, w_dn,
        bias_of(12 * D + 8 * D * stage, 4 * D)[None],
        jnp.concatenate(
            [bias_of(16 * D + 8 * D * stage + HALF * half, HALF)[None] for half in (core, 1 - core)], axis=1
        ),
        bias_of(28 * D + D * stage, D)[None],
    )

    step = pick(timesteps, core).astype(jnp.float32)
    signal, spread = noise_levels(step)
    lat, noi = pick(latents, core)[None], pick(noise, core)[None]
    counts = pick(valid, core).astype(jnp.float32)
    tok_half = to_half(patchify(signal * lat + spread * noi))[0]
    target = jnp.concatenate([patchify(signal * noi - spread * lat), patchify(noi)], axis=2)[0]
    x_first = matmul(tok_half, w_patch_all) + biases[30 * D : 31 * D] + position_table(GRID // 2, D)

    x_hop = swap(stage_forward(False, x_first, weights)[0], 2)
    x_in = jnp.where(stage == 0, x_first, x_hop.astype(jnp.float32))
    x_out, *kept = stage_forward(True, x_in, weights)
    loss, d_final, d_fmod, g_head, b_head = final_step(
        x_out, fmod, w_head_all, biases[35 * D :], target, counts, loss_scale
    )
    xm_a, qkv, attended, last_sib, branch_a, x_mid, xm_b, branch_b, pre, act_own, act_sib = kept
    d_hop = swap(stage_backward(d_final, x_in, weights, kept)[0], 2)
    d_out = jnp.where(stage == 1, d_final, d_hop.astype(jnp.float32))
    d_first, d_mod_a, d_mod_b, d_branch_a, d_branch_b, d_pre_own, d_pre_sib, d_qkv, right_own, right_sib = (
        stage_backward(d_out, x_in, weights, kept)
    )

    act_come, xb_come, xa_come, last_come = swap((act_sib, xm_b, xm_a, last_sib), 1)
    branch_come, pre_come, right_come = swap((d_branch_b, d_pre_sib, right_sib), 1)
    g_dn, g_up, g_attn = products(
        flags,
        (d_branch_b, branch_come, xm_b, xb_come, xm_a, xa_come, attended, last_come),
        (act_own, act_come, d_pre_own, pre_come, right_own, right_come),
    )

    extra = jnp.stack([jnp.pad(b_head, (0, D - HEAD_OUT)), jnp.pad(loss[None], (0, D - 1))])
    d_fmod = jnp.where(stage == 1, d_fmod, jnp.zeros_like(d_fmod))
    tok_wide = jnp.pad(tok_half, ((0, 0), (0, HEAD_OUT - PATCH_IN)))
    own_sums, d_mods, own_ends = collect(
        flags, (d_qkv, d_branch_a, d_branch_b, d_first), (d_pre_own, d_pre_sib), (d_mod_a, d_mod_b), d_fmod,
        extra, tok_wide, g_head,
    )
    own_sums = own_sums.reshape(SUM_ROWS, -1, 128).transpose(1, 0, 2)[: 2 * n]
    halves, crossed, dn_all, g_mod, g_fm, g_table, g_one, g_two, ends_all, biases_new, squares = (
        sum_gradients(
            g_dn, g_up, g_attn, d_mods, own_sums, own_ends, mod_half_w, w_fm, two_blocks, cond, pre_own,
            hidden_all, meta,
        )
    )
    crossed = crossed.astype(jnp.float32)
    g_blk = jnp.concatenate(
        [jnp.where(even, halves[1], crossed), jnp.where(even, crossed, halves[0])], axis=1
    )
    ends = [ends_all[k, :, :width].T for k in (0, 3)]
    g_tail = jnp.concatenate([g_fm, ends[1]], axis=1)

    bias_grad, loss_sum = biases_new.reshape(-1)[:NBIAS], biases_new[36, 0]
    grad_norm = jnp.sqrt(squares[0, 0])
    factor = jnp.minimum(1.0, clip_limit / (grad_norm + 1e-06))
    mod_out = nesterov(mod_w, mod_m, mod_e, g_mod[None], factor)
    block_out = nesterov(block_w, block_m, block_e, g_blk[None], factor)
    flip = lambda value: jnp.swapaxes(value, 1, 2)
    scalar = factor.reshape(1)
    down_out = tuple(map(flip, down_update(scalar, downs, flip(down_m), flip(down_e), dn_all)))
    stem_out = stem_update(
        scalar, stems, stem_m.T, stem_e.T, g_table, ends[0][:, :PATCH_IN], g_one, g_two
    )
    stem_out = tuple(value.T for value in stem_out)
    tail_out = nesterov(tail_w, tail_m, tail_e, g_tail, factor)
    bias_out = nesterov(biases, bias_m, bias_e, bias_grad, factor)
    return (
        (loss_sum, count, grad_norm)
        + mod_out + block_out + down_out + stem_out + tail_out + bias_out
    )


def solution(mesh):
    images = (P("dp", None, None, None),) * 2 + (P("dp"),) * 4
    owned = P("section", "dp", None)
    states = (owned,) * 6 + (P(None, None, "dp"),) * 3 + (P(None, "dp"),) * 3 + (P("dp", None),) * 3 + (P(),) * 3
    updates = (owned,) * 8 + (P(None, None, "dp"),) * 4 + (P(None, "dp"),) * 4 + (P("dp", None),) * 4 + (P(),) * 4
    return jax.shard_map(
        body,
        mesh=mesh,
        in_specs=images + states,
        out_specs=(P(), P(), P()) + updates,
        check_vma=False,
    )
```

```python
from functools import partial
import math

import jax
import jax.numpy as jnp
from jax import lax
from jax.experimental import pallas as pl
from jax.experimental.pallas import tpu as pltpu
from jax.sharding import PartitionSpec as P

HEADS = 16
HEAD_DIM = 72
D = 1152
FF = 4608
HALF = FF // 2
NCLS = 1001
FREQ = 256
GRID = 32
PATCHES = 256
PATCH_IN = 16
HEAD_OUT = 32
LAYERS = 2
NBIAS = 40352


epsilon_norm = 1e-06
momentum_rate = 0.9
ema_decay = 0.9
learn_rate = 4000.0
clip_limit = 0.02
MESH = pl.DeviceIdType.MESH
BF = jnp.bfloat16


def matmul(left, right):
    return jnp.dot(left, right, preferred_element_type=jnp.float32)


def matmul_nt(left, right):
    return lax.dot_general(
        left, right, (((1,), (1,)), ((), ())), preferred_element_type=jnp.float32
    )


def matmul_tn(left, right):
    return lax.dot_general(
        left, right, (((0,), (0,)), ((), ())), preferred_element_type=jnp.float32
    )


def to_half(value):
    return value.astype(BF)


def column_sums(value):
    return jnp.sum(value.astype(jnp.float32), axis=0)


def silu_back(value, grad):
    return jax.vjp(jax.nn.silu, value)[1](grad)[0]


def patchify(field):
    images, side = (field.shape[0], field.shape[1] // 2)
    return (
        field.reshape(images, side, 2, side, 2, 4)
        .transpose(0, 1, 3, 2, 4, 5)
        .reshape(images, side * side, 16)
    )


def sincos_rows(places, width):
    omega = 1.0 / 10000.0 ** (jnp.arange(width // 2, dtype=jnp.float32) / (width // 2))
    angle = places[:, None] * omega[None, :]
    return jnp.concatenate([jnp.sin(angle), jnp.cos(angle)], axis=1)


def position_table(side, width):
    line = sincos_rows(jnp.arange(side, dtype=jnp.float32), width // 2)
    column = jnp.broadcast_to(line[None], (side, side, width // 2))
    row = jnp.broadcast_to(line[:, None], (side, side, width // 2))
    return jnp.concatenate([column, row], axis=2).reshape(side * side, width)


def time_features(steps):
    half = FREQ // 2
    freqs = jnp.exp(-math.log(10000.0) * jnp.arange(half, dtype=jnp.float32) / half)
    angle = steps[:, None] * freqs[None, :]
    return jnp.concatenate([jnp.cos(angle), jnp.sin(angle)], axis=1)


def noise_levels(steps):
    level = jnp.cos((steps / 1000.0 + 0.008) / 1.008 * (math.pi / 2)) ** 2
    return (jnp.sqrt(level), jnp.sqrt(1.0 - level))


Z, X = 4, 2
GATHER_CHUNKS = (
    (0, 0, 48, True), (0, 48, 48, True), (0, 96, 48, False),
    (1, 0, 48, False), (1, 48, 48, False), (1, 96, 48, False),
)
CHUNKS = ((0, 16, True), (16, 32, False), (48, 32, False), (80, 32, False), (112, 32, False))
META = 384
WIDE = 256
ROWS_END = PATCH_IN + HEAD_OUT
PIECE = 768


def ring_fits(n, rows):
    return n == Z * X and rows == 144


def one_hot(classes, width):
    lane = lax.broadcasted_iota(jnp.int32, (classes.shape[0], width), 1).astype(jnp.float32)
    return to_half(jnp.maximum(1.0 - jnp.abs(lane - classes), 0.0))


def gather_kernel(
    blk_hbm, dn_hbm, stem_hbm, mod_hbm, tail_hbm, meta_ref, ends_ref, b_one, b_two,
    out_blk, out_dn, meta_out, ends_out, pre_out, hidden_out, cond_out, mods_out, mod_ref, fm_ref, two_ref,
    blk_f, dn_f, stem_f, mod_f, tail_f, blk_ref, dn_ref, one_ref, table_ref, load_sem, metas, hidden, part, parts, arrived_parts,
    meta_send, meta_recv, ends_send, ends_recv, hid_send, hid_recv, part_send, part_recv, local_sem,
    up_sem, down_sem, x_sem, sib_sem, recv_sem, sib_recv, own_sem,
):
    me = lax.axis_index("dp")
    section = lax.axis_index("section")
    z, x = me // X, lax.rem(me, X)
    core = lax.rem(section, 2)
    sibling = section + 1 - 2 * core
    across = me + 1 - 2 * x
    chunks = len(GATHER_CHUNKS)
    low = section - core
    group, place_in = Z * X * 2, me * 2 + core
    where = lambda p: {"dp": p // 2, "section": low + lax.rem(p, 2)}
    has_up, has_down = z < Z - 1, z > 0

    stage_rows = dn_hbm.at[section // 2, :, pl.ds(pl.multiple_of(core * HALF, 128), HALF)]
    loads = [
        pltpu.make_async_copy(src, dst, load_sem.at[k])
        for k, (src, dst) in enumerate(
            ((blk_hbm, blk_f), (stage_rows, dn_f), (stem_hbm, stem_f), (mod_hbm, mod_f), (tail_hbm, tail_f))
        )
    ]
    for copy_in in loads:
        copy_in.start()
    barrier = pltpu.get_barrier_semaphore()

    @pl.loop(1, group)
    def _(step):
        pl.semaphore_signal(
            barrier, 1, device_id=where(lax.rem(place_in + step, group)), device_id_type=MESH
        )

    pl.semaphore_wait(barrier, group - 1)

    def to_dp(src, dst, send, recv, step, p, slot):
        return pltpu.make_async_remote_copy(
            src_ref=src, dst_ref=dst.at[slot], send_sem=send.at[step], recv_sem=recv.at[step],
            device_id={"dp": p}, device_id_type=MESH,
        )

    meta_copy = partial(to_dp, meta_ref, metas, meta_send, meta_recv)
    ends_copy = partial(to_dp, ends_ref, ends_out, ends_send, ends_recv)
    hidden_copy = partial(to_dp, hidden, hidden_out, hid_send, hid_recv)

    def part_copy(step, p, slot):
        return pltpu.make_async_remote_copy(
            src_ref=parts.at[p], dst_ref=arrived_parts.at[slot],
            send_sem=part_send.at[step], recv_sem=part_recv.at[step],
            device_id=where(p), device_id_type=MESH,
        )

    own_meta = pltpu.make_async_copy(meta_ref, metas.at[me], local_sem.at[0])
    own_ends = pltpu.make_async_copy(ends_ref, ends_out.at[me], local_sem.at[1])
    own_hidden = pltpu.make_async_copy(hidden, hidden_out.at[me], local_sem.at[2])
    own_part = pltpu.make_async_copy(parts.at[place_in], arrived_parts.at[place_in], local_sem.at[3])

    def send_all(copy_to, size, index):
        @pl.loop(1, size)
        def _(step):
            copy_to(step, lax.rem(index + step, size), index).start()

    def wait_all(copy_to, size, index):
        @pl.loop(1, size)
        def _(step):
            p = lax.rem(index + size - step, size)
            copy_to(step, p, p).wait_recv()
            copy_to(step, p, p).wait_send()

    own_meta.start()
    own_ends.start()
    send_all(meta_copy, Z * X, me)

    def place(owner, k, side):
        which, first, rows, unused = GATHER_CHUNKS[k]
        return (out_dn if which else out_blk).at[side, pl.ds(pl.multiple_of(owner * 144 + first, 16), rows)]

    def source(owner, k, mine):
        if not mine:
            return place(owner, k, core)
        which, first, rows, unused = GATHER_CHUNKS[k]
        return (dn_ref if which else blk_ref).at[pl.ds(first, rows)]

    def copy(owner, k, mine, sem, target):
        unit = owner * chunks + k
        return pltpu.make_async_remote_copy(
            src_ref=source(owner, k, mine),
            dst_ref=place(owner, k, core),
            send_sem=sem.at[unit],
            recv_sem=recv_sem.at[unit],
            device_id={"dp": target},
            device_id_type=MESH,
        )

    def to_sibling(owner, k, mine):
        unit = owner * chunks + k
        return pltpu.make_async_remote_copy(
            src_ref=source(owner, k, mine),
            dst_ref=place(owner, k, core),
            send_sem=sib_sem.at[unit],
            recv_sem=sib_recv.at[unit],
            device_id={"section": sibling},
            device_id_type=MESH,
        )

    def own_copy(k):
        return pltpu.make_async_copy(source(me, k, True), place(me, k, core), own_sem.at[k])

    def arrived(owner, k):
        copy(owner, k, False, x_sem, across).wait_recv()

    for which in range(2):
        loads[which].wait()

        @pl.loop(0, 144 // 16)
        def _(step):
            rows = pl.ds(pl.multiple_of(step * 16, 16), 16)
            if which:
                dn_ref[rows] = to_half(dn_f[rows])
            else:
                blk_ref[rows] = to_half(blk_f[rows])

    for k in range(chunks):
        @pl.when(has_up)
        def _():
            copy(me, k, True, up_sem, me + X).start()

        @pl.when(has_down)
        def _():
            copy(me, k, True, down_sem, me - X).start()

        copy(me, k, True, x_sem, across).start()
        own_copy(k).start()
        to_sibling(me, k, True).start()

    send_all(ends_copy, Z * X, me)

    at_one, at_two = NCLS + PATCH_IN, NCLS + PATCH_IN + FREQ
    for copy_in in loads[2:]:
        copy_in.wait()
    for ref in (table_ref, one_ref, two_ref):
        ref[...] = jnp.zeros_like(ref)
    table_ref[:, :NCLS] = to_half(stem_f[:, :NCLS])
    one_ref[:144] = to_half(stem_f[:, at_one:at_two])
    for index in range(Z * X):
        two_ref[index, :, :144] = to_half(stem_f[:, at_two + 144 * index : at_two + 144 * (index + 1)])
    mod_ref[...] = to_half(mod_f[...])
    fm_ref[...] = to_half(tail_f[:, : 2 * D])

    def make_hidden():
        own_meta.wait()
        wait_all(meta_copy, Z * X, me)
        for index in range(Z * X):
            meta_out[2 * index : 2 * index + 2] = metas[index]
        pre = matmul_nt(to_half(meta_out[:, :FREQ]), one_ref[...]) + b_one[...]
        pre_out[...] = pre
        hidden[...] = to_half(jax.nn.silu(pre))
        own_hidden.start()
        send_all(hidden_copy, Z * X, me)

    def make_parts():
        own_hidden.wait()
        wait_all(hidden_copy, Z * X, me)
        cond = matmul_nt(one_hot(meta_out[:, FREQ : FREQ + 1], table_ref.shape[1]), table_ref[...]) + b_two[...]
        for index in range(Z * X):
            cond = cond + matmul_nt(hidden_out[index], two_ref[index])
        cond_out[...] = cond
        cond_low = to_half(cond).astype(jnp.float32)
        own_cond = jnp.where(section == 0, cond, cond_low)
        part[:, : 3 * D] = matmul(to_half(jax.nn.silu(own_cond)), mod_ref[...])
        part[:, 3 * D : 5 * D] = matmul(to_half(jax.nn.silu(cond_low)), fm_ref[...])
        part[:, 5 * D :] = jnp.zeros((group, 8 * PIECE - 5 * D), jnp.float32)
        for row in range(group):
            for k in range(8):
                parts[row, k : k + 1] = part[row : row + 1, PIECE * k : PIECE * (k + 1)]
        own_part.start()
        send_all(part_copy, group, place_in)

    def along(step, k):
        crosses = not (step == 1 and GATHER_CHUNKS[k][3])
        for sign in (-1, 1):
            @pl.when((z >= step) if sign < 0 else (z + step < Z))
            def _():
                owner = me + sign * X * step
                arrived(owner, k)

                @pl.when(has_up if sign < 0 else has_down)
                def _():
                    copy(owner, k, False, up_sem if sign < 0 else down_sem, me - sign * X).start()

                if crosses:
                    copy(owner, k, False, x_sem, across).start()
                to_sibling(owner, k, False).start()

    def crossed(step, k):
        if step == 0:
            arrived(across, k)
            if GATHER_CHUNKS[k][3]:
                @pl.when(has_up)
                def _():
                    copy(across, k, False, up_sem, me + X).start()

                @pl.when(has_down)
                def _():
                    copy(across, k, False, down_sem, me - X).start()
            to_sibling(across, k, False).start()
            return
        for sign in (-1, 1):
            @pl.when((z >= step) if sign < 0 else (z + step < Z))
            def _():
                owner = across + sign * X * step
                arrived(owner, k)
                to_sibling(owner, k, False).start()

    for step in range(1, Z + 1):
        for k in range(chunks):
            if step < Z:
                along(step, k)
            crossed(step - 1, k)
        if step == 1:
            make_hidden()
        if step == 2:
            make_parts()

    own_part.wait()
    wait_all(part_copy, group, place_in)
    own_ends.wait()
    wait_all(ends_copy, Z * X, me)
    for source_core in range(2):
        total = arrived_parts[source_core]
        for index in range(1, Z * X):
            total = total + arrived_parts[2 * index + source_core]
        mods_out[source_core] = total

    for k in range(chunks):
        near = GATHER_CHUNKS[k][3]
        own_copy(k).wait()
        for column in range(2):
            base = me if column == 0 else across
            for step in range(0, Z):
                for sign in (-1, 1) if step else (1,):
                    @pl.when((z >= step) if sign < 0 else (z + step < Z))
                    def _():
                        owner = base + sign * X * step
                        mine = column == 0 and step == 0
                        to_sibling(owner, k, mine).wait_send()
                        pltpu.make_async_remote_copy(
                            src_ref=place(owner, k, 1 - core),
                            dst_ref=place(owner, k, 1 - core),
                            send_sem=sib_sem.at[owner * chunks + k],
                            recv_sem=sib_recv.at[owner * chunks + k],
                            device_id={"section": sibling},
                            device_id_type=MESH,
                        ).wait_recv()
                        runs = column == 0 or (near and step == 0)
                        if runs and (step == 0 or sign < 0):
                            @pl.when(has_up)
                            def _():
                                copy(owner, k, mine, up_sem, me + X).wait_send()
                        if runs and (step == 0 or sign > 0):
                            @pl.when(has_down)
                            def _():
                                copy(owner, k, mine, down_sem, me - X).wait_send()
                        if column == 0 and not (step == 1 and near):
                            copy(owner, k, mine, x_sem, across).wait_send()


def gather_weights(block, downs, stems, mod, tail, meta, ends, b_one, b_two):
    n, width = lax.axis_size("dp"), block.shape[0]
    section = lax.axis_index("section")
    if not ring_fits(n, width):
        both = lambda own, sib: jnp.where(
            lax.rem(section, 2) == 0, jnp.stack([own, sib]), jnp.stack([sib, own])
        )
        core = lax.rem(section, 2)
        dn = lax.dynamic_slice(downs, (section // 2, 0, core * HALF), (1, width, HALF))[0]
        blk = lax.all_gather(to_half(block), "dp", axis=0, tiled=True)
        dn = lax.all_gather(to_half(dn), "dp", axis=0, tiled=True)
        at_one, at_two = NCLS + PATCH_IN, NCLS + PATCH_IN + FREQ
        stem, w_mod, w_fm = to_half(stems), to_half(mod), to_half(tail[:, : 2 * D])
        table = jnp.pad(stem[:, :NCLS], ((0, 0), (0, -NCLS % 128)))
        w_one = jnp.pad(stem[:, at_one:at_two], ((0, WIDE - width), (0, 0)))
        w_two = stem[:, at_two:].reshape(width, n, width).transpose(1, 0, 2)
        w_two = jnp.pad(w_two, ((0, 0), (0, 0), (0, WIDE - width)))
        meta, ends = exchange(2, "dp", ("all", "all"), meta, ends)
        meta = meta.reshape(2 * n, META)
        pre = matmul_nt(to_half(meta[:, :FREQ]), w_one) + b_one
        (hidden,) = exchange(8, "dp", ("all",), to_half(jax.nn.silu(pre)))
        cond = matmul_nt(one_hot(meta[:, FREQ : FREQ + 1], table.shape[1]), table) + b_two
        cond = cond + jnp.einsum("jik,jwk->iw", hidden, w_two, preferred_element_type=jnp.float32)
        cond_low = to_half(cond).astype(jnp.float32)
        own_cond = jnp.where(section == 0, cond, cond_low)
        parts = [
            matmul(to_half(jax.nn.silu(own_cond)), w_mod),
            matmul(to_half(jax.nn.silu(cond_low)), w_fm),
        ]
        parts = jnp.pad(jnp.concatenate(parts, axis=1), ((0, 0), (0, 8 * PIECE - 5 * D)))
        (parts,) = exchange(3, "stage", ("each",), parts.reshape(2 * n, 8, PIECE))
        mods = jnp.sum(parts.reshape(n, 2, 8, PIECE), axis=0)
        own = (both(blk, swap(blk, 1)), both(dn, swap(dn, 1)), meta, ends, pre, hidden, cond, mods)
        return own + (w_mod, w_fm, w_two)
    units, images = n * len(GATHER_CHUNKS), 2 * n
    hbm, vmem = pl.BlockSpec(memory_space=pl.ANY), pl.BlockSpec(memory_space=pltpu.VMEM)
    dma = lambda count: pltpu.SemaphoreType.DMA((count,))
    f32 = jnp.float32
    return pl.pallas_call(
        gather_kernel,
        out_shape=(
            jax.ShapeDtypeStruct((2, D, FF), BF), jax.ShapeDtypeStruct((2, D, HALF), BF),
            jax.ShapeDtypeStruct((images, META), f32), jax.ShapeDtypeStruct((n,) + ends.shape, BF),
            jax.ShapeDtypeStruct((images, WIDE), f32), jax.ShapeDtypeStruct((n, images, WIDE), BF),
            jax.ShapeDtypeStruct((images, width), f32), jax.ShapeDtypeStruct((2, 8, PIECE), f32),
            jax.ShapeDtypeStruct((width, 3 * D), BF), jax.ShapeDtypeStruct((width, 2 * D), BF),
            jax.ShapeDtypeStruct((n, width, WIDE), BF),
        ),
        in_specs=[hbm] * 5 + [vmem] * 4,
        out_specs=(hbm, hbm) + (vmem,) * 9,
        scratch_shapes=[
            pltpu.VMEM((width, FF), f32), pltpu.VMEM((width, HALF), f32), pltpu.VMEM(stems.shape, f32),
            pltpu.VMEM((width, 3 * D), f32), pltpu.VMEM(tail.shape, f32),
            pltpu.VMEM((width, FF), BF), pltpu.VMEM((width, HALF), BF), pltpu.VMEM((WIDE, FREQ), BF),
            pltpu.VMEM((width, 1024), BF), dma(5),
            pltpu.VMEM((n, 2, META), f32), pltpu.VMEM((images, WIDE), BF),
            pltpu.VMEM((images, 8 * PIECE), f32),
            pltpu.VMEM((images, 8, PIECE), f32), pltpu.VMEM((images, 8, PIECE), f32),
            dma(n), dma(n), dma(n), dma(n), dma(n), dma(n), dma(images), dma(images), dma(4),
        ]
        + [dma(units)] * 6
        + [dma(len(GATHER_CHUNKS))],
        compiler_params=pltpu.CompilerParams(
            collective_id=0, has_side_effects=True, vmem_limit_bytes=VMEM_BYTES
        ),
        cost_estimate=pl.CostEstimate(flops=0, bytes_accessed=400_000_000, transcendentals=0),
        name="gather_weights",
    )(block, downs, stems, mod, tail, meta, ends, b_one, b_two)


VMEM_BYTES = 60 * 1024 * 1024
SUM_CHUNKS = tuple((which,) + chunk for which in range(3) for chunk in CHUNKS)


def silu_slope(value):
    gate = jax.nn.sigmoid(value)
    return gate * (1.0 + value * (1.0 - gate))


def sum_kernel(
    g_dn, g_up, g_attn, dm_ref, bp_ref, en_ref, mod_ref, fm_ref, two_ref, cond_ref, pre_ref, hid_ref, meta_ref,
    out, cross_out, dn_out, gmod_out, gfm_out, gtab_out, gone_out, gtwo_out,
    ends_all, bias_out, sq_out,
    own_b, other_d, xb, xq, up_b, up_o, down_b, down_o, acc, acc_dn,
    dm_in, bp_in, en_in, dmat, ends_src, c_src, c_in, fmd_src, fmd_in, cs_src, dcond, ph, ph_in, news_src,
    sq_src, sq_all, sq_rows, cross_src, news_out, cs_all, fmsum_out,
    load_sem, x_send, x_recv, up_send, up_recv, down_send, down_recv,
    sib_send, sib_recv, y_send, y_recv, group_send, group_recv, sect_send, sect_recv,
    ph_send, ph_recv, news_send, news_recv, sq_send, sq_recv, cross_sem, local_sem,
):
    me = lax.axis_index("dp")
    section = lax.axis_index("section")
    z, x = me // X, lax.rem(me, X)
    core = lax.rem(section, 2)
    low, sibling, facing = section - core, section + 1 - 2 * core, lax.rem(section + 2, 4)
    across = me + 1 - 2 * x
    sources = (g_dn, g_up, g_attn)
    chunks = len(SUM_CHUNKS)
    has_up, has_down = z < Z - 1, z > 0
    devices, group = Z * X * 4, Z * X * 2
    me_all, me_group = me * 4 + section, me * 2 + core
    in_all = lambda p: {"dp": p // 4, "section": lax.rem(p, 4)}
    in_group = lambda p: {"dp": p // 2, "section": low + lax.rem(p, 2)}
    in_section = lambda p: {"section": p}
    in_dp = lambda p: {"dp": p}
    f32 = jnp.float32

    barrier = pltpu.get_barrier_semaphore()

    @pl.loop(1, devices)
    def _(step):
        pl.semaphore_signal(
            barrier, 1, device_id=in_all(lax.rem(me_all + step, devices)), device_id_type=MESH
        )

    def small(src_of, dst, send, recv, where, size, index):
        def copy(step, p, slot):
            return pltpu.make_async_remote_copy(
                src_ref=src_of(p), dst_ref=dst.at[slot], send_sem=send.at[step], recv_sem=recv.at[step],
                device_id=where(p), device_id_type=MESH,
            )
        return (copy, size, index, src_of, dst)

    gradients = [
        small(lambda p: dm_ref.at[lax.rem(p, 2)], dm_in, group_send.at[0], group_recv.at[0], in_group, group, me_group),
        small(lambda p: bp_ref.at[p], bp_in, group_send.at[1], group_recv.at[1], in_group, group, me_group),
        small(lambda p: en_ref.at[p // 2], en_in, group_send.at[2], group_recv.at[2], in_group, group, me_group),
    ]
    conds = [
        small(lambda p, src=src: src, dst, sect_send.at[k], sect_recv.at[k], in_section, 4, section)
        for k, (src, dst) in enumerate(
            ((c_src, c_in), (ends_src, ends_all), (fmd_src, fmd_in), (cs_src, cs_all))
        )
    ]
    hiddens = [small(lambda p: ph.at[p], ph_in, ph_send, ph_recv, in_dp, Z * X, me)]
    news = [small(lambda p: news_src, news_out, news_send, news_recv, in_all, devices, me_all)]
    norms = [small(lambda p: sq_src, sq_all, sq_send, sq_recv, in_all, devices, me_all)]

    def own_copies(batch, first):
        return [
            pltpu.make_async_copy(src_of(index), dst.at[index], local_sem.at[first + k])
            for k, (copy, size, index, src_of, dst) in enumerate(batch)
        ]

    def send_batch(batch, first):
        for copy in own_copies(batch, first):
            copy.start()
        for copy, size, index, src_of, dst in batch:
            @pl.loop(1, size)
            def _(step):
                copy(step, lax.rem(index + step, size), index).start()

    def wait_batch(batch, first):
        for copy in own_copies(batch, first):
            copy.wait()
        for copy, size, index, src_of, dst in batch:
            @pl.loop(1, size)
            def _(step):
                p = lax.rem(index + size - step, size)
                copy(step, p, p).wait_recv()
                copy(step, p, p).wait_send()

    def add_square(value):
        sq_src[...] += jnp.sum(value * value)

    def images_of():
        cond = cond_ref[...]
        cond_low = to_half(cond).astype(f32)
        return jnp.where(section == 0, cond, cond_low), cond_low

    def make_cond():
        wait_batch(gradients, 0)
        flat = dm_in[...].reshape(group * 48, 128)
        row = lax.broadcasted_iota(jnp.int32, (group, group * 48), 0) * 48
        column = lax.broadcasted_iota(jnp.int32, (group, group * 48), 1)
        for k in range(5 * D // 128):
            chosen = jnp.where(column == row + k, 1.0, 0.0).astype(BF)
            dmat[:, 128 * k : 128 * (k + 1)] = to_half(matmul(chosen, flat))
        news_src[...] = jnp.zeros_like(news_src)
        news_src[0:SUM_ROWS] = jnp.sum(bp_in[...], axis=0)
        ends_src[...] = jnp.sum(en_in[...], axis=0)
        own_cond, cond_low = images_of()
        d_mod, d_fm = dmat[:, : 3 * D], dmat[:, 3 * D :]
        fmd_src[...] = d_fm
        cs_src[...] = jnp.sum(d_mod.astype(f32), axis=0, keepdims=True)
        d_silu = matmul_nt(d_mod, mod_ref[...])
        d_silu = d_silu + (section == 3).astype(f32) * matmul_nt(d_fm, fm_ref[...])
        c_src[...] = jnp.zeros_like(c_src)
        c_src[:, :144] = silu_slope(own_cond) * d_silu
        send_batch(conds, 3)
        silu_own = to_half(jax.nn.silu(own_cond))
        for k in range(3):
            part_g = matmul_tn(silu_own, dmat[:, D * k : D * (k + 1)])
            gmod_out[:, D * k : D * (k + 1)] = part_g
            add_square(part_g)

    once = (section == 0).astype(f32)

    def make_hidden():
        wait_batch(conds, 3)
        total = to_half(c_in[3])
        for slot in (2, 1, 0):
            total = to_half(total.astype(f32) + c_in[slot])
        dcond[...] = total
        d_cond = dcond[:, :144]
        for index in range(Z * X):
            ph[index] = matmul(d_cond, two_ref[index])
        send_batch(hiddens, 7)
        own_cond, cond_low = images_of()
        silu_low = to_half(jax.nn.silu(cond_low))
        for k in range(2):
            part_g = matmul_tn(silu_low, fmd_in[3, :, D * k : D * (k + 1)])
            gfm_out[:, D * k : D * (k + 1)] = part_g
            add_square(jnp.sqrt(once) * part_g)
        fmsum_out[...] = jnp.sum(fmd_in[3].astype(f32), axis=0, keepdims=True)
        part_g = matmul_tn(d_cond, one_hot(meta_ref[:, FREQ : FREQ + 1], gtab_out.shape[1]))
        gtab_out[...] = part_g
        add_square(once * part_g)
        for index in range(Z * X):
            part_g = matmul_tn(d_cond, hid_ref[index])
            gtwo_out[:, 144 * index : 144 * (index + 1)] = part_g[:, :144]
            add_square(once * part_g)

    def make_news():
        wait_batch(hiddens, 7)
        total = ph_in[0]
        for index in range(1, Z * X):
            total = total + ph_in[index]
        d_pre = to_half(silu_slope(pre_ref[...]) * total)
        part_g = matmul_tn(d_pre, to_half(meta_ref[:, :FREQ]))
        gone_out[...] = part_g
        add_square(once * part_g)
        sums = jnp.sum(d_pre.astype(f32), axis=0, keepdims=True)
        sums_cond = jnp.sum(dcond[...].astype(f32), axis=0, keepdims=True)
        for k in range(2):
            news_src[SUM_ROWS + k : SUM_ROWS + k + 1] = sums[:, 128 * k : 128 * (k + 1)]
            news_src[SUM_ROWS + 2 + k : SUM_ROWS + 3 + k] = sums_cond[:, 128 * k : 128 * (k + 1)]
        send_batch(news, 8)
        first = (me == 0).astype(f32)
        add_square(news_src[0:10])
        add_square(once * sums)
        add_square(once * sums_cond)
        add_square(first * cs_src[...])
        add_square(first * once * fmsum_out[...])
        add_square(once * ends_all[0])
        add_square(once * ends_all[3])

    def make_biases():
        wait_batch(news, 8)
        bias_out[...] = jnp.zeros_like(bias_out)
        for slot in range(4):
            for k in range(3):
                row = 3 * slot + k
                bias_out[row : row + 1] = cs_all[slot, :, D * k : D * (k + 1)]
        for side in range(2):
            for block in range(D // 128):
                part = slice(128 * block, 128 * (block + 1))
                device = (block // 2) * 4 + 2 * side + block % 2
                bias_out[12 + 8 * side : 20 + 8 * side, part] = news_out[device, 0:8]
                bias_out[28 + side : 29 + side, part] = news_out[device, 8:9]
                row = 35 if side else 30
                bias_out[row : row + 1, part] = news_out[device, 9:10]
                if side:
                    bias_out[36:37, part] = news_out[device, 10:11]
        for index in range(Z * X):
            first = 144 * index
            for k in range(2):
                at = SUM_ROWS + 2 * k
                bias_out[31 + k : 32 + k, first : first + 128] = news_out[4 * index, at : at + 1]
                bias_out[31 + k : 32 + k, first + 128 : first + 144] = news_out[4 * index, at + 1 : at + 2, :16]
        for k in range(2):
            bias_out[33 + k : 34 + k] = fmsum_out[:, D * k : D * (k + 1)]

    def dn_copy(k, slot, to_sib):
        rows = pl.ds(SUM_CHUNKS[k][1], SUM_CHUNKS[k][2])
        unit = slot * chunks + k
        return pltpu.make_async_remote_copy(
            src_ref=dn_out.at[slot, rows], dst_ref=dn_out.at[slot, rows],
            send_sem=(sib_send if to_sib else y_send).at[unit],
            recv_sem=(sib_recv if to_sib else y_recv).at[unit],
            device_id={"section": sibling if to_sib else facing},
            device_id_type=MESH,
        )

    def each(distance, run):
        if distance == 0:
            run(z, None)
            return

        @pl.when(z + distance < Z)
        def _():
            run(z + distance, True)

        @pl.when(z >= distance)
        def _():
            run(z - distance, False)

    def part(k):
        return pl.ds(SUM_CHUNKS[k][1], SUM_CHUNKS[k][2])

    def hbm(k, zz, column):
        start = pl.multiple_of((zz * X + column) * 144 + SUM_CHUNKS[k][1], 16)
        return sources[SUM_CHUNKS[k][0]].at[pl.ds(start, SUM_CHUNKS[k][2])]

    def own(k, zz):
        return own_b.at[SUM_CHUNKS[k][0], zz, part(k)]

    def from_x(k, zz):
        return xq.at[SUM_CHUNKS[k][0]] if SUM_CHUNKS[k][3] else xb.at[SUM_CHUNKS[k][0], zz, part(k)]

    def from_z(k, zz, up, other):
        if other:
            return (up_o if up else down_o).at[SUM_CHUNKS[k][0], zz]
        return (up_b if up else down_b).at[SUM_CHUNKS[k][0], zz, part(k)]

    def other_of(k, zz):
        return other_d.at[SUM_CHUNKS[k][0], zz]

    def load(k, zz, other=False):
        index = ((chunks if other else 0) + k) * Z + zz
        return pltpu.make_async_copy(
            hbm(k, zz, (1 - x) if other else x),
            other_of(k, zz) if other else own(k, zz),
            load_sem.at[index],
        )

    def x_copy(k, zz, src):
        unit = k * Z + zz
        return pltpu.make_async_remote_copy(
            src_ref=src, dst_ref=from_x(k, zz), send_sem=x_send.at[unit], recv_sem=x_recv.at[unit],
            device_id={"dp": across}, device_id_type=MESH,
        )

    def z_copy(k, zz, up, other):
        unit = ((chunks if other else 0) + k) * Z + zz
        return pltpu.make_async_remote_copy(
            src_ref=other_of(k, zz) if other else own(k, zz),
            dst_ref=from_z(k, zz, up, other),
            send_sem=(up_send if up else down_send).at[unit],
            recv_sem=(up_recv if up else down_recv).at[unit],
            device_id={"dp": me + X if up else me - X},
            device_id_type=MESH,
        )

    def total(k, dst, srcs):
        @pl.loop(0, SUM_CHUNKS[k][2] // 16)
        def _(step):
            rows = pl.ds(pl.multiple_of(step * 16, 16), 16)
            value = srcs[0][rows].astype(jnp.float32)
            for src in srcs[1:]:
                value = value + src[rows].astype(jnp.float32)
            dst[rows] = value.astype(dst.dtype)

    for distance in (3, 2, 1, 0):
        for k in range(chunks):
            def run(zz, up):
                load(k, zz).start()
                if SUM_CHUNKS[k][3]:
                    load(k, zz, True).start()
            each(distance, run)

    sq_src[...] = jnp.zeros_like(sq_src)
    sq_rows[...] = jnp.zeros_like(sq_rows)
    pl.semaphore_wait(barrier, devices - 1)
    send_batch(gradients, 0)

    order = [
        (k, distance) for which, distance in ((0, 3), (0, 2), (0, 1), (1, 3), (0, 0), (1, 2), (1, 1), (2, 3), (1, 0), (2, 2), (2, 1), (2, 0))
        for k in range(chunks) if SUM_CHUNKS[k][0] == which and not SUM_CHUNKS[k][3]
    ]
    sent = []

    def send_x(until):
        while len(sent) < min(until, len(order)):
            k, distance = order[len(sent)]
            sent.append(1)
            each(distance, lambda zz, up: x_copy(k, zz, hbm(k, zz, 1 - x)).start())

    def after(k, distance):
        if not SUM_CHUNKS[k][3]:
            send_x(order.index((k, distance)) + 1 + 6)

    send_x(6)

    def pass_on(k, distance):
        def run(zz, up):
            behind = has_down if up else has_up
            if SUM_CHUNKS[k][3]:
                for other in (False, True):
                    mine = other_of(k, zz) if other else own(k, zz)
                    load(k, zz, other).wait()

                    @pl.when(behind)
                    def _():
                        z_copy(k, zz, up, other).wait_recv()
                        total(k, mine, [mine, from_z(k, zz, up, other)])

                    z_copy(k, zz, up, other).start()
                return
            load(k, zz).wait()
            x_copy(k, zz, hbm(k, zz, 1 - x)).wait_recv()

            @pl.when(behind)
            def _():
                z_copy(k, zz, up, False).wait_recv()
                total(k, own(k, zz), [own(k, zz), from_x(k, zz), from_z(k, zz, up, False)])

            @pl.when(jnp.logical_not(behind))
            def _():
                total(k, own(k, zz), [own(k, zz), from_x(k, zz)])

            z_copy(k, zz, up, False).start()
        each(distance, run)

    def add_z(dst, k, other):
        @pl.when(has_down)
        def _():
            z_copy(k, z, True, other).wait_recv()
            total(k, dst, [dst, from_z(k, z, True, other)])

        @pl.when(has_up)
        def _():
            z_copy(k, z, False, other).wait_recv()
            total(k, dst, [dst, from_z(k, z, False, other)])

    def send_direct(k):
        load(k, z, True).wait()
        total(k, acc, [other_of(k, z)])
        add_z(acc, k, True)
        total(k, other_of(k, z), [acc])
        x_copy(k, z, other_of(k, z)).start()

    def finish(k):
        which, rows = SUM_CHUNKS[k][0], SUM_CHUNKS[k][2]
        dst = out.at[which - 1, part(k)] if which else acc_dn.at[pl.ds(0, rows)]
        load(k, z).wait()
        if SUM_CHUNKS[k][3]:
            total(k, dst, [own(k, z)])
            add_z(dst, k, False)
            x_copy(k, z, other_of(k, z)).wait_recv()
            total(k, dst, [dst, from_x(k, z)])
        else:
            x_copy(k, z, hbm(k, z, 1 - x)).wait_recv()
            total(k, dst, [own(k, z), from_x(k, z)])
            add_z(dst, k, False)
        if not which:
            total(k, dn_out.at[section, part(k)], [dst])
            dn_copy(k, section, True).start()
            dn_copy(k, section, False).start()

        @pl.loop(0, rows // 16)
        def _(step):
            value = dst[pl.ds(pl.multiple_of(step * 16, 16), 16)]
            sq_rows[...] += jnp.sum(value * value, axis=0, keepdims=True)

    def of(which, direct=None):
        return [
            k for k in range(chunks)
            if SUM_CHUNKS[k][0] == which and (direct is None or SUM_CHUNKS[k][3] == direct)
        ]

    def pass_all(which, distance):
        for k in of(which):
            pass_on(k, distance)
            after(k, distance)

    def finish_all(which):
        for k in of(which, False) + of(which, True):
            finish(k)
            after(k, 0)

    def direct_all(which):
        for k in of(which, True):
            send_direct(k)

    for distance in (3, 2, 1):
        pass_all(0, distance)
    make_cond()
    pass_all(1, 3)
    direct_all(0)
    finish_all(0)
    pass_all(1, 2)
    make_hidden()
    pass_all(1, 1)
    for k in of(0):
        dn_copy(k, facing, False).wait_recv()
        dn_copy(k, facing, True).start()
    pass_all(2, 3)
    make_news()
    direct_all(1)
    finish_all(1)
    pass_all(2, 2)
    pass_all(2, 1)
    make_biases()
    direct_all(2)
    finish_all(2)

    @pl.loop(0, 144 // 16)
    def _(step):
        rows = pl.ds(pl.multiple_of(step * 16, 16), 16)
        cross_src[rows] = to_half(jnp.where(core == 0, out[0, rows], out[1, rows]))

    crossing = pltpu.make_async_remote_copy(
        src_ref=cross_src, dst_ref=cross_out, send_sem=cross_sem.at[0], recv_sem=cross_sem.at[1],
        device_id={"section": sibling}, device_id_type=MESH,
    )
    sq_src[...] += jnp.sum(sq_rows[...])
    send_batch(norms, 9)
    crossing.start()
    wait_batch(norms, 9)
    sq_out[...] = jnp.sum(sq_all[...], axis=0)
    crossing.wait()

    for k in range(chunks):
        for distance in (3, 2, 1, 0):
            def run(zz, up):
                if not SUM_CHUNKS[k][3]:
                    x_copy(k, zz, hbm(k, zz, 1 - x)).wait_send()
                elif distance == 0:
                    x_copy(k, zz, other_of(k, zz)).wait_send()
                if distance:
                    z_copy(k, zz, up, False).wait_send()
                    if SUM_CHUNKS[k][3]:
                        z_copy(k, zz, up, True).wait_send()
            each(distance, run)
        if not SUM_CHUNKS[k][0]:
            dn_copy(k, section, True).wait_send()
            dn_copy(k, section, False).wait_send()
            dn_copy(k, facing, True).wait_send()
            dn_copy(k, sibling, True).wait_recv()
            dn_copy(k, lax.rem(sibling + 2, 4), True).wait_recv()


def sum_gradients(g_dn, g_up, g_attn, d_mods, sums, ends, w_mod, w_fm, two_blocks, cond, pre, hidden, meta):
    n, width = lax.axis_size("dp"), cond.shape[1]
    f32 = jnp.float32
    if not ring_fits(n, width):
        return sum_plainly(g_dn, g_up, g_attn, d_mods, sums, ends, w_mod, w_fm, two_blocks, cond, pre, hidden, meta)
    chunks, images, devices = len(SUM_CHUNKS), 2 * n, 4 * n
    dma = lambda *count: pltpu.SemaphoreType.DMA(count)
    ring = pltpu.VMEM((3, Z, 144, HALF), BF)
    short = [rows for start, rows, direct in CHUNKS if direct][0]
    most = max(rows for start, rows, direct in CHUNKS)
    ring_o = pltpu.VMEM((3, Z, short, HALF), BF)
    hbm, vmem = pl.BlockSpec(memory_space=pl.ANY), pl.BlockSpec(memory_space=pltpu.VMEM)
    like = jax.ShapeDtypeStruct
    end_block = ends.shape[1:]
    shapes = (
        like((2, 144, HALF), f32), like((144, HALF), BF), like((4, 144, HALF), BF),
        like((144, 3 * D), f32), like((144, 2 * D), f32), like((144, 1024), f32), like((WIDE, FREQ), f32),
        like((144, D), f32), like((4,) + end_block, f32), like((40, D), f32), like((8, 128), f32),
    )
    return pl.pallas_call(
        sum_kernel,
        out_shape=shapes,
        in_specs=[hbm] * 3 + [vmem] * 10,
        out_specs=(vmem,) * len(shapes),
        scratch_shapes=[
            ring, ring_o, ring, pltpu.VMEM((3, short, HALF), BF),
            ring, ring_o, ring, ring_o, pltpu.VMEM((short, HALF), f32), pltpu.VMEM((most, HALF), f32),
            pltpu.VMEM((images, 48, 128), BF), pltpu.VMEM((images, SUM_ROWS, 128), f32),
            pltpu.VMEM((images,) + end_block, f32), pltpu.VMEM((images, 5 * D), BF),
            pltpu.VMEM(end_block, f32), pltpu.VMEM((images, WIDE), f32), pltpu.VMEM((4, images, WIDE), f32),
            pltpu.VMEM((images, 2 * D), BF), pltpu.VMEM((4, images, 2 * D), BF), pltpu.VMEM((1, 3 * D), f32),
            pltpu.VMEM((images, WIDE), BF), pltpu.VMEM((n, images, WIDE), f32), pltpu.VMEM((n, images, WIDE), f32),
            pltpu.VMEM((24, 128), f32), pltpu.VMEM((8, 128), f32), pltpu.VMEM((devices, 8, 128), f32),
            pltpu.VMEM((1, HALF), f32),
            pltpu.VMEM((144, HALF), BF), pltpu.VMEM((devices, 24, 128), f32), pltpu.VMEM((4, 1, 3 * D), f32),
            pltpu.VMEM((1, 2 * D), f32),
            dma(2 * chunks * Z), dma(chunks * Z), dma(chunks * Z),
            dma(2 * chunks * Z), dma(2 * chunks * Z), dma(2 * chunks * Z), dma(2 * chunks * Z),
            dma(4 * chunks), dma(4 * chunks), dma(4 * chunks), dma(4 * chunks),
            dma(3, images), dma(3, images), dma(4, 4), dma(4, 4),
            dma(n), dma(n), dma(devices), dma(devices), dma(devices), dma(devices), dma(2), dma(10),
        ],
        compiler_params=pltpu.CompilerParams(
            collective_id=1, has_side_effects=True, vmem_limit_bytes=VMEM_BYTES
        ),
        cost_estimate=pl.CostEstimate(flops=0, bytes_accessed=400_000_000, transcendentals=0),
        name="sum_gradients",
    )(g_dn, g_up, g_attn, d_mods, sums, ends, w_mod, w_fm, two_blocks, cond, pre, hidden, meta)


def sum_plainly(g_dn, g_up, g_attn, d_mods, sums, ends, w_mod, w_fm, two_blocks, cond, pre, hidden, meta):
    n, width = lax.axis_size("dp"), cond.shape[1]
    section, images, f32 = lax.axis_index("section"), 2 * n, jnp.float32
    once = (section == 0).astype(f32)
    anchor = (lax.axis_index("dp") == 0).astype(f32)
    total = lambda grad: lax.psum_scatter(grad, "dp", scatter_dimension=0, tiled=True)
    dn_own, out = total(g_dn), jnp.stack([total(g_up), total(g_attn)]).astype(f32)
    dn_all = lax.all_gather(dn_own, "section")
    cross = swap(to_half(jnp.where(lax.rem(section, 2) == 0, out[0], out[1])), 1)
    d_mods, sums, ends = exchange(4, "stage", ("core", "each", "dp"), d_mods, sums, ends)
    d_mods = d_mods.reshape(images, 48 * 128)
    d_mod, d_fm = d_mods[:, : 3 * D], d_mods[:, 3 * D : 5 * D]
    sums, ends = jnp.sum(sums, axis=0), jnp.sum(ends, axis=0)
    cond_low = to_half(cond).astype(f32)
    own_cond = jnp.where(section == 0, cond, cond_low)
    d_silu = matmul_nt(d_mod, w_mod) + (section == 3).astype(f32) * matmul_nt(d_fm, w_fm)
    c_own = jnp.pad(silu_slope(own_cond) * d_silu, ((0, 0), (0, WIDE - width)))
    cs = column_sums(d_mod)[None]
    c_all, ends_all, d_fm, cs_all = exchange(5, "section", ("all",) * 4, c_own, ends, d_fm, cs)
    d_fm = d_fm[3]
    d_cond = to_half(c_all[3])
    for slot in (2, 1, 0):
        d_cond = to_half(d_cond.astype(f32) + c_all[slot])
    narrow = d_cond[:, :width]
    part = jnp.einsum("iw,jwk->jik", narrow, two_blocks, preferred_element_type=f32)
    (part,) = exchange(6, "dp", ("each",), part)
    d_pre = to_half(silu_slope(pre) * jnp.sum(part, axis=0))
    g_mod = matmul_tn(to_half(jax.nn.silu(own_cond)), d_mod)
    g_fm = matmul_tn(to_half(jax.nn.silu(cond_low)), d_fm)
    g_table = matmul_tn(narrow, one_hot(meta[:, FREQ : FREQ + 1], 1024))
    g_one = matmul_tn(d_pre, to_half(meta[:, :FREQ]))
    g_two = jnp.einsum("iw,jik->wjk", narrow, hidden, preferred_element_type=f32)
    g_two = g_two[:, :, :width].reshape(width, D)
    fm_sum = column_sums(d_fm)[None]
    slices = [column_sums(value).reshape(2, 128) for value in (d_pre, d_cond)]
    news = jnp.concatenate([sums, *slices, jnp.zeros((4, 128), f32)])
    square = lambda value: jnp.sum(value * value)
    squares = square(out) + square(dn_own.astype(f32)) + square(g_mod) + square(sums[:10])
    squares = squares + anchor * square(cs) + anchor * once * square(fm_sum)
    for value in (g_fm, g_table, g_one, g_two, ends_all[0], ends_all[3], *slices):
        squares = squares + once * square(value)
    news, squares = exchange(7, "every", ("all", "all"), news, jnp.broadcast_to(squares, (8, 128)))
    squares = jnp.sum(squares, axis=0)
    news = news.reshape(n, 4, -1, 128)
    stages = []
    for k in range(2):
        pieces = news[:, 2 * k : 2 * k + 2, :SUM_ROWS].reshape(2 * n, SUM_ROWS, 128)[: D // 128]
        stages.append(pieces.transpose(1, 0, 2).reshape(-1))
    slices = news[:, 0, SUM_ROWS : SUM_ROWS + 4].reshape(n, 2, WIDE)[:, :, :width]
    bias_rows = jnp.concatenate(
        [cs_all.reshape(-1)]
        + [part[: 8 * D] for part in stages]
        + [part[8 * D : 9 * D] for part in stages]
        + [stages[0][9 * D : 10 * D]]
        + [slices[:, 0].reshape(-1), slices[:, 1].reshape(-1)]
        + [fm_sum[0], stages[1][9 * D : 11 * D], jnp.zeros((3 * D,), f32)]
    ).reshape(40, D)
    return (out, cross, dn_all, g_mod, g_fm, g_table, g_one, g_two, ends_all, bias_rows, squares)


def exchange_kernel(axes, modes, *refs):
    count = len(modes)
    ins, outs = refs[:count], refs[count : 2 * count]
    send_sem, recv_sem, own_sem = refs[2 * count :]
    dp, section = lax.axis_index("dp"), lax.axis_index("section")
    n, sections = lax.axis_size("dp"), lax.axis_size("section")
    if axes == "dp":
        size, me, where = n, dp, lambda p: {"dp": p}
    elif axes == "section":
        size, me, where = sections, section, lambda p: {"section": p}
    elif axes == "stage":
        low = section - lax.rem(section, 2)
        size, me = 2 * n, dp * 2 + lax.rem(section, 2)
        where = lambda p: {"dp": p // 2, "section": low + lax.rem(p, 2)}
    else:
        size, me = n * sections, dp * sections + section
        where = lambda p: {"dp": p // sections, "section": lax.rem(p, sections)}

    def part(k, p):
        if modes[k] == "all":
            return ins[k]
        index = {"each": p, "dp": p // 2, "core": lax.rem(p, 2)}[modes[k]]
        return ins[k].at[index]

    def copy(k, step, src, slot, p):
        return pltpu.make_async_remote_copy(
            src_ref=src, dst_ref=outs[k].at[slot],
            send_sem=send_sem.at[k, step], recv_sem=recv_sem.at[k, step],
            device_id=where(p), device_id_type=MESH,
        )

    barrier = pltpu.get_barrier_semaphore()

    @pl.loop(1, size)
    def _(step):
        pl.semaphore_signal(barrier, 1, device_id=where(lax.rem(me + step, size)), device_id_type=MESH)

    for k in range(count):
        pltpu.make_async_copy(part(k, me), outs[k].at[me], own_sem.at[k]).start()
    pl.semaphore_wait(barrier, size - 1)

    @pl.loop(1, size)
    def _(step):
        p = lax.rem(me + step, size)
        for k in range(count):
            copy(k, step, part(k, p), me, p).start()

    for k in range(count):
        pltpu.make_async_copy(part(k, me), outs[k].at[me], own_sem.at[k]).wait()

    @pl.loop(1, size)
    def _(step):
        p = lax.rem(me + size - step, size)
        for k in range(count):
            copy(k, step, part(k, p), p, p).wait_recv()
            copy(k, step, part(k, p), p, p).wait_send()


def exchange(ident, axes, modes, *arrays):
    n, sections = lax.axis_size("dp"), lax.axis_size("section")
    size = {"dp": n, "section": sections, "stage": 2 * n, "every": n * sections}[axes]
    blocks = [a.shape if mode == "all" else a.shape[1:] for a, mode in zip(arrays, modes)]
    count = len(arrays)
    vmem = pl.BlockSpec(memory_space=pltpu.VMEM)
    return pl.pallas_call(
        partial(exchange_kernel, axes, modes),
        out_shape=tuple(jax.ShapeDtypeStruct((size,) + b, a.dtype) for a, b in zip(arrays, blocks)),
        in_specs=[vmem] * count,
        out_specs=(vmem,) * count,
        scratch_shapes=[
            pltpu.SemaphoreType.DMA((count, size)),
            pltpu.SemaphoreType.DMA((count, size)),
            pltpu.SemaphoreType.DMA((count,)),
        ],
        compiler_params=pltpu.CompilerParams(
            collective_id=ident, has_side_effects=True, vmem_limit_bytes=VMEM_BYTES
        ),
        cost_estimate=pl.CostEstimate(flops=0, bytes_accessed=30_000_000, transcendentals=0),
        name="exchange_" + axes,
    )(*arrays)


def rows_of(value, size):
    value = value.reshape(-1)
    return jnp.pad(value, (0, size * 128 - value.shape[0])).reshape(size, 128)


def row_count(length, unit=8):
    return -(-length // (128 * unit)) * unit


TILE = 768
STEPS = HALF // TILE
GELU_SCALE = math.sqrt(2.0 / math.pi)
SCALE = HEAD_DIM ** (-0.5)


def mean_rows(value):
    return jnp.mean(value, axis=-1, keepdims=True)


def normalized(x):
    centered = x - mean_rows(x)
    inverse = lax.rsqrt(mean_rows(centered * centered) + epsilon_norm)
    return (centered * inverse, inverse)


def modulated_back(normed, inverse, scale, d_xm):
    d_normed = d_xm * (1.0 + scale)
    d_x = inverse * (d_normed - mean_rows(d_normed) - normed * mean_rows(d_normed * normed))
    return (d_x, jnp.sum(d_xm, axis=0), jnp.sum(d_xm * normed, axis=0))


def window(head):
    low = HEAD_DIM * head // 128 * 128
    high = -(-HEAD_DIM * (head + 1) // 128) * 128
    lane = lax.broadcasted_iota(jnp.int32, (PATCHES, high - low), 1) + low
    return slice(low, high), (lane >= HEAD_DIM * head) & (lane < HEAD_DIM * (head + 1))


def own_lanes(mask, value):
    return jnp.where(mask, value, jnp.zeros_like(value))


def softmax_rows(scores):
    shifted = jnp.exp(scores - jnp.max(scores, axis=-1, keepdims=True))
    return shifted / jnp.sum(shifted, axis=-1, keepdims=True)


def half_of(ref, which, side):
    return ref.at[which, :, pl.ds(pl.multiple_of(side * HALF, 128) if which else side * HALF, HALF)]


def weight_copies(sources, targets, sem):
    return [pltpu.make_async_copy(src, dst, sem.at[k]) for k, (src, dst) in enumerate(zip(sources, targets))]


def forward_kernel(
    save, flags, x_ref, mod_a, mod_m, b_attn, b_up, b_down, w_blk, w_dn, out_ref, *refs
):
    if save:
        xm_ref, qkv_ref, att_ref, last_ref, branch_a_ref, mid_ref, xm2_ref, branch_m_ref, pre_ref = refs[:9]
        act_refs = refs[9:11]
        wa, wu, wd, acc, sem = refs[11:]
    else:
        xm_ref, qkv_ref, att_ref, mid_ref, xm2_ref, wa, wu, wd, acc, sem = refs
    copies = weight_copies(
        [half_of(w_blk, 0, 0), half_of(w_blk, 0, 1)]
        + [ref for side in (flags[0], 1 - flags[0]) for ref in (half_of(w_blk, 1, side), w_dn.at[side])],
        (wa.at[0], wa.at[1], wu.at[0], wd.at[0], wu.at[1], wd.at[1]),
        sem,
    )
    for copy in copies:
        copy.start()
    normed, unused = normalized(x_ref[...])
    xm_ref[...] = to_half(normed * (1.0 + mod_a[1:2]) + mod_a[0:1])
    acc[...] = jnp.zeros_like(acc)
    for k in range(3):
        if k != 1:
            copies[k // 2].wait()
        half, first = (0, D * k) if k < 2 else (1, 0)
        part = slice(D * k, D * (k + 1))
        qkv_ref[:, part] = to_half(
            matmul(xm_ref[...], wa[half, :, first : first + D]) + b_attn[:, part]
        )
    for head in range(HEADS):
        lanes, mask = window(head)
        at = lambda k: slice(D * k + lanes.start, D * k + lanes.stop)
        query = own_lanes(mask, qkv_ref[:, at(0)])
        probs = softmax_rows(matmul_nt(query, qkv_ref[:, at(1)]) * SCALE)
        acc[:, lanes] += own_lanes(mask, matmul(to_half(probs), qkv_ref[:, at(2)]))
    att_ref[...] = to_half(acc[...])
    branch = matmul(att_ref[...], wa[1, :, D:]) + b_attn[:, 3 * D :]
    if save:
        branch_a_ref[...] = branch
        last_ref[...] = jnp.where(flags[0] == 0, att_ref[...], xm_ref[...])
    mid_ref[...] = to_half(x_ref[...] + mod_a[2:3] * branch).astype(jnp.float32)
    normed, unused = normalized(mid_ref[...])
    xm2_ref[...] = to_half(normed * (1.0 + mod_m[1:2]) + mod_m[0:1])
    acc[...] = jnp.broadcast_to(b_down[...], acc.shape)
    for half in range(2):
        copies[2 + 2 * half].wait()
        copies[3 + 2 * half].wait()
        for step in range(STEPS):
            own = slice(TILE * step, TILE * (step + 1))
            part = slice(HALF * half + TILE * step, HALF * half + TILE * (step + 1))
            pre = matmul(xm2_ref[...], wu[half, :, own]) + b_up[:, part]
            cube = pre + 0.044715 * (pre * pre * pre)
            act = to_half(pre * (0.5 * (1.0 + jnp.tanh(GELU_SCALE * cube))))
            if save:
                pre_ref[:, part] = pre
                act_refs[half][:, own] = act
            acc[...] += matmul_nt(act, wd[half, :, own])
    if save:
        branch_m_ref[...] = acc[...]
    out = mid_ref[...] + mod_m[2:3] * acc[...]
    out_ref[...] = out.astype(out_ref.dtype)


def backward_kernel(
    flags, d_ref, x_ref, mid_ref, mod_a, mod_m, branch_a, branch_m, qkv_ref, pre_hbm, w_blk, w_dn,
    d_in_ref, d_mod_a, d_mod_m, grad_a, grad_m, d_pre_own, d_pre_sib, d_qkv_ref, right_own, right_sib,
    wa, wu, wd, pre_ref, acc, d_acc, d_att, sem,
):
    copies = weight_copies(
        (
            w_dn.at[flags[0]], pre_hbm, half_of(w_blk, 1, flags[0]),
            w_dn.at[1 - flags[0]], half_of(w_blk, 1, 1 - flags[0]),
            half_of(w_blk, 0, 1), half_of(w_blk, 0, 0),
        ),
        (wd.at[0], pre_ref, wu.at[0], wd.at[1], wu.at[1], wa.at[1], wa.at[0]),
        sem,
    )
    for copy in copies:
        copy.start()
    grad_m[...] = to_half(d_ref[...] * mod_m[2:3])
    d_mod_m[2:3] = jnp.sum(d_ref[...] * branch_m[...], axis=0)[None]
    acc[...] = jnp.zeros_like(acc)
    for half in range(2):
        copies[0 if half == 0 else 3].wait()
        if half == 0:
            copies[1].wait()
        copies[2 if half == 0 else 4].wait()
        for step in range(STEPS):
            own = slice(TILE * step, TILE * (step + 1))
            part = slice(HALF * half + TILE * step, HALF * half + TILE * (step + 1))
            d_act = matmul(grad_m[...], wd[half, :, own])
            pre = pre_ref[:, part]
            square = pre * pre
            tanh = jnp.tanh(GELU_SCALE * (pre + 0.044715 * (square * pre)))
            slope = 0.5 * (1.0 + tanh) + (0.5 * pre) * (1.0 - tanh * tanh) * (
                GELU_SCALE * (1.0 + (3.0 * 0.044715) * square)
            )
            d_pre = to_half(d_act * slope)
            (d_pre_sib if half else d_pre_own)[:, own] = d_pre
            acc[...] += matmul_nt(d_pre, wu[half, :, own])
    normed, inverse = normalized(mid_ref[...])
    d_x, d_shift, d_scale = modulated_back(normed, inverse, mod_m[1:2], acc[...])
    d_mod_m[0:1] = d_shift[None]
    d_mod_m[1:2] = d_scale[None]
    acc[...] = to_half(d_ref[...] + d_x).astype(jnp.float32)

    d_mod_a[2:3] = jnp.sum(acc[...] * branch_a[...], axis=0)[None]
    grad_a[...] = to_half(acc[...] * mod_a[2:3])
    copies[5].wait()
    d_att[...] = to_half(matmul_nt(grad_a[...], wa[1, :, D:]))
    d_acc[...] = jnp.zeros_like(d_acc)
    for head in range(HEADS):
        lanes, mask = window(head)
        at = lambda k: slice(D * k + lanes.start, D * k + lanes.stop)
        query, key, value = (qkv_ref[:, at(k)] for k in range(3))
        probs = softmax_rows(matmul_nt(own_lanes(mask, query), key) * SCALE)
        outer = d_att[:, lanes]
        d_acc[:, at(2)] += own_lanes(mask, matmul_tn(to_half(probs), outer))
        d_probs = matmul_nt(own_lanes(mask, outer), value)
        d_scores = to_half(probs * (d_probs - jnp.sum(probs * d_probs, axis=-1, keepdims=True)))
        d_acc[:, at(0)] += own_lanes(mask, matmul(d_scores, key) * SCALE)
        d_acc[:, at(1)] += own_lanes(mask, matmul_tn(d_scores, query) * SCALE)
    d_qkv_ref[...] = to_half(d_acc[...])
    first = flags[0] == 0
    pairs = ((d_qkv_ref[:, :D], d_qkv_ref[:, 2 * D :]), (d_qkv_ref[:, D : 2 * D], grad_a[...]))
    for k, (one, two) in enumerate(pairs):
        right_own[:, D * k : D * (k + 1)] = jnp.where(first, one, two)
        right_sib[:, D * k : D * (k + 1)] = jnp.where(first, two, one)
    copies[6].wait()
    d_xm = matmul_nt(d_qkv_ref[:, 2 * D :], wa[1, :, :D]) + matmul_nt(d_qkv_ref[:, : 2 * D], wa[0])
    normed, inverse = normalized(x_ref[...])
    d_x, d_shift, d_scale = modulated_back(normed, inverse, mod_a[1:2], d_xm)
    d_mod_a[0:1] = d_shift[None]
    d_mod_a[1:2] = d_scale[None]
    d_in_ref[...] = to_half(acc[...] + d_x)


def weight_scratch():
    return [pltpu.VMEM((2, D, HALF), BF)] * 3


def stage_cost():
    flops = 2 * PATCHES * D * 12 * D + 4 * PATCHES * PATCHES * D
    return pl.CostEstimate(flops=2 * flops, bytes_accessed=24 * D * D, transcendentals=2 * PATCHES * FF)


def stage_forward(save, x_in, weights):
    flags, mod_a, mod_m, w_blk, w_dn, b_attn, b_up, b_down = weights
    vmem, hbm = pl.BlockSpec(memory_space=pltpu.VMEM), pl.BlockSpec(memory_space=pl.ANY)
    smem = pl.BlockSpec(memory_space=pltpu.SMEM)
    like = lambda columns, kind: jax.ShapeDtypeStruct((PATCHES, columns), kind)
    tokens, wide = pltpu.VMEM((PATCHES, D), BF), pltpu.VMEM((PATCHES, 3 * D), BF)
    total = pltpu.VMEM((PATCHES, D), jnp.float32)
    f32 = jnp.float32
    if save:
        shapes = [like(D, f32), like(D, BF), like(3 * D, BF), like(D, BF), like(D, BF), like(D, f32), like(D, f32)]
        shapes += [like(D, BF), like(D, f32), like(FF, f32), like(HALF, BF), like(HALF, BF)]
        scratch = []
    else:
        shapes, scratch = [like(D, BF)], [tokens, wide, tokens, total, tokens]
    return pl.pallas_call(
        partial(forward_kernel, save),
        out_shape=tuple(shapes),
        in_specs=[smem] + [vmem] * 6 + [hbm] * 2,
        out_specs=(vmem,) * len(shapes),
        scratch_shapes=scratch + weight_scratch() + [total, pltpu.SemaphoreType.DMA((6,))],
        compiler_params=pltpu.CompilerParams(vmem_limit_bytes=VMEM_BYTES),
        cost_estimate=stage_cost(),
        name="stage_forward",
    )(flags, x_in, mod_a, mod_m, b_attn, b_up, b_down, w_blk, w_dn)


def stage_backward(full, d_out, x_in, weights, kept):
    flags, mod_a, mod_m, w_blk, w_dn, b_attn, b_up, b_down = weights
    xm_a, qkv, att, last, branch_a, x_mid, xm_m, branch_m, pre, act_own, act_sib = kept
    vmem, hbm = pl.BlockSpec(memory_space=pltpu.VMEM), pl.BlockSpec(memory_space=pl.ANY)
    smem = pl.BlockSpec(memory_space=pltpu.SMEM)
    like = lambda columns, kind: jax.ShapeDtypeStruct((PATCHES, columns), kind)
    mods = jax.ShapeDtypeStruct((3, D), jnp.float32)
    rest = (mods, mods, like(D, BF), like(D, BF), like(HALF, BF), like(HALF, BF), like(3 * D, BF))
    rest += (like(HALF, BF), like(HALF, BF))
    return pl.pallas_call(
        backward_kernel,
        out_shape=(like(D, BF),) + (rest if full else ()),
        in_specs=[smem] + [vmem] * 8 + [hbm] * 3,
        out_specs=(vmem,) * (1 + len(rest) if full else 1),
        scratch_shapes=([] if full else [pltpu.VMEM(each.shape, each.dtype) for each in rest])
        + weight_scratch()
        + [
            pltpu.VMEM((PATCHES, FF), jnp.float32),
            pltpu.VMEM((PATCHES, D), jnp.float32),
            pltpu.VMEM((PATCHES, 3 * D), jnp.float32),
            pltpu.VMEM((PATCHES, D), BF),
            pltpu.SemaphoreType.DMA((7,)),
        ],
        compiler_params=pltpu.CompilerParams(vmem_limit_bytes=VMEM_BYTES),
        cost_estimate=stage_cost(),
        name="stage_backward",
    )(flags, d_out, x_in, x_mid, mod_a, mod_m, branch_a, branch_m, qkv, pre, w_blk, w_dn)


COLUMNS = 1152


def products_kernel(
    flags, dn_own, dn_sib, up_own, up_sib, xa_own, xa_sib, att_own, last_sib,
    act_own, act_sib, pre_own, pre_sib, right_own, right_sib,
    g_dn, g_up, g_attn, t_dn, t_up, t_one, t_two,
):
    step = pl.program_id(0)

    @pl.when(step == 0)
    def _():
        last_own = jnp.where(flags[0] == 0, xa_own[...], att_own[...])
        for target, own, sib in (
            (t_dn, dn_own[...], dn_sib), (t_up, up_own[...], up_sib),
            (t_one, xa_own[...], xa_sib), (t_two, last_own, last_sib),
        ):
            target[:, :PATCHES] = own.T
            target[:, PATCHES:] = sib[...].T

    def product(left, own, sib):
        return to_half(
            matmul(left[:, :PATCHES], own[...]) + matmul(left[:, PATCHES:], sib[...])
        )

    g_dn[...] = product(t_dn, act_own, act_sib)
    g_up[...] = product(t_up, pre_own, pre_sib)

    @pl.when(step < D // COLUMNS)
    def _():
        g_attn[...] = product(t_one, right_own, right_sib)

    @pl.when(step >= D // COLUMNS)
    def _():
        g_attn[...] = product(t_two, right_own, right_sib)


def products(flags, lefts, rights):
    left = whole_spec((PATCHES, D))
    right = pl.BlockSpec((PATCHES, COLUMNS), lambda step: (0, step))
    out = pl.BlockSpec((D, COLUMNS), lambda step: (0, step))
    return pl.pallas_call(
        products_kernel,
        grid=(HALF // COLUMNS,),
        out_shape=(jax.ShapeDtypeStruct((D, HALF), BF),) * 3,
        in_specs=[pl.BlockSpec(memory_space=pltpu.SMEM)] + [left] * 8 + [right] * 6,
        out_specs=(out,) * 3,
        scratch_shapes=[pltpu.VMEM((D, 2 * PATCHES), BF)] * 4,
        compiler_params=pltpu.CompilerParams(vmem_limit_bytes=VMEM_BYTES),
        cost_estimate=pl.CostEstimate(
            flops=12 * PATCHES * D * HALF, bytes_accessed=10 * D * HALF, transcendentals=0
        ),
        name="products",
    )(flags, *lefts, *rights)


def whole_spec(shape):
    return pl.BlockSpec(shape, lambda step: (0,) * len(shape))


SUM_ROWS = 16


def collect_kernel(flags_ref, *refs):
    tokens, d_pres, mods, fm_ref, extra_ref, tok_ref, head_ref = refs[:4], refs[4:6], refs[6:8], *refs[8:12]
    sums_ref, mods_ref, ends_ref, rows_ref = refs[12:]
    core, stage = flags_ref[0], flags_ref[1]
    ones = jnp.ones((8, PATCHES), BF)
    total = lambda value: matmul(ones, value)[0:1]
    sums_ref[...] = jnp.zeros_like(sums_ref)
    rows = [total(tokens[0][:, D * k : D * (k + 1)]) for k in range(3)]
    rows += [total(ref[...]) for ref in tokens[1:]]
    halves = [[total(ref[:, D * k : D * (k + 1)]) for k in range(2)] for ref in d_pres]
    own = halves[0] + halves[1]
    order = [jnp.where(core == 0, own[k], own[(k + 2) % 4]) for k in range(4)]
    last = jnp.where(stage == 0, rows[5], extra_ref[0:1])
    for place, row in enumerate(rows[:4] + order + [rows[4], last, extra_ref[1:2]]):
        sums_ref[place : place + 1, :D] = row
    ends = jnp.where(stage == 0, matmul_tn(tok_ref[...], tokens[3][...]), head_ref[...])
    ends_ref[...] = jnp.zeros_like(ends_ref)
    width = D // ends_ref.shape[0]
    for index in range(ends_ref.shape[0]):
        ends_ref[index, :, :width] = ends[:, width * index : width * (index + 1)]
    rows_ref[...] = jnp.zeros_like(rows_ref)
    for k in range(2):
        for row in range(5):
            source = mods[k][row : row + 1, :] if row < 3 else fm_ref[row - 3 : row - 2, :]
            for part in range(D // 128):
                at = row * (D // 128) + part
                rows_ref[at : at + 1] = source[:, 128 * part : 128 * (part + 1)]
        mods_ref[k] = to_half(rows_ref[...])


def collect(flags, tokens, d_pres, mods, fm, extra, tok, g_head):
    n = lax.axis_size("dp")
    vmem = pl.BlockSpec(memory_space=pltpu.VMEM)
    return pl.pallas_call(
        collect_kernel,
        out_shape=(
            jax.ShapeDtypeStruct((SUM_ROWS, 128 * max(2 * n, 9)), jnp.float32),
            jax.ShapeDtypeStruct((2, 48, 128), BF),
            jax.ShapeDtypeStruct((n, HEAD_OUT, WIDE), jnp.float32),
        ),
        scratch_shapes=[pltpu.VMEM((48, 128), jnp.float32)],
        in_specs=[pl.BlockSpec(memory_space=pltpu.SMEM)] + [vmem] * 12,
        out_specs=(vmem,) * 3,
        compiler_params=pltpu.CompilerParams(vmem_limit_bytes=VMEM_BYTES),
        name="collect",
    )(flags, *tokens, *d_pres, *mods, fm, extra, tok, g_head)


def final_step(x_out, fmod, w_head, b_head, target, counts, loss_scale):
    normed, inverse = normalized(x_out)
    xf_half = to_half(normed * (1.0 + fmod[1:2]) + fmod[0:1])
    error = matmul_nt(xf_half, w_head) + b_head - target
    loss = counts * jnp.sum(error * error)
    d_pred = to_half(2.0 * loss_scale * counts * error)
    g_head = matmul_tn(d_pred, xf_half)
    d_x, d_shift, d_scale = modulated_back(normed, inverse, fmod[1:2], matmul(d_pred, w_head))
    return (loss, d_x, jnp.stack([d_shift, d_scale]), g_head, column_sums(d_pred))


def nesterov(weight, moment, average, grad, factor):
    clipped = grad * factor
    moment_new = momentum_rate * moment + clipped
    weight_new = weight - learn_rate * (clipped + momentum_rate * moment_new)
    average_new = ema_decay * average + (1.0 - ema_decay) * weight_new
    return (weight_new, moment_new, average_new, weight_new.astype(jnp.bfloat16))


def down_update_kernel(factor, weight, moment, average, grad, *outs):
    values = nesterov(
        weight[...], moment[...], average[...], grad[...].astype(jnp.float32), factor[0]
    )
    for out, value in zip(outs, values):
        out[...] = value


def updated(like):
    f32 = jax.ShapeDtypeStruct(like.shape, jnp.float32)
    return (f32, f32, f32, jax.ShapeDtypeStruct(like.shape, BF))


def down_update(factor, weight, moment, average, grads):
    width = weight.shape[1]
    rows = width
    state = pl.BlockSpec((1, rows, HALF), lambda l, h, r: (l, r, h))
    return pl.pallas_call(
        down_update_kernel,
        grid=(LAYERS, 2, width // rows),
        out_shape=updated(weight),
        in_specs=[pl.BlockSpec(memory_space=pltpu.SMEM), state, state, state]
        + [pl.BlockSpec((1, rows, HALF), lambda l, h, r: (2 * l + h, r, 0))],
        out_specs=(state,) * 4,
        compiler_params=pltpu.CompilerParams(vmem_limit_bytes=VMEM_BYTES),
        cost_estimate=pl.CostEstimate(flops=10 * weight.size, bytes_accessed=28 * weight.size, transcendentals=0),
        name="down_update",
    )(factor, weight, moment, average, grads)


def stem_update_kernel(factor, weight, moment, average, g_table, g_patch, g_one, g_two, *outs):
    width, first = weight.shape[0], 0
    for grad, length in ((g_table, NCLS), (g_patch, PATCH_IN), (g_one, FREQ), (g_two, D)):
        part = slice(first, first + length)
        values = nesterov(
            weight[:, part], moment[:, part], average[:, part], grad[:width, :length], factor[0]
        )
        for out, value in zip(outs, values):
            out[:, part] = value
        first += length


def stem_update(factor, weight, moment, average, *grads):
    vmem = pl.BlockSpec(memory_space=pltpu.VMEM)
    return pl.pallas_call(
        stem_update_kernel,
        out_shape=updated(weight),
        in_specs=[pl.BlockSpec(memory_space=pltpu.SMEM)] + [vmem] * 7,
        out_specs=(vmem,) * 4,
        compiler_params=pltpu.CompilerParams(vmem_limit_bytes=VMEM_BYTES),
        cost_estimate=pl.CostEstimate(flops=10 * weight.size, bytes_accessed=30 * weight.size, transcendentals=0),
        name="stem_update",
    )(factor, weight, moment, average, *grads)


def swap(array, by):
    peers = lax.axis_size("section")
    return lax.ppermute(array, "section", [(k, k ^ by) for k in range(peers)])


def pick(parts, index):
    return lax.dynamic_index_in_dim(parts, index, 0, keepdims=False)


def body(
    latents, noise, timesteps, labels, null_mask, valid,
    mod_w, mod_m, mod_e, block_w, block_m, block_e, down_w, down_m, down_e,
    stem_w, stem_m, stem_e, tail_w, tail_m, tail_e, biases, bias_m, bias_e,
):
    place = lax.axis_index("dp")
    section = lax.axis_index("section")
    stage = section // 2
    core = lax.rem(section, 2)
    even = core == 0
    n = lax.axis_size("dp")
    width = D // n

    flags = jnp.stack([core, stage]).astype(jnp.int32)
    downs, stems = jnp.swapaxes(down_w, 1, 2), stem_w.T
    to_wide = lambda value: jnp.pad(value, ((0, 0),) * (value.ndim - 1) + ((0, WIDE - width),))
    ends = jnp.concatenate([stems[:, NCLS : NCLS + PATCH_IN], tail_w[:, 2 * D :]], axis=1)
    ends = to_wide(to_half(ends).T)
    classes = jnp.where(null_mask > 0, NCLS - 1, labels)
    freq = to_half(time_features(timesteps.astype(jnp.float32))).astype(jnp.float32)
    facts = jnp.stack([classes, valid], axis=1).astype(jnp.float32)
    meta = jnp.concatenate([freq, facts, jnp.zeros((2, META - FREQ - 2), jnp.float32)], axis=1)
    b_one, b_two = (lax.dynamic_slice_in_dim(biases, k * D + place * width, width)[None] for k in (31, 32))
    w_blk, w_dn, meta, ends, pre_own, hidden_all, cond, mods, mod_half_w, w_fm, two_blocks = gather_weights(
        block_w[0], downs, stems, mod_w[0], tail_w, meta, ends, to_wide(b_one), b_two
    )
    ends = ends[:, :, :width].transpose(1, 0, 2).reshape(ROWS_END, D)
    w_patch_all, w_head_all = ends[:PATCH_IN], ends[PATCH_IN:]
    images = 2 * n
    count = jnp.sum(meta[:, FREQ + 1])
    loss_scale = 1.0 / (count * PATCHES * HEAD_OUT)
    mods = mods.reshape(2, 8 * PIECE)
    bias_of = lambda first, length: lax.dynamic_slice_in_dim(biases, first, length)
    mod_a = (mods[0, : 3 * D] + bias_of(6 * D * stage, 3 * D)).reshape(3, D)
    mod_b = (mods[1, : 3 * D] + bias_of(6 * D * stage + 3 * D, 3 * D)).reshape(3, D)
    fmod = (mods[0, 3 * D : 5 * D] + biases[33 * D : 35 * D]).reshape(2, D)
    weights = (
        flags, mod_a, mod_b, w_blk, w_dn,
        bias_of(12 * D + 8 * D * stage, 4 * D)[None],
        jnp.concatenate(
            [bias_of(16 * D + 8 * D * stage + HALF * half, HALF)[None] for half in (core, 1 - core)], axis=1
        ),
        bias_of(28 * D + D * stage, D)[None],
    )

    step = pick(timesteps, core).astype(jnp.float32)
    signal, spread = noise_levels(step)
    lat, noi = pick(latents, core)[None], pick(noise, core)[None]
    counts = pick(valid, core).astype(jnp.float32)
    tok_half = to_half(patchify(signal * lat + spread * noi))[0]
    target = jnp.concatenate([patchify(signal * noi - spread * lat), patchify(noi)], axis=2)[0]
    x_first = matmul(tok_half, w_patch_all) + biases[30 * D : 31 * D] + position_table(GRID // 2, D)

    x_hop = swap(stage_forward(False, x_first, weights)[0], 2)
    x_in = jnp.where(stage == 0, x_first, x_hop.astype(jnp.float32))
    x_out, *kept = stage_forward(True, x_in, weights)
    loss, d_final, d_fmod, g_head, b_head = final_step(
        x_out, fmod, w_head_all, biases[35 * D :], target, counts, loss_scale
    )
    xm_a, qkv, attended, last_sib, branch_a, x_mid, xm_b, branch_b, pre, act_own, act_sib = kept
    d_hop = swap(stage_backward(False, d_final, x_in, weights, kept)[0], 2)
    d_out = jnp.where(stage == 1, d_final, d_hop.astype(jnp.float32))
    d_first, d_mod_a, d_mod_b, d_branch_a, d_branch_b, d_pre_own, d_pre_sib, d_qkv, right_own, right_sib = (
        stage_backward(True, d_out, x_in, weights, kept)
    )

    act_come, xb_come, xa_come, last_come = swap((act_sib, xm_b, xm_a, last_sib), 1)
    branch_come, pre_come, right_come = swap((d_branch_b, d_pre_sib, right_sib), 1)
    g_dn, g_up, g_attn = products(
        flags,
        (d_branch_b, branch_come, xm_b, xb_come, xm_a, xa_come, attended, last_come),
        (act_own, act_come, d_pre_own, pre_come, right_own, right_come),
    )

    extra = jnp.stack([jnp.pad(b_head, (0, D - HEAD_OUT)), jnp.pad(loss[None], (0, D - 1))])
    d_fmod = jnp.where(stage == 1, d_fmod, jnp.zeros_like(d_fmod))
    tok_wide = jnp.pad(tok_half, ((0, 0), (0, HEAD_OUT - PATCH_IN)))
    own_sums, d_mods, own_ends = collect(
        flags, (d_qkv, d_branch_a, d_branch_b, d_first), (d_pre_own, d_pre_sib), (d_mod_a, d_mod_b), d_fmod,
        extra, tok_wide, g_head,
    )
    own_sums = own_sums.reshape(SUM_ROWS, -1, 128).transpose(1, 0, 2)[: 2 * n]
    halves, crossed, dn_all, g_mod, g_fm, g_table, g_one, g_two, ends_all, biases_new, squares = (
        sum_gradients(
            g_dn, g_up, g_attn, d_mods, own_sums, own_ends, mod_half_w, w_fm, two_blocks, cond, pre_own,
            hidden_all, meta,
        )
    )
    crossed = crossed.astype(jnp.float32)
    g_blk = jnp.concatenate(
        [jnp.where(even, halves[1], crossed), jnp.where(even, crossed, halves[0])], axis=1
    )
    ends = [ends_all[k, :, :width].T for k in (0, 3)]
    g_tail = jnp.concatenate([g_fm, ends[1]], axis=1)

    bias_grad, loss_sum = biases_new.reshape(-1)[:NBIAS], biases_new[36, 0]
    grad_norm = jnp.sqrt(squares[0, 0])
    factor = jnp.minimum(1.0, clip_limit / (grad_norm + 1e-06))
    mod_out = nesterov(mod_w, mod_m, mod_e, g_mod[None], factor)
    block_out = nesterov(block_w, block_m, block_e, g_blk[None], factor)
    flip = lambda value: jnp.swapaxes(value, 1, 2)
    scalar = factor.reshape(1)
    down_out = tuple(map(flip, down_update(scalar, downs, flip(down_m), flip(down_e), dn_all)))
    stem_out = stem_update(
        scalar, stems, stem_m.T, stem_e.T, g_table, ends[0][:, :PATCH_IN], g_one, g_two
    )
    stem_out = tuple(value.T for value in stem_out)
    tail_out = nesterov(tail_w, tail_m, tail_e, g_tail, factor)
    bias_out = nesterov(biases, bias_m, bias_e, bias_grad, factor)
    return (
        (loss_sum, count, grad_norm)
        + mod_out + block_out + down_out + stem_out + tail_out + bias_out
    )


def solution(mesh):
    images = (P("dp", None, None, None),) * 2 + (P("dp"),) * 4
    owned = P("section", "dp", None)
    states = (owned,) * 6 + (P(None, None, "dp"),) * 3 + (P(None, "dp"),) * 3 + (P("dp", None),) * 3 + (P(),) * 3
    updates = (owned,) * 8 + (P(None, None, "dp"),) * 4 + (P(None, "dp"),) * 4 + (P("dp", None),) * 4 + (P(),) * 4
    return jax.shard_map(
        body,
        mesh=mesh,
        in_specs=images + states,
        out_specs=(P(), P(), P()) + updates,
        check_vma=False,
    )
```

```python
from functools import partial
import math

import jax
import jax.numpy as jnp
from jax import lax
from jax.experimental import pallas as pl
from jax.experimental.pallas import tpu as pltpu
from jax.sharding import PartitionSpec as P

HEADS = 16
HEAD_DIM = 72
D = 1152
FF = 4608
HALF = FF // 2
NCLS = 1001
FREQ = 256
GRID = 32
PATCHES = 256
PATCH_IN = 16
HEAD_OUT = 32
LAYERS = 2
NBIAS = 40352


epsilon_norm = 1e-06
momentum_rate = 0.9
ema_decay = 0.9
learn_rate = 4000.0
clip_limit = 0.02
MESH = pl.DeviceIdType.MESH
BF = jnp.bfloat16


def matmul(left, right):
    return jnp.dot(left, right, preferred_element_type=jnp.float32)


def matmul_nt(left, right):
    return lax.dot_general(
        left, right, (((1,), (1,)), ((), ())), preferred_element_type=jnp.float32
    )


def matmul_tn(left, right):
    return lax.dot_general(
        left, right, (((0,), (0,)), ((), ())), preferred_element_type=jnp.float32
    )


def to_half(value):
    return value.astype(BF)


def column_sums(value):
    return jnp.sum(value.astype(jnp.float32), axis=0)


def silu_back(value, grad):
    return jax.vjp(jax.nn.silu, value)[1](grad)[0]


def patchify(field):
    images, side = (field.shape[0], field.shape[1] // 2)
    return (
        field.reshape(images, side, 2, side, 2, 4)
        .transpose(0, 1, 3, 2, 4, 5)
        .reshape(images, side * side, 16)
    )


def sincos_rows(places, width):
    omega = 1.0 / 10000.0 ** (jnp.arange(width // 2, dtype=jnp.float32) / (width // 2))
    angle = places[:, None] * omega[None, :]
    return jnp.concatenate([jnp.sin(angle), jnp.cos(angle)], axis=1)


def position_table(side, width):
    line = sincos_rows(jnp.arange(side, dtype=jnp.float32), width // 2)
    column = jnp.broadcast_to(line[None], (side, side, width // 2))
    row = jnp.broadcast_to(line[:, None], (side, side, width // 2))
    return jnp.concatenate([column, row], axis=2).reshape(side * side, width)


def time_features(steps):
    half = FREQ // 2
    freqs = jnp.exp(-math.log(10000.0) * jnp.arange(half, dtype=jnp.float32) / half)
    angle = steps[:, None] * freqs[None, :]
    return jnp.concatenate([jnp.cos(angle), jnp.sin(angle)], axis=1)


def noise_levels(steps):
    level = jnp.cos((steps / 1000.0 + 0.008) / 1.008 * (math.pi / 2)) ** 2
    return (jnp.sqrt(level), jnp.sqrt(1.0 - level))


Z, X = 4, 2
GATHER_CHUNKS = (
    (0, 0, 48, True), (0, 48, 48, True), (0, 96, 48, False),
    (1, 0, 48, False), (1, 48, 48, False), (1, 96, 48, False),
)
CHUNKS = ((0, 16, True), (16, 32, False), (48, 32, False), (80, 32, False), (112, 32, False))
META = 384
WIDE = 256
ROWS_END = PATCH_IN + HEAD_OUT
PIECE = 768


def ring_fits(n, rows):
    return n == Z * X and rows == 144


def one_hot(classes, width):
    lane = lax.broadcasted_iota(jnp.int32, (classes.shape[0], width), 1).astype(jnp.float32)
    return to_half(jnp.maximum(1.0 - jnp.abs(lane - classes), 0.0))


def gather_kernel(
    blk_hbm, dn_hbm, stem_hbm, mod_hbm, tail_hbm, meta_ref, ends_ref, b_one, b_two,
    out_blk, out_dn, meta_out, ends_out, pre_out, hidden_out, cond_out, mods_out, mod_ref, fm_ref, two_ref,
    blk_f, dn_f, stem_f, mod_f, tail_f, blk_ref, dn_ref, one_ref, table_ref, load_sem, metas, hidden, part, parts, arrived_parts,
    meta_send, meta_recv, ends_send, ends_recv, hid_send, hid_recv, part_send, part_recv, local_sem,
    up_sem, down_sem, x_sem, sib_sem, recv_sem, sib_recv, own_sem,
):
    me = lax.axis_index("dp")
    section = lax.axis_index("section")
    z, x = me // X, lax.rem(me, X)
    core = lax.rem(section, 2)
    sibling = section + 1 - 2 * core
    across = me + 1 - 2 * x
    chunks = len(GATHER_CHUNKS)
    low = section - core
    group, place_in = Z * X * 2, me * 2 + core
    where = lambda p: {"dp": p // 2, "section": low + lax.rem(p, 2)}
    has_up, has_down = z < Z - 1, z > 0

    stage_rows = dn_hbm.at[section // 2, :, pl.ds(pl.multiple_of(core * HALF, 128), HALF)]
    loads = [
        pltpu.make_async_copy(src, dst, load_sem.at[k])
        for k, (src, dst) in enumerate(
            ((blk_hbm, blk_f), (stage_rows, dn_f), (stem_hbm, stem_f), (mod_hbm, mod_f), (tail_hbm, tail_f))
        )
    ]
    for copy_in in loads:
        copy_in.start()
    barrier = pltpu.get_barrier_semaphore()

    @pl.loop(1, group)
    def _(step):
        pl.semaphore_signal(
            barrier, 1, device_id=where(lax.rem(place_in + step, group)), device_id_type=MESH
        )

    pl.semaphore_wait(barrier, group - 1)

    def to_dp(src, dst, send, recv, step, p, slot):
        return pltpu.make_async_remote_copy(
            src_ref=src, dst_ref=dst.at[slot], send_sem=send.at[step], recv_sem=recv.at[step],
            device_id={"dp": p}, device_id_type=MESH,
        )

    meta_copy = partial(to_dp, meta_ref, metas, meta_send, meta_recv)
    ends_copy = partial(to_dp, ends_ref, ends_out, ends_send, ends_recv)
    hidden_copy = partial(to_dp, hidden, hidden_out, hid_send, hid_recv)

    def part_copy(step, p, slot):
        return pltpu.make_async_remote_copy(
            src_ref=parts.at[p], dst_ref=arrived_parts.at[slot],
            send_sem=part_send.at[step], recv_sem=part_recv.at[step],
            device_id=where(p), device_id_type=MESH,
        )

    own_meta = pltpu.make_async_copy(meta_ref, metas.at[me], local_sem.at[0])
    own_ends = pltpu.make_async_copy(ends_ref, ends_out.at[me], local_sem.at[1])
    own_hidden = pltpu.make_async_copy(hidden, hidden_out.at[me], local_sem.at[2])
    own_part = pltpu.make_async_copy(parts.at[place_in], arrived_parts.at[place_in], local_sem.at[3])

    def send_all(copy_to, size, index):
        @pl.loop(1, size)
        def _(step):
            copy_to(step, lax.rem(index + step, size), index).start()

    def wait_all(copy_to, size, index):
        @pl.loop(1, size)
        def _(step):
            p = lax.rem(index + size - step, size)
            copy_to(step, p, p).wait_recv()
            copy_to(step, p, p).wait_send()

    own_meta.start()
    own_ends.start()
    send_all(meta_copy, Z * X, me)

    def place(owner, k, side):
        which, first, rows, unused = GATHER_CHUNKS[k]
        return (out_dn if which else out_blk).at[side, pl.ds(pl.multiple_of(owner * 144 + first, 16), rows)]

    def source(owner, k, mine):
        if not mine:
            return place(owner, k, core)
        which, first, rows, unused = GATHER_CHUNKS[k]
        return (dn_ref if which else blk_ref).at[pl.ds(first, rows)]

    def copy(owner, k, mine, sem, target):
        unit = owner * chunks + k
        return pltpu.make_async_remote_copy(
            src_ref=source(owner, k, mine),
            dst_ref=place(owner, k, core),
            send_sem=sem.at[unit],
            recv_sem=recv_sem.at[unit],
            device_id={"dp": target},
            device_id_type=MESH,
        )

    def to_sibling(owner, k, mine):
        unit = owner * chunks + k
        return pltpu.make_async_remote_copy(
            src_ref=source(owner, k, mine),
            dst_ref=place(owner, k, core),
            send_sem=sib_sem.at[unit],
            recv_sem=sib_recv.at[unit],
            device_id={"section": sibling},
            device_id_type=MESH,
        )

    def own_copy(k):
        return pltpu.make_async_copy(source(me, k, True), place(me, k, core), own_sem.at[k])

    def arrived(owner, k):
        copy(owner, k, False, x_sem, across).wait_recv()

    for which in range(2):
        loads[which].wait()

        @pl.loop(0, 144 // 16)
        def _(step):
            rows = pl.ds(pl.multiple_of(step * 16, 16), 16)
            if which:
                dn_ref[rows] = to_half(dn_f[rows])
            else:
                blk_ref[rows] = to_half(blk_f[rows])

    for k in range(chunks):
        @pl.when(has_up)
        def _():
            copy(me, k, True, up_sem, me + X).start()

        @pl.when(has_down)
        def _():
            copy(me, k, True, down_sem, me - X).start()

        copy(me, k, True, x_sem, across).start()
        own_copy(k).start()
        to_sibling(me, k, True).start()

    send_all(ends_copy, Z * X, me)

    at_one, at_two = NCLS + PATCH_IN, NCLS + PATCH_IN + FREQ
    for copy_in in loads[2:]:
        copy_in.wait()
    for ref in (table_ref, one_ref, two_ref):
        ref[...] = jnp.zeros_like(ref)
    table_ref[:, :NCLS] = to_half(stem_f[:, :NCLS])
    one_ref[:144] = to_half(stem_f[:, at_one:at_two])
    for index in range(Z * X):
        two_ref[index, :, :144] = to_half(stem_f[:, at_two + 144 * index : at_two + 144 * (index + 1)])
    mod_ref[...] = to_half(mod_f[...])
    fm_ref[...] = to_half(tail_f[:, : 2 * D])

    def make_hidden():
        own_meta.wait()
        wait_all(meta_copy, Z * X, me)
        for index in range(Z * X):
            meta_out[2 * index : 2 * index + 2] = metas[index]
        pre = matmul_nt(to_half(meta_out[:, :FREQ]), one_ref[...]) + b_one[...]
        pre_out[...] = pre
        hidden[...] = to_half(jax.nn.silu(pre))
        own_hidden.start()
        send_all(hidden_copy, Z * X, me)

    def make_parts():
        own_hidden.wait()
        wait_all(hidden_copy, Z * X, me)
        cond = matmul_nt(one_hot(meta_out[:, FREQ : FREQ + 1], table_ref.shape[1]), table_ref[...]) + b_two[...]
        for index in range(Z * X):
            cond = cond + matmul_nt(hidden_out[index], two_ref[index])
        cond_out[...] = cond
        cond_low = to_half(cond).astype(jnp.float32)
        own_cond = jnp.where(section == 0, cond, cond_low)
        part[:, : 3 * D] = matmul(to_half(jax.nn.silu(own_cond)), mod_ref[...])
        part[:, 3 * D : 5 * D] = matmul(to_half(jax.nn.silu(cond_low)), fm_ref[...])
        part[:, 5 * D :] = jnp.zeros((group, 8 * PIECE - 5 * D), jnp.float32)
        for row in range(group):
            for k in range(8):
                parts[row, k : k + 1] = part[row : row + 1, PIECE * k : PIECE * (k + 1)]
        own_part.start()
        send_all(part_copy, group, place_in)

    def along(step, k):
        crosses = not (step == 1 and GATHER_CHUNKS[k][3])
        for sign in (-1, 1):
            @pl.when((z >= step) if sign < 0 else (z + step < Z))
            def _():
                owner = me + sign * X * step
                arrived(owner, k)

                @pl.when(has_up if sign < 0 else has_down)
                def _():
                    copy(owner, k, False, up_sem if sign < 0 else down_sem, me - sign * X).start()

                if crosses:
                    copy(owner, k, False, x_sem, across).start()
                to_sibling(owner, k, False).start()

    def crossed(step, k):
        if step == 0:
            arrived(across, k)
            if GATHER_CHUNKS[k][3]:
                @pl.when(has_up)
                def _():
                    copy(across, k, False, up_sem, me + X).start()

                @pl.when(has_down)
                def _():
                    copy(across, k, False, down_sem, me - X).start()
            to_sibling(across, k, False).start()
            return
        for sign in (-1, 1):
            @pl.when((z >= step) if sign < 0 else (z + step < Z))
            def _():
                owner = across + sign * X * step
                arrived(owner, k)
                to_sibling(owner, k, False).start()

    for step in range(1, Z + 1):
        for k in range(chunks):
            if step < Z:
                along(step, k)
            crossed(step - 1, k)
        if step == 1:
            make_hidden()
        if step == 2:
            make_parts()

    own_part.wait()
    wait_all(part_copy, group, place_in)
    own_ends.wait()
    wait_all(ends_copy, Z * X, me)
    for source_core in range(2):
        total = arrived_parts[source_core]
        for index in range(1, Z * X):
            total = total + arrived_parts[2 * index + source_core]
        mods_out[source_core] = total

    for k in range(chunks):
        near = GATHER_CHUNKS[k][3]
        own_copy(k).wait()
        for column in range(2):
            base = me if column == 0 else across
            for step in range(0, Z):
                for sign in (-1, 1) if step else (1,):
                    @pl.when((z >= step) if sign < 0 else (z + step < Z))
                    def _():
                        owner = base + sign * X * step
                        mine = column == 0 and step == 0
                        to_sibling(owner, k, mine).wait_send()
                        pltpu.make_async_remote_copy(
                            src_ref=place(owner, k, 1 - core),
                            dst_ref=place(owner, k, 1 - core),
                            send_sem=sib_sem.at[owner * chunks + k],
                            recv_sem=sib_recv.at[owner * chunks + k],
                            device_id={"section": sibling},
                            device_id_type=MESH,
                        ).wait_recv()
                        runs = column == 0 or (near and step == 0)
                        if runs and (step == 0 or sign < 0):
                            @pl.when(has_up)
                            def _():
                                copy(owner, k, mine, up_sem, me + X).wait_send()
                        if runs and (step == 0 or sign > 0):
                            @pl.when(has_down)
                            def _():
                                copy(owner, k, mine, down_sem, me - X).wait_send()
                        if column == 0 and not (step == 1 and near):
                            copy(owner, k, mine, x_sem, across).wait_send()


def gather_weights(block, downs, stems, mod, tail, meta, ends, b_one, b_two):
    n, width = lax.axis_size("dp"), block.shape[0]
    section = lax.axis_index("section")
    if not ring_fits(n, width):
        both = lambda own, sib: jnp.where(
            lax.rem(section, 2) == 0, jnp.stack([own, sib]), jnp.stack([sib, own])
        )
        core = lax.rem(section, 2)
        dn = lax.dynamic_slice(downs, (section // 2, 0, core * HALF), (1, width, HALF))[0]
        blk = lax.all_gather(to_half(block), "dp", axis=0, tiled=True)
        dn = lax.all_gather(to_half(dn), "dp", axis=0, tiled=True)
        at_one, at_two = NCLS + PATCH_IN, NCLS + PATCH_IN + FREQ
        stem, w_mod, w_fm = to_half(stems), to_half(mod), to_half(tail[:, : 2 * D])
        table = jnp.pad(stem[:, :NCLS], ((0, 0), (0, -NCLS % 128)))
        w_one = jnp.pad(stem[:, at_one:at_two], ((0, WIDE - width), (0, 0)))
        w_two = stem[:, at_two:].reshape(width, n, width).transpose(1, 0, 2)
        w_two = jnp.pad(w_two, ((0, 0), (0, 0), (0, WIDE - width)))
        meta, ends = exchange(2, "dp", ("all", "all"), meta, ends)
        meta = meta.reshape(2 * n, META)
        pre = matmul_nt(to_half(meta[:, :FREQ]), w_one) + b_one
        (hidden,) = exchange(8, "dp", ("all",), to_half(jax.nn.silu(pre)))
        cond = matmul_nt(one_hot(meta[:, FREQ : FREQ + 1], table.shape[1]), table) + b_two
        cond = cond + jnp.einsum("jik,jwk->iw", hidden, w_two, preferred_element_type=jnp.float32)
        cond_low = to_half(cond).astype(jnp.float32)
        own_cond = jnp.where(section == 0, cond, cond_low)
        parts = [
            matmul(to_half(jax.nn.silu(own_cond)), w_mod),
            matmul(to_half(jax.nn.silu(cond_low)), w_fm),
        ]
        parts = jnp.pad(jnp.concatenate(parts, axis=1), ((0, 0), (0, 8 * PIECE - 5 * D)))
        (parts,) = exchange(3, "stage", ("each",), parts.reshape(2 * n, 8, PIECE))
        mods = jnp.sum(parts.reshape(n, 2, 8, PIECE), axis=0)
        own = (both(blk, swap(blk, 1)), both(dn, swap(dn, 1)), meta, ends, pre, hidden, cond, mods)
        return own + (w_mod, w_fm, w_two)
    units, images = n * len(GATHER_CHUNKS), 2 * n
    hbm, vmem = pl.BlockSpec(memory_space=pl.ANY), pl.BlockSpec(memory_space=pltpu.VMEM)
    dma = lambda count: pltpu.SemaphoreType.DMA((count,))
    f32 = jnp.float32
    return pl.pallas_call(
        gather_kernel,
        out_shape=(
            jax.ShapeDtypeStruct((2, D, FF), BF), jax.ShapeDtypeStruct((2, D, HALF), BF),
            jax.ShapeDtypeStruct((images, META), f32), jax.ShapeDtypeStruct((n,) + ends.shape, BF),
            jax.ShapeDtypeStruct((images, WIDE), f32), jax.ShapeDtypeStruct((n, images, WIDE), BF),
            jax.ShapeDtypeStruct((images, width), f32), jax.ShapeDtypeStruct((2, 8, PIECE), f32),
            jax.ShapeDtypeStruct((width, 3 * D), BF), jax.ShapeDtypeStruct((width, 2 * D), BF),
            jax.ShapeDtypeStruct((n, width, WIDE), BF),
        ),
        in_specs=[hbm] * 5 + [vmem] * 4,
        out_specs=(hbm, hbm) + (vmem,) * 9,
        scratch_shapes=[
            pltpu.VMEM((width, FF), f32), pltpu.VMEM((width, HALF), f32), pltpu.VMEM(stems.shape, f32),
            pltpu.VMEM((width, 3 * D), f32), pltpu.VMEM(tail.shape, f32),
            pltpu.VMEM((width, FF), BF), pltpu.VMEM((width, HALF), BF), pltpu.VMEM((WIDE, FREQ), BF),
            pltpu.VMEM((width, 1024), BF), dma(5),
            pltpu.VMEM((n, 2, META), f32), pltpu.VMEM((images, WIDE), BF),
            pltpu.VMEM((images, 8 * PIECE), f32),
            pltpu.VMEM((images, 8, PIECE), f32), pltpu.VMEM((images, 8, PIECE), f32),
            dma(n), dma(n), dma(n), dma(n), dma(n), dma(n), dma(images), dma(images), dma(4),
        ]
        + [dma(units)] * 6
        + [dma(len(GATHER_CHUNKS))],
        compiler_params=pltpu.CompilerParams(
            collective_id=0, has_side_effects=True, vmem_limit_bytes=VMEM_BYTES
        ),
        cost_estimate=pl.CostEstimate(flops=0, bytes_accessed=400_000_000, transcendentals=0),
        name="gather_weights",
    )(block, downs, stems, mod, tail, meta, ends, b_one, b_two)


VMEM_BYTES = 60 * 1024 * 1024
SUM_CHUNKS = tuple((which,) + chunk for which in range(3) for chunk in CHUNKS)


def silu_slope(value):
    gate = jax.nn.sigmoid(value)
    return gate * (1.0 + value * (1.0 - gate))


def sum_kernel(
    g_dn, g_up, g_attn, dm_ref, bp_ref, en_ref, mod_ref, fm_ref, two_ref, cond_ref, pre_ref, hid_ref, meta_ref,
    out, cross_out, dn_out, gmod_out, gfm_out, gtab_out, gone_out, gtwo_out,
    ends_all, bias_out, sq_out,
    own_b, other_d, xb, xq, up_b, up_o, down_b, down_o, acc, acc_dn,
    dm_in, bp_in, en_in, dmat, ends_src, c_src, c_in, fmd_src, fmd_in, cs_src, dcond, ph, ph_in, news_src,
    sq_src, sq_all, sq_rows, cross_src, news_out, cs_all, fmsum_out,
    load_sem, x_send, x_recv, up_send, up_recv, down_send, down_recv,
    sib_send, sib_recv, y_send, y_recv, group_send, group_recv, sect_send, sect_recv,
    ph_send, ph_recv, news_send, news_recv, sq_send, sq_recv, cross_sem, local_sem,
):
    me = lax.axis_index("dp")
    section = lax.axis_index("section")
    z, x = me // X, lax.rem(me, X)
    core = lax.rem(section, 2)
    low, sibling, facing = section - core, section + 1 - 2 * core, lax.rem(section + 2, 4)
    across = me + 1 - 2 * x
    sources = (g_dn, g_up, g_attn)
    chunks = len(SUM_CHUNKS)
    has_up, has_down = z < Z - 1, z > 0
    devices, group = Z * X * 4, Z * X * 2
    me_all, me_group = me * 4 + section, me * 2 + core
    in_all = lambda p: {"dp": p // 4, "section": lax.rem(p, 4)}
    in_group = lambda p: {"dp": p // 2, "section": low + lax.rem(p, 2)}
    in_section = lambda p: {"section": p}
    in_dp = lambda p: {"dp": p}
    f32 = jnp.float32

    barrier = pltpu.get_barrier_semaphore()

    @pl.loop(1, devices)
    def _(step):
        pl.semaphore_signal(
            barrier, 1, device_id=in_all(lax.rem(me_all + step, devices)), device_id_type=MESH
        )

    def small(src_of, dst, send, recv, where, size, index):
        def copy(step, p, slot):
            return pltpu.make_async_remote_copy(
                src_ref=src_of(p), dst_ref=dst.at[slot], send_sem=send.at[step], recv_sem=recv.at[step],
                device_id=where(p), device_id_type=MESH,
            )
        return (copy, size, index, src_of, dst)

    gradients = [
        small(lambda p: dm_ref.at[lax.rem(p, 2)], dm_in, group_send.at[0], group_recv.at[0], in_group, group, me_group),
        small(lambda p: bp_ref.at[p], bp_in, group_send.at[1], group_recv.at[1], in_group, group, me_group),
        small(lambda p: en_ref.at[p // 2], en_in, group_send.at[2], group_recv.at[2], in_group, group, me_group),
    ]
    conds = [
        small(lambda p, src=src: src, dst, sect_send.at[k], sect_recv.at[k], in_section, 4, section)
        for k, (src, dst) in enumerate(
            ((c_src, c_in), (ends_src, ends_all), (fmd_src, fmd_in), (cs_src, cs_all))
        )
    ]
    hiddens = [small(lambda p: ph.at[p], ph_in, ph_send, ph_recv, in_dp, Z * X, me)]
    news = [small(lambda p: news_src, news_out, news_send, news_recv, in_all, devices, me_all)]
    norms = [small(lambda p: sq_src, sq_all, sq_send, sq_recv, in_all, devices, me_all)]

    def own_copies(batch, first):
        return [
            pltpu.make_async_copy(src_of(index), dst.at[index], local_sem.at[first + k])
            for k, (copy, size, index, src_of, dst) in enumerate(batch)
        ]

    def send_batch(batch, first):
        for copy in own_copies(batch, first):
            copy.start()
        for copy, size, index, src_of, dst in batch:
            @pl.loop(1, size)
            def _(step):
                copy(step, lax.rem(index + step, size), index).start()

    def wait_batch(batch, first):
        for copy in own_copies(batch, first):
            copy.wait()
        for copy, size, index, src_of, dst in batch:
            @pl.loop(1, size)
            def _(step):
                p = lax.rem(index + size - step, size)
                copy(step, p, p).wait_recv()
                copy(step, p, p).wait_send()

    def add_square(value):
        sq_src[...] += jnp.sum(value * value)

    def images_of():
        cond = cond_ref[...]
        cond_low = to_half(cond).astype(f32)
        return jnp.where(section == 0, cond, cond_low), cond_low

    def make_cond():
        wait_batch(gradients, 0)
        flat = dm_in[...].reshape(group * 48, 128)
        row = lax.broadcasted_iota(jnp.int32, (group, group * 48), 0) * 48
        column = lax.broadcasted_iota(jnp.int32, (group, group * 48), 1)
        for k in range(5 * D // 128):
            chosen = jnp.where(column == row + k, 1.0, 0.0).astype(BF)
            dmat[:, 128 * k : 128 * (k + 1)] = to_half(matmul(chosen, flat))
        news_src[...] = jnp.zeros_like(news_src)
        news_src[0:SUM_ROWS] = jnp.sum(bp_in[...], axis=0)
        ends_src[...] = jnp.sum(en_in[...], axis=0)
        own_cond, cond_low = images_of()
        d_mod, d_fm = dmat[:, : 3 * D], dmat[:, 3 * D :]
        fmd_src[...] = d_fm
        cs_src[...] = jnp.sum(d_mod.astype(f32), axis=0, keepdims=True)
        d_silu = matmul_nt(d_mod, mod_ref[...])
        d_silu = d_silu + (section == 3).astype(f32) * matmul_nt(d_fm, fm_ref[...])
        c_src[...] = jnp.zeros_like(c_src)
        c_src[:, :144] = silu_slope(own_cond) * d_silu
        send_batch(conds, 3)
        silu_own = to_half(jax.nn.silu(own_cond))
        for k in range(3):
            part_g = matmul_tn(silu_own, dmat[:, D * k : D * (k + 1)])
            gmod_out[:, D * k : D * (k + 1)] = part_g
            add_square(part_g)

    once = (section == 0).astype(f32)

    def make_hidden():
        wait_batch(conds, 3)
        total = to_half(c_in[3])
        for slot in (2, 1, 0):
            total = to_half(total.astype(f32) + c_in[slot])
        dcond[...] = total
        d_cond = dcond[:, :144]
        for index in range(Z * X):
            ph[index] = matmul(d_cond, two_ref[index])
        send_batch(hiddens, 7)
        own_cond, cond_low = images_of()
        silu_low = to_half(jax.nn.silu(cond_low))
        for k in range(2):
            part_g = matmul_tn(silu_low, fmd_in[3, :, D * k : D * (k + 1)])
            gfm_out[:, D * k : D * (k + 1)] = part_g
            add_square(jnp.sqrt(once) * part_g)
        fmsum_out[...] = jnp.sum(fmd_in[3].astype(f32), axis=0, keepdims=True)
        part_g = matmul_tn(d_cond, one_hot(meta_ref[:, FREQ : FREQ + 1], gtab_out.shape[1]))
        gtab_out[...] = part_g
        add_square(once * part_g)
        for index in range(Z * X):
            part_g = matmul_tn(d_cond, hid_ref[index])
            gtwo_out[:, 144 * index : 144 * (index + 1)] = part_g[:, :144]
            add_square(once * part_g)

    def make_news():
        wait_batch(hiddens, 7)
        total = ph_in[0]
        for index in range(1, Z * X):
            total = total + ph_in[index]
        d_pre = to_half(silu_slope(pre_ref[...]) * total)
        part_g = matmul_tn(d_pre, to_half(meta_ref[:, :FREQ]))
        gone_out[...] = part_g
        add_square(once * part_g)
        sums = jnp.sum(d_pre.astype(f32), axis=0, keepdims=True)
        sums_cond = jnp.sum(dcond[...].astype(f32), axis=0, keepdims=True)
        for k in range(2):
            news_src[SUM_ROWS + k : SUM_ROWS + k + 1] = sums[:, 128 * k : 128 * (k + 1)]
            news_src[SUM_ROWS + 2 + k : SUM_ROWS + 3 + k] = sums_cond[:, 128 * k : 128 * (k + 1)]
        send_batch(news, 8)
        first = (me == 0).astype(f32)
        add_square(news_src[0:10])
        add_square(once * sums)
        add_square(once * sums_cond)
        add_square(first * cs_src[...])
        add_square(first * once * fmsum_out[...])
        add_square(once * ends_all[0])
        add_square(once * ends_all[3])

    def make_biases():
        wait_batch(news, 8)
        bias_out[...] = jnp.zeros_like(bias_out)
        for slot in range(4):
            for k in range(3):
                row = 3 * slot + k
                bias_out[row : row + 1] = cs_all[slot, :, D * k : D * (k + 1)]
        for side in range(2):
            for block in range(D // 128):
                part = slice(128 * block, 128 * (block + 1))
                device = (block // 2) * 4 + 2 * side + block % 2
                bias_out[12 + 8 * side : 20 + 8 * side, part] = news_out[device, 0:8]
                bias_out[28 + side : 29 + side, part] = news_out[device, 8:9]
                row = 35 if side else 30
                bias_out[row : row + 1, part] = news_out[device, 9:10]
                if side:
                    bias_out[36:37, part] = news_out[device, 10:11]
        for index in range(Z * X):
            first = 144 * index
            for k in range(2):
                at = SUM_ROWS + 2 * k
                bias_out[31 + k : 32 + k, first : first + 128] = news_out[4 * index, at : at + 1]
                bias_out[31 + k : 32 + k, first + 128 : first + 144] = news_out[4 * index, at + 1 : at + 2, :16]
        for k in range(2):
            bias_out[33 + k : 34 + k] = fmsum_out[:, D * k : D * (k + 1)]

    def dn_copy(k, slot, to_sib):
        rows = pl.ds(SUM_CHUNKS[k][1], SUM_CHUNKS[k][2])
        unit = slot * chunks + k
        return pltpu.make_async_remote_copy(
            src_ref=dn_out.at[slot, rows], dst_ref=dn_out.at[slot, rows],
            send_sem=(sib_send if to_sib else y_send).at[unit],
            recv_sem=(sib_recv if to_sib else y_recv).at[unit],
            device_id={"section": sibling if to_sib else facing},
            device_id_type=MESH,
        )

    def each(distance, run):
        if distance == 0:
            run(z, None)
            return

        @pl.when(z + distance < Z)
        def _():
            run(z + distance, True)

        @pl.when(z >= distance)
        def _():
            run(z - distance, False)

    def part(k):
        return pl.ds(SUM_CHUNKS[k][1], SUM_CHUNKS[k][2])

    def hbm(k, zz, column):
        start = pl.multiple_of((zz * X + column) * 144 + SUM_CHUNKS[k][1], 16)
        return sources[SUM_CHUNKS[k][0]].at[pl.ds(start, SUM_CHUNKS[k][2])]

    def own(k, zz):
        return own_b.at[SUM_CHUNKS[k][0], zz, part(k)]

    def from_x(k, zz):
        return xq.at[SUM_CHUNKS[k][0]] if SUM_CHUNKS[k][3] else xb.at[SUM_CHUNKS[k][0], zz, part(k)]

    def from_z(k, zz, up, other):
        if other:
            return (up_o if up else down_o).at[SUM_CHUNKS[k][0], zz]
        return (up_b if up else down_b).at[SUM_CHUNKS[k][0], zz, part(k)]

    def other_of(k, zz):
        return other_d.at[SUM_CHUNKS[k][0], zz]

    def load(k, zz, other=False):
        index = ((chunks if other else 0) + k) * Z + zz
        return pltpu.make_async_copy(
            hbm(k, zz, (1 - x) if other else x),
            other_of(k, zz) if other else own(k, zz),
            load_sem.at[index],
        )

    def x_copy(k, zz, src):
        unit = k * Z + zz
        return pltpu.make_async_remote_copy(
            src_ref=src, dst_ref=from_x(k, zz), send_sem=x_send.at[unit], recv_sem=x_recv.at[unit],
            device_id={"dp": across}, device_id_type=MESH,
        )

    def z_copy(k, zz, up, other):
        unit = ((chunks if other else 0) + k) * Z + zz
        return pltpu.make_async_remote_copy(
            src_ref=other_of(k, zz) if other else own(k, zz),
            dst_ref=from_z(k, zz, up, other),
            send_sem=(up_send if up else down_send).at[unit],
            recv_sem=(up_recv if up else down_recv).at[unit],
            device_id={"dp": me + X if up else me - X},
            device_id_type=MESH,
        )

    def total(k, dst, srcs):
        @pl.loop(0, SUM_CHUNKS[k][2] // 16)
        def _(step):
            rows = pl.ds(pl.multiple_of(step * 16, 16), 16)
            value = srcs[0][rows].astype(jnp.float32)
            for src in srcs[1:]:
                value = value + src[rows].astype(jnp.float32)
            dst[rows] = value.astype(dst.dtype)

    for distance in (3, 2, 1, 0):
        for k in range(chunks):
            def run(zz, up):
                load(k, zz).start()
                if SUM_CHUNKS[k][3]:
                    load(k, zz, True).start()
            each(distance, run)

    sq_src[...] = jnp.zeros_like(sq_src)
    sq_rows[...] = jnp.zeros_like(sq_rows)
    pl.semaphore_wait(barrier, devices - 1)
    send_batch(gradients, 0)

    order = [
        (k, distance) for which, distance in ((0, 3), (0, 2), (0, 1), (1, 3), (0, 0), (1, 2), (1, 1), (2, 3), (1, 0), (2, 2), (2, 1), (2, 0))
        for k in range(chunks) if SUM_CHUNKS[k][0] == which and not SUM_CHUNKS[k][3]
    ]
    sent = []

    def send_x(until):
        while len(sent) < min(until, len(order)):
            k, distance = order[len(sent)]
            sent.append(1)
            each(distance, lambda zz, up: x_copy(k, zz, hbm(k, zz, 1 - x)).start())

    def after(k, distance):
        if not SUM_CHUNKS[k][3]:
            send_x(order.index((k, distance)) + 1 + 6)

    send_x(6)

    def pass_on(k, distance):
        def run(zz, up):
            behind = has_down if up else has_up
            if SUM_CHUNKS[k][3]:
                for other in (False, True):
                    mine = other_of(k, zz) if other else own(k, zz)
                    load(k, zz, other).wait()

                    @pl.when(behind)
                    def _():
                        z_copy(k, zz, up, other).wait_recv()
                        total(k, mine, [mine, from_z(k, zz, up, other)])

                    z_copy(k, zz, up, other).start()
                return
            load(k, zz).wait()
            x_copy(k, zz, hbm(k, zz, 1 - x)).wait_recv()

            @pl.when(behind)
            def _():
                z_copy(k, zz, up, False).wait_recv()
                total(k, own(k, zz), [own(k, zz), from_x(k, zz), from_z(k, zz, up, False)])

            @pl.when(jnp.logical_not(behind))
            def _():
                total(k, own(k, zz), [own(k, zz), from_x(k, zz)])

            z_copy(k, zz, up, False).start()
        each(distance, run)

    def add_z(dst, k, other):
        @pl.when(has_down)
        def _():
            z_copy(k, z, True, other).wait_recv()
            total(k, dst, [dst, from_z(k, z, True, other)])

        @pl.when(has_up)
        def _():
            z_copy(k, z, False, other).wait_recv()
            total(k, dst, [dst, from_z(k, z, False, other)])

    def send_direct(k):
        load(k, z, True).wait()
        total(k, acc, [other_of(k, z)])
        add_z(acc, k, True)
        total(k, other_of(k, z), [acc])
        x_copy(k, z, other_of(k, z)).start()

    def finish(k):
        which, rows = SUM_CHUNKS[k][0], SUM_CHUNKS[k][2]
        dst = out.at[which - 1, part(k)] if which else acc_dn.at[pl.ds(0, rows)]
        load(k, z).wait()
        if SUM_CHUNKS[k][3]:
            total(k, dst, [own(k, z)])
            add_z(dst, k, False)
            x_copy(k, z, other_of(k, z)).wait_recv()
            total(k, dst, [dst, from_x(k, z)])
        else:
            x_copy(k, z, hbm(k, z, 1 - x)).wait_recv()
            total(k, dst, [own(k, z), from_x(k, z)])
            add_z(dst, k, False)
        if not which:
            total(k, dn_out.at[section, part(k)], [dst])
            dn_copy(k, section, True).start()
            dn_copy(k, section, False).start()

        @pl.loop(0, rows // 16)
        def _(step):
            value = dst[pl.ds(pl.multiple_of(step * 16, 16), 16)]
            sq_rows[...] += jnp.sum(value * value, axis=0, keepdims=True)

    def of(which, direct=None):
        return [
            k for k in range(chunks)
            if SUM_CHUNKS[k][0] == which and (direct is None or SUM_CHUNKS[k][3] == direct)
        ]

    def pass_all(which, distance):
        for k in of(which):
            pass_on(k, distance)
            after(k, distance)

    def finish_all(which):
        for k in of(which, False) + of(which, True):
            finish(k)
            after(k, 0)

    def direct_all(which):
        for k in of(which, True):
            send_direct(k)

    for distance in (3, 2, 1):
        pass_all(0, distance)
    make_cond()
    pass_all(1, 3)
    direct_all(0)
    finish_all(0)
    pass_all(1, 2)
    make_hidden()
    pass_all(1, 1)
    for k in of(0):
        dn_copy(k, facing, False).wait_recv()
        dn_copy(k, facing, True).start()
    pass_all(2, 3)
    make_news()
    direct_all(1)
    finish_all(1)
    pass_all(2, 2)
    pass_all(2, 1)
    make_biases()
    direct_all(2)
    finish_all(2)

    @pl.loop(0, 144 // 16)
    def _(step):
        rows = pl.ds(pl.multiple_of(step * 16, 16), 16)
        cross_src[rows] = to_half(jnp.where(core == 0, out[0, rows], out[1, rows]))

    crossing = pltpu.make_async_remote_copy(
        src_ref=cross_src, dst_ref=cross_out, send_sem=cross_sem.at[0], recv_sem=cross_sem.at[1],
        device_id={"section": sibling}, device_id_type=MESH,
    )
    sq_src[...] += jnp.sum(sq_rows[...])
    send_batch(norms, 9)
    crossing.start()
    wait_batch(norms, 9)
    sq_out[...] = jnp.sum(sq_all[...], axis=0)
    crossing.wait()

    for k in range(chunks):
        for distance in (3, 2, 1, 0):
            def run(zz, up):
                if not SUM_CHUNKS[k][3]:
                    x_copy(k, zz, hbm(k, zz, 1 - x)).wait_send()
                elif distance == 0:
                    x_copy(k, zz, other_of(k, zz)).wait_send()
                if distance:
                    z_copy(k, zz, up, False).wait_send()
                    if SUM_CHUNKS[k][3]:
                        z_copy(k, zz, up, True).wait_send()
            each(distance, run)
        if not SUM_CHUNKS[k][0]:
            dn_copy(k, section, True).wait_send()
            dn_copy(k, section, False).wait_send()
            dn_copy(k, facing, True).wait_send()
            dn_copy(k, sibling, True).wait_recv()
            dn_copy(k, lax.rem(sibling + 2, 4), True).wait_recv()


def sum_gradients(g_dn, g_up, g_attn, d_mods, sums, ends, w_mod, w_fm, two_blocks, cond, pre, hidden, meta):
    n, width = lax.axis_size("dp"), cond.shape[1]
    f32 = jnp.float32
    if not ring_fits(n, width):
        return sum_plainly(g_dn, g_up, g_attn, d_mods, sums, ends, w_mod, w_fm, two_blocks, cond, pre, hidden, meta)
    chunks, images, devices = len(SUM_CHUNKS), 2 * n, 4 * n
    dma = lambda *count: pltpu.SemaphoreType.DMA(count)
    ring = pltpu.VMEM((3, Z, 144, HALF), BF)
    short = [rows for start, rows, direct in CHUNKS if direct][0]
    most = max(rows for start, rows, direct in CHUNKS)
    ring_o = pltpu.VMEM((3, Z, short, HALF), BF)
    hbm, vmem = pl.BlockSpec(memory_space=pl.ANY), pl.BlockSpec(memory_space=pltpu.VMEM)
    like = jax.ShapeDtypeStruct
    end_block = ends.shape[1:]
    shapes = (
        like((2, 144, HALF), f32), like((144, HALF), BF), like((4, 144, HALF), BF),
        like((144, 3 * D), f32), like((144, 2 * D), f32), like((144, 1024), f32), like((WIDE, FREQ), f32),
        like((144, D), f32), like((4,) + end_block, f32), like((40, D), f32), like((8, 128), f32),
    )
    return pl.pallas_call(
        sum_kernel,
        out_shape=shapes,
        in_specs=[hbm] * 3 + [vmem] * 10,
        out_specs=(vmem,) * len(shapes),
        scratch_shapes=[
            ring, ring_o, ring, pltpu.VMEM((3, short, HALF), BF),
            ring, ring_o, ring, ring_o, pltpu.VMEM((short, HALF), f32), pltpu.VMEM((most, HALF), f32),
            pltpu.VMEM((images, 48, 128), BF), pltpu.VMEM((images, SUM_ROWS, 128), f32),
            pltpu.VMEM((images,) + end_block, f32), pltpu.VMEM((images, 5 * D), BF),
            pltpu.VMEM(end_block, f32), pltpu.VMEM((images, WIDE), f32), pltpu.VMEM((4, images, WIDE), f32),
            pltpu.VMEM((images, 2 * D), BF), pltpu.VMEM((4, images, 2 * D), BF), pltpu.VMEM((1, 3 * D), f32),
            pltpu.VMEM((images, WIDE), BF), pltpu.VMEM((n, images, WIDE), f32), pltpu.VMEM((n, images, WIDE), f32),
            pltpu.VMEM((24, 128), f32), pltpu.VMEM((8, 128), f32), pltpu.VMEM((devices, 8, 128), f32),
            pltpu.VMEM((1, HALF), f32),
            pltpu.VMEM((144, HALF), BF), pltpu.VMEM((devices, 24, 128), f32), pltpu.VMEM((4, 1, 3 * D), f32),
            pltpu.VMEM((1, 2 * D), f32),
            dma(2 * chunks * Z), dma(chunks * Z), dma(chunks * Z),
            dma(2 * chunks * Z), dma(2 * chunks * Z), dma(2 * chunks * Z), dma(2 * chunks * Z),
            dma(4 * chunks), dma(4 * chunks), dma(4 * chunks), dma(4 * chunks),
            dma(3, images), dma(3, images), dma(4, 4), dma(4, 4),
            dma(n), dma(n), dma(devices), dma(devices), dma(devices), dma(devices), dma(2), dma(10),
        ],
        compiler_params=pltpu.CompilerParams(
            collective_id=1, has_side_effects=True, vmem_limit_bytes=VMEM_BYTES
        ),
        cost_estimate=pl.CostEstimate(flops=0, bytes_accessed=400_000_000, transcendentals=0),
        name="sum_gradients",
    )(g_dn, g_up, g_attn, d_mods, sums, ends, w_mod, w_fm, two_blocks, cond, pre, hidden, meta)


def sum_plainly(g_dn, g_up, g_attn, d_mods, sums, ends, w_mod, w_fm, two_blocks, cond, pre, hidden, meta):
    n, width = lax.axis_size("dp"), cond.shape[1]
    section, images, f32 = lax.axis_index("section"), 2 * n, jnp.float32
    once = (section == 0).astype(f32)
    anchor = (lax.axis_index("dp") == 0).astype(f32)
    total = lambda grad: lax.psum_scatter(grad, "dp", scatter_dimension=0, tiled=True)
    dn_own, out = total(g_dn), jnp.stack([total(g_up), total(g_attn)]).astype(f32)
    dn_all = lax.all_gather(dn_own, "section")
    cross = swap(to_half(jnp.where(lax.rem(section, 2) == 0, out[0], out[1])), 1)
    d_mods, sums, ends = exchange(4, "stage", ("core", "each", "dp"), d_mods, sums, ends)
    d_mods = d_mods.reshape(images, 48 * 128)
    d_mod, d_fm = d_mods[:, : 3 * D], d_mods[:, 3 * D : 5 * D]
    sums, ends = jnp.sum(sums, axis=0), jnp.sum(ends, axis=0)
    cond_low = to_half(cond).astype(f32)
    own_cond = jnp.where(section == 0, cond, cond_low)
    d_silu = matmul_nt(d_mod, w_mod) + (section == 3).astype(f32) * matmul_nt(d_fm, w_fm)
    c_own = jnp.pad(silu_slope(own_cond) * d_silu, ((0, 0), (0, WIDE - width)))
    cs = column_sums(d_mod)[None]
    c_all, ends_all, d_fm, cs_all = exchange(5, "section", ("all",) * 4, c_own, ends, d_fm, cs)
    d_fm = d_fm[3]
    d_cond = to_half(c_all[3])
    for slot in (2, 1, 0):
        d_cond = to_half(d_cond.astype(f32) + c_all[slot])
    narrow = d_cond[:, :width]
    part = jnp.einsum("iw,jwk->jik", narrow, two_blocks, preferred_element_type=f32)
    (part,) = exchange(6, "dp", ("each",), part)
    d_pre = to_half(silu_slope(pre) * jnp.sum(part, axis=0))
    g_mod = matmul_tn(to_half(jax.nn.silu(own_cond)), d_mod)
    g_fm = matmul_tn(to_half(jax.nn.silu(cond_low)), d_fm)
    g_table = matmul_tn(narrow, one_hot(meta[:, FREQ : FREQ + 1], 1024))
    g_one = matmul_tn(d_pre, to_half(meta[:, :FREQ]))
    g_two = jnp.einsum("iw,jik->wjk", narrow, hidden, preferred_element_type=f32)
    g_two = g_two[:, :, :width].reshape(width, D)
    fm_sum = column_sums(d_fm)[None]
    slices = [column_sums(value).reshape(2, 128) for value in (d_pre, d_cond)]
    news = jnp.concatenate([sums, *slices, jnp.zeros((4, 128), f32)])
    square = lambda value: jnp.sum(value * value)
    squares = square(out) + square(dn_own.astype(f32)) + square(g_mod) + square(sums[:10])
    squares = squares + anchor * square(cs) + anchor * once * square(fm_sum)
    for value in (g_fm, g_table, g_one, g_two, ends_all[0], ends_all[3], *slices):
        squares = squares + once * square(value)
    news, squares = exchange(7, "every", ("all", "all"), news, jnp.broadcast_to(squares, (8, 128)))
    squares = jnp.sum(squares, axis=0)
    news = news.reshape(n, 4, -1, 128)
    stages = []
    for k in range(2):
        pieces = news[:, 2 * k : 2 * k + 2, :SUM_ROWS].reshape(2 * n, SUM_ROWS, 128)[: D // 128]
        stages.append(pieces.transpose(1, 0, 2).reshape(-1))
    slices = news[:, 0, SUM_ROWS : SUM_ROWS + 4].reshape(n, 2, WIDE)[:, :, :width]
    bias_rows = jnp.concatenate(
        [cs_all.reshape(-1)]
        + [part[: 8 * D] for part in stages]
        + [part[8 * D : 9 * D] for part in stages]
        + [stages[0][9 * D : 10 * D]]
        + [slices[:, 0].reshape(-1), slices[:, 1].reshape(-1)]
        + [fm_sum[0], stages[1][9 * D : 11 * D], jnp.zeros((3 * D,), f32)]
    ).reshape(40, D)
    return (out, cross, dn_all, g_mod, g_fm, g_table, g_one, g_two, ends_all, bias_rows, squares)


def exchange_kernel(axes, modes, *refs):
    count = len(modes)
    ins, outs = refs[:count], refs[count : 2 * count]
    send_sem, recv_sem, own_sem = refs[2 * count :]
    dp, section = lax.axis_index("dp"), lax.axis_index("section")
    n, sections = lax.axis_size("dp"), lax.axis_size("section")
    if axes == "dp":
        size, me, where = n, dp, lambda p: {"dp": p}
    elif axes == "section":
        size, me, where = sections, section, lambda p: {"section": p}
    elif axes == "stage":
        low = section - lax.rem(section, 2)
        size, me = 2 * n, dp * 2 + lax.rem(section, 2)
        where = lambda p: {"dp": p // 2, "section": low + lax.rem(p, 2)}
    else:
        size, me = n * sections, dp * sections + section
        where = lambda p: {"dp": p // sections, "section": lax.rem(p, sections)}

    def part(k, p):
        if modes[k] == "all":
            return ins[k]
        index = {"each": p, "dp": p // 2, "core": lax.rem(p, 2)}[modes[k]]
        return ins[k].at[index]

    def copy(k, step, src, slot, p):
        return pltpu.make_async_remote_copy(
            src_ref=src, dst_ref=outs[k].at[slot],
            send_sem=send_sem.at[k, step], recv_sem=recv_sem.at[k, step],
            device_id=where(p), device_id_type=MESH,
        )

    barrier = pltpu.get_barrier_semaphore()

    @pl.loop(1, size)
    def _(step):
        pl.semaphore_signal(barrier, 1, device_id=where(lax.rem(me + step, size)), device_id_type=MESH)

    for k in range(count):
        pltpu.make_async_copy(part(k, me), outs[k].at[me], own_sem.at[k]).start()
    pl.semaphore_wait(barrier, size - 1)

    @pl.loop(1, size)
    def _(step):
        p = lax.rem(me + step, size)
        for k in range(count):
            copy(k, step, part(k, p), me, p).start()

    for k in range(count):
        pltpu.make_async_copy(part(k, me), outs[k].at[me], own_sem.at[k]).wait()

    @pl.loop(1, size)
    def _(step):
        p = lax.rem(me + size - step, size)
        for k in range(count):
            copy(k, step, part(k, p), p, p).wait_recv()
            copy(k, step, part(k, p), p, p).wait_send()


def exchange(ident, axes, modes, *arrays):
    n, sections = lax.axis_size("dp"), lax.axis_size("section")
    size = {"dp": n, "section": sections, "stage": 2 * n, "every": n * sections}[axes]
    blocks = [a.shape if mode == "all" else a.shape[1:] for a, mode in zip(arrays, modes)]
    count = len(arrays)
    vmem = pl.BlockSpec(memory_space=pltpu.VMEM)
    return pl.pallas_call(
        partial(exchange_kernel, axes, modes),
        out_shape=tuple(jax.ShapeDtypeStruct((size,) + b, a.dtype) for a, b in zip(arrays, blocks)),
        in_specs=[vmem] * count,
        out_specs=(vmem,) * count,
        scratch_shapes=[
            pltpu.SemaphoreType.DMA((count, size)),
            pltpu.SemaphoreType.DMA((count, size)),
            pltpu.SemaphoreType.DMA((count,)),
        ],
        compiler_params=pltpu.CompilerParams(
            collective_id=ident, has_side_effects=True, vmem_limit_bytes=VMEM_BYTES
        ),
        cost_estimate=pl.CostEstimate(flops=0, bytes_accessed=30_000_000, transcendentals=0),
        name="exchange_" + axes,
    )(*arrays)


def rows_of(value, size):
    value = value.reshape(-1)
    return jnp.pad(value, (0, size * 128 - value.shape[0])).reshape(size, 128)


def row_count(length, unit=8):
    return -(-length // (128 * unit)) * unit


TILE = 768
STEPS = HALF // TILE
GELU_SCALE = math.sqrt(2.0 / math.pi)
SCALE = HEAD_DIM ** (-0.5)


def mean_rows(value):
    return jnp.mean(value, axis=-1, keepdims=True)


def normalized(x):
    centered = x - mean_rows(x)
    inverse = lax.rsqrt(mean_rows(centered * centered) + epsilon_norm)
    return (centered * inverse, inverse)


def modulated_back(normed, inverse, scale, d_xm):
    d_normed = d_xm * (1.0 + scale)
    d_x = inverse * (d_normed - mean_rows(d_normed) - normed * mean_rows(d_normed * normed))
    return (d_x, jnp.sum(d_xm, axis=0), jnp.sum(d_xm * normed, axis=0))


def window(head):
    low = HEAD_DIM * head // 128 * 128
    high = -(-HEAD_DIM * (head + 1) // 128) * 128
    lane = lax.broadcasted_iota(jnp.int32, (PATCHES, high - low), 1) + low
    return slice(low, high), (lane >= HEAD_DIM * head) & (lane < HEAD_DIM * (head + 1))


def own_lanes(mask, value):
    return jnp.where(mask, value, jnp.zeros_like(value))


def softmax_rows(scores):
    shifted = jnp.exp(scores - jnp.max(scores, axis=-1, keepdims=True))
    return shifted / jnp.sum(shifted, axis=-1, keepdims=True)


def half_of(ref, which, side):
    return ref.at[which, :, pl.ds(pl.multiple_of(side * HALF, 128) if which else side * HALF, HALF)]


def weight_copies(sources, targets, sem):
    return [pltpu.make_async_copy(src, dst, sem.at[k]) for k, (src, dst) in enumerate(zip(sources, targets))]


def forward_kernel(
    save, flags, x_ref, mod_a, mod_m, b_attn, b_up, b_down, w_blk, w_dn, out_ref, *refs
):
    if save:
        xm_ref, qkv_ref, att_ref, last_ref, branch_a_ref, mid_ref, xm2_ref, branch_m_ref, pre_ref = refs[:9]
        act_refs = refs[9:11]
        wa, wu, wd, acc, sem = refs[11:]
    else:
        xm_ref, qkv_ref, att_ref, mid_ref, xm2_ref, wa, wu, wd, acc, sem = refs
    copies = weight_copies(
        [half_of(w_blk, 0, 0), half_of(w_blk, 0, 1)]
        + [ref for side in (flags[0], 1 - flags[0]) for ref in (half_of(w_blk, 1, side), w_dn.at[side])],
        (wa.at[0], wa.at[1], wu.at[0], wd.at[0], wu.at[1], wd.at[1]),
        sem,
    )
    for copy in copies:
        copy.start()
    normed, unused = normalized(x_ref[...])
    xm_ref[...] = to_half(normed * (1.0 + mod_a[1:2]) + mod_a[0:1])
    acc[...] = jnp.zeros_like(acc)
    for k in range(3):
        if k != 1:
            copies[k // 2].wait()
        half, first = (0, D * k) if k < 2 else (1, 0)
        part = slice(D * k, D * (k + 1))
        qkv_ref[:, part] = to_half(
            matmul(xm_ref[...], wa[half, :, first : first + D]) + b_attn[:, part]
        )
    for head in range(HEADS):
        lanes, mask = window(head)
        at = lambda k: slice(D * k + lanes.start, D * k + lanes.stop)
        query = own_lanes(mask, qkv_ref[:, at(0)])
        probs = softmax_rows(matmul_nt(query, qkv_ref[:, at(1)]) * SCALE)
        acc[:, lanes] += own_lanes(mask, matmul(to_half(probs), qkv_ref[:, at(2)]))
    att_ref[...] = to_half(acc[...])
    branch = matmul(att_ref[...], wa[1, :, D:]) + b_attn[:, 3 * D :]
    if save:
        branch_a_ref[...] = branch
        last_ref[...] = jnp.where(flags[0] == 0, att_ref[...], xm_ref[...])
    mid_ref[...] = to_half(x_ref[...] + mod_a[2:3] * branch).astype(jnp.float32)
    normed, unused = normalized(mid_ref[...])
    xm2_ref[...] = to_half(normed * (1.0 + mod_m[1:2]) + mod_m[0:1])
    acc[...] = jnp.broadcast_to(b_down[...], acc.shape)
    for half in range(2):
        copies[2 + 2 * half].wait()
        copies[3 + 2 * half].wait()
        for step in range(STEPS):
            own = slice(TILE * step, TILE * (step + 1))
            part = slice(HALF * half + TILE * step, HALF * half + TILE * (step + 1))
            pre = matmul(xm2_ref[...], wu[half, :, own]) + b_up[:, part]
            cube = pre + 0.044715 * (pre * pre * pre)
            act = to_half(pre * (0.5 * (1.0 + jnp.tanh(GELU_SCALE * cube))))
            if save:
                pre_ref[:, part] = pre
                act_refs[half][:, own] = act
            acc[...] += matmul_nt(act, wd[half, :, own])
    if save:
        branch_m_ref[...] = acc[...]
    out = mid_ref[...] + mod_m[2:3] * acc[...]
    out_ref[...] = out.astype(out_ref.dtype)


def backward_kernel(
    flags, d_ref, x_ref, mid_ref, mod_a, mod_m, branch_a, branch_m, qkv_ref, pre_hbm, w_blk, w_dn,
    d_in_ref, d_mod_a, d_mod_m, grad_a, grad_m, d_pre_own, d_pre_sib, d_qkv_ref, right_own, right_sib,
    wa, wu, wd, pre_ref, acc, d_acc, d_att, sem,
):
    copies = weight_copies(
        (
            w_dn.at[flags[0]], pre_hbm, half_of(w_blk, 1, flags[0]),
            w_dn.at[1 - flags[0]], half_of(w_blk, 1, 1 - flags[0]),
            half_of(w_blk, 0, 1), half_of(w_blk, 0, 0),
        ),
        (wd.at[0], pre_ref, wu.at[0], wd.at[1], wu.at[1], wa.at[1], wa.at[0]),
        sem,
    )
    for copy in copies:
        copy.start()
    grad_m[...] = to_half(d_ref[...] * mod_m[2:3])
    d_mod_m[2:3] = jnp.sum(d_ref[...] * branch_m[...], axis=0)[None]
    acc[...] = jnp.zeros_like(acc)
    for half in range(2):
        copies[0 if half == 0 else 3].wait()
        if half == 0:
            copies[1].wait()
        copies[2 if half == 0 else 4].wait()
        for step in range(STEPS):
            own = slice(TILE * step, TILE * (step + 1))
            part = slice(HALF * half + TILE * step, HALF * half + TILE * (step + 1))
            d_act = matmul(grad_m[...], wd[half, :, own])
            pre = pre_ref[:, part]
            square = pre * pre
            tanh = jnp.tanh(GELU_SCALE * (pre + 0.044715 * (square * pre)))
            slope = 0.5 * (1.0 + tanh) + (0.5 * pre) * (1.0 - tanh * tanh) * (
                GELU_SCALE * (1.0 + (3.0 * 0.044715) * square)
            )
            d_pre = to_half(d_act * slope)
            (d_pre_sib if half else d_pre_own)[:, own] = d_pre
            acc[...] += matmul_nt(d_pre, wu[half, :, own])
    normed, inverse = normalized(mid_ref[...])
    d_x, d_shift, d_scale = modulated_back(normed, inverse, mod_m[1:2], acc[...])
    d_mod_m[0:1] = d_shift[None]
    d_mod_m[1:2] = d_scale[None]
    acc[...] = to_half(d_ref[...] + d_x).astype(jnp.float32)

    d_mod_a[2:3] = jnp.sum(acc[...] * branch_a[...], axis=0)[None]
    grad_a[...] = to_half(acc[...] * mod_a[2:3])
    copies[5].wait()
    d_att[...] = to_half(matmul_nt(grad_a[...], wa[1, :, D:]))
    d_acc[...] = jnp.zeros_like(d_acc)
    for head in range(HEADS):
        lanes, mask = window(head)
        at = lambda k: slice(D * k + lanes.start, D * k + lanes.stop)
        query, key, value = (qkv_ref[:, at(k)] for k in range(3))
        probs = softmax_rows(matmul_nt(own_lanes(mask, query), key) * SCALE)
        outer = d_att[:, lanes]
        d_acc[:, at(2)] += own_lanes(mask, matmul_tn(to_half(probs), outer))
        d_probs = matmul_nt(own_lanes(mask, outer), value)
        d_scores = to_half(probs * (d_probs - jnp.sum(probs * d_probs, axis=-1, keepdims=True)))
        d_acc[:, at(0)] += own_lanes(mask, matmul(d_scores, key) * SCALE)
        d_acc[:, at(1)] += own_lanes(mask, matmul_tn(d_scores, query) * SCALE)
    d_qkv_ref[...] = to_half(d_acc[...])
    first = flags[0] == 0
    pairs = ((d_qkv_ref[:, :D], d_qkv_ref[:, 2 * D :]), (d_qkv_ref[:, D : 2 * D], grad_a[...]))
    for k, (one, two) in enumerate(pairs):
        right_own[:, D * k : D * (k + 1)] = jnp.where(first, one, two)
        right_sib[:, D * k : D * (k + 1)] = jnp.where(first, two, one)
    copies[6].wait()
    d_xm = matmul_nt(d_qkv_ref[:, 2 * D :], wa[1, :, :D]) + matmul_nt(d_qkv_ref[:, : 2 * D], wa[0])
    normed, inverse = normalized(x_ref[...])
    d_x, d_shift, d_scale = modulated_back(normed, inverse, mod_a[1:2], d_xm)
    d_mod_a[0:1] = d_shift[None]
    d_mod_a[1:2] = d_scale[None]
    d_in_ref[...] = to_half(acc[...] + d_x)


def weight_scratch():
    return [pltpu.VMEM((2, D, HALF), BF)] * 3


def stage_cost():
    flops = 2 * PATCHES * D * 12 * D + 4 * PATCHES * PATCHES * D
    return pl.CostEstimate(flops=2 * flops, bytes_accessed=24 * D * D, transcendentals=2 * PATCHES * FF)


def stage_forward(save, x_in, weights):
    flags, mod_a, mod_m, w_blk, w_dn, b_attn, b_up, b_down = weights
    vmem, hbm = pl.BlockSpec(memory_space=pltpu.VMEM), pl.BlockSpec(memory_space=pl.ANY)
    smem = pl.BlockSpec(memory_space=pltpu.SMEM)
    like = lambda columns, kind: jax.ShapeDtypeStruct((PATCHES, columns), kind)
    tokens, wide = pltpu.VMEM((PATCHES, D), BF), pltpu.VMEM((PATCHES, 3 * D), BF)
    total = pltpu.VMEM((PATCHES, D), jnp.float32)
    f32 = jnp.float32
    if save:
        shapes = [like(D, f32), like(D, BF), like(3 * D, BF), like(D, BF), like(D, BF), like(D, f32), like(D, f32)]
        shapes += [like(D, BF), like(D, f32), like(FF, f32), like(HALF, BF), like(HALF, BF)]
        scratch = []
    else:
        shapes, scratch = [like(D, BF)], [tokens, wide, tokens, total, tokens]
    return pl.pallas_call(
        partial(forward_kernel, save),
        out_shape=tuple(shapes),
        in_specs=[smem] + [vmem] * 6 + [hbm] * 2,
        out_specs=(vmem,) * len(shapes),
        scratch_shapes=scratch + weight_scratch() + [total, pltpu.SemaphoreType.DMA((6,))],
        compiler_params=pltpu.CompilerParams(vmem_limit_bytes=VMEM_BYTES),
        cost_estimate=stage_cost(),
        name="stage_forward",
    )(flags, x_in, mod_a, mod_m, b_attn, b_up, b_down, w_blk, w_dn)


def stage_backward(d_out, x_in, weights, kept):
    flags, mod_a, mod_m, w_blk, w_dn, b_attn, b_up, b_down = weights
    xm_a, qkv, att, last, branch_a, x_mid, xm_m, branch_m, pre, act_own, act_sib = kept
    vmem, hbm = pl.BlockSpec(memory_space=pltpu.VMEM), pl.BlockSpec(memory_space=pl.ANY)
    smem = pl.BlockSpec(memory_space=pltpu.SMEM)
    like = lambda columns, kind: jax.ShapeDtypeStruct((PATCHES, columns), kind)
    mods = jax.ShapeDtypeStruct((3, D), jnp.float32)
    return pl.pallas_call(
        backward_kernel,
        out_shape=(like(D, BF), mods, mods, like(D, BF), like(D, BF))
        + (like(HALF, BF), like(HALF, BF), like(3 * D, BF), like(HALF, BF), like(HALF, BF)),
        in_specs=[smem] + [vmem] * 8 + [hbm] * 3,
        out_specs=(vmem,) * 10,
        scratch_shapes=weight_scratch()
        + [
            pltpu.VMEM((PATCHES, FF), jnp.float32),
            pltpu.VMEM((PATCHES, D), jnp.float32),
            pltpu.VMEM((PATCHES, 3 * D), jnp.float32),
            pltpu.VMEM((PATCHES, D), BF),
            pltpu.SemaphoreType.DMA((7,)),
        ],
        compiler_params=pltpu.CompilerParams(vmem_limit_bytes=VMEM_BYTES),
        cost_estimate=stage_cost(),
        name="stage_backward",
    )(flags, d_out, x_in, x_mid, mod_a, mod_m, branch_a, branch_m, qkv, pre, w_blk, w_dn)


COLUMNS = 384


def products_kernel(
    flags, dn_own, dn_sib, up_own, up_sib, xa_own, xa_sib, att_own, last_sib,
    act_own, act_sib, pre_own, pre_sib, right_own, right_sib,
    g_dn, g_up, g_attn, t_dn, t_up, t_one, t_two,
):
    step = pl.program_id(0)

    @pl.when(step == 0)
    def _():
        last_own = jnp.where(flags[0] == 0, xa_own[...], att_own[...])
        for target, own, sib in (
            (t_dn, dn_own[...], dn_sib), (t_up, up_own[...], up_sib),
            (t_one, xa_own[...], xa_sib), (t_two, last_own, last_sib),
        ):
            target[:, :PATCHES] = own.T
            target[:, PATCHES:] = sib[...].T

    def product(left, own, sib):
        return to_half(
            matmul(left[:, :PATCHES], own[...]) + matmul(left[:, PATCHES:], sib[...])
        )

    g_dn[...] = product(t_dn, act_own, act_sib)
    g_up[...] = product(t_up, pre_own, pre_sib)

    @pl.when(step < D // COLUMNS)
    def _():
        g_attn[...] = product(t_one, right_own, right_sib)

    @pl.when(step >= D // COLUMNS)
    def _():
        g_attn[...] = product(t_two, right_own, right_sib)


def products(flags, lefts, rights):
    left = whole_spec((PATCHES, D))
    right = pl.BlockSpec((PATCHES, COLUMNS), lambda step: (0, step))
    out = pl.BlockSpec((D, COLUMNS), lambda step: (0, step))
    return pl.pallas_call(
        products_kernel,
        grid=(HALF // COLUMNS,),
        out_shape=(jax.ShapeDtypeStruct((D, HALF), BF),) * 3,
        in_specs=[pl.BlockSpec(memory_space=pltpu.SMEM)] + [left] * 8 + [right] * 6,
        out_specs=(out,) * 3,
        scratch_shapes=[pltpu.VMEM((D, 2 * PATCHES), BF)] * 4,
        compiler_params=pltpu.CompilerParams(vmem_limit_bytes=VMEM_BYTES),
        cost_estimate=pl.CostEstimate(
            flops=12 * PATCHES * D * HALF, bytes_accessed=10 * D * HALF, transcendentals=0
        ),
        name="products",
    )(flags, *lefts, *rights)


def whole_spec(shape):
    return pl.BlockSpec(shape, lambda step: (0,) * len(shape))


SUM_ROWS = 16


def collect_kernel(flags_ref, *refs):
    tokens, d_pres, mods, fm_ref, extra_ref, tok_ref, head_ref = refs[:4], refs[4:6], refs[6:8], *refs[8:12]
    sums_ref, mods_ref, ends_ref, rows_ref = refs[12:]
    core, stage = flags_ref[0], flags_ref[1]
    ones = jnp.ones((8, PATCHES), BF)
    total = lambda value: matmul(ones, value)[0:1]
    sums_ref[...] = jnp.zeros_like(sums_ref)
    rows = [total(tokens[0][:, D * k : D * (k + 1)]) for k in range(3)]
    rows += [total(ref[...]) for ref in tokens[1:]]
    halves = [[total(ref[:, D * k : D * (k + 1)]) for k in range(2)] for ref in d_pres]
    own = halves[0] + halves[1]
    order = [jnp.where(core == 0, own[k], own[(k + 2) % 4]) for k in range(4)]
    last = jnp.where(stage == 0, rows[5], extra_ref[0:1])
    for place, row in enumerate(rows[:4] + order + [rows[4], last, extra_ref[1:2]]):
        for block in range(D // 128):
            sums_ref[block, place : place + 1] = row[:, 128 * block : 128 * (block + 1)]
    ends = jnp.where(stage == 0, matmul_tn(tok_ref[...], tokens[3][...]), head_ref[...])
    ends_ref[...] = jnp.zeros_like(ends_ref)
    width = D // ends_ref.shape[0]
    for index in range(ends_ref.shape[0]):
        ends_ref[index, :, :width] = ends[:, width * index : width * (index + 1)]
    rows_ref[...] = jnp.zeros_like(rows_ref)
    for k in range(2):
        for row in range(5):
            source = mods[k][row : row + 1, :] if row < 3 else fm_ref[row - 3 : row - 2, :]
            for part in range(D // 128):
                at = row * (D // 128) + part
                rows_ref[at : at + 1] = source[:, 128 * part : 128 * (part + 1)]
        mods_ref[k] = to_half(rows_ref[...])


def collect(flags, tokens, d_pres, mods, fm, extra, tok, g_head):
    n = lax.axis_size("dp")
    vmem = pl.BlockSpec(memory_space=pltpu.VMEM)
    return pl.pallas_call(
        collect_kernel,
        out_shape=(
            jax.ShapeDtypeStruct((2 * n, SUM_ROWS, 128), jnp.float32),
            jax.ShapeDtypeStruct((2, 48, 128), BF),
            jax.ShapeDtypeStruct((n, HEAD_OUT, WIDE), jnp.float32),
        ),
        scratch_shapes=[pltpu.VMEM((48, 128), jnp.float32)],
        in_specs=[pl.BlockSpec(memory_space=pltpu.SMEM)] + [vmem] * 12,
        out_specs=(vmem,) * 3,
        compiler_params=pltpu.CompilerParams(vmem_limit_bytes=VMEM_BYTES),
        name="collect",
    )(flags, *tokens, *d_pres, *mods, fm, extra, tok, g_head)


def final_step(x_out, fmod, w_head, b_head, target, counts, loss_scale):
    normed, inverse = normalized(x_out)
    xf_half = to_half(normed * (1.0 + fmod[1:2]) + fmod[0:1])
    error = matmul_nt(xf_half, w_head) + b_head - target
    loss = counts * jnp.sum(error * error)
    d_pred = to_half(2.0 * loss_scale * counts * error)
    g_head = matmul_tn(d_pred, xf_half)
    d_x, d_shift, d_scale = modulated_back(normed, inverse, fmod[1:2], matmul(d_pred, w_head))
    return (loss, d_x, jnp.stack([d_shift, d_scale]), g_head, column_sums(d_pred))


def nesterov(weight, moment, average, grad, factor):
    clipped = grad * factor
    moment_new = momentum_rate * moment + clipped
    weight_new = weight - learn_rate * (clipped + momentum_rate * moment_new)
    average_new = ema_decay * average + (1.0 - ema_decay) * weight_new
    return (weight_new, moment_new, average_new, weight_new.astype(jnp.bfloat16))


def down_update_kernel(factor, weight, moment, average, grad, *outs):
    values = nesterov(
        weight[...], moment[...], average[...], grad[...].astype(jnp.float32), factor[0]
    )
    for out, value in zip(outs, values):
        out[...] = value


def updated(like):
    f32 = jax.ShapeDtypeStruct(like.shape, jnp.float32)
    return (f32, f32, f32, jax.ShapeDtypeStruct(like.shape, BF))


def down_update(factor, weight, moment, average, grads):
    width = weight.shape[1]
    rows = width
    state = pl.BlockSpec((1, rows, HALF), lambda l, h, r: (l, r, h))
    return pl.pallas_call(
        down_update_kernel,
        grid=(LAYERS, 2, width // rows),
        out_shape=updated(weight),
        in_specs=[pl.BlockSpec(memory_space=pltpu.SMEM), state, state, state]
        + [pl.BlockSpec((1, rows, HALF), lambda l, h, r: (2 * l + h, r, 0))],
        out_specs=(state,) * 4,
        compiler_params=pltpu.CompilerParams(vmem_limit_bytes=VMEM_BYTES),
        cost_estimate=pl.CostEstimate(flops=10 * weight.size, bytes_accessed=28 * weight.size, transcendentals=0),
        name="down_update",
    )(factor, weight, moment, average, grads)


def stem_update_kernel(factor, weight, moment, average, g_table, g_patch, g_one, g_two, *outs):
    width, first = weight.shape[0], 0
    for grad, length in ((g_table, NCLS), (g_patch, PATCH_IN), (g_one, FREQ), (g_two, D)):
        part = slice(first, first + length)
        values = nesterov(
            weight[:, part], moment[:, part], average[:, part], grad[:width, :length], factor[0]
        )
        for out, value in zip(outs, values):
            out[:, part] = value
        first += length


def stem_update(factor, weight, moment, average, *grads):
    vmem = pl.BlockSpec(memory_space=pltpu.VMEM)
    return pl.pallas_call(
        stem_update_kernel,
        out_shape=updated(weight),
        in_specs=[pl.BlockSpec(memory_space=pltpu.SMEM)] + [vmem] * 7,
        out_specs=(vmem,) * 4,
        compiler_params=pltpu.CompilerParams(vmem_limit_bytes=VMEM_BYTES),
        cost_estimate=pl.CostEstimate(flops=10 * weight.size, bytes_accessed=30 * weight.size, transcendentals=0),
        name="stem_update",
    )(factor, weight, moment, average, *grads)


def swap(array, by):
    peers = lax.axis_size("section")
    return lax.ppermute(array, "section", [(k, k ^ by) for k in range(peers)])


def pick(parts, index):
    return lax.dynamic_index_in_dim(parts, index, 0, keepdims=False)


def body(
    latents, noise, timesteps, labels, null_mask, valid,
    mod_w, mod_m, mod_e, block_w, block_m, block_e, down_w, down_m, down_e,
    stem_w, stem_m, stem_e, tail_w, tail_m, tail_e, biases, bias_m, bias_e,
):
    place = lax.axis_index("dp")
    section = lax.axis_index("section")
    stage = section // 2
    core = lax.rem(section, 2)
    even = core == 0
    n = lax.axis_size("dp")
    width = D // n

    flags = jnp.stack([core, stage]).astype(jnp.int32)
    downs, stems = jnp.swapaxes(down_w, 1, 2), stem_w.T
    to_wide = lambda value: jnp.pad(value, ((0, 0),) * (value.ndim - 1) + ((0, WIDE - width),))
    ends = jnp.concatenate([stems[:, NCLS : NCLS + PATCH_IN], tail_w[:, 2 * D :]], axis=1)
    ends = to_wide(to_half(ends).T)
    classes = jnp.where(null_mask > 0, NCLS - 1, labels)
    freq = to_half(time_features(timesteps.astype(jnp.float32))).astype(jnp.float32)
    facts = jnp.stack([classes, valid], axis=1).astype(jnp.float32)
    meta = jnp.concatenate([freq, facts, jnp.zeros((2, META - FREQ - 2), jnp.float32)], axis=1)
    b_one, b_two = (lax.dynamic_slice_in_dim(biases, k * D + place * width, width)[None] for k in (31, 32))
    w_blk, w_dn, meta, ends, pre_own, hidden_all, cond, mods, mod_half_w, w_fm, two_blocks = gather_weights(
        block_w[0], downs, stems, mod_w[0], tail_w, meta, ends, to_wide(b_one), b_two
    )
    ends = ends[:, :, :width].transpose(1, 0, 2).reshape(ROWS_END, D)
    w_patch_all, w_head_all = ends[:PATCH_IN], ends[PATCH_IN:]
    images = 2 * n
    count = jnp.sum(meta[:, FREQ + 1])
    loss_scale = 1.0 / (count * PATCHES * HEAD_OUT)
    mods = mods.reshape(2, 8 * PIECE)
    bias_of = lambda first, length: lax.dynamic_slice_in_dim(biases, first, length)
    mod_a = (mods[0, : 3 * D] + bias_of(6 * D * stage, 3 * D)).reshape(3, D)
    mod_b = (mods[1, : 3 * D] + bias_of(6 * D * stage + 3 * D, 3 * D)).reshape(3, D)
    fmod = (mods[0, 3 * D : 5 * D] + biases[33 * D : 35 * D]).reshape(2, D)
    weights = (
        flags, mod_a, mod_b, w_blk, w_dn,
        bias_of(12 * D + 8 * D * stage, 4 * D)[None],
        jnp.concatenate(
            [bias_of(16 * D + 8 * D * stage + HALF * half, HALF)[None] for half in (core, 1 - core)], axis=1
        ),
        bias_of(28 * D + D * stage, D)[None],
    )

    step = pick(timesteps, core).astype(jnp.float32)
    signal, spread = noise_levels(step)
    lat, noi = pick(latents, core)[None], pick(noise, core)[None]
    counts = pick(valid, core).astype(jnp.float32)
    tok_half = to_half(patchify(signal * lat + spread * noi))[0]
    target = jnp.concatenate([patchify(signal * noi - spread * lat), patchify(noi)], axis=2)[0]
    x_first = matmul(tok_half, w_patch_all) + biases[30 * D : 31 * D] + position_table(GRID // 2, D)

    x_hop = swap(stage_forward(False, x_first, weights)[0], 2)
    x_in = jnp.where(stage == 0, x_first, x_hop.astype(jnp.float32))
    x_out, *kept = stage_forward(True, x_in, weights)
    loss, d_final, d_fmod, g_head, b_head = final_step(
        x_out, fmod, w_head_all, biases[35 * D :], target, counts, loss_scale
    )
    xm_a, qkv, attended, last_sib, branch_a, x_mid, xm_b, branch_b, pre, act_own, act_sib = kept
    d_hop = swap(stage_backward(d_final, x_in, weights, kept)[0], 2)
    d_out = jnp.where(stage == 1, d_final, d_hop.astype(jnp.float32))
    d_first, d_mod_a, d_mod_b, d_branch_a, d_branch_b, d_pre_own, d_pre_sib, d_qkv, right_own, right_sib = (
        stage_backward(d_out, x_in, weights, kept)
    )

    act_come, xb_come, xa_come, last_come = swap((act_sib, xm_b, xm_a, last_sib), 1)
    branch_come, pre_come, right_come = swap((d_branch_b, d_pre_sib, right_sib), 1)
    g_dn, g_up, g_attn = products(
        flags,
        (d_branch_b, branch_come, xm_b, xb_come, xm_a, xa_come, attended, last_come),
        (act_own, act_come, d_pre_own, pre_come, right_own, right_come),
    )

    extra = jnp.stack([jnp.pad(b_head, (0, D - HEAD_OUT)), jnp.pad(loss[None], (0, D - 1))])
    d_fmod = jnp.where(stage == 1, d_fmod, jnp.zeros_like(d_fmod))
    tok_wide = jnp.pad(tok_half, ((0, 0), (0, HEAD_OUT - PATCH_IN)))
    own_sums, d_mods, own_ends = collect(
        flags, (d_qkv, d_branch_a, d_branch_b, d_first), (d_pre_own, d_pre_sib), (d_mod_a, d_mod_b), d_fmod,
        extra, tok_wide, g_head,
    )
    halves, crossed, dn_all, g_mod, g_fm, g_table, g_one, g_two, ends_all, biases_new, squares = (
        sum_gradients(
            g_dn, g_up, g_attn, d_mods, own_sums, own_ends, mod_half_w, w_fm, two_blocks, cond, pre_own,
            hidden_all, meta,
        )
    )
    crossed = crossed.astype(jnp.float32)
    g_blk = jnp.concatenate(
        [jnp.where(even, halves[1], crossed), jnp.where(even, crossed, halves[0])], axis=1
    )
    ends = [ends_all[k, :, :width].T for k in (0, 3)]
    g_tail = jnp.concatenate([g_fm, ends[1]], axis=1)

    bias_grad, loss_sum = biases_new.reshape(-1)[:NBIAS], biases_new[36, 0]
    grad_norm = jnp.sqrt(squares[0, 0])
    factor = jnp.minimum(1.0, clip_limit / (grad_norm + 1e-06))
    mod_out = nesterov(mod_w, mod_m, mod_e, g_mod[None], factor)
    block_out = nesterov(block_w, block_m, block_e, g_blk[None], factor)
    flip = lambda value: jnp.swapaxes(value, 1, 2)
    scalar = factor.reshape(1)
    down_out = tuple(map(flip, down_update(scalar, downs, flip(down_m), flip(down_e), dn_all)))
    stem_out = stem_update(
        scalar, stems, stem_m.T, stem_e.T, g_table, ends[0][:, :PATCH_IN], g_one, g_two
    )
    stem_out = tuple(value.T for value in stem_out)
    tail_out = nesterov(tail_w, tail_m, tail_e, g_tail, factor)
    bias_out = nesterov(biases, bias_m, bias_e, bias_grad, factor)
    return (
        (loss_sum, count, grad_norm)
        + mod_out + block_out + down_out + stem_out + tail_out + bias_out
    )


def solution(mesh):
    images = (P("dp", None, None, None),) * 2 + (P("dp"),) * 4
    owned = P("section", "dp", None)
    states = (owned,) * 6 + (P(None, None, "dp"),) * 3 + (P(None, "dp"),) * 3 + (P("dp", None),) * 3 + (P(),) * 3
    updates = (owned,) * 8 + (P(None, None, "dp"),) * 4 + (P(None, "dp"),) * 4 + (P("dp", None),) * 4 + (P(),) * 4
    return jax.shard_map(
        body,
        mesh=mesh,
        in_specs=images + states,
        out_specs=(P(), P(), P()) + updates,
        check_vma=False,
    )
```
